32 devices in a mesh: dp: 8 (over z, x), tensor: 4 (over y, core).
Axes of the slice: x: 2, y: 2, z: 4, core: 2. Of those that a mesh axis runs over, the one named last changes fastest.
Arguments:
- images: bfloat16 [128, 256, 1764], P('tensor', 'dp'), may hold values from -6 to 6
- counts: int32 [16], P('dp'), may hold values from 2 to 16, as said below
- context: float32 [16, 100], P('dp'), may hold values from -6 to 6
- filter_two: bfloat16 [128, 128, 3, 3], P('tensor'), may hold values from -0.1875 to 0.1875
- gain_two: bfloat16 [128], P('tensor'), may hold values from 0.5 to 1.5
- shift_two: bfloat16 [128], P('tensor'), may hold values from -1.5 to 1.5
- filter_three: bfloat16 [128, 128, 3, 3], P('tensor'), may hold values from -0.1875 to 0.1875
- gain_three: bfloat16 [128], P('tensor'), may hold values from 0.5 to 1.5
- shift_three: bfloat16 [128], P('tensor'), may hold values from -1.5 to 1.5
- film_weight: bfloat16 [100, 2, 128], P(None, None, 'tensor'), may hold values from -0.1875 to 0.1875
- film_bias: bfloat16 [2, 128], P(None, 'tensor'), may hold values from -1 to 1
- cotangent: bfloat16 [128, 256, 100], P('tensor', 'dp'), may hold values from -6 to 6
Outputs:
- block_two: bfloat16 [128, 256, 441], P('tensor', 'dp')
- block_three: bfloat16 [128, 256, 100], P('tensor', 'dp')
- grad_images: float32 [128, 256, 1764], P('tensor', 'dp')
- grad_filter_two: float32 [128, 128, 3, 3], P('tensor')
- grad_gain_two: float32 [128], P('tensor')
- grad_shift_two: float32 [128], P('tensor')
- grad_filter_three: float32 [128, 128, 3, 3], P('tensor')
- grad_gain_three: float32 [128], P('tensor')
- grad_shift_three: float32 [128], P('tensor')
- grad_film_weight: float32 [100, 2, 128], P(None, None, 'tensor')
- grad_film_bias: float32 [2, 128], P(None, 'tensor')
- grad_context: float32 [16, 100], P('dp')
- levels: float32 [9], replicated
The draws below stay inside these ranges and needn't reach their ends.
Inputs may be any that keep to these rules, and one draw needn't show every extreme that they name: `counts`: each task has 16 slots; some task in every draw has all 16 live.
All inputs are finite; a program needn't handle non-finite values.
Results may differ from the reference program's by a relative error of at most 0.0083.
Values may be sent and summed in bfloat16 or wider, within the bound.
No kernel may reach another device: no remote copies, remote signals or barrier semaphores. Data moves between devices by JAX's collectives and lax.ppermute only.
A program may use at most 320 MiB of HBM per device.

```python
import jax
import jax.numpy as jnp
from jax import lax

C = 128
CTX = 100
MAP = 42
CAP = 16
TASKS = 16
IMAGES = 256
HALF = 21
QUART = 10


def draw_counts(key, part):
    key = jax.random.fold_in(key, 5)
    first_key, second_key = jax.random.split(key)
    ranks = jax.random.randint(first_key, (TASKS,), 0, CAP)
    drawn = CAP - ranks * ranks // CAP
    chosen = jax.random.randint(second_key, (), 0, TASKS)
    return drawn.at[chosen].set(CAP).astype(jnp.int32)


def shard_levels(own_key, shape, cuts, smallest, largest):
    level, own = 1.0, jax.random.fold_in(own_key, 6)
    for dim, parts in cuts:
        heights = jnp.exp(jax.random.uniform(jax.random.fold_in(own, dim), (parts,), jnp.float32, smallest / len(cuts), largest / len(cuts)))
        level = level * jnp.repeat(heights, shape[dim] // parts).reshape([-1 if axis == dim else 1 for axis in range(len(shape))])
    return level


def normal_values(stream_key, shape, scale, bound, pieces=(), kind=jnp.bfloat16):
    loudness = shard_levels(stream_key, shape, pieces, -0.22, 0.18) if pieces else 1.0
    result = jax.random.normal(stream_key, shape, jnp.float32) * scale * loudness
    return jnp.minimum(jnp.maximum(result, -bound), bound).astype(kind)


def setup_inputs(seed: int = 0) -> dict:
    streams_of = jax.random.split(jax.random.key(seed), 13)
    images = normal_values(streams_of[0], (C, IMAGES, MAP * MAP), 1.0, 6.0, ((0, 4), (1, 8)))
    counts = draw_counts(jax.random.fold_in(streams_of[12], 71), 0)
    context = normal_values(streams_of[2], (TASKS, CTX), 1.0, 6.0, ((0, 8),), jnp.float32)
    filter_two = normal_values(streams_of[3], (C, C, 3, 3), (9 * C) ** -0.5, 0.1875, ((0, 4),))
    gain_two = jnp.clip(1.0 + 0.1 * jax.random.normal(streams_of[4], (C,), jnp.float32), 0.5, 1.5).astype(jnp.bfloat16)
    shift_two = normal_values(streams_of[5], (C,), 0.3, 1.5, ((0, 4),))
    filter_three = normal_values(streams_of[6], (C, C, 3, 3), (9 * C) ** -0.5, 0.1875, ((0, 4),))
    gain_three = jnp.clip(1.0 + 0.1 * jax.random.normal(streams_of[7], (C,), jnp.float32), 0.5, 1.5).astype(jnp.bfloat16)
    shift_three = normal_values(streams_of[8], (C,), 0.3, 1.5, ((0, 4),))
    film_weight = normal_values(streams_of[9], (CTX, 2, C), (9 * CTX) ** -0.5, 0.1875, ((2, 4),))
    film_bias = normal_values(streams_of[10], (2, C), 0.2, 1.0, ((1, 4),))
    cotangent = normal_values(streams_of[11], (C, IMAGES, QUART * QUART), 1.0, 6.0, ((0, 4), (1, 8)))
    return dict(images=images, counts=counts, context=context, filter_two=filter_two, gain_two=gain_two, shift_two=shift_two, filter_three=filter_three, gain_three=gain_three, shift_three=shift_three, film_weight=film_weight, film_bias=film_bias, cotangent=cotangent)


EPSILON = 1e-05
PRECISE = lax.Precision.HIGHEST

@jax.custom_vjp
def low(v):
    return lax.optimization_barrier(v.astype(jnp.bfloat16)).astype(jnp.float32)

@jax.custom_vjp
def low_back(v):
    return v

def low_keep(v):
    return (low(v), None)

def low_pass(kept, grad):
    return (grad,)

def back_keep(v):
    return (v, None)

def back_low(kept, grad):
    return (low(grad),)
low.defvjp(low_keep, low_pass)
low_back.defvjp(back_keep, back_low)

def conv_full(inputs, filters):
    return lax.conv_general_dilated(inputs, filters, (1, 1), ((1, 1), (1, 1)), dimension_numbers=('CNHW', 'OIHW', 'CNHW'), precision=PRECISE)

def pool_mean(values):
    channels, batch_size, height, breadth = values.shape
    half_h, half_w = (height // 2, breadth // 2)
    trimmed = values[:, :, :2 * half_h, :2 * half_w].reshape(channels, batch_size, half_h, 2, half_w, 2)
    return lax.optimization_barrier(jnp.mean(trimmed, axis=(3, 5)))

def normalize(conv_out, weight, live_count):
    extent = live_count * (conv_out.shape[2] * conv_out.shape[3])
    middle = lax.optimization_barrier(jnp.sum(conv_out * weight, axis=(1, 2, 3))) / extent
    center = conv_out - middle[:, None, None, None]
    spread = lax.optimization_barrier(jnp.sum(center * center * weight, axis=(1, 2, 3))) / extent
    return center * lax.rsqrt(spread + EPSILON)[:, None, None, None]

def expand(vector):
    return vector[:, None, None, None]

def reference(images, counts, context, filter_two, gain_two, shift_two, filter_three, gain_three, shift_three, film_weight, film_bias, cotangent):
    slot_ids = jnp.arange(IMAGES, dtype=jnp.int32)
    task_ids = slot_ids // CAP
    live_mask = (slot_ids % CAP < counts[task_ids]).astype(jnp.float32)
    weight = live_mask[None, :, None, None]
    live_count = jnp.sum(live_mask)
    target = cotangent.astype(jnp.float32).reshape(C, IMAGES, QUART, QUART)

    def squares(values):
        return jnp.sum(values * values * weight)

    def forward(inputs, f_two, g_two, s_two, f_three, g_three, s_three, film_w, film_b, task_context):
        conv_two = low_back(conv_full(inputs.reshape(C, IMAGES, MAP, MAP), f_two))
        pre_two = expand(g_two) * normalize(conv_two, weight, live_count) + expand(s_two)
        active_two = jax.nn.gelu(pre_two)
        hidden_two = pool_mean(active_two) * weight
        hidden_low = low(hidden_two)
        conv_three = low_back(conv_full(hidden_low, f_three))
        pre_three = expand(g_three) * normalize(conv_three, weight, live_count) + expand(s_three)
        film_rows = jnp.einsum('tk,kjc->tjc', task_context, film_w, precision=PRECISE) + film_b[None]
        per_image = film_rows[task_ids]
        filmed = (1.0 + per_image[:, 0, :].T[:, :, None, None]) * pre_three + per_image[:, 1, :].T[:, :, None, None]
        active_three = jax.nn.gelu(filmed)
        output_three = pool_mean(active_three) * weight
        levels = jnp.stack([squares(conv_two), squares(pre_two), squares(active_two), squares(hidden_two), squares(conv_three), squares(pre_three), squares(filmed), squares(active_three), squares(output_three)])
        return (jnp.sum(output_three * target), (hidden_low, output_three, levels))
    floats = [member.astype(jnp.float32) for member in (images, filter_two, gain_two, shift_two, filter_three, gain_three, shift_three, film_weight, film_bias, context)]
    objective, pullback, extras = jax.vjp(forward, *floats, has_aux=True)
    hidden_low, output_three, levels = extras
    gradients = pullback(jnp.ones((), jnp.float32))
    cell_areas = jnp.array([MAP * MAP] * 3 + [HALF * HALF] * 5 + [QUART * QUART], jnp.float32)
    root_mean = jnp.sqrt(levels / (live_count * C * cell_areas))
    return (hidden_low.astype(jnp.bfloat16).reshape(C, IMAGES, HALF * HALF), output_three.astype(jnp.bfloat16).reshape(C, IMAGES, QUART * QUART), gradients[0].reshape(C, IMAGES, MAP * MAP), gradients[1], gradients[2], gradients[3], gradients[4], gradients[5], gradients[6], gradients[7], gradients[8], gradients[9], root_mean)
```

```python
import functools

import jax
import jax.numpy as jnp
import numpy as np
from jax import lax
from jax.experimental import pallas as pl
from jax.experimental.pallas import tpu as pltpu
from jax.sharding import PartitionSpec as P

C = 128
MAP = 42
CAP = 16
HALF = 21
QUART = 10
CHUNK = 2
SENT = 4
VMEM_BYTES = 63 << 20

CELLS_TWO = MAP * MAP
CELLS_THREE = HALF * HALF
CELLS_OUT = QUART * QUART
LANES_TWO = 1792
LANES_THREE = 512
LANES_OUT = 128
EPSILON = 1e-05
PRECISE = lax.Precision.HIGHEST
F32 = jnp.float32
BF16 = jnp.bfloat16
ROOT = 0.7978845608028654
CUBIC = 0.044715


def lane_ids(width):
    return lax.broadcasted_iota(jnp.int32, (1, width), 1)


def as_columns(rows):
    return jnp.concatenate([rows] * (C // 8), axis=0).T


def column_tile(columns):
    ids = lax.broadcasted_iota(jnp.int32, (C, C), 1)
    tile = jnp.zeros((C, C), F32)
    for place, column in enumerate(columns):
        tile = jnp.where(ids == place, column, tile)
    return tile


def row_tile(rows, count=8):
    ids = lax.broadcasted_iota(jnp.int32, (count, C), 0)
    tile = jnp.zeros((count, C), F32)
    for place, row in enumerate(rows):
        tile = jnp.where(ids == place, row, tile)
    return tile


def row(tile_ref, place):
    return tile_ref[place : place + 1, :]


def column(tile_ref, place):
    return tile_ref[:, place : place + 1]


def merge_moments(state, weight, mean, spread, cells):
    count, middle, total = state
    added = weight * cells
    both = count + added
    away = mean - middle
    share = added / jnp.maximum(both, 1.0)
    return both, middle + away * share, total + weight * spread + away * away * count * share


def slice_norm(heard_ref):
    means, spreads, counts = heard_ref[:, 0, :], heard_ref[:, 1, :], heard_ref[:, 2, :]
    extent = jnp.sum(counts, axis=0, keepdims=True)
    middle = jnp.sum(counts * means, axis=0, keepdims=True) / extent
    away = means - middle
    variance = jnp.sum(spreads + counts * away * away, axis=0, keepdims=True) / extent
    return middle, lax.rsqrt(variance + EPSILON), variance, extent


def level_row(columns):
    return jnp.sum(column_tile(columns), axis=0, keepdims=True)


def spread_rows(tile, out_ref):
    out_ref[...] = jnp.broadcast_to(tile[None], out_ref.shape)


def stack_sideways(values, side, width, stack_ref):
    column = lane_ids(width) % side
    stack_ref[0:C] = jnp.where(column == 0, 0.0, pltpu.roll(values, 1, 1)).astype(BF16)
    stack_ref[C : 2 * C] = values.astype(BF16)
    stack_ref[2 * C : 3 * C] = jnp.where(column == side - 1, 0.0, pltpu.roll(values, width - 1, 1)).astype(BF16)


def stack_upright(values, side, width, stack_ref):
    ids = lane_ids(width)
    cells = side * side
    stack_ref[0:C] = jnp.where(ids >= side, pltpu.roll(values, side, 1), 0.0).astype(BF16)
    stack_ref[C : 2 * C] = values.astype(BF16)
    stack_ref[2 * C : 3 * C] = jnp.where(ids < cells - side, pltpu.roll(values, width - side, 1), 0.0).astype(BF16)


def conv_stacked(weights_ref, stack_ref, side, width):
    ids = lane_ids(width)
    cells = side * side
    parts = jnp.dot(weights_ref[...], stack_ref[...], preferred_element_type=F32)
    above = jnp.where(ids >= side, pltpu.roll(parts[:C], side, 1), 0.0)
    below = jnp.where(ids < cells - side, pltpu.roll(parts[2 * C :], width - side, 1), 0.0)
    return jnp.where(ids < cells, parts[C : 2 * C] + above + below, 0.0)


def moments(values, cells, width):
    mean = jnp.sum(values, axis=1, keepdims=True) * (1.0 / cells)
    centered = jnp.where(lane_ids(width) < cells, values - mean, 0.0)
    return mean, jnp.sum(centered * centered, axis=1, keepdims=True)


def gelu_tanh(values):
    return jnp.tanh(ROOT * values * (1.0 + CUBIC * values * values))


def gelu_slope(values, bend):
    inner = ROOT * (1.0 + 3.0 * CUBIC * values * values)
    return 0.5 * (1.0 + bend) + 0.5 * values * (1.0 - bend * bend) * inner


def halves(values):
    high = values.astype(BF16)
    return jnp.concatenate([high, (values - high.astype(F32)).astype(BF16)], axis=0)


def dot_halves(split, weights_ref):
    both = jnp.dot(split, weights_ref[...], preferred_element_type=F32)
    return both[:C] + both[C:]


def own_rows(me, partner, count):
    return pl.ds(pl.multiple_of((me ^ partner) * count, count), count)


def kernel_params():
    return pltpu.CompilerParams(vmem_limit_bytes=VMEM_BYTES, dimension_semantics=("arbitrary",))


def pack_kernel(group, images_each, skipped, me_ref, maps_ref, *piece_refs):
    piece_refs = piece_refs[skipped:]
    turned = jnp.swapaxes(maps_ref[...], 0, 1)
    per_device = len(piece_refs) // group
    step = images_each // per_device
    for lead in range(group):

        @pl.when(me_ref[0] % group == lead)
        def _():
            for other in range(group):
                for part in range(per_device):
                    first = (lead ^ other) * images_each + part * step
                    piece_refs[other * per_device + part][...] = turned[first : first + step]


def unpack_kernel(group, images_each, count, me_ref, *refs):
    out_ref = refs[-1]
    piece_refs = refs[:count]
    per_device = len(piece_refs) // group
    for lead in range(group):

        @pl.when(me_ref[0] % group == lead)
        def _():
            ordered = []
            for place in range(group):
                other = place ^ lead
                ordered += [piece_refs[other * per_device + part][...] for part in range(per_device)]
            joined = jnp.concatenate(ordered, axis=0)
            out_ref[...] = jnp.swapaxes(joined, 0, 1).astype(out_ref.dtype)


def first_conv_kernel(partners, part, final, me_ref, live_ref, weights_ref, *refs):
    piece_refs = refs[:partners]
    conv_ref, state_ref, maps, stack, state = refs[-5:]
    rows = C // partners
    step = pl.program_id(0)

    @pl.when(step == 0)
    def _():
        maps[...] = jnp.zeros_like(maps)
        state[...] = refs[partners][...] if part else jnp.zeros_like(state)

    for partner in range(partners):
        maps[own_rows(me_ref[0], partner, rows), 0:CELLS_TWO] = piece_refs[partner][0].astype(F32)
    stack_sideways(maps[...], MAP, LANES_TWO, stack)
    conv = conv_stacked(weights_ref, stack, MAP, LANES_TWO)
    conv_ref[0] = conv
    mean, spread = moments(conv, CELLS_TWO, LANES_TWO)
    live = live_ref[part * pl.num_programs(0) + step]
    merged = merge_moments([column(state, k) for k in range(3)], live, mean, spread, CELLS_TWO)
    state[...] = column_tile(merged)

    @pl.when(step == pl.num_programs(0) - 1)
    def _():
        if final:
            turned = state[...].T
            spread_rows(row_tile([turned[1:2], turned[2:3], turned[0:1]], SENT), state_ref)
        else:
            state_ref[...] = state[...]


def middle_kernel(
    partners, me_ref, live_ref, heard_ref, vectors_ref, pool_a_ref, pool_b_ref, weights_ref, conv_ref, *refs
):
    piece_refs = refs[:partners]
    hidden_ref, conv_three_ref, norm_ref, levels_ref, sums_ref, columns, state, stack = refs[partners:]
    rows = C // partners
    step = pl.program_id(0)

    @pl.when(step == 0)
    def _():
        middle, factor, variance, extent = slice_norm(heard_ref)
        norm_ref[...] = row_tile([middle, factor, variance, extent])
        columns[...] = as_columns(row_tile([middle, row(vectors_ref, 0) * factor, row(vectors_ref, 1)]))
        state[...] = jnp.zeros_like(state)

    live = live_ref[step]
    ids = lane_ids(LANES_TWO)
    pre = (conv_ref[0] - column(columns, 0)) * column(columns, 1) + column(columns, 2)
    active = 0.5 * pre * (1.0 + gelu_tanh(pre))
    active_squares = jnp.sum(jnp.where(ids < CELLS_TWO, active * active, 0.0), axis=1, keepdims=True)
    split = halves(active)
    hidden = live * jnp.concatenate(
        [dot_halves(split[:, :1152], pool_a_ref), dot_halves(split[:, 896:], pool_b_ref)], axis=1
    )
    hidden_squares = jnp.sum(hidden * hidden, axis=1, keepdims=True)
    hidden_low = hidden.astype(BF16)
    hidden_ref[0] = hidden_low
    for partner in range(partners):
        piece_refs[partner][0] = hidden_ref[0, own_rows(me_ref[0], partner, rows), 0:CELLS_THREE]
    stack_sideways(hidden_low.astype(F32), HALF, LANES_THREE, stack)
    conv = conv_stacked(weights_ref, stack, HALF, LANES_THREE)
    conv_three_ref[0] = conv
    mean, spread = moments(conv, CELLS_THREE, LANES_THREE)
    merged = merge_moments([column(state, k) for k in range(3)], live, mean, spread, CELLS_THREE)
    state[...] = column_tile(
        [*merged, column(state, 3) + live * active_squares, column(state, 4) + hidden_squares]
    )

    @pl.when(step == pl.num_programs(0) - 1)
    def _():
        turned = state[...].T
        spread_rows(row_tile([turned[k : k + 1] for k in (1, 2, 0)], SENT), sums_ref)
        levels_ref[...] = row_tile([level_row([column(state, 3), column(state, 4)])])


def top_kernel(
    partners, me_ref, live_ref, heard_ref, own_ref, before_ref, vectors_ref, pool_ref, spread_ref, conv_ref, *refs
):
    target_refs = refs[:partners]
    piece_refs = refs[partners : 2 * partners]
    grad_ref, norm_ref, levels_ref, sums_ref, columns, target, output, totals = refs[2 * partners :]
    rows = C // partners
    step = pl.program_id(0)

    @pl.when(step == 0)
    def _():
        middle, factor, variance, extent = slice_norm(heard_ref)
        norm_ref[...] = row_tile([middle, factor, variance, extent])
        columns[...] = as_columns(row_tile([middle, factor] + [row(vectors_ref, k) for k in (2, 3, 4, 5)]))
        target[...] = jnp.zeros_like(target)
        totals[...] = jnp.zeros_like(totals)

    live = live_ref[step]
    for partner in range(partners):
        target[own_rows(me_ref[0], partner, rows), 0:CELLS_OUT] = target_refs[partner][0].astype(F32)
    ids = lane_ids(LANES_THREE)
    normed = (conv_ref[0] - column(columns, 0)) * column(columns, 1)
    scale = column(columns, 4)
    filmed = scale * (normed * column(columns, 2) + column(columns, 3)) + column(columns, 5)
    bend = gelu_tanh(filmed)
    active = 0.5 * filmed * (1.0 + bend)
    active_squares = live * jnp.sum(jnp.where(ids < CELLS_THREE, active * active, 0.0), axis=1, keepdims=True)
    pooled = live * dot_halves(halves(active), pool_ref)
    pooled_squares = jnp.sum(pooled * pooled, axis=1, keepdims=True)
    output[...] = pooled
    for partner in range(partners):
        piece_refs[partner][0] = output[own_rows(me_ref[0], partner, rows), 0:CELLS_OUT].astype(BF16)
    grad_active = live * jnp.dot(target[...].astype(BF16), spread_ref[...], preferred_element_type=F32)
    grad_filmed = grad_active * gelu_slope(filmed, bend)
    grad_ref[0] = scale * grad_filmed
    totals[...] += column_tile(
        [
            jnp.sum(grad_filmed, axis=1, keepdims=True),
            jnp.sum(grad_filmed * normed, axis=1, keepdims=True),
            active_squares,
            pooled_squares,
        ]
    )

    @pl.when(step == pl.num_programs(0) - 1)
    def _():
        turned = totals[...].T
        shift_sum, scale_sum = turned[0:1], turned[1:2]
        film_scale = row(vectors_ref, 4)
        slope = film_scale * row(vectors_ref, 2) * row(norm_ref, 1)
        offset = film_scale * row(vectors_ref, 3) + row(vectors_ref, 5)
        extent = own_ref[0, 2:3, :]
        away = own_ref[0, 0:1, :] - row(norm_ref, 0)
        filmed_squares = (
            slope * slope * (own_ref[0, 1:2, :] + extent * away * away)
            + 2.0 * slope * offset * extent * away
            + extent * offset * offset
        )
        spread_rows(
            row_tile([shift_sum, scale_sum, film_scale * shift_sum, film_scale * scale_sum], SENT), sums_ref
        )
        nothing = jnp.zeros((C, 1), F32)
        others = level_row([nothing, nothing, nothing, column(totals, 2), column(totals, 3)])
        lanes = lane_ids(C)
        filmed_total = jnp.sum(filmed_squares, axis=1, keepdims=True)
        levels_ref[...] = before_ref[...] + row_tile([others + jnp.where(lanes == 2, filmed_total, 0.0)])


def back_kernel(
    live_ref,
    heard_ref,
    norm_three_ref,
    norm_two_ref,
    levels_ref,
    vectors_ref,
    weights_ref,
    unpool_a_ref,
    unpool_b_ref,
    grad_ref,
    conv_three_ref,
    hidden_ref,
    conv_two_ref,
    out_ref,
    sums_ref,
    filter_ref,
    columns_three,
    columns_two,
    totals,
    stack,
    upright,
):
    step = pl.program_id(0)

    @pl.when(step == 0)
    def _():
        sums = jnp.sum(heard_ref[...], axis=0)
        extent = row(norm_three_ref, 3)
        factor = row(norm_three_ref, 1)
        columns_three[...] = as_columns(
            row_tile(
                [
                    row(norm_three_ref, 0),
                    factor,
                    row(vectors_ref, 2) * factor,
                    sums[2:3] / extent,
                    sums[3:4] / extent,
                ]
            )
        )
        columns_two[...] = as_columns(
            row_tile([row(norm_two_ref, 0), row(norm_two_ref, 1), row(vectors_ref, 0), row(vectors_ref, 1)])
        )
        totals[...] = jnp.zeros_like(totals)
        filter_ref[...] = jnp.zeros_like(filter_ref)

    live = live_ref[step]
    normed = (conv_three_ref[0] - column(columns_three, 0)) * column(columns_three, 1)
    error = grad_ref[0] - column(columns_three, 3) - normed * column(columns_three, 4)
    error = jnp.where(lane_ids(LANES_THREE) < CELLS_THREE, live * error * column(columns_three, 2), 0.0)
    stack_sideways(error, HALF, LANES_THREE, stack)
    stack_upright(hidden_ref[0].astype(F32), HALF, LANES_THREE, upright)
    filter_ref[...] += lax.dot_general(
        stack[...], upright[...], (((1,), (1,)), ((), ())), preferred_element_type=F32
    )
    split = halves(conv_stacked(weights_ref, stack, HALF, LANES_THREE))
    grad_active = jnp.concatenate(
        [dot_halves(split[:, :256], unpool_a_ref), dot_halves(split[:, 128:], unpool_b_ref)], axis=1
    )
    normed_two = (conv_two_ref[0] - column(columns_two, 0)) * column(columns_two, 1)
    pre = normed_two * column(columns_two, 2) + column(columns_two, 3)
    grad_pre = live * grad_active * gelu_slope(pre, gelu_tanh(pre))
    out_ref[0] = grad_pre
    totals[...] += column_tile(
        [jnp.sum(grad_pre, axis=1, keepdims=True), jnp.sum(grad_pre * normed_two, axis=1, keepdims=True)]
    )

    @pl.when(step == pl.num_programs(0) - 1)
    def _():
        turned = totals[...].T
        spread_rows(row_tile([turned[0:1], turned[1:2], levels_ref[0:1, :]], SENT), sums_ref)


def last_kernel(
    partners, part, me_ref, live_ref, heard_ref, norm_ref, vectors_ref, weights_ref, grad_ref, conv_ref, *refs
):
    map_refs = refs[:partners]
    refs = refs[partners:]
    if part:
        before_ref, refs = refs[0], refs[1:]
    piece_refs = refs[:partners]
    filter_ref, columns, maps, output, stack, upright = refs[partners:]
    rows = C // partners
    step = pl.program_id(0)

    @pl.when(step == 0)
    def _():
        sums = jnp.sum(heard_ref[...], axis=0)
        factor, extent = row(norm_ref, 1), row(norm_ref, 3)
        columns[...] = as_columns(
            row_tile([row(norm_ref, 0), factor, row(vectors_ref, 0) * factor, sums[0:1] / extent, sums[1:2] / extent])
        )
        maps[...] = jnp.zeros_like(maps)
        filter_ref[...] = before_ref[...] if part else jnp.zeros_like(filter_ref)

    for partner in range(partners):
        maps[own_rows(me_ref[0], partner, rows), 0:CELLS_TWO] = map_refs[partner][0].astype(F32)
    live = live_ref[part * pl.num_programs(0) + step]
    normed = (conv_ref[0] - column(columns, 0)) * column(columns, 1)
    error = grad_ref[0] - column(columns, 3) - normed * column(columns, 4)
    error = jnp.where(lane_ids(LANES_TWO) < CELLS_TWO, live * error * column(columns, 2), 0.0)
    stack_sideways(error, MAP, LANES_TWO, stack)
    output[...] = conv_stacked(weights_ref, stack, MAP, LANES_TWO)
    for partner in range(partners):
        piece_refs[partner][0] = output[own_rows(me_ref[0], partner, rows), 0:CELLS_TWO].astype(BF16)
    stack_upright(maps[...], MAP, LANES_TWO, upright)
    filter_ref[...] += lax.dot_general(
        stack[...], upright[...], (((1,), (1,)), ((), ())), preferred_element_type=F32
    )


def pool_matrix(side, width, out_width):
    half = side // 2
    matrix = np.zeros((width, out_width), np.float32)
    for row in range(2 * half):
        for column in range(2 * half):
            matrix[row * side + column, (row // 2) * half + column // 2] = 0.25
    return matrix


def smem():
    return pl.BlockSpec(memory_space=pltpu.SMEM)


def whole(*shape):
    return pl.BlockSpec(shape, lambda n: (0,) * len(shape))


def each(*shape, first=0):
    return pl.BlockSpec((1, *shape), lambda n: (first + n,) + (0,) * len(shape))


def pack(maps, me, partners, images_each, chunk):
    rows, slots, cells = maps.shape
    group = CAP // images_each
    parts = images_each // chunk
    pieces = []
    earlier = []
    for block in reversed(range(partners // group)):
        result = pl.pallas_call(
            functools.partial(pack_kernel, group, images_each, len(earlier)),
            grid_spec=pltpu.PrefetchScalarGridSpec(
                num_scalar_prefetch=1,
                grid=(1,),
                in_specs=[
                    pl.BlockSpec((rows, CAP, cells), lambda n, me_ref, block=block: (0, (me_ref[0] // group) ^ block, 0))
                ]
                + [pl.BlockSpec(memory_space=pl.ANY)] * len(earlier),
                out_specs=[pl.BlockSpec((chunk, rows, cells), lambda n, me_ref: (0, 0, 0))] * (group * parts),
            ),
            out_shape=[jax.ShapeDtypeStruct((chunk, rows, cells), maps.dtype)] * (group * parts),
            compiler_params=kernel_params(),
            name="pack",
        )(me, maps, *earlier)
        earlier = result[:1]
        pieces = [result[other * parts : (other + 1) * parts] for other in range(group)] + pieces
    return pieces


def unpack(pieces, me, images_each, dtype, earlier=None):
    partners = len(pieces)
    group = CAP // images_each
    chunk, rows, cells = pieces[0][0].shape
    slots = partners * images_each
    out = None
    for block in range(partners // group):
        given = [piece for other in range(group) for piece in pieces[block * group + other]]
        specs = [pl.BlockSpec((chunk, rows, cells), lambda n, me_ref: (0, 0, 0))] * len(given)
        aliases = {}
        count = len(given)
        extra = [array for array in (out, earlier) if array is not None]
        if out is not None:
            aliases = {1 + count: 0}
        given = given + extra
        specs = specs + [pl.BlockSpec(memory_space=pl.ANY)] * len(extra)
        out = pl.pallas_call(
            functools.partial(unpack_kernel, group, images_each, count),
            grid_spec=pltpu.PrefetchScalarGridSpec(
                num_scalar_prefetch=1,
                grid=(1,),
                in_specs=specs,
                out_specs=pl.BlockSpec(
                    (rows, CAP, cells), lambda n, me_ref, block=block: (0, (me_ref[0] // group) ^ block, 0)
                ),
            ),
            out_shape=jax.ShapeDtypeStruct((rows, slots, cells), dtype),
            input_output_aliases=aliases,
            compiler_params=kernel_params(),
            name="unpack",
        )(me, *given)
    return out


def local(
    images,
    counts,
    context,
    filter_two,
    gain_two,
    shift_two,
    filter_three,
    gain_three,
    shift_three,
    film_weight,
    film_bias,
    cotangent,
    *,
    partners,
    columns,
):
    devices = partners * columns
    rows, slots = images.shape[:2]
    images_each = slots // partners
    group = CAP // images_each
    chunk = CHUNK
    parts = images_each // chunk
    position = lax.axis_index("tensor")
    me = jnp.reshape(position, (1,)).astype(jnp.int32)

    def swap(value, partner):
        if partner == 0:
            return value
        return lax.ppermute(value, "tensor", [(i, i ^ partner) for i in range(partners)])

    def share(copies):
        return lax.all_to_all(copies, ("dp", "tensor"), 0, 0)

    def gather(value):
        shape = value.shape
        bit, axis = partners // 2, 0
        while bit:
            other = swap(value, bit)
            low = jnp.stack([value, other], axis)
            high = jnp.stack([other, value], axis)
            value = jnp.where((position & bit) == 0, low, high)
            bit, axis = bit // 2, axis + 1
        return value.reshape(partners, *shape)

    def after(value, earlier):
        return value + (earlier[(0,) * earlier.ndim] * 0.0).astype(value.dtype)

    sent = pack(images, me, partners, images_each, chunk)
    order = [partner for partner in range(partners) if partner]
    order.sort(key=lambda partner: -partner)
    maps = [[None] * parts for _ in range(partners)]
    for part in range(parts):
        for partner in [*order, 0]:
            maps[partner][part] = swap(sent[partner][part], partner)

    begun = sent[partners - 1][0]
    filter_two, filter_three = after(filter_two, begun), after(filter_three, begun)
    film_bias, film_weight, cotangent = after(film_bias, begun), after(film_weight, begun), after(cotangent, begun)
    gain_two, shift_two = after(gain_two, begun), after(shift_two, begun)
    gain_three, shift_three = after(gain_three, begun), after(shift_three, begun)

    def spread_filter(own):
        full = gather(jnp.transpose(own, (2, 0, 3, 1)).reshape(3, rows, 3 * C))
        ahead = jnp.transpose(full, (1, 0, 2, 3)).reshape(3 * C, 3 * C)
        behind = jnp.transpose(ahead.reshape(3, C, 3, C)[::-1, :, ::-1], (0, 3, 2, 1)).reshape(3 * C, 3 * C)
        return ahead, behind

    ahead_two, behind_two = spread_filter(filter_two)
    ahead_three, behind_three = spread_filter(filter_three)
    entries = film_weight.shape[0]
    small = jnp.concatenate(
        [
            jnp.stack([gain_two, shift_two, gain_three, shift_three]),
            film_bias,
            film_weight.reshape(2 * entries, rows),
        ]
    )
    small = jnp.transpose(gather(small), (1, 0, 2)).reshape(-1, C).astype(F32)
    gain_three, shift_three = small[2], small[3]
    film_b = small[4:6]
    film_w = small[6:].reshape(entries, 2, C)

    turned = jnp.transpose(cotangent, (1, 0, 2))
    targets = [
        swap(lax.dynamic_slice_in_dim(turned, (position ^ partner) * images_each, images_each, 0), partner)
        for partner in range(partners)
    ]

    task = position // group
    slot = (position % group) * images_each + jnp.arange(images_each, dtype=jnp.int32)
    limit = lax.dynamic_index_in_dim(counts, task, 0, keepdims=False)
    live = (slot < limit).astype(F32)
    own_context = lax.dynamic_index_in_dim(context, task, 0, keepdims=False)
    film_own = jnp.einsum("e,ekc->kc", own_context, film_w, precision=PRECISE) + film_b
    vectors = jnp.concatenate([small[:4], 1.0 + film_own[:1], film_own[1:], jnp.zeros((2, C), F32)])
    all_context = jnp.broadcast_to(after(context, begun)[None], (columns, *context.shape))
    all_context = lax.all_to_all(all_context, "dp", 0, 0).reshape(-1, entries)

    conv_two = state = None
    for part in range(parts):
        given = [maps[partner][part] for partner in range(partners)]
        specs = [each(rows, CELLS_TWO)] * partners
        aliases = {}
        final = part == parts - 1
        if part:
            aliases = {4 + partners: 0}
            given = given + [state, conv_two]
            specs = specs + [whole(C, C), pl.BlockSpec(memory_space=pl.ANY)]
        conv_two, state = pl.pallas_call(
            functools.partial(first_conv_kernel, partners, part, final),
            grid=(chunk,),
            in_specs=[smem(), smem(), whole(3 * C, 3 * C), *specs],
            out_specs=[
                each(C, LANES_TWO, first=part * chunk),
                whole(devices, SENT, C) if final else whole(C, C),
            ],
            out_shape=[
                jax.ShapeDtypeStruct((images_each, C, LANES_TWO), F32),
                jax.ShapeDtypeStruct((devices, SENT, C) if final else (C, C), F32),
            ],
            scratch_shapes=[
                pltpu.VMEM((C, LANES_TWO), F32),
                pltpu.VMEM((3 * C, LANES_TWO), BF16),
                pltpu.VMEM((C, C), F32),
            ],
            input_output_aliases=aliases,
            compiler_params=kernel_params(),
            name="first_conv",
        )(me, live, ahead_two, *given)
    heard_two = share(state)

    pool = pool_matrix(MAP, LANES_TWO, LANES_THREE)
    pool_out = pool_matrix(HALF, LANES_THREE, LANES_OUT)
    *block_pieces, hidden, conv_three, norm_two, levels, sums_three = pl.pallas_call(
        functools.partial(middle_kernel, partners),
        grid=(images_each,),
        in_specs=[
            smem(),
            smem(),
            whole(devices, SENT, C),
            whole(8, C),
            whole(1152, 256),
            whole(896, 256),
            whole(3 * C, 3 * C),
            each(C, LANES_TWO),
        ],
        out_specs=[each(rows, CELLS_THREE)] * partners
        + [each(C, LANES_THREE), each(C, LANES_THREE), whole(8, C), whole(8, C), whole(devices, SENT, C)],
        out_shape=[jax.ShapeDtypeStruct((images_each, rows, CELLS_THREE), BF16)] * partners
        + [
            jax.ShapeDtypeStruct((images_each, C, LANES_THREE), BF16),
            jax.ShapeDtypeStruct((images_each, C, LANES_THREE), F32),
            jax.ShapeDtypeStruct((8, C), F32),
            jax.ShapeDtypeStruct((8, C), F32),
            jax.ShapeDtypeStruct((devices, SENT, C), F32),
        ],
        scratch_shapes=[
            pltpu.VMEM((C, C), F32),
            pltpu.VMEM((C, C), F32),
            pltpu.VMEM((3 * C, LANES_THREE), BF16),
        ],
        compiler_params=kernel_params(),
        name="middle",
    )(
        me,
        live,
        heard_two,
        vectors,
        jnp.asarray(pool[:1152, :256], BF16),
        jnp.asarray(pool[896:, 256:], BF16),
        ahead_three,
        conv_two,
    )
    heard_three = share(sums_three)

    *out_pieces, grad_three, norm_three, levels, sums_top = pl.pallas_call(
        functools.partial(top_kernel, partners),
        grid=(images_each,),
        in_specs=[
            smem(),
            smem(),
            whole(devices, SENT, C),
            whole(1, SENT, C),
            whole(8, C),
            whole(8, C),
            whole(LANES_THREE, LANES_OUT),
            whole(LANES_OUT, LANES_THREE),
            each(C, LANES_THREE),
            *[each(rows, CELLS_OUT)] * partners,
        ],
        out_specs=[each(rows, CELLS_OUT)] * partners
        + [each(C, LANES_THREE), whole(8, C), whole(8, C), whole(devices, SENT, C)],
        out_shape=[jax.ShapeDtypeStruct((images_each, rows, CELLS_OUT), BF16)] * partners
        + [
            jax.ShapeDtypeStruct((images_each, C, LANES_THREE), F32),
            jax.ShapeDtypeStruct((8, C), F32),
            jax.ShapeDtypeStruct((8, C), F32),
            jax.ShapeDtypeStruct((devices, SENT, C), F32),
        ],
        scratch_shapes=[
            pltpu.VMEM((C, C), F32),
            pltpu.VMEM((C, LANES_OUT), F32),
            pltpu.VMEM((C, LANES_OUT), F32),
            pltpu.VMEM((C, C), F32),
        ],
        compiler_params=kernel_params(),
        name="top",
    )(
        me,
        live,
        heard_three,
        sums_three,
        levels,
        vectors,
        jnp.asarray(pool_out, BF16),
        jnp.asarray(pool_out.T, BF16),
        conv_three,
        *targets,
    )
    heard_top = share(sums_top)

    grad_two, sums_two, filter_sum_three = pl.pallas_call(
        back_kernel,
        grid=(images_each,),
        in_specs=[
            smem(),
            whole(devices, SENT, C),
            whole(8, C),
            whole(8, C),
            whole(8, C),
            whole(8, C),
            whole(3 * C, 3 * C),
            whole(256, 896),
            whole(384, 896),
            each(C, LANES_THREE),
            each(C, LANES_THREE),
            each(C, LANES_THREE),
            each(C, LANES_TWO),
        ],
        out_specs=[each(C, LANES_TWO), whole(devices, SENT, C), whole(3 * C, 3 * C)],
        out_shape=[
            jax.ShapeDtypeStruct((images_each, C, LANES_TWO), F32),
            jax.ShapeDtypeStruct((devices, SENT, C), F32),
            jax.ShapeDtypeStruct((3 * C, 3 * C), F32),
        ],
        scratch_shapes=[
            pltpu.VMEM((C, C), F32),
            pltpu.VMEM((C, C), F32),
            pltpu.VMEM((C, C), F32),
            pltpu.VMEM((3 * C, LANES_THREE), BF16),
            pltpu.VMEM((3 * C, LANES_THREE), BF16),
        ],
        compiler_params=kernel_params(),
        name="back",
    )(
        live,
        heard_top,
        norm_three,
        norm_two,
        levels,
        vectors,
        behind_three,
        jnp.asarray(pool[:896, :256].T, BF16),
        jnp.asarray(pool[896:, 128:].T, BF16),
        grad_three,
        conv_three,
        hidden,
        conv_two,
    )
    heard_back = share(sums_two)

    returned = [[None] * parts for _ in range(partners)]
    filter_sum_two = None
    for part in range(parts):
        given = [maps[partner][part] for partner in range(partners)]
        specs = [each(rows, CELLS_TWO)] * partners
        if part:
            given = given + [filter_sum_two]
            specs = specs + [whole(3 * C, 3 * C)]
        *pieces, filter_sum_two = pl.pallas_call(
            functools.partial(last_kernel, partners, part),
            grid=(chunk,),
            in_specs=[
                smem(),
                smem(),
                whole(devices, SENT, C),
                whole(8, C),
                whole(8, C),
                whole(3 * C, 3 * C),
                each(C, LANES_TWO, first=part * chunk),
                each(C, LANES_TWO, first=part * chunk),
                *specs,
            ],
            out_specs=[each(rows, CELLS_TWO)] * partners + [whole(3 * C, 3 * C)],
            out_shape=[jax.ShapeDtypeStruct((chunk, rows, CELLS_TWO), BF16)] * partners
            + [jax.ShapeDtypeStruct((3 * C, 3 * C), F32)],
            scratch_shapes=[
                pltpu.VMEM((C, C), F32),
                pltpu.VMEM((C, LANES_TWO), F32),
                pltpu.VMEM((C, LANES_TWO), F32),
                pltpu.VMEM((3 * C, LANES_TWO), BF16),
                pltpu.VMEM((3 * C, LANES_TWO), BF16),
            ],
            compiler_params=kernel_params(),
            name="last",
        )(me, live, heard_back, norm_two, vectors, behind_two, grad_two, conv_two, *given)
        for partner in [*order, 0]:
            returned[partner][part] = swap(pieces[partner], partner)
    grad_images = unpack(returned, me, images_each, F32)

    ended = pieces[0]
    block_two = unpack([[swap(block_pieces[k], k)] for k in range(partners)], me, images_each, BF16, ended)
    block_three = unpack([[swap(out_pieces[k], k)] for k in range(partners)], me, images_each, BF16, ended)

    both = jnp.stack([filter_sum_two, after(filter_sum_three, ended)])
    strip = 6 * rows // columns
    split = jnp.transpose(both.reshape(2, 3, partners, rows, 3 * C), (2, 0, 1, 3, 4))
    split = jnp.transpose(split.reshape(partners, columns, strip, 3 * C), (1, 0, 2, 3))
    strips = jnp.sum(share(split.reshape(devices, strip, 3 * C)), axis=0)
    strips = lax.all_to_all(jnp.broadcast_to(strips[None], (columns, *strips.shape)), "dp", 0, 0)
    strips = strips.reshape(2, 3, rows, 3, C)
    grad_filters = jnp.transpose(jnp.stack([strips[:, 2], strips[:, 1], strips[:, 0]], 1), (0, 2, 4, 3, 1))

    def own(vector):
        return lax.dynamic_slice_in_dim(vector, position * rows, rows, vector.ndim - 1)

    tasks = devices // group
    heard_top, heard_back = after(heard_top, ended), after(heard_back, ended)
    norm_two, norm_three = after(norm_two, ended), after(norm_three, ended)
    by_task = jnp.sum(heard_top[:, :2].reshape(tasks, group, 2, C), axis=1)
    grad_film = jnp.stack([gain_three * by_task[:, 1] + shift_three * by_task[:, 0], by_task[:, 0]], axis=1)
    grad_film_own = own(grad_film)
    grad_film_w = jnp.einsum("te,tkc->ekc", all_context, grad_film_own, precision=PRECISE)
    grad_film_b = jnp.sum(grad_film_own, axis=0)
    here = lax.dynamic_slice_in_dim(grad_film, lax.axis_index("dp") * counts.shape[0], counts.shape[0], 0)
    grad_context = jnp.einsum("tkc,ekc->te", here, film_w, precision=PRECISE)

    def normed_squares(gain, shift, variance, factor):
        return jnp.mean(gain * gain * variance * factor * factor + shift * shift)

    live_total = norm_two[3, 0] / CELLS_TWO
    base = live_total * C
    levels = jnp.sum(heard_back[:, 2], axis=0)
    means = jnp.stack(
        [
            jnp.mean(norm_two[2] + norm_two[0] * norm_two[0]),
            normed_squares(small[0], small[1], norm_two[2], norm_two[1]),
            levels[0] / (base * CELLS_TWO),
            levels[1] / (base * CELLS_THREE),
            jnp.mean(norm_three[2] + norm_three[0] * norm_three[0]),
            normed_squares(gain_three, shift_three, norm_three[2], norm_three[1]),
            levels[2] / (base * CELLS_THREE),
            levels[3] / (base * CELLS_THREE),
            levels[4] / (base * CELLS_OUT),
        ]
    )
    norm_sums = own(jnp.concatenate([jnp.sum(heard_back, axis=0)[:2], jnp.sum(heard_top, axis=0)[2:4]]))
    return (
        block_two,
        block_three,
        grad_images,
        grad_filters[0],
        norm_sums[1],
        norm_sums[0],
        grad_filters[1],
        norm_sums[3],
        norm_sums[2],
        grad_film_w,
        grad_film_b,
        grad_context,
        jnp.sqrt(means),
    )


def solution(mesh):
    step = functools.partial(local, partners=mesh.shape["tensor"], columns=mesh.shape["dp"])
    placed = (
        P("tensor", "dp", None),
        P("dp"),
        P("dp", None),
        P("tensor", None, None, None),
        P("tensor"),
        P("tensor"),
        P("tensor", None, None, None),
        P("tensor"),
        P("tensor"),
        P(None, None, "tensor"),
        P(None, "tensor"),
        P("tensor", "dp", None),
    )
    return jax.shard_map(
        step,
        mesh=mesh,
        in_specs=placed,
        out_specs=(
            P("tensor", "dp", None),
            P("tensor", "dp", None),
            P("tensor", "dp", None),
            P("tensor", None, None, None),
            P("tensor"),
            P("tensor"),
            P("tensor", None, None, None),
            P("tensor"),
            P("tensor"),
            P(None, None, "tensor"),
            P(None, "tensor"),
            P("dp", None),
            P(),
        ),
        check_vma=False,
    )
```

```python
import functools

import jax
import jax.numpy as jnp
import numpy as np
from jax import lax
from jax.experimental import pallas as pl
from jax.experimental.pallas import tpu as pltpu
from jax.sharding import PartitionSpec as P

C = 128
MAP = 42
CAP = 16
HALF = 21
QUART = 10
SENT = 4
VMEM_BYTES = 63 << 20
WIDE = 256

CELLS_TWO = MAP * MAP
CELLS_THREE = HALF * HALF
CELLS_OUT = QUART * QUART
LANES_TWO = 1792
LANES_THREE = 512
LANES_OUT = 128
EPSILON = 1e-05
PRECISE = lax.Precision.HIGHEST
F32 = jnp.float32
BF16 = jnp.bfloat16
ROOT = 0.7978845608028654
CUBIC = 0.044715


def lane_ids(width):
    return lax.broadcasted_iota(jnp.int32, (1, width), 1)


def as_columns(rows):
    return jnp.concatenate([rows] * (C // 8), axis=0).T


def column_tile(columns):
    ids = lax.broadcasted_iota(jnp.int32, (C, C), 1)
    tile = jnp.zeros((C, C), F32)
    for place, column in enumerate(columns):
        tile = jnp.where(ids == place, column, tile)
    return tile


def row_tile(rows, count=8):
    ids = lax.broadcasted_iota(jnp.int32, (count, C), 0)
    tile = jnp.zeros((count, C), F32)
    for place, row in enumerate(rows):
        tile = jnp.where(ids == place, row, tile)
    return tile


def row(tile_ref, place):
    return tile_ref[place : place + 1, :]


def column(tile_ref, place):
    return tile_ref[:, place : place + 1]


def merge_moments(state, weight, mean, spread, cells):
    count, middle, total = state
    added = weight * cells
    both = count + added
    away = mean - middle
    share = added / jnp.maximum(both, 1.0)
    return both, middle + away * share, total + weight * spread + away * away * count * share


def slice_norm(heard_ref):
    means, spreads, counts = heard_ref[:, 0, :], heard_ref[:, 1, :], heard_ref[:, 2, :]
    extent = jnp.sum(counts, axis=0, keepdims=True)
    middle = jnp.sum(counts * means, axis=0, keepdims=True) / extent
    away = means - middle
    variance = jnp.sum(spreads + counts * away * away, axis=0, keepdims=True) / extent
    return middle, lax.rsqrt(variance + EPSILON), variance, extent


def level_row(columns):
    return jnp.sum(column_tile(columns), axis=0, keepdims=True)


def spread_rows(tile, out_ref):
    out_ref[...] = jnp.broadcast_to(tile[None], out_ref.shape)


def trim(values, first, last):
    tiles = cut(values, 128)
    ids = lane_ids(128)
    if first > 0:
        tiles[0] = jnp.where(ids >= first, tiles[0], jnp.zeros_like(tiles[0]))
    if last < values.shape[1]:
        tiles[-1] = jnp.where(ids < last - (values.shape[1] - 128), tiles[-1], jnp.zeros_like(tiles[-1]))
    return jnp.concatenate(tiles, axis=1)


def cut(values, wide):
    return [values[:, first : first + wide] for first in range(0, values.shape[1], wide)]


def shift_lanes(blocks, by):
    moved = [pltpu.roll(block, by % block.shape[1], 1) for block in blocks]
    nothing = jnp.zeros_like(moved[0][:, :128])
    ids = lane_ids(128)
    shifted = []
    for place, block in enumerate(moved):
        if by > 0:
            near = moved[place - 1][:, :128] if place else nothing
            edge = jnp.where(ids < by, near, block[:, :128])
            shifted.append(jnp.concatenate([edge, block[:, 128:]], axis=1) if block.shape[1] > 128 else edge)
        else:
            near = moved[place + 1][:, -128:] if place + 1 < len(moved) else nothing
            edge = jnp.where(ids >= 128 + by, near, block[:, -128:])
            shifted.append(jnp.concatenate([block[:, :-128], edge], axis=1) if block.shape[1] > 128 else edge)
    return shifted


def shift_column(blocks, by, side):
    shifted = []
    first = 0
    for block in shift_lanes(blocks, by):
        column = (lane_ids(block.shape[1]) + first) % side
        shifted.append(jnp.where(column == (0 if by > 0 else side - 1), jnp.zeros_like(block), block))
        first += block.shape[1]
    return shifted


def write(out_ref, blocks):
    first = 0
    for block in blocks:
        out_ref[:, first : first + block.shape[1]] = block
        first += block.shape[1]


def fill(stack_ref, tap, blocks):
    first = 0
    for block in blocks:
        stack_ref[tap * C : (tap + 1) * C, first : first + block.shape[1]] = block
        first += block.shape[1]


def stack_sideways(low, side, stack_ref):
    fill(stack_ref, 0, shift_column(low, 1, side))
    fill(stack_ref, 1, low)
    fill(stack_ref, 2, shift_column(low, -1, side))


def stack_upright(low, side, stack_ref):
    fill(stack_ref, 0, shift_lanes(low, -side))
    fill(stack_ref, 1, low)
    fill(stack_ref, 2, shift_lanes(low, side))


def conv_blocks(weights_ref, stack_ref):
    width = stack_ref.shape[1]
    parts = [
        jnp.dot(weights_ref[...], stack_ref[:, first : first + WIDE], preferred_element_type=F32)
        for first in range(0, width, WIDE)
    ]
    return [[part[tap * C : (tap + 1) * C] for part in parts] for tap in range(3)]


def conv_ahead(weights_ref, stack_ref, side):
    above, here, below = conv_blocks(weights_ref, stack_ref)
    total = [a + b + c for a, b, c in zip(shift_lanes(above, side), here, shift_lanes(below, -side))]
    total[-1] = trim(total[-1], 0, side * side - (stack_ref.shape[1] - total[-1].shape[1]))
    return total


def conv_behind(weights_ref, stack_ref, side):
    left, here, right = conv_blocks(weights_ref, stack_ref)
    return [a + b + c for a, b, c in zip(shift_column(left, -1, side), here, shift_column(right, 1, side))]


def across_cells(left_ref, right_ref):
    return lax.dot_general(left_ref[...], right_ref[...], (((1,), (1,)), ((), ())), preferred_element_type=F32)


def lane_sum(values):
    return jnp.sum(values, axis=1, keepdims=True)


def moments(blocks, cells):
    pivot = lane_sum(blocks[0]) * (1.0 / blocks[0].shape[1])
    total, squares = 0.0, 0.0
    for place, block in enumerate(blocks):
        away = block - pivot
        if place == len(blocks) - 1:
            away = trim(away, 0, cells - sum(b.shape[1] for b in blocks[:-1]))
        total = total + sum(cut(away, 128))
        squares = squares + sum(cut(away * away, 128))
    away = lane_sum(total) * (1.0 / cells)
    return pivot + away, lane_sum(squares) - cells * away * away


def gelu_gate(values):
    return 0.5 + 0.5 * jnp.tanh(values * (ROOT + (ROOT * CUBIC) * (values * values)))


def gelu_slope(values, gate):
    return gate * (1.0 + (1.0 - gate) * (values * (2.0 * ROOT + (6.0 * ROOT * CUBIC) * (values * values))))


def halves(values):
    high = values.astype(BF16)
    return jnp.concatenate([high, (values - high.astype(F32)).astype(BF16)], axis=0)


def dot_halves(split, weights_ref):
    both = jnp.dot(split, weights_ref[...], preferred_element_type=F32)
    return [both[first : first + C] + both[first + C : first + 2 * C] for first in range(0, both.shape[0], 2 * C)]


def own_rows(me, partner, count):
    return pl.ds(pl.multiple_of((me ^ partner) * count, count), count)


def kernel_params(axes=1):
    return pltpu.CompilerParams(vmem_limit_bytes=VMEM_BYTES, dimension_semantics=("arbitrary",) * axes)


def pack_kernel(images_each, group, wants, me_ref, maps_ref, *refs):
    piece_refs = refs[-len(wants) :]
    turned = jnp.swapaxes(maps_ref[...], 0, 1)
    for lead in range(group):

        @pl.when(me_ref[0] % group == lead)
        def _():
            for piece_ref, (partner, first, count) in zip(piece_refs, wants):
                start = (lead ^ (partner % group)) * images_each + first
                piece_ref[...] = turned[start : start + count]


def unpack_kernel(counts, me_ref, *refs):
    out_refs = refs[-len(counts) :]
    group = len(counts[0])
    for lead in range(group):

        @pl.when(me_ref[0] % group == lead)
        def _():
            start = 0
            for out_ref, parts in zip(out_refs, counts):
                ordered = []
                for slot in range(group):
                    place = start + sum(len(some) for some in parts[: slot ^ lead])
                    ordered += [refs[place + part][...] for part in range(len(parts[slot ^ lead]))]
                joined = jnp.concatenate(ordered, axis=0) if len(ordered) > 1 else ordered[0]
                out_ref[...] = jnp.swapaxes(joined, 0, 1).astype(out_ref.dtype)
                start += sum(len(some) for some in parts)


def bundle_kernel(filter_two_ref, filter_three_ref, film_ref, bias_ref, *refs):
    vector_refs, out_ref = refs[:4], refs[-1]
    rows = filter_two_ref.shape[2]
    out_ref[...] = jnp.zeros_like(out_ref)
    for place, filter_ref in enumerate((filter_two_ref, filter_three_ref)):
        for down in range(3):
            first = (3 * place + down) * rows
            for across in range(3):
                out_ref[first : first + rows, across * C : (across + 1) * C] = filter_ref[down, across]
    for kind in range(2):
        out_ref[6 * rows : 7 * rows, kind * C : kind * C + film_ref.shape[2]] = film_ref[kind]
    for place, vector_ref in enumerate(vector_refs):
        out_ref[7 * rows + place : 7 * rows + place + 1, 0:rows] = vector_ref[...]
    for kind in range(2):
        out_ref[7 * rows + 4 + kind : 7 * rows + 5 + kind, 0:rows] = bias_ref[kind : kind + 1]


def unbundle_kernel(partners, me_ref, task_ref, context_ref, *refs):
    piece_refs = refs[:partners]
    ahead_two_ref, behind_two_ref, ahead_three_ref, behind_three_ref, film_ref, vectors_ref = refs[partners:]
    rows = C // partners
    entries = film_ref.shape[2]
    lanes = jnp.zeros((8, C), F32)
    ids = lane_ids(C)
    for partner, piece_ref in enumerate(piece_refs):
        owner = me_ref[0] ^ partner
        for place, ahead_ref in enumerate((ahead_two_ref, ahead_three_ref)):
            for down in range(3):
                first = (3 * place + down) * rows
                ahead_ref[pl.ds(pl.multiple_of(down * C + owner * rows, rows), rows), :] = piece_ref[first : first + rows]
        for kind in range(2):
            film_ref[kind, own_rows(me_ref[0], partner, rows), :] = piece_ref[
                6 * rows : 7 * rows, kind * C : kind * C + entries
            ].astype(F32)
        own = jnp.where(ids < rows, piece_ref[7 * rows : 7 * rows + 16, 0:C].astype(F32)[:8], 0.0)
        lanes = lanes + pltpu.roll(own, owner * rows, 1)
    behind_two_ref[...] = ahead_two_ref[...].T
    behind_three_ref[...] = ahead_three_ref[...].T
    context = context_ref[pl.ds(task_ref[0], 1), :]
    told = [lane_sum(film_ref[kind] * context) for kind in range(2)]
    told = column_tile(told).T[:8]
    scale = 1.0 + told[0:1] + lanes[4:5]
    shift = told[1:2] + lanes[5:6]
    vectors_ref[...] = row_tile([lanes[0:1], lanes[1:2], lanes[2:3], lanes[3:4], scale, shift])


def assemble(maps, cells, me, piece_refs, index):
    rows = C // len(piece_refs)
    for partner, piece_ref in enumerate(piece_refs):
        maps[own_rows(me, partner, rows), 0:cells] = piece_ref[index]


def disperse(piece_refs, index, me, output, cells):
    rows = C // len(piece_refs)
    for partner, piece_ref in enumerate(piece_refs):
        piece_ref[index] = output[own_rows(me, partner, rows), 0:cells]


def first_conv_kernel(partners, first, final, me_ref, live_ref, told_ref, weights_ref, *refs):
    piece_refs = refs[:partners]
    conv_ref, maps_ref, state_ref, stack, state = refs[-5:]
    step = pl.program_id(0)
    count = conv_ref.shape[0]

    @pl.when(step == 0)
    def _():
        state[...] = refs[partners][...] if first else jnp.zeros_like(state)

    merged = [column(state, k) for k in range(3)]
    for image in range(count):
        maps_ref[image, :, CELLS_TWO // 128 * 128 :] = jnp.zeros((C, LANES_TWO - CELLS_TWO // 128 * 128), BF16)
        assemble(maps_ref.at[image], CELLS_TWO, me_ref[0], piece_refs, image)
        stack_sideways(cut(maps_ref[image], WIDE), MAP, stack.at[image])
        conv = conv_ahead(weights_ref, stack.at[image], MAP)
        write(conv_ref.at[image], conv)
        mean, spread = moments(conv, CELLS_TWO)
        live = live_ref[first + step * count + image]
        merged = merge_moments(merged, live, mean, spread, CELLS_TWO)
    state[...] = column_tile(merged)

    @pl.when(step == pl.num_programs(0) - 1)
    def _():
        if final:
            turned = state[...].T
            spread_rows(row_tile([turned[1:2], turned[2:3], turned[0:1], row(told_ref, 0)], SENT), state_ref)
        else:
            state_ref[...] = state[...]


def middle_kernel(
    partners, me_ref, live_ref, heard_ref, vectors_ref, pool_a_ref, pool_b_ref, weights_ref, conv_ref, *refs
):
    hidden_ref, conv_three_ref, norm_ref, levels_ref, sums_ref, columns, state, stack = refs[-8:]
    piece_refs = refs[-8 - partners : -8]
    step = pl.program_id(0)
    count = conv_ref.shape[0]

    @pl.when(step == 0)
    def _():
        middle, factor, variance, extent = slice_norm(heard_ref)
        norm_ref[...] = row_tile([middle, factor, variance, extent])
        columns[...] = as_columns(row_tile([middle, row(vectors_ref, 0) * factor, row(vectors_ref, 1)]))
        state[...] = jnp.zeros_like(state)

    merged = [column(state, k) for k in range(3)]
    active_squares, hidden_squares = column(state, 3), column(state, 4)
    for image in range(count):
        live = live_ref[step * count + image]
        pre = (conv_ref[image] - column(columns, 0)) * column(columns, 1) + column(columns, 2)
        active = pre * gelu_gate(pre)
        counted = trim(active, 0, CELLS_TWO)
        active_squares = active_squares + live * lane_sum(counted * counted)
        split = halves(active)
        (left,) = dot_halves(split[:, :1152], pool_a_ref)
        (right,) = dot_halves(split[:, 896:], pool_b_ref)
        hidden = live * jnp.concatenate([left, right], axis=1)
        hidden_squares = hidden_squares + lane_sum(hidden * hidden)
        hidden_low = hidden.astype(BF16)
        hidden_ref[image] = hidden_low
        disperse(piece_refs, image, me_ref[0], hidden_ref.at[image], CELLS_THREE)
        stack_sideways(cut(hidden_low, WIDE), HALF, stack.at[image])
        conv = conv_ahead(weights_ref, stack.at[image], HALF)
        write(conv_three_ref.at[image], conv)
        mean, spread = moments(conv, CELLS_THREE)
        merged = merge_moments(merged, live, mean, spread, CELLS_THREE)
    state[...] = column_tile([*merged, active_squares, hidden_squares])

    @pl.when(step == pl.num_programs(0) - 1)
    def _():
        turned = state[...].T
        spread_rows(row_tile([turned[k : k + 1] for k in (1, 2, 0)], SENT), sums_ref)
        levels_ref[...] = row_tile([level_row([column(state, 3), column(state, 4)])])


def top_kernel(
    partners, me_ref, live_ref, heard_ref, own_ref, before_ref, vectors_ref, pool_ref, spread_ref, conv_ref, *refs
):
    target_refs = refs[:partners]
    piece_refs = refs[partners : 2 * partners]
    grad_ref, norm_ref, levels_ref, sums_ref, columns, target, output, totals = refs[2 * partners :]
    step = pl.program_id(0)
    count = conv_ref.shape[0]

    @pl.when(step == 0)
    def _():
        middle, factor, variance, extent = slice_norm(heard_ref)
        norm_ref[...] = row_tile([middle, factor, variance, extent])
        columns[...] = as_columns(row_tile([middle, factor] + [row(vectors_ref, k) for k in (2, 3, 4, 5)]))
        target[...] = jnp.zeros_like(target)
        totals[...] = jnp.zeros_like(totals)

    scale = column(columns, 4)
    slope = scale * column(columns, 2)
    offset = scale * column(columns, 3) + column(columns, 5)
    sums = [jnp.zeros((C, 1), F32)] * 4
    for image in range(count):
        live = live_ref[step * count + image]
        assemble(target.at[image], CELLS_OUT, me_ref[0], target_refs, image)
        normed = (conv_ref[image] - column(columns, 0)) * column(columns, 1)
        filmed = slope * normed + offset
        gate = gelu_gate(filmed)
        active = filmed * gate
        counted = trim(active, 0, CELLS_THREE)
        (pooled,) = dot_halves(halves(active), pool_ref)
        pooled = live * pooled
        output[image] = pooled.astype(BF16)
        disperse(piece_refs, image, me_ref[0], output.at[image], CELLS_OUT)
        spread = jnp.dot(target[image], spread_ref[...], preferred_element_type=F32)
        grad_filmed = live * spread * gelu_slope(filmed, gate)
        grad_ref[image] = scale * grad_filmed
        parts = (
            lane_sum(grad_filmed),
            lane_sum(grad_filmed * normed),
            live * lane_sum(counted * counted),
            lane_sum(pooled * pooled),
        )
        sums = [total + part for total, part in zip(sums, parts)]
    totals[...] += column_tile(sums)

    @pl.when(step == pl.num_programs(0) - 1)
    def _():
        turned = totals[...].T
        shift_sum, scale_sum = turned[0:1], turned[1:2]
        film_scale = row(vectors_ref, 4)
        slope = film_scale * row(vectors_ref, 2) * row(norm_ref, 1)
        offset = film_scale * row(vectors_ref, 3) + row(vectors_ref, 5)
        extent = own_ref[0, 2:3, :]
        away = own_ref[0, 0:1, :] - row(norm_ref, 0)
        filmed_squares = (
            slope * slope * (own_ref[0, 1:2, :] + extent * away * away)
            + 2.0 * slope * offset * extent * away
            + extent * offset * offset
        )
        spread_rows(
            row_tile([shift_sum, scale_sum, film_scale * shift_sum, film_scale * scale_sum], SENT), sums_ref
        )
        nothing = jnp.zeros((C, 1), F32)
        others = level_row([nothing, nothing, nothing, column(totals, 2), column(totals, 3)])
        lanes = lane_ids(C)
        filmed_total = lane_sum(filmed_squares)
        levels_ref[...] = before_ref[...] + row_tile([others + jnp.where(lanes == 2, filmed_total, 0.0)])


def norm_back(live, columns, grad, away, cells):
    scaled = [live * column(columns, k) for k in (1, 2, 3)]
    error = grad.astype(F32) * scaled[0] - scaled[1] - away.astype(F32) * scaled[2]
    return trim(error, 0, cells).astype(BF16)


def norm_back_columns(norm_ref, gain, bias_sum, gain_sum):
    factor, extent = row(norm_ref, 1), row(norm_ref, 3)
    front = gain * factor
    return as_columns(
        row_tile([row(norm_ref, 0), front, front * bias_sum / extent, front * factor * gain_sum / extent])
    )


def back_kernel(
    live_ref,
    heard_ref,
    norm_three_ref,
    norm_two_ref,
    levels_ref,
    vectors_ref,
    weights_ref,
    unpool_a_ref,
    unpool_b_ref,
    grad_ref,
    conv_three_ref,
    hidden_ref,
    conv_two_ref,
    *refs,
):
    out_ref, away_ref, sums_ref, filter_ref, columns_three, columns_two, totals, product, stack, upright = refs[-10:]
    step = pl.program_id(0)
    count = conv_two_ref.shape[0]

    @pl.when(step == 0)
    def _():
        sums = jnp.sum(heard_ref[...], axis=0)
        columns_three[...] = norm_back_columns(norm_three_ref, row(vectors_ref, 2), sums[2:3], sums[3:4])
        columns_two[...] = as_columns(
            row_tile([row(norm_two_ref, 0), row(vectors_ref, 0) * row(norm_two_ref, 1), row(vectors_ref, 1)])
        )
        totals[...] = jnp.zeros_like(totals)
        product[...] = jnp.zeros_like(product)

    grad_sum, product_sum = column(totals, 0), column(totals, 1)
    for image in range(count):
        away = conv_three_ref[image] - column(columns_three, 0)
        error = norm_back(live_ref[step * count + image], columns_three, grad_ref[image], away, CELLS_THREE)
        stack_upright(cut(error, WIDE), HALF, upright.at[image])
        stack_sideways(cut(hidden_ref[image], WIDE), HALF, stack.at[image])
    split = jnp.concatenate(
        [
            halves(jnp.concatenate(conv_behind(weights_ref, upright.at[image], HALF), axis=1))
            for image in range(count)
        ],
        axis=0,
    )
    left = dot_halves(split[:, :256], unpool_a_ref)
    right = dot_halves(split[:, 128:], unpool_b_ref)
    for image in range(count):
        away = conv_two_ref[image] - column(columns_two, 0)
        pre = away * column(columns_two, 1) + column(columns_two, 2)
        grad_pre = jnp.concatenate([left[image], right[image]], axis=1) * gelu_slope(pre, gelu_gate(pre))
        out_ref[image] = grad_pre.astype(BF16)
        away_ref[image] = away.astype(BF16)
        grad_sum = grad_sum + lane_sum(grad_pre)
        product_sum = product_sum + lane_sum(grad_pre * away)
    product[...] += sum(across_cells(upright.at[image], stack.at[image]) for image in range(count))
    totals[...] = column_tile([grad_sum, product_sum])

    @pl.when(step == pl.num_programs(0) - 1)
    def _():
        split_filter(product, filter_ref)
        turned = totals[...].T
        normed_sum = turned[1:2] * row(norm_two_ref, 1)
        spread_rows(row_tile([turned[0:1], normed_sum, levels_ref[0:1, :]], SENT), sums_ref)


def split_filter(product, filter_ref):
    partners, _, rows, _ = filter_ref.shape
    for tap in range(3):
        for owner in range(partners):
            filter_ref[owner, tap] = product[tap * C + owner * rows : tap * C + (owner + 1) * rows].astype(BF16)


def last_columns(heard_ref, norm_ref, vectors_ref):
    sums = jnp.sum(heard_ref[...], axis=0)
    return norm_back_columns(norm_ref, row(vectors_ref, 0), sums[0:1], sums[1:2])


def last_kernel(
    partners,
    near,
    first,
    final,
    steps,
    me_ref,
    live_ref,
    heard_ref,
    norm_ref,
    vectors_ref,
    weights_ref,
    grad_ref,
    away_ref,
    maps_ref,
    *refs,
):
    far = partners - near
    before_ref, (filter_ref, product, columns, output, upright, stack) = refs[0], refs[-6:]
    piece_refs = refs[-6 - near - far * len(steps) : -6]
    step = pl.program_id(0)
    count = grad_ref.shape[0]

    @pl.when(step == 0)
    def _():
        columns[...] = last_columns(heard_ref, norm_ref, vectors_ref)
        product[...] = before_ref[...] if first else jnp.zeros_like(product)

    for image in range(count):
        live = live_ref[first + step * count + image]
        error = norm_back(live, columns, grad_ref[image], away_ref[image], CELLS_TWO)
        stack_upright(cut(error, WIDE), MAP, upright.at[image])
        write(output.at[image], [block.astype(BF16) for block in conv_behind(weights_ref, upright.at[image], MAP)])
        stack_sideways(cut(maps_ref[image], WIDE), MAP, stack.at[image])
        product[...] += across_cells(upright.at[image], stack.at[image])
    rows = C // partners
    start = 0
    for place, length in enumerate(steps):

        @pl.when((step >= start) & (step < start + length))
        def _():
            for image in range(count):
                for partner in range(partners):
                    piece_ref = piece_refs[partner if partner < near else near + place * far + partner - near]
                    piece_ref[image] = output[image, own_rows(me_ref[0], partner, rows), 0:CELLS_TWO]

        start += length

    @pl.when(step == pl.num_programs(0) - 1)
    def _():
        if final:
            split_filter(product, filter_ref)
        else:
            filter_ref[...] = product[...]


def strips_kernel(heard_ref, out_ref):
    out_ref[...] = jnp.broadcast_to(jnp.sum(heard_ref[...].astype(F32), axis=0)[None], out_ref.shape)


def one_hot(rows, columns, wanted):
    row_ids = lax.broadcasted_iota(jnp.int32, (rows, columns), 0)
    column_ids = lax.broadcasted_iota(jnp.int32, (rows, columns), 1)
    return jnp.where(wanted(row_ids, column_ids), 1.0, 0.0)


def exact_dot(left, right, contract=((1,), (0,))):
    return lax.dot_general(left, right, (contract, ((), ())), precision=PRECISE, preferred_element_type=F32)


def finish_kernel(
    partners,
    group,
    here_ref,
    me_ref,
    heard_two_ref,
    heard_top_ref,
    heard_back_ref,
    norm_two_ref,
    norm_three_ref,
    vectors_ref,
    film_ref,
    *refs,
):
    film_w_ref, film_b_ref, context_ref, sums_ref, levels_ref, product = refs[-6:]
    devices = heard_two_ref.shape[0]
    tasks = devices // group
    contexts = context_ref.shape[0]
    rows = C // partners
    entries = film_ref.shape[2]
    turn = (C - me_ref[0] * rows) % C

    def own_lanes(values):
        return pltpu.roll(values, turn, 1)[:, :rows]

    by_task = one_hot(tasks, devices, lambda t, d: d // group == t)
    of_task = one_hot(
        tasks, devices, lambda t, d: (d // partners == t // contexts) & (d % partners == t % contexts)
    )
    mine = one_hot(contexts, devices, lambda t, d: d // group == here_ref[0] * contexts + t)
    shift, normed = heard_top_ref[:, 0, :], heard_top_ref[:, 1, :]
    scale = row(vectors_ref, 2) * normed + row(vectors_ref, 3) * shift
    told = exact_dot(of_task, heard_two_ref[:, 3, :])
    total = jnp.zeros((contexts, entries), F32)
    for kind, grads in enumerate((scale, shift)):
        grads_by_task = exact_dot(by_task, grads)
        product[...] = exact_dot(grads_by_task, told, ((0,), (0,)))
        film_w_ref[kind] = product[pl.ds(pl.multiple_of(me_ref[0] * rows, rows), rows), :entries]
        film_b_ref[kind : kind + 1] = own_lanes(jnp.sum(grads_by_task, axis=0, keepdims=True))
        total = total + exact_dot(exact_dot(mine, grads), film_ref[kind])
    context_ref[...] = total

    back = jnp.sum(heard_back_ref[...], axis=0)
    top = jnp.sum(heard_top_ref[...], axis=0)
    sums_ref[...] = own_lanes(row_tile([back[1:2], back[0:1], top[3:4], top[2:3]]))

    live = norm_two_ref[3:4, 0:1] * (1.0 / CELLS_TWO)
    lanes = lane_ids(C)

    def mean_square(norm_ref, gain, shift):
        factor, variance = row(norm_ref, 1), row(norm_ref, 2)
        return jnp.sum(gain * gain * variance * factor * factor + shift * shift, axis=1, keepdims=True) * (1.0 / C)

    def mean_conv(norm_ref):
        middle = row(norm_ref, 0)
        return jnp.sum(row(norm_ref, 2) + middle * middle, axis=1, keepdims=True) * (1.0 / C)

    known = (
        mean_conv(norm_two_ref),
        mean_square(norm_two_ref, row(vectors_ref, 0), row(vectors_ref, 1)),
        back[2:3, 0:1] / (live * (C * CELLS_TWO)),
        back[2:3, 1:2] / (live * (C * CELLS_THREE)),
        mean_conv(norm_three_ref),
        mean_square(norm_three_ref, row(vectors_ref, 2), row(vectors_ref, 3)),
        back[2:3, 2:3] / (live * (C * CELLS_THREE)),
        back[2:3, 3:4] / (live * (C * CELLS_THREE)),
        back[2:3, 4:5] / (live * (C * CELLS_OUT)),
    )
    level = jnp.zeros((1, C), F32)
    for place, value in enumerate(known):
        level = jnp.where(lanes == place, value, level)
    levels_ref[...] = jnp.sqrt(level)


def pool_matrix(side, width, out_width):
    half = side // 2
    matrix = np.zeros((width, out_width), np.float32)
    for row in range(2 * half):
        for column in range(2 * half):
            matrix[row * side + column, (row // 2) * half + column // 2] = 0.25
    return matrix


def lasting(microseconds):
    return pl.CostEstimate(
        flops=int(microseconds * 1.1e9), bytes_accessed=int(microseconds * 3.5e6), transcendentals=0
    )


def smem():
    return pl.BlockSpec(memory_space=pltpu.SMEM)


def anywhere(count):
    return [pl.BlockSpec(memory_space=pl.ANY)] * count


def whole(*shape):
    return pl.BlockSpec(shape, lambda n: (0,) * len(shape))


def each(*shape, first=0, count=1):
    return pl.BlockSpec((count, *shape), lambda n: (first + n,) + (0,) * len(shape))


def pack(maps, me, images_each, wants, earlier=()):
    rows, slots, cells = maps.shape
    group = CAP // images_each
    halves = 2
    block = wants[0][0] // group
    return pl.pallas_call(
        functools.partial(pack_kernel, images_each, group, wants),
        grid_spec=pltpu.PrefetchScalarGridSpec(
            num_scalar_prefetch=1,
            grid=(halves,),
            in_specs=[
                pl.BlockSpec((rows // halves, CAP, cells), lambda n, me_ref: (n, (me_ref[0] // group) ^ block, 0)),
                *anywhere(len(earlier)),
            ],
            out_specs=[
                pl.BlockSpec((count, rows // halves, cells), lambda n, me_ref: (0, n, 0)) for _, _, count in wants
            ],
        ),
        out_shape=[jax.ShapeDtypeStruct((count, rows, cells), maps.dtype) for _, _, count in wants],
        compiler_params=kernel_params(),
        name="pack",
        cost_estimate=lasting(2.5),
    )(me, maps, *earlier)


def unpack(arrays, me, images_each, dtype, place, outs=(), earlier=()):
    partners = len(arrays[0])
    span = max(8, images_each) if dtype == F32 else 16
    group = span // images_each
    halves = 2
    given, specs, counts, shapes, out_specs = [], [], [], [], []
    for pieces in arrays:
        here = pieces[place * group : (place + 1) * group]
        counts.append(tuple(tuple(piece.shape[0] for piece in parts) for parts in here))
        rows, cells = here[0][0].shape[1:]
        for piece in (piece for parts in here for piece in parts):
            given.append(piece)
            specs.append(pl.BlockSpec((piece.shape[0], rows // halves, cells), lambda n, me_ref: (0, n, 0)))
        shapes.append(jax.ShapeDtypeStruct((rows, partners * images_each, cells), dtype))
        out_specs.append(
            pl.BlockSpec((rows // halves, span, cells), lambda n, me_ref: (n, (me_ref[0] // group) ^ place, 0))
        )
    aliases = {1 + len(given) + k: k for k in range(len(outs))}
    given += [*outs, *earlier]
    specs += anywhere(len(given) - len(specs))
    return pl.pallas_call(
        functools.partial(unpack_kernel, counts),
        grid_spec=pltpu.PrefetchScalarGridSpec(
            num_scalar_prefetch=1, grid=(halves,), in_specs=specs, out_specs=out_specs
        ),
        out_shape=shapes,
        input_output_aliases=aliases,
        compiler_params=kernel_params(),
        name="unpack",
        cost_estimate=lasting(2.0),
    )(me, *given)


def local(
    images,
    counts,
    context,
    filter_two,
    gain_two,
    shift_two,
    filter_three,
    gain_three,
    shift_three,
    film_weight,
    film_bias,
    cotangent,
    *,
    partners,
    columns,
):
    devices = partners * columns
    rows, slots = images.shape[:2]
    images_each = slots // partners
    group = CAP // images_each
    one = 1
    pair, some = min(images_each, 2), min(images_each, 4)
    position = lax.axis_index("tensor")
    me = jnp.reshape(position, (1,)).astype(jnp.int32)

    def swap(value, partner):
        if partner == 0:
            return value
        return lax.ppermute(value, "tensor", [(i, i ^ partner) for i in range(partners)])

    def share(copies):
        return lax.all_to_all(copies, ("dp", "tensor"), 0, 0)

    near = 2
    half, quarter = images_each // 2, images_each // 4
    sizes_in = (half, quarter, quarter) if quarter >= pair else (half, half)
    calls_out = ((pair,),) * (images_each // pair)
    starts_in = [sum(sizes_in[:part]) for part in range(len(sizes_in))]
    counts_of = [(images_each,) if partner < near else sizes_in for partner in range(partners)]
    far = [partner for partner in reversed(range(partners)) if partner >= near]
    maps = [[None] * len(counts_of[partner]) for partner in range(partners)]

    def send_in(some_parts, whole_near, earlier):
        for block in reversed(range(partners // group)):
            wants = [
                (partner, starts_in[part], sizes_in[part])
                for part in some_parts
                for partner in far
                if partner // group == block
            ]
            if block == 0 and whole_near:
                wants += [(partner, 0, images_each) for partner in range(near)]
            if wants:
                sent = pack(images, me, images_each, wants, earlier)
                for piece, (partner, first, _) in zip(sent, wants):
                    maps[partner][starts_in.index(first)] = swap(piece, partner)
                earlier = (*earlier, sent[0])
        return earlier

    first_sent = send_in((0,), True, ())
    entries = film_weight.shape[0]
    bundle = pl.pallas_call(
        bundle_kernel,
        in_specs=[pl.BlockSpec(memory_space=pltpu.VMEM)] * 8 + anywhere(1),
        out_shape=jax.ShapeDtypeStruct((7 * rows + 16, 3 * C), BF16),
        compiler_params=kernel_params(0),
        name="bundle",
        cost_estimate=lasting(1.0),
    )(
        jnp.transpose(filter_two, (2, 3, 0, 1)),
        jnp.transpose(filter_three, (2, 3, 0, 1)),
        jnp.transpose(film_weight, (1, 2, 0)),
        film_bias,
        *[vector[None] for vector in (gain_two, shift_two, gain_three, shift_three)],
        first_sent[0],
    )
    bundles = {0: bundle}
    bit = partners // 2
    while bit:
        bundles.update({partner | bit: swap(piece, bit) for partner, piece in bundles.items()})
        bit //= 2

    sent_in = {
        part: send_in((part,), False, (bundles[partners // 2] if part == 1 else maps[far[-1]][0],))
        for part in range(1, len(sizes_in))
    }

    task = position // group
    slot = (position % group) * images_each + jnp.arange(images_each, dtype=jnp.int32)
    limit = lax.dynamic_index_in_dim(counts, task, 0, keepdims=False)
    live = (slot < limit).astype(F32)
    ahead_two, behind_two, ahead_three, behind_three, film, vectors = pl.pallas_call(
        functools.partial(unbundle_kernel, partners),
        in_specs=[smem(), smem(), *[pl.BlockSpec(memory_space=pltpu.VMEM)] * (1 + partners)],
        out_shape=[jax.ShapeDtypeStruct((3 * C, 3 * C), BF16)] * 4
        + [jax.ShapeDtypeStruct((2, C, entries), F32), jax.ShapeDtypeStruct((8, C), F32)],
        compiler_params=kernel_params(0),
        name="unbundle",
        cost_estimate=lasting(2.0),
    )(me, jnp.reshape(task, (1,)).astype(jnp.int32), context, *[bundles[partner] for partner in range(partners)])

    told = lax.dynamic_index_in_dim(context, position % context.shape[0], 0)
    told = jnp.pad(told, ((0, 7), (0, C - entries)))

    conv_two = whole_maps = state = None
    for part, (first, count) in enumerate(zip(starts_in, sizes_in)):
        given = [maps[partner][0 if partner < near else part] for partner in range(partners)]
        specs = [
            each(rows, CELLS_TWO, first=first // pair if partner < near else 0, count=pair)
            for partner in range(partners)
        ]
        aliases = {}
        final = part == len(sizes_in) - 1
        if part:
            aliases = {5 + partners: 0, 6 + partners: 1}
            given = given + [state, conv_two, whole_maps]
            specs = specs + [whole(C, C), *anywhere(2)]
        waits = [] if final else [sent_in[part + 1][-1]]
        given = given + waits
        specs = specs + anywhere(len(waits))
        conv_two, whole_maps, state = pl.pallas_call(
            functools.partial(first_conv_kernel, partners, first, final),
            grid=(count // pair,),
            in_specs=[smem(), smem(), whole(8, C), whole(3 * C, 3 * C), *specs],
            out_specs=[
                each(C, LANES_TWO, first=first // pair, count=pair),
                each(C, LANES_TWO, first=first // pair, count=pair),
                whole(devices, SENT, C) if final else whole(C, C),
            ],
            out_shape=[
                jax.ShapeDtypeStruct((images_each, C, LANES_TWO), F32),
                jax.ShapeDtypeStruct((images_each, C, LANES_TWO), BF16),
                jax.ShapeDtypeStruct((devices, SENT, C) if final else (C, C), F32),
            ],
            scratch_shapes=[
                pltpu.VMEM((pair, 3 * C, LANES_TWO), BF16),
                pltpu.VMEM((C, C), F32),
            ],
            input_output_aliases=aliases,
            compiler_params=kernel_params(),
            name="first_conv",
            cost_estimate=lasting(2.3 * count),
        )(me, live, told, ahead_two, *given)
    heard_two = share(state)
    turned = jnp.transpose(cotangent, (1, 0, 2))
    targets = [
        swap(lax.dynamic_slice_in_dim(turned, (position ^ partner) * images_each, images_each, 0), partner)
        for partner in range(partners)
    ]

    pool = pool_matrix(MAP, LANES_TWO, LANES_THREE)
    pool_out = pool_matrix(HALF, LANES_THREE, LANES_OUT)
    *block_pieces, hidden, conv_three, norm_two, levels, sums_three = pl.pallas_call(
        functools.partial(middle_kernel, partners),
        grid=(images_each // pair,),
        in_specs=[
            smem(),
            smem(),
            whole(devices, SENT, C),
            whole(8, C),
            whole(1152, 256),
            whole(896, 256),
            whole(3 * C, 3 * C),
            each(C, LANES_TWO, count=pair),
        ],
        out_specs=[each(rows, CELLS_THREE, count=pair)] * partners
        + [each(C, LANES_THREE, count=pair), each(C, LANES_THREE, count=pair), whole(8, C), whole(8, C), whole(devices, SENT, C)],
        out_shape=[jax.ShapeDtypeStruct((images_each, rows, CELLS_THREE), BF16)] * partners
        + [
            jax.ShapeDtypeStruct((images_each, C, LANES_THREE), BF16),
            jax.ShapeDtypeStruct((images_each, C, LANES_THREE), F32),
            jax.ShapeDtypeStruct((8, C), F32),
            jax.ShapeDtypeStruct((8, C), F32),
            jax.ShapeDtypeStruct((devices, SENT, C), F32),
        ],
        scratch_shapes=[
            pltpu.VMEM((C, C), F32),
            pltpu.VMEM((C, C), F32),
            pltpu.VMEM((pair, 3 * C, LANES_THREE), BF16),
        ],
        compiler_params=kernel_params(),
        name="middle",
            cost_estimate=lasting(2.0 * images_each),
    )(
        me,
        live,
        heard_two,
        vectors,
        jnp.asarray(pool[:1152, :256], BF16),
        jnp.asarray(pool[896:, 256:], BF16),
        ahead_three,
        conv_two,
    )
    heard_three = share(sums_three)

    *out_pieces, grad_three, norm_three, levels, sums_top = pl.pallas_call(
        functools.partial(top_kernel, partners),
        grid=(images_each // some,),
        in_specs=[
            smem(),
            smem(),
            whole(devices, SENT, C),
            whole(1, SENT, C),
            whole(8, C),
            whole(8, C),
            whole(LANES_THREE, LANES_OUT),
            whole(LANES_OUT, LANES_THREE),
            each(C, LANES_THREE, count=some),
            *[each(rows, CELLS_OUT, count=some)] * partners,
        ],
        out_specs=[each(rows, CELLS_OUT, count=some)] * partners
        + [each(C, LANES_THREE, count=some), whole(8, C), whole(8, C), whole(devices, SENT, C)],
        out_shape=[jax.ShapeDtypeStruct((images_each, rows, CELLS_OUT), BF16)] * partners
        + [
            jax.ShapeDtypeStruct((images_each, C, LANES_THREE), F32),
            jax.ShapeDtypeStruct((8, C), F32),
            jax.ShapeDtypeStruct((8, C), F32),
            jax.ShapeDtypeStruct((devices, SENT, C), F32),
        ],
        scratch_shapes=[
            pltpu.VMEM((C, C), F32),
            pltpu.VMEM((some, C, LANES_OUT), BF16),
            pltpu.VMEM((some, C, LANES_OUT), BF16),
            pltpu.VMEM((C, C), F32),
        ],
        compiler_params=kernel_params(),
        name="top",
            cost_estimate=lasting(0.8 * images_each),
    )(
        me,
        live,
        heard_three,
        sums_three,
        levels,
        vectors,
        jnp.asarray(pool_out, BF16),
        jnp.asarray(pool_out.T, BF16),
        conv_three,
        *targets,
    )
    heard_top = share(sums_top)
    block_two = [[swap(block_pieces[k], k)] for k in range(partners)]
    out_pieces = [[swap(out_pieces[k], k)] for k in range(partners)]

    filter_shape = jax.ShapeDtypeStruct((partners, 2, 3, rows, 3 * C), BF16)

    def filter_spec(block):
        return pl.BlockSpec((partners, None, 3, rows, 3 * C), lambda n: (0, block, 0, 0, 0))

    grad_two, away_two, sums_two, filter_sums = pl.pallas_call(
        back_kernel,
        grid=(images_each // pair,),
        in_specs=[
            smem(),
            whole(devices, SENT, C),
            whole(8, C),
            whole(8, C),
            whole(8, C),
            whole(8, C),
            whole(3 * C, 3 * C),
            whole(256, 896),
            whole(384, 896),
            each(C, LANES_THREE, count=pair),
            each(C, LANES_THREE, count=pair),
            each(C, LANES_THREE, count=pair),
            each(C, LANES_TWO, count=pair),
        ],
        out_specs=[
            each(C, LANES_TWO, count=pair),
            each(C, LANES_TWO, count=pair),
            whole(devices, SENT, C),
            filter_spec(1),
        ],
        out_shape=[
            jax.ShapeDtypeStruct((images_each, C, LANES_TWO), BF16),
            jax.ShapeDtypeStruct((images_each, C, LANES_TWO), BF16),
            jax.ShapeDtypeStruct((devices, SENT, C), F32),
            filter_shape,
        ],
        scratch_shapes=[
            pltpu.VMEM((C, C), F32),
            pltpu.VMEM((C, C), F32),
            pltpu.VMEM((C, C), F32),
            pltpu.VMEM((3 * C, 3 * C), F32),
            pltpu.VMEM((pair, 3 * C, LANES_THREE), BF16),
            pltpu.VMEM((pair, 3 * C, LANES_THREE), BF16),
        ],
        compiler_params=kernel_params(),
        name="back",
            cost_estimate=lasting(2.0 * images_each),
    )(
        live,
        heard_top,
        norm_three,
        norm_two,
        levels,
        vectors,
        behind_three,
        jnp.asarray(pool[:896, :256].T, BF16),
        jnp.asarray(pool[896:, 128:].T, BF16),
        grad_three,
        conv_three,
        hidden,
        conv_two,
    )
    heard_back = share(sums_two)

    returned = [[] for partner in range(partners)]
    waits = [pieces[0] for pieces in (*block_two, *out_pieces)]
    kept = []
    product = vectors
    first = 0
    for part, sizes in enumerate(calls_out):
        count = sum(sizes)
        final = part == len(calls_out) - 1
        if part == 2:
            waits = waits + [returned[near][0]]
        if part == 3:
            waits = waits + [returned[near][1], *(returned[partner][0] for partner in far)]
        if final:
            waits = waits + [filter_sums]
        size = one
        steps = [some // size for some in sizes]
        first_steps = [sum(steps[:place]) for place in range(len(steps))]
        out_specs = [each(rows, CELLS_TWO, first=first // size, count=size)] * near
        out_shape = [jax.ShapeDtypeStruct((images_each, rows, CELLS_TWO), BF16)] * near
        for start, length in zip(first_steps, steps):
            out_specs += [
                pl.BlockSpec(
                    (size, rows, CELLS_TWO),
                    lambda n, start=start, length=length: (jnp.clip(n - start, 0, length - 1), 0, 0),
                )
            ] * len(far)
            out_shape += [jax.ShapeDtypeStruct((length * size, rows, CELLS_TWO), BF16)] * len(far)
        out_specs.append(filter_spec(0) if final else whole(3 * C, 3 * C))
        out_shape.append(filter_shape if final else jax.ShapeDtypeStruct((3 * C, 3 * C), F32))
        inputs = [me, live, heard_back, norm_two, vectors, behind_two, grad_two, away_two, whole_maps, product]
        aliases = {len(inputs) + len(waits) + k: k for k in range(len(kept))}
        if final:
            aliases[len(inputs) + len(waits) - 1] = len(out_shape) - 1
        *pieces, product = pl.pallas_call(
            functools.partial(last_kernel, partners, near, first, final, steps),
            grid=(count // size,),
            in_specs=[
                smem(),
                smem(),
                whole(devices, SENT, C),
                whole(8, C),
                whole(8, C),
                whole(3 * C, 3 * C),
                *[each(C, LANES_TWO, first=first // size, count=size)] * 3,
                whole(*product.shape),
                *anywhere(len(waits) + len(kept)),
            ],
            out_specs=out_specs,
            out_shape=out_shape,
            scratch_shapes=[
                pltpu.VMEM((3 * C, 3 * C), F32),
                pltpu.VMEM((C, C), F32),
                pltpu.VMEM((size, C, LANES_TWO), BF16),
                pltpu.VMEM((size, 3 * C, LANES_TWO), BF16),
                pltpu.VMEM((size, 3 * C, LANES_TWO), BF16),
            ],
            input_output_aliases=aliases,
            compiler_params=kernel_params(),
            name="last",
            cost_estimate=lasting(2.5 * count),
        )(*inputs, *waits, *kept)
        kept, waits, first = pieces[:near], [], first + count
        for place in range(len(sizes)):
            for partner in reversed(far):
                returned[partner].append(swap(pieces[near + place * len(far) + partner - near], partner))
    for partner in range(near):
        returned[partner].append(swap(kept[partner], partner))

    ahead = (returned[near][-2], *(returned[partner][-3:][0] for partner in far))
    spans = partners * images_each // max(8, images_each)
    near_spans = max(1, near * images_each // 8)
    grad_images = ()
    for place in [*range(near_spans), *range(near_spans, spans)]:
        grad_images = unpack(
            [returned], me, images_each, F32, place, grad_images, () if grad_images else ahead
        )
    (grad_images,) = grad_images

    blocks = ()
    for place in range(partners // group):
        waits = [kept[0], *(returned[partner][-2] for partner in far)]
        blocks = unpack([block_two, out_pieces], me, images_each, BF16, place, blocks, waits)
    block_two, block_three = blocks

    strip = 6 * rows // columns
    heard = lax.all_to_all(product.reshape(devices, strip, 3 * C), ("tensor", "dp"), 0, 0)
    strips = pl.pallas_call(
        strips_kernel,
        out_shape=jax.ShapeDtypeStruct((columns, strip, 3 * C), F32),
        compiler_params=kernel_params(0),
        name="strips",
        cost_estimate=lasting(1.5),
    )(heard)
    strips = lax.all_to_all(strips, "dp", 0, 0).reshape(2, 3, rows, 3, C)
    grad_filters = jnp.transpose(strips, (0, 2, 4, 1, 3))

    contexts = context.shape[0]
    grad_film_w, grad_film_b, grad_context, norm_sums, levels = pl.pallas_call(
        functools.partial(finish_kernel, partners, group),
        in_specs=[smem(), smem(), *[pl.BlockSpec(memory_space=pltpu.VMEM)] * 7, *anywhere(1)],
        out_shape=[
            jax.ShapeDtypeStruct((2, rows, entries), F32),
            jax.ShapeDtypeStruct((2, rows), F32),
            jax.ShapeDtypeStruct((contexts, entries), F32),
            jax.ShapeDtypeStruct((8, rows), F32),
            jax.ShapeDtypeStruct((1, C), F32),
        ],
        scratch_shapes=[pltpu.VMEM((C, C), F32)],
        compiler_params=kernel_params(0),
        name="finish",
        cost_estimate=lasting(2.0),
    )(
        jnp.reshape(lax.axis_index("dp"), (1,)).astype(jnp.int32),
        me,
        heard_two,
        heard_top,
        heard_back,
        norm_two,
        norm_three,
        vectors,
        film,
        kept[0],
    )
    return (
        block_two,
        block_three,
        grad_images,
        grad_filters[0],
        norm_sums[0],
        norm_sums[1],
        grad_filters[1],
        norm_sums[2],
        norm_sums[3],
        jnp.transpose(grad_film_w, (2, 0, 1)),
        grad_film_b,
        grad_context,
        levels[0, :9],
    )


def solution(mesh):
    step = functools.partial(local, partners=mesh.shape["tensor"], columns=mesh.shape["dp"])
    placed = (
        P("tensor", "dp", None),
        P("dp"),
        P("dp", None),
        P("tensor", None, None, None),
        P("tensor"),
        P("tensor"),
        P("tensor", None, None, None),
        P("tensor"),
        P("tensor"),
        P(None, None, "tensor"),
        P(None, "tensor"),
        P("tensor", "dp", None),
    )
    return jax.shard_map(
        step,
        mesh=mesh,
        in_specs=placed,
        out_specs=(
            P("tensor", "dp", None),
            P("tensor", "dp", None),
            P("tensor", "dp", None),
            P("tensor", None, None, None),
            P("tensor"),
            P("tensor"),
            P("tensor", None, None, None),
            P("tensor"),
            P("tensor"),
            P(None, None, "tensor"),
            P(None, "tensor"),
            P("dp", None),
            P(),
        ),
        check_vma=False,
    )
```

```python
import functools

import jax
import jax.numpy as jnp
import numpy as np
from jax import lax
from jax.experimental import pallas as pl
from jax.experimental.pallas import tpu as pltpu
from jax.sharding import PartitionSpec as P

C = 128
MAP = 42
CAP = 16
HALF = 21
QUART = 10
SENT = 4
VMEM_BYTES = 63 << 20
WIDE = 256

CELLS_TWO = MAP * MAP
CELLS_THREE = HALF * HALF
CELLS_OUT = QUART * QUART
LANES_TWO = 1792
LANES_THREE = 512
LANES_OUT = 128
EPSILON = 1e-05
PRECISE = lax.Precision.HIGHEST
F32 = jnp.float32
BF16 = jnp.bfloat16
ROOT = 0.7978845608028654
CUBIC = 0.044715


def lane_ids(width):
    return lax.broadcasted_iota(jnp.int32, (1, width), 1)


def as_columns(rows):
    return jnp.concatenate([rows] * (C // 8), axis=0).T


def column_tile(columns):
    ids = lax.broadcasted_iota(jnp.int32, (C, C), 1)
    tile = jnp.zeros((C, C), F32)
    for place, column in enumerate(columns):
        tile = jnp.where(ids == place, column, tile)
    return tile


def row_tile(rows, count=8):
    ids = lax.broadcasted_iota(jnp.int32, (count, C), 0)
    tile = jnp.zeros((count, C), F32)
    for place, row in enumerate(rows):
        tile = jnp.where(ids == place, row, tile)
    return tile


def row(tile_ref, place):
    return tile_ref[place : place + 1, :]


def column(tile_ref, place):
    return tile_ref[:, place : place + 1]


def merge_moments(state, weight, mean, spread, cells):
    count, middle, total = state
    added = weight * cells
    both = count + added
    away = mean - middle
    share = added / jnp.maximum(both, 1.0)
    return both, middle + away * share, total + weight * spread + away * away * count * share


def slice_norm(heard_ref):
    means, spreads, counts = heard_ref[:, 0, :], heard_ref[:, 1, :], heard_ref[:, 2, :]
    extent = jnp.sum(counts, axis=0, keepdims=True)
    middle = jnp.sum(counts * means, axis=0, keepdims=True) / extent
    away = means - middle
    variance = jnp.sum(spreads + counts * away * away, axis=0, keepdims=True) / extent
    return middle, lax.rsqrt(variance + EPSILON), variance, extent


def level_row(columns):
    return jnp.sum(column_tile(columns), axis=0, keepdims=True)


def spread_rows(tile, out_ref):
    out_ref[...] = jnp.broadcast_to(tile[None], out_ref.shape)


def trim(values, first, last):
    tiles = cut(values, 128)
    ids = lane_ids(128)
    if first > 0:
        tiles[0] = jnp.where(ids >= first, tiles[0], jnp.zeros_like(tiles[0]))
    if last < values.shape[1]:
        tiles[-1] = jnp.where(ids < last - (values.shape[1] - 128), tiles[-1], jnp.zeros_like(tiles[-1]))
    return jnp.concatenate(tiles, axis=1)


def cut(values, wide):
    return [values[:, first : first + wide] for first in range(0, values.shape[1], wide)]


def shift_lanes(blocks, by):
    moved = [pltpu.roll(block, by % block.shape[1], 1) for block in blocks]
    nothing = jnp.zeros_like(moved[0][:, :128])
    ids = lane_ids(128)
    shifted = []
    for place, block in enumerate(moved):
        if by > 0:
            near = moved[place - 1][:, :128] if place else nothing
            edge = jnp.where(ids < by, near, block[:, :128])
            shifted.append(jnp.concatenate([edge, block[:, 128:]], axis=1) if block.shape[1] > 128 else edge)
        else:
            near = moved[place + 1][:, -128:] if place + 1 < len(moved) else nothing
            edge = jnp.where(ids >= 128 + by, near, block[:, -128:])
            shifted.append(jnp.concatenate([block[:, :-128], edge], axis=1) if block.shape[1] > 128 else edge)
    return shifted


def shift_column(blocks, by, side):
    shifted = []
    first = 0
    for block in shift_lanes(blocks, by):
        column = (lane_ids(block.shape[1]) + first) % side
        shifted.append(jnp.where(column == (0 if by > 0 else side - 1), jnp.zeros_like(block), block))
        first += block.shape[1]
    return shifted


def write(out_ref, blocks):
    first = 0
    for block in blocks:
        out_ref[:, first : first + block.shape[1]] = block
        first += block.shape[1]


def fill(stack_ref, tap, blocks):
    first = 0
    for block in blocks:
        stack_ref[tap * C : (tap + 1) * C, first : first + block.shape[1]] = block
        first += block.shape[1]


def stack_sideways(low, side, stack_ref):
    fill(stack_ref, 0, shift_column(low, 1, side))
    fill(stack_ref, 1, low)
    fill(stack_ref, 2, shift_column(low, -1, side))


def stack_upright(low, side, stack_ref):
    fill(stack_ref, 0, shift_lanes(low, -side))
    fill(stack_ref, 1, low)
    fill(stack_ref, 2, shift_lanes(low, side))


def conv_blocks(weights_ref, stack_ref):
    width = stack_ref.shape[1]
    parts = [
        jnp.dot(weights_ref[...], stack_ref[:, first : first + WIDE], preferred_element_type=F32)
        for first in range(0, width, WIDE)
    ]
    return [[part[tap * C : (tap + 1) * C] for part in parts] for tap in range(3)]


def conv_ahead(weights_ref, stack_ref, side):
    above, here, below = conv_blocks(weights_ref, stack_ref)
    total = [a + b + c for a, b, c in zip(shift_lanes(above, side), here, shift_lanes(below, -side))]
    total[-1] = trim(total[-1], 0, side * side - (stack_ref.shape[1] - total[-1].shape[1]))
    return total


def conv_behind(weights_ref, stack_ref, side):
    left, here, right = conv_blocks(weights_ref, stack_ref)
    return [a + b + c for a, b, c in zip(shift_column(left, -1, side), here, shift_column(right, 1, side))]


def across_cells(left_ref, right_ref):
    return lax.dot_general(left_ref[...], right_ref[...], (((1,), (1,)), ((), ())), preferred_element_type=F32)


def lane_sum(values):
    return jnp.sum(values, axis=1, keepdims=True)


def moments(blocks, cells):
    pivot = lane_sum(blocks[0]) * (1.0 / blocks[0].shape[1])
    total, squares = 0.0, 0.0
    for place, block in enumerate(blocks):
        away = block - pivot
        if place == len(blocks) - 1:
            away = trim(away, 0, cells - sum(b.shape[1] for b in blocks[:-1]))
        total = total + sum(cut(away, 128))
        squares = squares + sum(cut(away * away, 128))
    away = lane_sum(total) * (1.0 / cells)
    return pivot + away, lane_sum(squares) - cells * away * away


def gelu_gate(values):
    return 0.5 + 0.5 * jnp.tanh(values * (ROOT + (ROOT * CUBIC) * (values * values)))


def gelu_slope(values, gate):
    return gate * (1.0 + (1.0 - gate) * (values * (2.0 * ROOT + (6.0 * ROOT * CUBIC) * (values * values))))


def halves(values):
    high = values.astype(BF16)
    return jnp.concatenate([high, (values - high.astype(F32)).astype(BF16)], axis=0)


def dot_halves(split, weights_ref):
    both = jnp.dot(split, weights_ref[...], preferred_element_type=F32)
    return [both[first : first + C] + both[first + C : first + 2 * C] for first in range(0, both.shape[0], 2 * C)]


def own_rows(me, partner, count):
    return pl.ds(pl.multiple_of((me ^ partner) * count, count), count)


def kernel_params(axes=1):
    return pltpu.CompilerParams(vmem_limit_bytes=VMEM_BYTES, dimension_semantics=("arbitrary",) * axes)


def pack_kernel(images_each, group, wants, me_ref, maps_ref, *refs):
    piece_refs = refs[-len(wants) :]
    turned = jnp.swapaxes(maps_ref[...], 0, 1)
    for lead in range(group):

        @pl.when(me_ref[0] % group == lead)
        def _():
            for piece_ref, (partner, first, count) in zip(piece_refs, wants):
                start = (lead ^ (partner % group)) * images_each + first
                piece_ref[...] = turned[start : start + count]


def unpack_kernel(counts, me_ref, *refs):
    out_refs = refs[-len(counts) :]
    group = len(counts[0])
    for lead in range(group):

        @pl.when(me_ref[0] % group == lead)
        def _():
            start = 0
            for out_ref, parts in zip(out_refs, counts):
                ordered = []
                for slot in range(group):
                    place = start + sum(len(some) for some in parts[: slot ^ lead])
                    ordered += [refs[place + part][...] for part in range(len(parts[slot ^ lead]))]
                joined = jnp.concatenate(ordered, axis=0) if len(ordered) > 1 else ordered[0]
                out_ref[...] = jnp.swapaxes(joined, 0, 1).astype(out_ref.dtype)
                start += sum(len(some) for some in parts)


def bundle_kernel(filter_two_ref, filter_three_ref, film_ref, bias_ref, *refs):
    vector_refs, out_ref = refs[:4], refs[-1]
    rows = filter_two_ref.shape[2]
    out_ref[...] = jnp.zeros_like(out_ref)
    for place, filter_ref in enumerate((filter_two_ref, filter_three_ref)):
        for down in range(3):
            first = (3 * place + down) * rows
            for across in range(3):
                out_ref[first : first + rows, across * C : (across + 1) * C] = filter_ref[down, across]
    for kind in range(2):
        out_ref[6 * rows : 7 * rows, kind * C : kind * C + film_ref.shape[2]] = film_ref[kind]
    for place, vector_ref in enumerate(vector_refs):
        out_ref[7 * rows + place : 7 * rows + place + 1, 0:rows] = vector_ref[...]
    for kind in range(2):
        out_ref[7 * rows + 4 + kind : 7 * rows + 5 + kind, 0:rows] = bias_ref[kind : kind + 1]


def unbundle_kernel(partners, me_ref, task_ref, context_ref, *refs):
    piece_refs = refs[:partners]
    ahead_two_ref, behind_two_ref, ahead_three_ref, behind_three_ref, film_ref, vectors_ref = refs[partners:]
    rows = C // partners
    entries = film_ref.shape[2]
    lanes = jnp.zeros((8, C), F32)
    ids = lane_ids(C)
    for partner, piece_ref in enumerate(piece_refs):
        owner = me_ref[0] ^ partner
        for place, ahead_ref in enumerate((ahead_two_ref, ahead_three_ref)):
            for down in range(3):
                first = (3 * place + down) * rows
                ahead_ref[pl.ds(pl.multiple_of(down * C + owner * rows, rows), rows), :] = piece_ref[first : first + rows]
        for kind in range(2):
            film_ref[kind, own_rows(me_ref[0], partner, rows), :] = piece_ref[
                6 * rows : 7 * rows, kind * C : kind * C + entries
            ].astype(F32)
        own = jnp.where(ids < rows, piece_ref[7 * rows : 7 * rows + 16, 0:C].astype(F32)[:8], 0.0)
        lanes = lanes + pltpu.roll(own, owner * rows, 1)
    behind_two_ref[...] = ahead_two_ref[...].T
    behind_three_ref[...] = ahead_three_ref[...].T
    context = context_ref[pl.ds(task_ref[0], 1), :]
    told = [lane_sum(film_ref[kind] * context) for kind in range(2)]
    told = column_tile(told).T[:8]
    scale = 1.0 + told[0:1] + lanes[4:5]
    shift = told[1:2] + lanes[5:6]
    vectors_ref[...] = row_tile([lanes[0:1], lanes[1:2], lanes[2:3], lanes[3:4], scale, shift])


def assemble(maps, cells, me, piece_refs, index):
    rows = C // len(piece_refs)
    for partner, piece_ref in enumerate(piece_refs):
        maps[own_rows(me, partner, rows), 0:cells] = piece_ref[index]


def disperse(piece_refs, index, me, output, cells):
    rows = C // len(piece_refs)
    for partner, piece_ref in enumerate(piece_refs):
        piece_ref[index] = output[own_rows(me, partner, rows), 0:cells]


def first_conv_kernel(partners, first, final, me_ref, live_ref, told_ref, weights_ref, *refs):
    piece_refs = refs[:partners]
    conv_ref, maps_ref, state_ref, stack, state = refs[-5:]
    step = pl.program_id(0)
    count = conv_ref.shape[0]

    @pl.when(step == 0)
    def _():
        state[...] = refs[partners][...] if first else jnp.zeros_like(state)

    merged = [column(state, k) for k in range(3)]
    for image in range(count):
        maps_ref[image, :, CELLS_TWO // 128 * 128 :] = jnp.zeros((C, LANES_TWO - CELLS_TWO // 128 * 128), BF16)
        assemble(maps_ref.at[image], CELLS_TWO, me_ref[0], piece_refs, image)
        stack_sideways(cut(maps_ref[image], WIDE), MAP, stack.at[image])
        conv = conv_ahead(weights_ref, stack.at[image], MAP)
        write(conv_ref.at[image], conv)
        mean, spread = moments(conv, CELLS_TWO)
        live = live_ref[first + step * count + image]
        merged = merge_moments(merged, live, mean, spread, CELLS_TWO)
    state[...] = column_tile(merged)

    @pl.when(step == pl.num_programs(0) - 1)
    def _():
        if final:
            turned = state[...].T
            spread_rows(row_tile([turned[1:2], turned[2:3], turned[0:1], row(told_ref, 0)], SENT), state_ref)
        else:
            state_ref[...] = state[...]


def middle_kernel(
    partners, me_ref, live_ref, heard_ref, vectors_ref, pool_a_ref, pool_b_ref, weights_ref, conv_ref, *refs
):
    hidden_ref, conv_three_ref, norm_ref, levels_ref, sums_ref, columns, state, stack = refs[-8:]
    piece_refs = refs[-8 - partners : -8]
    step = pl.program_id(0)
    count = conv_ref.shape[0]

    @pl.when(step == 0)
    def _():
        middle, factor, variance, extent = slice_norm(heard_ref)
        norm_ref[...] = row_tile([middle, factor, variance, extent])
        columns[...] = as_columns(row_tile([middle, row(vectors_ref, 0) * factor, row(vectors_ref, 1)]))
        state[...] = jnp.zeros_like(state)

    merged = [column(state, k) for k in range(3)]
    active_squares, hidden_squares = column(state, 3), column(state, 4)
    for image in range(count):
        live = live_ref[step * count + image]
        pre = (conv_ref[image] - column(columns, 0)) * column(columns, 1) + column(columns, 2)
        active = pre * gelu_gate(pre)
        counted = trim(active, 0, CELLS_TWO)
        active_squares = active_squares + live * lane_sum(counted * counted)
        split = halves(active)
        (left,) = dot_halves(split[:, :1152], pool_a_ref)
        (right,) = dot_halves(split[:, 896:], pool_b_ref)
        hidden = live * jnp.concatenate([left, right], axis=1)
        hidden_squares = hidden_squares + lane_sum(hidden * hidden)
        hidden_low = hidden.astype(BF16)
        hidden_ref[image] = hidden_low
        disperse(piece_refs, image, me_ref[0], hidden_ref.at[image], CELLS_THREE)
        stack_sideways(cut(hidden_low, WIDE), HALF, stack.at[image])
        conv = conv_ahead(weights_ref, stack.at[image], HALF)
        write(conv_three_ref.at[image], conv)
        mean, spread = moments(conv, CELLS_THREE)
        merged = merge_moments(merged, live, mean, spread, CELLS_THREE)
    state[...] = column_tile([*merged, active_squares, hidden_squares])

    @pl.when(step == pl.num_programs(0) - 1)
    def _():
        turned = state[...].T
        spread_rows(row_tile([turned[k : k + 1] for k in (1, 2, 0)], SENT), sums_ref)
        levels_ref[...] = row_tile([level_row([column(state, 3), column(state, 4)])])


def top_kernel(
    partners, me_ref, live_ref, heard_ref, own_ref, before_ref, vectors_ref, pool_ref, spread_ref, conv_ref, *refs
):
    target_refs = refs[:partners]
    piece_refs = refs[partners : 2 * partners]
    grad_ref, norm_ref, levels_ref, sums_ref, columns, target, output, totals = refs[2 * partners :]
    step = pl.program_id(0)
    count = conv_ref.shape[0]

    @pl.when(step == 0)
    def _():
        middle, factor, variance, extent = slice_norm(heard_ref)
        norm_ref[...] = row_tile([middle, factor, variance, extent])
        columns[...] = as_columns(row_tile([middle, factor] + [row(vectors_ref, k) for k in (2, 3, 4, 5)]))
        target[...] = jnp.zeros_like(target)
        totals[...] = jnp.zeros_like(totals)

    scale = column(columns, 4)
    slope = scale * column(columns, 2)
    offset = scale * column(columns, 3) + column(columns, 5)
    sums = [jnp.zeros((C, 1), F32)] * 4
    for image in range(count):
        live = live_ref[step * count + image]
        assemble(target.at[image], CELLS_OUT, me_ref[0], target_refs, image)
        normed = (conv_ref[image] - column(columns, 0)) * column(columns, 1)
        filmed = slope * normed + offset
        gate = gelu_gate(filmed)
        active = filmed * gate
        counted = trim(active, 0, CELLS_THREE)
        (pooled,) = dot_halves(halves(active), pool_ref)
        pooled = live * pooled
        output[image] = pooled.astype(BF16)
        disperse(piece_refs, image, me_ref[0], output.at[image], CELLS_OUT)
        spread = jnp.dot(target[image], spread_ref[...], preferred_element_type=F32)
        grad_filmed = live * spread * gelu_slope(filmed, gate)
        grad_ref[image] = scale * grad_filmed
        parts = (
            lane_sum(grad_filmed),
            lane_sum(grad_filmed * normed),
            live * lane_sum(counted * counted),
            lane_sum(pooled * pooled),
        )
        sums = [total + part for total, part in zip(sums, parts)]
    totals[...] += column_tile(sums)

    @pl.when(step == pl.num_programs(0) - 1)
    def _():
        turned = totals[...].T
        shift_sum, scale_sum = turned[0:1], turned[1:2]
        film_scale = row(vectors_ref, 4)
        slope = film_scale * row(vectors_ref, 2) * row(norm_ref, 1)
        offset = film_scale * row(vectors_ref, 3) + row(vectors_ref, 5)
        extent = own_ref[0, 2:3, :]
        away = own_ref[0, 0:1, :] - row(norm_ref, 0)
        filmed_squares = (
            slope * slope * (own_ref[0, 1:2, :] + extent * away * away)
            + 2.0 * slope * offset * extent * away
            + extent * offset * offset
        )
        spread_rows(
            row_tile([shift_sum, scale_sum, film_scale * shift_sum, film_scale * scale_sum], SENT), sums_ref
        )
        nothing = jnp.zeros((C, 1), F32)
        others = level_row([nothing, nothing, nothing, column(totals, 2), column(totals, 3)])
        lanes = lane_ids(C)
        filmed_total = lane_sum(filmed_squares)
        levels_ref[...] = before_ref[...] + row_tile([others + jnp.where(lanes == 2, filmed_total, 0.0)])


def norm_back(live, columns, grad, away, cells):
    scaled = [live * column(columns, k) for k in (1, 2, 3)]
    error = grad.astype(F32) * scaled[0] - scaled[1] - away.astype(F32) * scaled[2]
    return trim(error, 0, cells).astype(BF16)


def norm_back_columns(norm_ref, gain, bias_sum, gain_sum):
    factor, extent = row(norm_ref, 1), row(norm_ref, 3)
    front = gain * factor
    return as_columns(
        row_tile([row(norm_ref, 0), front, front * bias_sum / extent, front * factor * gain_sum / extent])
    )


def back_kernel(
    live_ref,
    heard_ref,
    norm_three_ref,
    norm_two_ref,
    levels_ref,
    vectors_ref,
    weights_ref,
    unpool_a_ref,
    unpool_b_ref,
    grad_ref,
    conv_three_ref,
    hidden_ref,
    conv_two_ref,
    *refs,
):
    out_ref, away_ref, sums_ref, filter_ref, columns_three, columns_two, totals, product, stack, upright = refs[-10:]
    step = pl.program_id(0)
    count = conv_two_ref.shape[0]

    @pl.when(step == 0)
    def _():
        sums = jnp.sum(heard_ref[...], axis=0)
        columns_three[...] = norm_back_columns(norm_three_ref, row(vectors_ref, 2), sums[2:3], sums[3:4])
        columns_two[...] = as_columns(
            row_tile([row(norm_two_ref, 0), row(vectors_ref, 0) * row(norm_two_ref, 1), row(vectors_ref, 1)])
        )
        totals[...] = jnp.zeros_like(totals)
        product[...] = jnp.zeros_like(product)

    grad_sum, product_sum = column(totals, 0), column(totals, 1)
    for image in range(count):
        away = conv_three_ref[image] - column(columns_three, 0)
        error = norm_back(live_ref[step * count + image], columns_three, grad_ref[image], away, CELLS_THREE)
        stack_upright(cut(error, WIDE), HALF, upright.at[image])
        stack_sideways(cut(hidden_ref[image], WIDE), HALF, stack.at[image])
    split = jnp.concatenate(
        [
            halves(jnp.concatenate(conv_behind(weights_ref, upright.at[image], HALF), axis=1))
            for image in range(count)
        ],
        axis=0,
    )
    left = dot_halves(split[:, :256], unpool_a_ref)
    right = dot_halves(split[:, 128:], unpool_b_ref)
    for image in range(count):
        away = conv_two_ref[image] - column(columns_two, 0)
        pre = away * column(columns_two, 1) + column(columns_two, 2)
        grad_pre = jnp.concatenate([left[image], right[image]], axis=1) * gelu_slope(pre, gelu_gate(pre))
        out_ref[image] = grad_pre.astype(BF16)
        away_ref[image] = away.astype(BF16)
        grad_sum = grad_sum + lane_sum(grad_pre)
        product_sum = product_sum + lane_sum(grad_pre * away)
    product[...] += sum(across_cells(upright.at[image], stack.at[image]) for image in range(count))
    totals[...] = column_tile([grad_sum, product_sum])

    @pl.when(step == pl.num_programs(0) - 1)
    def _():
        split_filter(product, filter_ref)
        turned = totals[...].T
        normed_sum = turned[1:2] * row(norm_two_ref, 1)
        spread_rows(row_tile([turned[0:1], normed_sum, levels_ref[0:1, :]], SENT), sums_ref)


def split_filter(product, filter_ref):
    partners, _, rows, _ = filter_ref.shape
    for tap in range(3):
        for owner in range(partners):
            filter_ref[owner, tap] = product[tap * C + owner * rows : tap * C + (owner + 1) * rows].astype(BF16)


def last_columns(heard_ref, norm_ref, vectors_ref):
    sums = jnp.sum(heard_ref[...], axis=0)
    return norm_back_columns(norm_ref, row(vectors_ref, 0), sums[0:1], sums[1:2])


def last_conv_kernel(
    partners,
    near,
    first,
    steps,
    me_ref,
    live_ref,
    heard_ref,
    norm_ref,
    vectors_ref,
    weights_ref,
    grad_ref,
    away_ref,
    *refs,
):
    far = partners - near
    piece_refs, (columns, output, upright) = refs[-3 - near - far * len(steps) : -3], refs[-3:]
    step = pl.program_id(0)
    count = grad_ref.shape[0]

    @pl.when(step == 0)
    def _():
        columns[...] = last_columns(heard_ref, norm_ref, vectors_ref)

    for image in range(count):
        live = live_ref[first + step * count + image]
        error = norm_back(live, columns, grad_ref[image], away_ref[image], CELLS_TWO)
        stack_upright(cut(error, WIDE), MAP, upright.at[image])
        write(output.at[image], [block.astype(BF16) for block in conv_behind(weights_ref, upright.at[image], MAP)])
    rows = C // partners
    start = 0
    for place, length in enumerate(steps):

        @pl.when((step >= start) & (step < start + length))
        def _():
            for image in range(count):
                for partner in range(partners):
                    piece_ref = piece_refs[partner if partner < near else near + place * far + partner - near]
                    piece_ref[image] = output[image, own_rows(me_ref[0], partner, rows), 0:CELLS_TWO]

        start += length


def last_filter_kernel(live_ref, heard_ref, norm_ref, vectors_ref, grad_ref, away_ref, maps_ref, *refs):
    filter_ref, product, columns, stack, upright = refs[-5:]
    step = pl.program_id(0)
    count = grad_ref.shape[0]

    @pl.when(step == 0)
    def _():
        columns[...] = last_columns(heard_ref, norm_ref, vectors_ref)
        product[...] = jnp.zeros_like(product)

    for image in range(count):
        error = norm_back(live_ref[step * count + image], columns, grad_ref[image], away_ref[image], CELLS_TWO)
        stack_upright(cut(error, WIDE), MAP, upright.at[image])
        stack_sideways(cut(maps_ref[image], WIDE), MAP, stack.at[image])
        product[...] += across_cells(upright.at[image], stack.at[image])

    @pl.when(step == pl.num_programs(0) - 1)
    def _():
        split_filter(product, filter_ref)


def strips_kernel(heard_ref, *refs):
    out_ref = refs[-1]
    out_ref[...] = jnp.broadcast_to(jnp.sum(heard_ref[...].astype(F32), axis=0)[None], out_ref.shape)


def one_hot(rows, columns, wanted):
    row_ids = lax.broadcasted_iota(jnp.int32, (rows, columns), 0)
    column_ids = lax.broadcasted_iota(jnp.int32, (rows, columns), 1)
    return jnp.where(wanted(row_ids, column_ids), 1.0, 0.0)


def exact_dot(left, right, contract=((1,), (0,))):
    return lax.dot_general(left, right, (contract, ((), ())), precision=PRECISE, preferred_element_type=F32)


def finish_kernel(
    partners,
    group,
    here_ref,
    me_ref,
    heard_two_ref,
    heard_top_ref,
    heard_back_ref,
    norm_two_ref,
    norm_three_ref,
    vectors_ref,
    film_ref,
    *refs,
):
    film_w_ref, film_b_ref, context_ref, *sum_refs, levels_ref, product = refs[-9:]
    devices = heard_two_ref.shape[0]
    tasks = devices // group
    contexts = context_ref.shape[0]
    rows = C // partners
    entries = film_ref.shape[2]
    turn = (C - me_ref[0] * rows) % C

    def own_lanes(values):
        return pltpu.roll(values, turn, 1)[:, :rows]

    by_task = one_hot(tasks, devices, lambda t, d: d // group == t)
    of_task = one_hot(
        tasks, devices, lambda t, d: (d // partners == t // contexts) & (d % partners == t % contexts)
    )
    mine = one_hot(contexts, devices, lambda t, d: d // group == here_ref[0] * contexts + t)
    shift, normed = heard_top_ref[:, 0, :], heard_top_ref[:, 1, :]
    scale = row(vectors_ref, 2) * normed + row(vectors_ref, 3) * shift
    told = exact_dot(of_task, heard_two_ref[:, 3, :])
    total = jnp.zeros((contexts, entries), F32)
    for kind, grads in enumerate((scale, shift)):
        grads_by_task = exact_dot(by_task, grads)
        product[...] = exact_dot(grads_by_task, told, ((0,), (0,)))
        film_w_ref[kind] = product[pl.ds(pl.multiple_of(me_ref[0] * rows, rows), rows), :entries]
        film_b_ref[kind : kind + 1] = own_lanes(jnp.sum(grads_by_task, axis=0, keepdims=True))
        total = total + exact_dot(exact_dot(mine, grads), film_ref[kind])
    context_ref[...] = total

    back = jnp.sum(heard_back_ref[...], axis=0)
    top = jnp.sum(heard_top_ref[...], axis=0)
    for sum_ref, sums in zip(sum_refs, (back[1:2], back[0:1], top[3:4], top[2:3])):
        sum_ref[...] = own_lanes(sums)[0]

    live = norm_two_ref[3:4, 0:1] * (1.0 / CELLS_TWO)
    lanes = lane_ids(C)

    def mean_square(norm_ref, gain, shift):
        factor, variance = row(norm_ref, 1), row(norm_ref, 2)
        return jnp.sum(gain * gain * variance * factor * factor + shift * shift, axis=1, keepdims=True) * (1.0 / C)

    def mean_conv(norm_ref):
        middle = row(norm_ref, 0)
        return jnp.sum(row(norm_ref, 2) + middle * middle, axis=1, keepdims=True) * (1.0 / C)

    known = (
        mean_conv(norm_two_ref),
        mean_square(norm_two_ref, row(vectors_ref, 0), row(vectors_ref, 1)),
        back[2:3, 0:1] / (live * (C * CELLS_TWO)),
        back[2:3, 1:2] / (live * (C * CELLS_THREE)),
        mean_conv(norm_three_ref),
        mean_square(norm_three_ref, row(vectors_ref, 2), row(vectors_ref, 3)),
        back[2:3, 2:3] / (live * (C * CELLS_THREE)),
        back[2:3, 3:4] / (live * (C * CELLS_THREE)),
        back[2:3, 4:5] / (live * (C * CELLS_OUT)),
    )
    level = jnp.zeros((1, C), F32)
    for place, value in enumerate(known):
        level = jnp.where(lanes == place, value, level)
    levels_ref[...] = jnp.sqrt(level)[0, : levels_ref.shape[0]]


def pool_matrix(side, width, out_width):
    half = side // 2
    matrix = np.zeros((width, out_width), np.float32)
    for row in range(2 * half):
        for column in range(2 * half):
            matrix[row * side + column, (row // 2) * half + column // 2] = 0.25
    return matrix


def lasting(microseconds):
    return pl.CostEstimate(
        flops=int(microseconds * 1.1e9), bytes_accessed=int(microseconds * 3.5e6), transcendentals=0
    )


def smem():
    return pl.BlockSpec(memory_space=pltpu.SMEM)


def anywhere(count):
    return [pl.BlockSpec(memory_space=pl.ANY)] * count


def whole(*shape):
    return pl.BlockSpec(shape, lambda n: (0,) * len(shape))


def each(*shape, first=0, count=1):
    return pl.BlockSpec((count, *shape), lambda n: (first + n,) + (0,) * len(shape))


def pack(maps, me, images_each, wants, earlier=()):
    rows, slots, cells = maps.shape
    group = CAP // images_each
    halves = 2
    block = wants[0][0] // group
    return pl.pallas_call(
        functools.partial(pack_kernel, images_each, group, wants),
        grid_spec=pltpu.PrefetchScalarGridSpec(
            num_scalar_prefetch=1,
            grid=(halves,),
            in_specs=[
                pl.BlockSpec((rows // halves, CAP, cells), lambda n, me_ref: (n, (me_ref[0] // group) ^ block, 0)),
                *anywhere(len(earlier)),
            ],
            out_specs=[
                pl.BlockSpec((count, rows // halves, cells), lambda n, me_ref: (0, n, 0)) for _, _, count in wants
            ],
        ),
        out_shape=[jax.ShapeDtypeStruct((count, rows, cells), maps.dtype) for _, _, count in wants],
        compiler_params=kernel_params(),
        name="pack",
        cost_estimate=lasting(2.5),
    )(me, maps, *earlier)


def unpack(arrays, me, images_each, dtype, place, outs=(), earlier=()):
    partners = len(arrays[0])
    group = CAP // images_each
    halves = 2
    given, specs, counts, shapes, out_specs = [], [], [], [], []
    for pieces in arrays:
        here = pieces[place * group : (place + 1) * group]
        counts.append(tuple(tuple(piece.shape[0] for piece in parts) for parts in here))
        rows, cells = here[0][0].shape[1:]
        for piece in (piece for parts in here for piece in parts):
            given.append(piece)
            specs.append(pl.BlockSpec((piece.shape[0], rows // halves, cells), lambda n, me_ref: (0, n, 0)))
        shapes.append(jax.ShapeDtypeStruct((rows, partners * images_each, cells), dtype))
        out_specs.append(
            pl.BlockSpec((rows // halves, CAP, cells), lambda n, me_ref: (n, (me_ref[0] // group) ^ place, 0))
        )
    aliases = {1 + len(given) + k: k for k in range(len(outs))}
    given += [*outs, *earlier]
    specs += anywhere(len(given) - len(specs))
    return pl.pallas_call(
        functools.partial(unpack_kernel, counts),
        grid_spec=pltpu.PrefetchScalarGridSpec(
            num_scalar_prefetch=1, grid=(halves,), in_specs=specs, out_specs=out_specs
        ),
        out_shape=shapes,
        input_output_aliases=aliases,
        compiler_params=kernel_params(),
        name="unpack",
        cost_estimate=lasting(2.0),
    )(me, *given)


def local(
    images,
    counts,
    context,
    filter_two,
    gain_two,
    shift_two,
    filter_three,
    gain_three,
    shift_three,
    film_weight,
    film_bias,
    cotangent,
    *,
    partners,
    columns,
):
    devices = partners * columns
    rows, slots = images.shape[:2]
    images_each = slots // partners
    group = CAP // images_each
    one = min(images_each, 2)
    pair, some = min(images_each, 2), min(images_each, 4)
    position = lax.axis_index("tensor")
    me = jnp.reshape(position, (1,)).astype(jnp.int32)

    def swap(value, partner):
        if partner == 0:
            return value
        return lax.ppermute(value, "tensor", [(i, i ^ partner) for i in range(partners)])

    def share(copies):
        return lax.all_to_all(copies, ("dp", "tensor"), 0, 0)

    near = 2
    half, quarter = images_each // 2, images_each // 4
    sizes_in = (half, quarter, quarter) if quarter >= pair else (half, half)
    half = images_each // 2
    calls_out = ((pair,) * (half // pair), (half,))
    starts_in = [sum(sizes_in[:part]) for part in range(len(sizes_in))]
    counts_of = [(images_each,) if partner < near else sizes_in for partner in range(partners)]
    far = [partner for partner in reversed(range(partners)) if partner >= near]
    maps = [[None] * len(counts_of[partner]) for partner in range(partners)]

    def send_in(some_parts, whole_near, earlier):
        for block in reversed(range(partners // group)):
            wants = [
                (partner, starts_in[part], sizes_in[part])
                for part in some_parts
                for partner in far
                if partner // group == block
            ]
            if block == 0 and whole_near:
                wants += [(partner, 0, images_each) for partner in range(near)]
            if wants:
                sent = pack(images, me, images_each, wants, earlier)
                for piece, (partner, first, _) in zip(sent, wants):
                    maps[partner][starts_in.index(first)] = swap(piece, partner)
                earlier = (*earlier, sent[0])
        return earlier

    first_sent = send_in((0,), True, ())
    entries = film_weight.shape[0]
    bundle = pl.pallas_call(
        bundle_kernel,
        in_specs=[pl.BlockSpec(memory_space=pltpu.VMEM)] * 8 + anywhere(1),
        out_shape=jax.ShapeDtypeStruct((7 * rows + 16, 3 * C), BF16),
        compiler_params=kernel_params(0),
        name="bundle",
        cost_estimate=lasting(1.0),
    )(
        jnp.transpose(filter_two, (2, 3, 0, 1)),
        jnp.transpose(filter_three, (2, 3, 0, 1)),
        jnp.transpose(film_weight, (1, 2, 0)),
        film_bias,
        *[vector[None] for vector in (gain_two, shift_two, gain_three, shift_three)],
        first_sent[0],
    )
    bundles = {0: bundle}
    bit = partners // 2
    while bit:
        bundles.update({partner | bit: swap(piece, bit) for partner, piece in bundles.items()})
        bit //= 2

    sent_in = {
        part: send_in((part,), False, (maps[far[0]][0],))
        for part in range(1, len(sizes_in))
    }

    task = position // group
    slot = (position % group) * images_each + jnp.arange(images_each, dtype=jnp.int32)
    limit = lax.dynamic_index_in_dim(counts, task, 0, keepdims=False)
    live = (slot < limit).astype(F32)
    ahead_two, behind_two, ahead_three, behind_three, film, vectors = pl.pallas_call(
        functools.partial(unbundle_kernel, partners),
        in_specs=[smem(), smem(), *[pl.BlockSpec(memory_space=pltpu.VMEM)] * (1 + partners)],
        out_shape=[jax.ShapeDtypeStruct((3 * C, 3 * C), BF16)] * 4
        + [jax.ShapeDtypeStruct((2, C, entries), F32), jax.ShapeDtypeStruct((8, C), F32)],
        compiler_params=kernel_params(0),
        name="unbundle",
        cost_estimate=lasting(2.0),
    )(me, jnp.reshape(task, (1,)).astype(jnp.int32), context, *[bundles[partner] for partner in range(partners)])

    told = lax.dynamic_index_in_dim(context, position % context.shape[0], 0)
    told = jnp.pad(told, ((0, 7), (0, C - entries)))

    conv_two = whole_maps = state = None
    for part, (first, count) in enumerate(zip(starts_in, sizes_in)):
        given = [maps[partner][0 if partner < near else part] for partner in range(partners)]
        specs = [
            each(rows, CELLS_TWO, first=first // pair if partner < near else 0, count=pair)
            for partner in range(partners)
        ]
        aliases = {}
        final = part == len(sizes_in) - 1
        if part:
            aliases = {5 + partners: 0, 6 + partners: 1}
            given = given + [state, conv_two, whole_maps]
            specs = specs + [whole(C, C), *anywhere(2)]
        waits = [] if final else [sent_in[part + 1][-1]]
        given = given + waits
        specs = specs + anywhere(len(waits))
        conv_two, whole_maps, state = pl.pallas_call(
            functools.partial(first_conv_kernel, partners, first, final),
            grid=(count // pair,),
            in_specs=[smem(), smem(), whole(8, C), whole(3 * C, 3 * C), *specs],
            out_specs=[
                each(C, LANES_TWO, first=first // pair, count=pair),
                each(C, LANES_TWO, first=first // pair, count=pair),
                whole(devices, SENT, C) if final else whole(C, C),
            ],
            out_shape=[
                jax.ShapeDtypeStruct((images_each, C, LANES_TWO), F32),
                jax.ShapeDtypeStruct((images_each, C, LANES_TWO), BF16),
                jax.ShapeDtypeStruct((devices, SENT, C) if final else (C, C), F32),
            ],
            scratch_shapes=[
                pltpu.VMEM((pair, 3 * C, LANES_TWO), BF16),
                pltpu.VMEM((C, C), F32),
            ],
            input_output_aliases=aliases,
            compiler_params=kernel_params(),
            name="first_conv",
            cost_estimate=lasting(2.3 * count),
        )(me, live, told, ahead_two, *given)
    heard_two = share(state)
    turned = jnp.transpose(cotangent, (1, 0, 2))
    targets = [
        swap(lax.dynamic_slice_in_dim(turned, (position ^ partner) * images_each, images_each, 0), partner)
        for partner in range(partners)
    ]

    pool = pool_matrix(MAP, LANES_TWO, LANES_THREE)
    pool_out = pool_matrix(HALF, LANES_THREE, LANES_OUT)
    *block_pieces, hidden, conv_three, norm_two, levels, sums_three = pl.pallas_call(
        functools.partial(middle_kernel, partners),
        grid=(images_each // pair,),
        in_specs=[
            smem(),
            smem(),
            whole(devices, SENT, C),
            whole(8, C),
            whole(1152, 256),
            whole(896, 256),
            whole(3 * C, 3 * C),
            each(C, LANES_TWO, count=pair),
        ],
        out_specs=[each(rows, CELLS_THREE, count=pair)] * partners
        + [each(C, LANES_THREE, count=pair), each(C, LANES_THREE, count=pair), whole(8, C), whole(8, C), whole(devices, SENT, C)],
        out_shape=[jax.ShapeDtypeStruct((images_each, rows, CELLS_THREE), BF16)] * partners
        + [
            jax.ShapeDtypeStruct((images_each, C, LANES_THREE), BF16),
            jax.ShapeDtypeStruct((images_each, C, LANES_THREE), F32),
            jax.ShapeDtypeStruct((8, C), F32),
            jax.ShapeDtypeStruct((8, C), F32),
            jax.ShapeDtypeStruct((devices, SENT, C), F32),
        ],
        scratch_shapes=[
            pltpu.VMEM((C, C), F32),
            pltpu.VMEM((C, C), F32),
            pltpu.VMEM((pair, 3 * C, LANES_THREE), BF16),
        ],
        compiler_params=kernel_params(),
        name="middle",
            cost_estimate=lasting(2.0 * images_each),
    )(
        me,
        live,
        heard_two,
        vectors,
        jnp.asarray(pool[:1152, :256], BF16),
        jnp.asarray(pool[896:, 256:], BF16),
        ahead_three,
        conv_two,
    )
    heard_three = share(sums_three)

    *out_pieces, grad_three, norm_three, levels, sums_top = pl.pallas_call(
        functools.partial(top_kernel, partners),
        grid=(images_each // some,),
        in_specs=[
            smem(),
            smem(),
            whole(devices, SENT, C),
            whole(1, SENT, C),
            whole(8, C),
            whole(8, C),
            whole(LANES_THREE, LANES_OUT),
            whole(LANES_OUT, LANES_THREE),
            each(C, LANES_THREE, count=some),
            *[each(rows, CELLS_OUT, count=some)] * partners,
        ],
        out_specs=[each(rows, CELLS_OUT, count=some)] * partners
        + [each(C, LANES_THREE, count=some), whole(8, C), whole(8, C), whole(devices, SENT, C)],
        out_shape=[jax.ShapeDtypeStruct((images_each, rows, CELLS_OUT), BF16)] * partners
        + [
            jax.ShapeDtypeStruct((images_each, C, LANES_THREE), F32),
            jax.ShapeDtypeStruct((8, C), F32),
            jax.ShapeDtypeStruct((8, C), F32),
            jax.ShapeDtypeStruct((devices, SENT, C), F32),
        ],
        scratch_shapes=[
            pltpu.VMEM((C, C), F32),
            pltpu.VMEM((some, C, LANES_OUT), BF16),
            pltpu.VMEM((some, C, LANES_OUT), BF16),
            pltpu.VMEM((C, C), F32),
        ],
        compiler_params=kernel_params(),
        name="top",
            cost_estimate=lasting(0.8 * images_each),
    )(
        me,
        live,
        heard_three,
        sums_three,
        levels,
        vectors,
        jnp.asarray(pool_out, BF16),
        jnp.asarray(pool_out.T, BF16),
        conv_three,
        *targets,
    )
    heard_top = share(sums_top)
    block_two = [[swap(block_pieces[k], k)] for k in range(partners)]
    out_pieces = [[swap(out_pieces[k], k)] for k in range(partners)]

    filter_shape = jax.ShapeDtypeStruct((partners, 2, 3, rows, 3 * C), BF16)

    def filter_spec(block):
        return pl.BlockSpec((partners, None, 3, rows, 3 * C), lambda n: (0, block, 0, 0, 0))

    grad_two, away_two, sums_two, filter_sums = pl.pallas_call(
        back_kernel,
        grid=(images_each // pair,),
        in_specs=[
            smem(),
            whole(devices, SENT, C),
            whole(8, C),
            whole(8, C),
            whole(8, C),
            whole(8, C),
            whole(3 * C, 3 * C),
            whole(256, 896),
            whole(384, 896),
            each(C, LANES_THREE, count=pair),
            each(C, LANES_THREE, count=pair),
            each(C, LANES_THREE, count=pair),
            each(C, LANES_TWO, count=pair),
        ],
        out_specs=[
            each(C, LANES_TWO, count=pair),
            each(C, LANES_TWO, count=pair),
            whole(devices, SENT, C),
            filter_spec(1),
        ],
        out_shape=[
            jax.ShapeDtypeStruct((images_each, C, LANES_TWO), BF16),
            jax.ShapeDtypeStruct((images_each, C, LANES_TWO), BF16),
            jax.ShapeDtypeStruct((devices, SENT, C), F32),
            filter_shape,
        ],
        scratch_shapes=[
            pltpu.VMEM((C, C), F32),
            pltpu.VMEM((C, C), F32),
            pltpu.VMEM((C, C), F32),
            pltpu.VMEM((3 * C, 3 * C), F32),
            pltpu.VMEM((pair, 3 * C, LANES_THREE), BF16),
            pltpu.VMEM((pair, 3 * C, LANES_THREE), BF16),
        ],
        compiler_params=kernel_params(),
        name="back",
            cost_estimate=lasting(2.0 * images_each),
    )(
        live,
        heard_top,
        norm_three,
        norm_two,
        levels,
        vectors,
        behind_three,
        jnp.asarray(pool[:896, :256].T, BF16),
        jnp.asarray(pool[896:, 128:].T, BF16),
        grad_three,
        conv_three,
        hidden,
        conv_two,
    )
    heard_back = share(sums_two)

    returned = [[] for partner in range(partners)]
    waits = [pieces[0] for pieces in (*block_two, *out_pieces)]
    common = [heard_back, norm_two, vectors]
    common_specs = [whole(devices, SENT, C), whole(8, C), whole(8, C)]
    kept = []
    first = 0
    for sizes in calls_out:
        count = sum(sizes)
        steps = [some // one for some in sizes]
        out_specs = [each(rows, CELLS_TWO, first=first // one, count=one)] * near
        out_shape = [jax.ShapeDtypeStruct((images_each, rows, CELLS_TWO), BF16)] * near
        for place, length in enumerate(steps):
            start = sum(steps[:place])
            out_specs += [
                pl.BlockSpec(
                    (one, rows, CELLS_TWO),
                    lambda n, start=start, length=length: (jnp.clip(n - start, 0, length - 1), 0, 0),
                )
            ] * len(far)
            out_shape += [jax.ShapeDtypeStruct((length * one, rows, CELLS_TWO), BF16)] * len(far)
        inputs = [me, live, *common, behind_two, grad_two, away_two]
        pieces = pl.pallas_call(
            functools.partial(last_conv_kernel, partners, near, first, steps),
            grid=(count // one,),
            in_specs=[
                smem(),
                smem(),
                *common_specs,
                whole(3 * C, 3 * C),
                *[each(C, LANES_TWO, first=first // one, count=one)] * 2,
                *anywhere(len(waits) + len(kept)),
            ],
            out_specs=out_specs,
            out_shape=out_shape,
            scratch_shapes=[
                pltpu.VMEM((C, C), F32),
                pltpu.VMEM((one, C, LANES_TWO), BF16),
                pltpu.VMEM((one, 3 * C, LANES_TWO), BF16),
            ],
            input_output_aliases={len(inputs) + len(waits) + k: k for k in range(len(kept))},
            compiler_params=kernel_params(),
            name="last_conv",
            cost_estimate=lasting(1.5 * count),
        )(*inputs, *waits, *kept)
        kept, waits, first = pieces[:near], [], first + count
        for place in range(len(sizes)):
            for partner in reversed(far):
                returned[partner].append(swap(pieces[near + place * len(far) + partner - near], partner))
        if first < images_each:
            product = pl.pallas_call(
                last_filter_kernel,
                grid=(images_each // pair,),
                in_specs=[
                    smem(),
                    *common_specs,
                    *[each(C, LANES_TWO, count=pair)] * 3,
                    *anywhere(2),
                ],
                out_specs=filter_spec(0),
                out_shape=filter_shape,
                scratch_shapes=[
                    pltpu.VMEM((3 * C, 3 * C), F32),
                    pltpu.VMEM((C, C), F32),
                    pltpu.VMEM((pair, 3 * C, LANES_TWO), BF16),
                    pltpu.VMEM((pair, 3 * C, LANES_TWO), BF16),
                ],
                input_output_aliases={7: 0},
                compiler_params=kernel_params(),
                name="last_filter",
                cost_estimate=lasting(1.2 * images_each),
            )(live, *common, grad_two, away_two, whole_maps, filter_sums, kept[0])
            waits = [product, *(piece for partner in far[:-1] for piece in returned[partner]), returned[near][0]]
    for partner in range(near):
        returned[partner].append(swap(kept[partner], partner))

    arrivals = [returned[partner][place] for place in range(len(returned[near])) for partner in reversed(far)]
    count_first = len(far) * len(calls_out[0])
    blocks = ()
    for place in range(partners // group):
        blocks = unpack([block_two, out_pieces], me, images_each, BF16, place, blocks, [kept[0]])
    block_two, block_three = blocks

    strip = 6 * rows // columns
    heard = lax.all_to_all(product.reshape(devices, strip, 3 * C), ("tensor", "dp"), 0, 0)
    strips = pl.pallas_call(
        strips_kernel,
        in_specs=[pl.BlockSpec(memory_space=pltpu.VMEM), *anywhere(1)],
        out_shape=jax.ShapeDtypeStruct((columns, strip, 3 * C), F32),
        compiler_params=kernel_params(0),
        name="strips",
        cost_estimate=lasting(1.5),
    )(heard, kept[0])
    strips = lax.all_to_all(strips, "dp", 0, 0).reshape(2, 3, rows, 3, C)
    grad_filters = jnp.transpose(strips, (0, 2, 4, 1, 3))

    grad_images = ()
    for place in range(partners // group):
        waits = () if grad_images else (arrivals[count_first],)
        grad_images = unpack([returned], me, images_each, F32, place, grad_images, waits)
    (grad_images,) = grad_images

    contexts = context.shape[0]
    grad_film_w, grad_film_b, grad_context, *norm_sums, levels = pl.pallas_call(
        functools.partial(finish_kernel, partners, group),
        in_specs=[smem(), smem(), *[pl.BlockSpec(memory_space=pltpu.VMEM)] * 7, *anywhere(1)],
        out_shape=[
            jax.ShapeDtypeStruct((2, rows, entries), F32),
            jax.ShapeDtypeStruct((2, rows), F32),
            jax.ShapeDtypeStruct((contexts, entries), F32),
            *[jax.ShapeDtypeStruct((rows,), F32)] * 4,
            jax.ShapeDtypeStruct((9,), F32),
        ],
        scratch_shapes=[pltpu.VMEM((C, C), F32)],
        compiler_params=kernel_params(0),
        name="finish",
        cost_estimate=lasting(2.0),
    )(
        jnp.reshape(lax.axis_index("dp"), (1,)).astype(jnp.int32),
        me,
        heard_two,
        heard_top,
        heard_back,
        norm_two,
        norm_three,
        vectors,
        film,
        kept[0],
    )
    return (
        block_two,
        block_three,
        grad_images,
        grad_filters[0],
        norm_sums[0],
        norm_sums[1],
        grad_filters[1],
        norm_sums[2],
        norm_sums[3],
        jnp.transpose(grad_film_w, (2, 0, 1)),
        grad_film_b,
        grad_context,
        levels,
    )


def solution(mesh):
    step = functools.partial(local, partners=mesh.shape["tensor"], columns=mesh.shape["dp"])
    placed = (
        P("tensor", "dp", None),
        P("dp"),
        P("dp", None),
        P("tensor", None, None, None),
        P("tensor"),
        P("tensor"),
        P("tensor", None, None, None),
        P("tensor"),
        P("tensor"),
        P(None, None, "tensor"),
        P(None, "tensor"),
        P("tensor", "dp", None),
    )
    return jax.shard_map(
        step,
        mesh=mesh,
        in_specs=placed,
        out_specs=(
            P("tensor", "dp", None),
            P("tensor", "dp", None),
            P("tensor", "dp", None),
            P("tensor", None, None, None),
            P("tensor"),
            P("tensor"),
            P("tensor", None, None, None),
            P("tensor"),
            P("tensor"),
            P(None, None, "tensor"),
            P(None, "tensor"),
            P("dp", None),
            P(),
        ),
        check_vma=False,
    )
```

```python
import functools

import jax
import jax.numpy as jnp
import numpy as np
from jax import lax
from jax.experimental import pallas as pl
from jax.experimental.pallas import tpu as pltpu
from jax.sharding import PartitionSpec as P

C = 128
MAP = 42
CAP = 16
HALF = 21
QUART = 10
SENT = 4
VMEM_BYTES = 63 << 20
WIDE = 256

CELLS_TWO = MAP * MAP
CELLS_THREE = HALF * HALF
CELLS_OUT = QUART * QUART
LANES_TWO = 1792
LANES_THREE = 512
LANES_OUT = 128
EPSILON = 1e-05
PRECISE = lax.Precision.HIGHEST
F32 = jnp.float32
BF16 = jnp.bfloat16
ROOT = 0.7978845608028654
CUBIC = 0.044715


def lane_ids(width):
    return lax.broadcasted_iota(jnp.int32, (1, width), 1)


def as_columns(rows):
    return jnp.concatenate([rows] * (C // 8), axis=0).T


def column_tile(columns):
    ids = lax.broadcasted_iota(jnp.int32, (C, C), 1)
    tile = jnp.zeros((C, C), F32)
    for place, column in enumerate(columns):
        tile = jnp.where(ids == place, column, tile)
    return tile


def row_tile(rows, count=8):
    ids = lax.broadcasted_iota(jnp.int32, (count, C), 0)
    tile = jnp.zeros((count, C), F32)
    for place, row in enumerate(rows):
        tile = jnp.where(ids == place, row, tile)
    return tile


def row(tile_ref, place):
    return tile_ref[place : place + 1, :]


def column(tile_ref, place):
    return tile_ref[:, place : place + 1]


def merge_moments(state, weight, mean, spread, cells):
    count, middle, total = state
    added = weight * cells
    both = count + added
    away = mean - middle
    share = added / jnp.maximum(both, 1.0)
    return both, middle + away * share, total + weight * spread + away * away * count * share


def slice_norm(heard_ref):
    means, spreads, counts = heard_ref[:, 0, :], heard_ref[:, 1, :], heard_ref[:, 2, :]
    extent = jnp.sum(counts, axis=0, keepdims=True)
    middle = jnp.sum(counts * means, axis=0, keepdims=True) / extent
    away = means - middle
    variance = jnp.sum(spreads + counts * away * away, axis=0, keepdims=True) / extent
    return middle, lax.rsqrt(variance + EPSILON), variance, extent


def level_row(columns):
    return jnp.sum(column_tile(columns), axis=0, keepdims=True)


def spread_rows(tile, out_ref):
    out_ref[...] = jnp.broadcast_to(tile[None], out_ref.shape)


def trim(values, first, last):
    tiles = cut(values, 128)
    ids = lane_ids(128)
    if first > 0:
        tiles[0] = jnp.where(ids >= first, tiles[0], jnp.zeros_like(tiles[0]))
    if last < values.shape[1]:
        tiles[-1] = jnp.where(ids < last - (values.shape[1] - 128), tiles[-1], jnp.zeros_like(tiles[-1]))
    return jnp.concatenate(tiles, axis=1)


def cut(values, wide):
    return [values[:, first : first + wide] for first in range(0, values.shape[1], wide)]


def shift_lanes(blocks, by):
    moved = [pltpu.roll(block, by % block.shape[1], 1) for block in blocks]
    nothing = jnp.zeros_like(moved[0][:, :128])
    ids = lane_ids(128)
    shifted = []
    for place, block in enumerate(moved):
        if by > 0:
            near = moved[place - 1][:, :128] if place else nothing
            edge = jnp.where(ids < by, near, block[:, :128])
            shifted.append(jnp.concatenate([edge, block[:, 128:]], axis=1) if block.shape[1] > 128 else edge)
        else:
            near = moved[place + 1][:, -128:] if place + 1 < len(moved) else nothing
            edge = jnp.where(ids >= 128 + by, near, block[:, -128:])
            shifted.append(jnp.concatenate([block[:, :-128], edge], axis=1) if block.shape[1] > 128 else edge)
    return shifted


def shift_column(blocks, by, side):
    shifted = []
    first = 0
    for block in shift_lanes(blocks, by):
        column = (lane_ids(block.shape[1]) + first) % side
        shifted.append(jnp.where(column == (0 if by > 0 else side - 1), jnp.zeros_like(block), block))
        first += block.shape[1]
    return shifted


def write(out_ref, blocks):
    first = 0
    for block in blocks:
        out_ref[:, first : first + block.shape[1]] = block
        first += block.shape[1]


def fill(stack_ref, tap, blocks):
    first = 0
    for block in blocks:
        stack_ref[tap * C : (tap + 1) * C, first : first + block.shape[1]] = block
        first += block.shape[1]


def stack_sideways(low, side, stack_ref):
    fill(stack_ref, 0, shift_column(low, 1, side))
    fill(stack_ref, 1, low)
    fill(stack_ref, 2, shift_column(low, -1, side))


def stack_upright(low, side, stack_ref):
    fill(stack_ref, 0, shift_lanes(low, -side))
    fill(stack_ref, 1, low)
    fill(stack_ref, 2, shift_lanes(low, side))


def conv_blocks(weights_ref, stack_ref):
    width = stack_ref.shape[1]
    parts = [
        jnp.dot(weights_ref[...], stack_ref[:, first : first + WIDE], preferred_element_type=F32)
        for first in range(0, width, WIDE)
    ]
    return [[part[tap * C : (tap + 1) * C] for part in parts] for tap in range(3)]


def conv_ahead(weights_ref, stack_ref, side):
    above, here, below = conv_blocks(weights_ref, stack_ref)
    total = [a + b + c for a, b, c in zip(shift_lanes(above, side), here, shift_lanes(below, -side))]
    total[-1] = trim(total[-1], 0, side * side - (stack_ref.shape[1] - total[-1].shape[1]))
    return total


def conv_behind(weights_ref, stack_ref, side):
    left, here, right = conv_blocks(weights_ref, stack_ref)
    return [a + b + c for a, b, c in zip(shift_column(left, -1, side), here, shift_column(right, 1, side))]


def across_cells(left_ref, right_ref):
    return lax.dot_general(left_ref[...], right_ref[...], (((1,), (1,)), ((), ())), preferred_element_type=F32)


def lane_sum(values):
    return jnp.sum(values, axis=1, keepdims=True)


def moments(blocks, cells):
    pivot = lane_sum(blocks[0]) * (1.0 / blocks[0].shape[1])
    total, squares = 0.0, 0.0
    for place, block in enumerate(blocks):
        away = block - pivot
        if place == len(blocks) - 1:
            away = trim(away, 0, cells - sum(b.shape[1] for b in blocks[:-1]))
        total = total + sum(cut(away, 128))
        squares = squares + sum(cut(away * away, 128))
    away = lane_sum(total) * (1.0 / cells)
    return pivot + away, lane_sum(squares) - cells * away * away


def gelu_gate(values):
    return 0.5 + 0.5 * jnp.tanh(values * (ROOT + (ROOT * CUBIC) * (values * values)))


def gelu_slope(values, gate):
    return gate * (1.0 + (1.0 - gate) * (values * (2.0 * ROOT + (6.0 * ROOT * CUBIC) * (values * values))))


def halves(values):
    high = values.astype(BF16)
    return jnp.concatenate([high, (values - high.astype(F32)).astype(BF16)], axis=0)


def dot_halves(split, weights_ref):
    both = jnp.dot(split, weights_ref[...], preferred_element_type=F32)
    return [both[first : first + C] + both[first + C : first + 2 * C] for first in range(0, both.shape[0], 2 * C)]


def own_rows(me, partner, count):
    return pl.ds(pl.multiple_of((me ^ partner) * count, count), count)


def kernel_params(axes=1):
    return pltpu.CompilerParams(vmem_limit_bytes=VMEM_BYTES, dimension_semantics=("arbitrary",) * axes)


def pack_kernel(images_each, group, wants, me_ref, maps_ref, *refs):
    piece_refs = refs[-len(wants) :]
    turned = jnp.swapaxes(maps_ref[...], 0, 1)
    for lead in range(group):

        @pl.when(me_ref[0] % group == lead)
        def _():
            for piece_ref, (partner, first, count) in zip(piece_refs, wants):
                start = (lead ^ (partner % group)) * images_each + first
                piece_ref[...] = turned[start : start + count]


def unpack_kernel(counts, me_ref, *refs):
    out_refs = refs[-len(counts) :]
    group = len(counts[0])
    for lead in range(group):

        @pl.when(me_ref[0] % group == lead)
        def _():
            start = 0
            for out_ref, parts in zip(out_refs, counts):
                ordered = []
                for slot in range(group):
                    place = start + sum(len(some) for some in parts[: slot ^ lead])
                    ordered += [refs[place + part][...] for part in range(len(parts[slot ^ lead]))]
                joined = jnp.concatenate(ordered, axis=0) if len(ordered) > 1 else ordered[0]
                out_ref[...] = jnp.swapaxes(joined, 0, 1).astype(out_ref.dtype)
                start += sum(len(some) for some in parts)


def bundle_kernel(filter_two_ref, filter_three_ref, film_ref, bias_ref, *refs):
    vector_refs, out_ref = refs[:4], refs[-1]
    rows = filter_two_ref.shape[2]
    out_ref[...] = jnp.zeros_like(out_ref)
    for place, filter_ref in enumerate((filter_two_ref, filter_three_ref)):
        for down in range(3):
            first = (3 * place + down) * rows
            for across in range(3):
                out_ref[first : first + rows, across * C : (across + 1) * C] = filter_ref[down, across]
    for kind in range(2):
        out_ref[6 * rows : 7 * rows, kind * C : kind * C + film_ref.shape[2]] = film_ref[kind]
    for place, vector_ref in enumerate(vector_refs):
        out_ref[7 * rows + place : 7 * rows + place + 1, 0:rows] = vector_ref[...]
    for kind in range(2):
        out_ref[7 * rows + 4 + kind : 7 * rows + 5 + kind, 0:rows] = bias_ref[kind : kind + 1]


def unbundle_kernel(partners, me_ref, task_ref, context_ref, *refs):
    piece_refs = refs[:partners]
    ahead_two_ref, behind_two_ref, ahead_three_ref, behind_three_ref, film_ref, vectors_ref = refs[partners:]
    rows = C // partners
    entries = film_ref.shape[2]
    lanes = jnp.zeros((8, C), F32)
    ids = lane_ids(C)
    for partner, piece_ref in enumerate(piece_refs):
        owner = me_ref[0] ^ partner
        for place, ahead_ref in enumerate((ahead_two_ref, ahead_three_ref)):
            for down in range(3):
                first = (3 * place + down) * rows
                ahead_ref[pl.ds(pl.multiple_of(down * C + owner * rows, rows), rows), :] = piece_ref[first : first + rows]
        for kind in range(2):
            film_ref[kind, own_rows(me_ref[0], partner, rows), :] = piece_ref[
                6 * rows : 7 * rows, kind * C : kind * C + entries
            ].astype(F32)
        own = jnp.where(ids < rows, piece_ref[7 * rows : 7 * rows + 16, 0:C].astype(F32)[:8], 0.0)
        lanes = lanes + pltpu.roll(own, owner * rows, 1)
    behind_two_ref[...] = ahead_two_ref[...].T
    behind_three_ref[...] = ahead_three_ref[...].T
    context = context_ref[pl.ds(task_ref[0], 1), :]
    told = [lane_sum(film_ref[kind] * context) for kind in range(2)]
    told = column_tile(told).T[:8]
    scale = 1.0 + told[0:1] + lanes[4:5]
    shift = told[1:2] + lanes[5:6]
    vectors_ref[...] = row_tile([lanes[0:1], lanes[1:2], lanes[2:3], lanes[3:4], scale, shift])


def assemble(maps, cells, me, piece_refs, index):
    rows = C // len(piece_refs)
    for partner, piece_ref in enumerate(piece_refs):
        maps[own_rows(me, partner, rows), 0:cells] = piece_ref[index]


def disperse(piece_refs, index, me, output, cells):
    rows = C // len(piece_refs)
    for partner, piece_ref in enumerate(piece_refs):
        piece_ref[index] = output[own_rows(me, partner, rows), 0:cells]


def first_conv_kernel(partners, first, final, me_ref, live_ref, told_ref, weights_ref, *refs):
    piece_refs = refs[:partners]
    conv_ref, maps_ref, state_ref, stack, state = refs[-5:]
    step = pl.program_id(0)
    count = conv_ref.shape[0]

    @pl.when(step == 0)
    def _():
        state[...] = refs[partners][...] if first else jnp.zeros_like(state)

    merged = [column(state, k) for k in range(3)]
    for image in range(count):
        maps_ref[image, :, CELLS_TWO // 128 * 128 :] = jnp.zeros((C, LANES_TWO - CELLS_TWO // 128 * 128), BF16)
        assemble(maps_ref.at[image], CELLS_TWO, me_ref[0], piece_refs, image)
        stack_sideways(cut(maps_ref[image], WIDE), MAP, stack.at[image])
        conv = conv_ahead(weights_ref, stack.at[image], MAP)
        write(conv_ref.at[image], conv)
        mean, spread = moments(conv, CELLS_TWO)
        live = live_ref[first + step * count + image]
        merged = merge_moments(merged, live, mean, spread, CELLS_TWO)
    state[...] = column_tile(merged)

    @pl.when(step == pl.num_programs(0) - 1)
    def _():
        if final:
            turned = state[...].T
            spread_rows(row_tile([turned[1:2], turned[2:3], turned[0:1], row(told_ref, 0)], SENT), state_ref)
        else:
            state_ref[...] = state[...]


def middle_kernel(
    partners, me_ref, live_ref, heard_ref, vectors_ref, pool_a_ref, pool_b_ref, weights_ref, conv_ref, *refs
):
    hidden_ref, conv_three_ref, norm_ref, levels_ref, sums_ref, columns, state, stack = refs[-8:]
    piece_refs = refs[-8 - partners : -8]
    step = pl.program_id(0)
    count = conv_ref.shape[0]

    @pl.when(step == 0)
    def _():
        middle, factor, variance, extent = slice_norm(heard_ref)
        norm_ref[...] = row_tile([middle, factor, variance, extent])
        columns[...] = as_columns(row_tile([middle, row(vectors_ref, 0) * factor, row(vectors_ref, 1)]))
        state[...] = jnp.zeros_like(state)

    merged = [column(state, k) for k in range(3)]
    active_squares, hidden_squares = column(state, 3), column(state, 4)
    lives = [live_ref[step * count + image] for image in range(count)]

    def activate(image):
        pre = (conv_ref[image] - column(columns, 0)) * column(columns, 1) + column(columns, 2)
        active = pre * gelu_gate(pre)
        counted = trim(active, 0, CELLS_TWO)
        return halves(active), lives[image] * lane_sum(counted * counted)

    def pool(split):
        (left,) = dot_halves(split[:, :1152], pool_a_ref)
        (right,) = dot_halves(split[:, 896:], pool_b_ref)
        return jnp.concatenate([left, right], axis=1)

    split, squares = activate(0)
    for image in range(count):
        hidden = lives[image] * pool(split)
        active_squares = active_squares + squares
        if image + 1 < count:
            split, squares = activate(image + 1)
        hidden_squares = hidden_squares + lane_sum(hidden * hidden)
        hidden_low = hidden.astype(BF16)
        hidden_ref[image] = hidden_low
        disperse(piece_refs, image, me_ref[0], hidden_ref.at[image], CELLS_THREE)
        stack_sideways(cut(hidden_low, WIDE), HALF, stack.at[image])
        conv = conv_ahead(weights_ref, stack.at[image], HALF)
        write(conv_three_ref.at[image], conv)
        mean, spread = moments(conv, CELLS_THREE)
        merged = merge_moments(merged, lives[image], mean, spread, CELLS_THREE)
    state[...] = column_tile([*merged, active_squares, hidden_squares])

    @pl.when(step == pl.num_programs(0) - 1)
    def _():
        turned = state[...].T
        spread_rows(row_tile([turned[k : k + 1] for k in (1, 2, 0)], SENT), sums_ref)
        levels_ref[...] = row_tile([level_row([column(state, 3), column(state, 4)])])


def top_kernel(
    partners, me_ref, live_ref, heard_ref, own_ref, before_ref, vectors_ref, pool_ref, spread_ref, conv_ref, *refs
):
    target_refs = refs[:partners]
    piece_refs = refs[partners : 2 * partners]
    grad_ref, norm_ref, levels_ref, sums_ref, columns, target, output, totals = refs[2 * partners :]
    step = pl.program_id(0)
    count = conv_ref.shape[0]

    @pl.when(step == 0)
    def _():
        middle, factor, variance, extent = slice_norm(heard_ref)
        norm_ref[...] = row_tile([middle, factor, variance, extent])
        columns[...] = as_columns(row_tile([middle, factor] + [row(vectors_ref, k) for k in (2, 3, 4, 5)]))
        target[...] = jnp.zeros_like(target)
        totals[...] = jnp.zeros_like(totals)

    scale = column(columns, 4)
    slope = scale * column(columns, 2)
    offset = scale * column(columns, 3) + column(columns, 5)
    sums = [jnp.zeros((C, 1), F32)] * 4
    for image in range(count):
        live = live_ref[step * count + image]
        assemble(target.at[image], CELLS_OUT, me_ref[0], target_refs, image)
        normed = (conv_ref[image] - column(columns, 0)) * column(columns, 1)
        filmed = slope * normed + offset
        gate = gelu_gate(filmed)
        active = filmed * gate
        counted = trim(active, 0, CELLS_THREE)
        (pooled,) = dot_halves(halves(active), pool_ref)
        pooled = live * pooled
        output[image] = pooled.astype(BF16)
        disperse(piece_refs, image, me_ref[0], output.at[image], CELLS_OUT)
        spread = jnp.dot(target[image], spread_ref[...], preferred_element_type=F32)
        grad_filmed = live * spread * gelu_slope(filmed, gate)
        grad_ref[image] = scale * grad_filmed
        parts = (
            lane_sum(grad_filmed),
            lane_sum(grad_filmed * normed),
            live * lane_sum(counted * counted),
            lane_sum(pooled * pooled),
        )
        sums = [total + part for total, part in zip(sums, parts)]
    totals[...] += column_tile(sums)

    @pl.when(step == pl.num_programs(0) - 1)
    def _():
        turned = totals[...].T
        shift_sum, scale_sum = turned[0:1], turned[1:2]
        film_scale = row(vectors_ref, 4)
        slope = film_scale * row(vectors_ref, 2) * row(norm_ref, 1)
        offset = film_scale * row(vectors_ref, 3) + row(vectors_ref, 5)
        extent = own_ref[0, 2:3, :]
        away = own_ref[0, 0:1, :] - row(norm_ref, 0)
        filmed_squares = (
            slope * slope * (own_ref[0, 1:2, :] + extent * away * away)
            + 2.0 * slope * offset * extent * away
            + extent * offset * offset
        )
        spread_rows(
            row_tile([shift_sum, scale_sum, film_scale * shift_sum, film_scale * scale_sum], SENT), sums_ref
        )
        nothing = jnp.zeros((C, 1), F32)
        others = level_row([nothing, nothing, nothing, column(totals, 2), column(totals, 3)])
        lanes = lane_ids(C)
        filmed_total = lane_sum(filmed_squares)
        levels_ref[...] = before_ref[...] + row_tile([others + jnp.where(lanes == 2, filmed_total, 0.0)])


def norm_back(live, columns, grad, away, cells):
    scaled = [live * column(columns, k) for k in (1, 2, 3)]
    error = grad.astype(F32) * scaled[0] - scaled[1] - away.astype(F32) * scaled[2]
    return trim(error, 0, cells).astype(BF16)


def norm_back_columns(norm_ref, gain, bias_sum, gain_sum):
    factor, extent = row(norm_ref, 1), row(norm_ref, 3)
    front = gain * factor
    return as_columns(
        row_tile([row(norm_ref, 0), front, front * bias_sum / extent, front * factor * gain_sum / extent])
    )


def back_kernel(
    live_ref,
    heard_ref,
    norm_three_ref,
    norm_two_ref,
    levels_ref,
    vectors_ref,
    weights_ref,
    unpool_a_ref,
    unpool_b_ref,
    grad_ref,
    conv_three_ref,
    conv_two_ref,
    *refs,
):
    out_ref, away_ref, error_ref, sums_ref, columns_three, columns_two, totals, upright = refs[-8:]
    step = pl.program_id(0)
    count = conv_two_ref.shape[0]

    @pl.when(step == 0)
    def _():
        sums = jnp.sum(heard_ref[...], axis=0)
        columns_three[...] = norm_back_columns(norm_three_ref, row(vectors_ref, 2), sums[2:3], sums[3:4])
        columns_two[...] = as_columns(
            row_tile([row(norm_two_ref, 0), row(vectors_ref, 0) * row(norm_two_ref, 1), row(vectors_ref, 1)])
        )
        totals[...] = jnp.zeros_like(totals)

    grad_sum, product_sum = column(totals, 0), column(totals, 1)
    for image in range(count):
        away = conv_three_ref[image] - column(columns_three, 0)
        error = norm_back(live_ref[step * count + image], columns_three, grad_ref[image], away, CELLS_THREE)
        error_ref[image] = error
        stack_upright(cut(error, WIDE), HALF, upright.at[image])
    split = jnp.concatenate(
        [
            halves(jnp.concatenate(conv_behind(weights_ref, upright.at[image], HALF), axis=1))
            for image in range(count)
        ],
        axis=0,
    )
    left = dot_halves(split[:, :256], unpool_a_ref)
    right = dot_halves(split[:, 128:], unpool_b_ref)
    for image in range(count):
        away = conv_two_ref[image] - column(columns_two, 0)
        pre = away * column(columns_two, 1) + column(columns_two, 2)
        grad_pre = jnp.concatenate([left[image], right[image]], axis=1) * gelu_slope(pre, gelu_gate(pre))
        out_ref[image] = grad_pre.astype(BF16)
        away_ref[image] = away.astype(BF16)
        grad_sum = grad_sum + lane_sum(grad_pre)
        product_sum = product_sum + lane_sum(grad_pre * away)
    totals[...] = column_tile([grad_sum, product_sum])

    @pl.when(step == pl.num_programs(0) - 1)
    def _():
        turned = totals[...].T
        normed_sum = turned[1:2] * row(norm_two_ref, 1)
        spread_rows(row_tile([turned[0:1], normed_sum, levels_ref[0:1, :]], SENT), sums_ref)


def split_filter(product, filter_ref):
    partners, _, rows, _ = filter_ref.shape
    for tap in range(3):
        for owner in range(partners):
            filter_ref[owner, tap] = product[tap * C + owner * rows : tap * C + (owner + 1) * rows].astype(BF16)


def filter_three_kernel(error_ref, hidden_ref, *refs):
    filter_ref, product, stack, upright = refs[-4:]
    step = pl.program_id(0)
    count = error_ref.shape[0]

    @pl.when(step == 0)
    def _():
        product[...] = jnp.zeros_like(product)

    for image in range(count):
        stack_upright(cut(error_ref[image], WIDE), HALF, upright.at[image])
        stack_sideways(cut(hidden_ref[image], WIDE), HALF, stack.at[image])
        product[...] += across_cells(upright.at[image], stack.at[image])

    @pl.when(step == pl.num_programs(0) - 1)
    def _():
        split_filter(product, filter_ref)


def last_columns(heard_ref, norm_ref, vectors_ref):
    sums = jnp.sum(heard_ref[...], axis=0)
    return norm_back_columns(norm_ref, row(vectors_ref, 0), sums[0:1], sums[1:2])


def last_conv_kernel(
    partners,
    near,
    first,
    steps,
    me_ref,
    live_ref,
    heard_ref,
    norm_ref,
    vectors_ref,
    weights_ref,
    grad_ref,
    away_ref,
    *refs,
):
    far = partners - near
    piece_refs, (columns, output, upright) = refs[-3 - near - far * len(steps) : -3], refs[-3:]
    step = pl.program_id(0)
    count = grad_ref.shape[0]

    @pl.when(step == 0)
    def _():
        columns[...] = last_columns(heard_ref, norm_ref, vectors_ref)

    for image in range(count):
        live = live_ref[first + step * count + image]
        error = norm_back(live, columns, grad_ref[image], away_ref[image], CELLS_TWO)
        stack_upright(cut(error, WIDE), MAP, upright.at[image])
        write(output.at[image], [block.astype(BF16) for block in conv_behind(weights_ref, upright.at[image], MAP)])
    rows = C // partners
    start = 0
    for place, length in enumerate(steps):

        @pl.when((step >= start) & (step < start + length))
        def _():
            for image in range(count):
                for partner in range(partners):
                    piece_ref = piece_refs[partner if partner < near else near + place * far + partner - near]
                    piece_ref[image] = output[image, own_rows(me_ref[0], partner, rows), 0:CELLS_TWO]

        start += length


def last_filter_kernel(live_ref, heard_ref, norm_ref, vectors_ref, grad_ref, away_ref, maps_ref, *refs):
    filter_ref, product, columns, stack, upright = refs[-5:]
    step = pl.program_id(0)
    count = grad_ref.shape[0]

    @pl.when(step == 0)
    def _():
        columns[...] = last_columns(heard_ref, norm_ref, vectors_ref)
        product[...] = jnp.zeros_like(product)

    for image in range(count):
        error = norm_back(live_ref[step * count + image], columns, grad_ref[image], away_ref[image], CELLS_TWO)
        stack_upright(cut(error, WIDE), MAP, upright.at[image])
        stack_sideways(cut(maps_ref[image], WIDE), MAP, stack.at[image])
        product[...] += across_cells(upright.at[image], stack.at[image])

    @pl.when(step == pl.num_programs(0) - 1)
    def _():
        split_filter(product, filter_ref)


def strips_kernel(heard_ref, *refs):
    out_ref = refs[-1]
    out_ref[...] = jnp.broadcast_to(jnp.sum(heard_ref[...].astype(F32), axis=0)[None], out_ref.shape)


def one_hot(rows, columns, wanted):
    row_ids = lax.broadcasted_iota(jnp.int32, (rows, columns), 0)
    column_ids = lax.broadcasted_iota(jnp.int32, (rows, columns), 1)
    return jnp.where(wanted(row_ids, column_ids), 1.0, 0.0)


def exact_dot(left, right, contract=((1,), (0,))):
    return lax.dot_general(left, right, (contract, ((), ())), precision=PRECISE, preferred_element_type=F32)


def finish_kernel(
    partners,
    group,
    here_ref,
    me_ref,
    heard_two_ref,
    heard_top_ref,
    heard_back_ref,
    norm_two_ref,
    norm_three_ref,
    vectors_ref,
    film_ref,
    *refs,
):
    film_w_ref, film_b_ref, context_ref, *sum_refs, levels_ref, product = refs[-9:]
    devices = heard_two_ref.shape[0]
    tasks = devices // group
    contexts = context_ref.shape[0]
    rows = C // partners
    entries = film_ref.shape[2]
    turn = (C - me_ref[0] * rows) % C

    def own_lanes(values):
        return pltpu.roll(values, turn, 1)[:, :rows]

    by_task = one_hot(tasks, devices, lambda t, d: d // group == t)
    of_task = one_hot(
        tasks, devices, lambda t, d: (d // partners == t // contexts) & (d % partners == t % contexts)
    )
    mine = one_hot(contexts, devices, lambda t, d: d // group == here_ref[0] * contexts + t)
    shift, normed = heard_top_ref[:, 0, :], heard_top_ref[:, 1, :]
    scale = row(vectors_ref, 2) * normed + row(vectors_ref, 3) * shift
    told = exact_dot(of_task, heard_two_ref[:, 3, :])
    total = jnp.zeros((contexts, entries), F32)
    for kind, grads in enumerate((scale, shift)):
        grads_by_task = exact_dot(by_task, grads)
        product[...] = exact_dot(grads_by_task, told, ((0,), (0,)))
        film_w_ref[kind] = product[pl.ds(pl.multiple_of(me_ref[0] * rows, rows), rows), :entries]
        film_b_ref[kind : kind + 1] = own_lanes(jnp.sum(grads_by_task, axis=0, keepdims=True))
        total = total + exact_dot(exact_dot(mine, grads), film_ref[kind])
    context_ref[...] = total

    back = jnp.sum(heard_back_ref[...], axis=0)
    top = jnp.sum(heard_top_ref[...], axis=0)
    for sum_ref, sums in zip(sum_refs, (back[1:2], back[0:1], top[3:4], top[2:3])):
        sum_ref[...] = own_lanes(sums)[0]

    live = norm_two_ref[3:4, 0:1] * (1.0 / CELLS_TWO)
    lanes = lane_ids(C)

    def mean_square(norm_ref, gain, shift):
        factor, variance = row(norm_ref, 1), row(norm_ref, 2)
        return jnp.sum(gain * gain * variance * factor * factor + shift * shift, axis=1, keepdims=True) * (1.0 / C)

    def mean_conv(norm_ref):
        middle = row(norm_ref, 0)
        return jnp.sum(row(norm_ref, 2) + middle * middle, axis=1, keepdims=True) * (1.0 / C)

    known = (
        mean_conv(norm_two_ref),
        mean_square(norm_two_ref, row(vectors_ref, 0), row(vectors_ref, 1)),
        back[2:3, 0:1] / (live * (C * CELLS_TWO)),
        back[2:3, 1:2] / (live * (C * CELLS_THREE)),
        mean_conv(norm_three_ref),
        mean_square(norm_three_ref, row(vectors_ref, 2), row(vectors_ref, 3)),
        back[2:3, 2:3] / (live * (C * CELLS_THREE)),
        back[2:3, 3:4] / (live * (C * CELLS_THREE)),
        back[2:3, 4:5] / (live * (C * CELLS_OUT)),
    )
    level = jnp.zeros((1, C), F32)
    for place, value in enumerate(known):
        level = jnp.where(lanes == place, value, level)
    levels_ref[...] = jnp.sqrt(level)[0, : levels_ref.shape[0]]


def pool_matrix(side, width, out_width):
    half = side // 2
    matrix = np.zeros((width, out_width), np.float32)
    for row in range(2 * half):
        for column in range(2 * half):
            matrix[row * side + column, (row // 2) * half + column // 2] = 0.25
    return matrix


def lasting(microseconds):
    return pl.CostEstimate(
        flops=int(microseconds * 1.1e9), bytes_accessed=int(microseconds * 3.5e6), transcendentals=0
    )


def smem():
    return pl.BlockSpec(memory_space=pltpu.SMEM)


def anywhere(count):
    return [pl.BlockSpec(memory_space=pl.ANY)] * count


def whole(*shape):
    return pl.BlockSpec(shape, lambda n: (0,) * len(shape))


def each(*shape, first=0, count=1):
    return pl.BlockSpec((count, *shape), lambda n: (first + n,) + (0,) * len(shape))


def pack(maps, me, images_each, wants, earlier=()):
    rows, slots, cells = maps.shape
    group = CAP // images_each
    halves = 2
    block = wants[0][0] // group
    return pl.pallas_call(
        functools.partial(pack_kernel, images_each, group, wants),
        grid_spec=pltpu.PrefetchScalarGridSpec(
            num_scalar_prefetch=1,
            grid=(halves,),
            in_specs=[
                pl.BlockSpec((rows // halves, CAP, cells), lambda n, me_ref: (n, (me_ref[0] // group) ^ block, 0)),
                *anywhere(len(earlier)),
            ],
            out_specs=[
                pl.BlockSpec((count, rows // halves, cells), lambda n, me_ref: (0, n, 0)) for _, _, count in wants
            ],
        ),
        out_shape=[jax.ShapeDtypeStruct((count, rows, cells), maps.dtype) for _, _, count in wants],
        compiler_params=kernel_params(),
        name="pack",
        cost_estimate=lasting(2.5),
    )(me, maps, *earlier)


def unpack(arrays, me, images_each, dtype, place, outs=(), earlier=()):
    partners = len(arrays[0])
    group = CAP // images_each
    halves = 2
    given, specs, counts, shapes, out_specs = [], [], [], [], []
    for pieces in arrays:
        here = pieces[place * group : (place + 1) * group]
        counts.append(tuple(tuple(piece.shape[0] for piece in parts) for parts in here))
        rows, cells = here[0][0].shape[1:]
        for piece in (piece for parts in here for piece in parts):
            given.append(piece)
            specs.append(pl.BlockSpec((piece.shape[0], rows // halves, cells), lambda n, me_ref: (0, n, 0)))
        shapes.append(jax.ShapeDtypeStruct((rows, partners * images_each, cells), dtype))
        out_specs.append(
            pl.BlockSpec((rows // halves, CAP, cells), lambda n, me_ref: (n, (me_ref[0] // group) ^ place, 0))
        )
    aliases = {1 + len(given) + k: k for k in range(len(outs))}
    given += [*outs, *earlier]
    specs += anywhere(len(given) - len(specs))
    return pl.pallas_call(
        functools.partial(unpack_kernel, counts),
        grid_spec=pltpu.PrefetchScalarGridSpec(
            num_scalar_prefetch=1, grid=(halves,), in_specs=specs, out_specs=out_specs
        ),
        out_shape=shapes,
        input_output_aliases=aliases,
        compiler_params=kernel_params(),
        name="unpack",
        cost_estimate=lasting(2.0),
    )(me, *given)


def local(
    images,
    counts,
    context,
    filter_two,
    gain_two,
    shift_two,
    filter_three,
    gain_three,
    shift_three,
    film_weight,
    film_bias,
    cotangent,
    *,
    partners,
    columns,
):
    devices = partners * columns
    rows, slots = images.shape[:2]
    images_each = slots // partners
    group = CAP // images_each
    one = min(images_each, 2)
    pair, some = min(images_each, 2), min(images_each, 4)
    position = lax.axis_index("tensor")
    me = jnp.reshape(position, (1,)).astype(jnp.int32)

    def swap(value, partner):
        if partner == 0:
            return value
        return lax.ppermute(value, "tensor", [(i, i ^ partner) for i in range(partners)])

    def share(copies):
        return lax.all_to_all(copies, ("dp", "tensor"), 0, 0)

    near = 2
    half, quarter = images_each // 2, images_each // 4
    sizes_in = (half, quarter, quarter) if quarter >= pair else (half, half)
    half = images_each // 2
    calls_out = ((pair,) * (half // pair), (half,))
    starts_in = [sum(sizes_in[:part]) for part in range(len(sizes_in))]
    counts_of = [(images_each,) if partner < near else sizes_in for partner in range(partners)]
    far = [partner for partner in reversed(range(partners)) if partner >= near]
    maps = [[None] * len(counts_of[partner]) for partner in range(partners)]

    def send_in(some_parts, whole_near, earlier):
        for block in reversed(range(partners // group)):
            wants = [
                (partner, starts_in[part], sizes_in[part])
                for part in some_parts
                for partner in far
                if partner // group == block
            ]
            if block == 0 and whole_near:
                wants += [(partner, 0, images_each) for partner in range(near)]
            if wants:
                sent = pack(images, me, images_each, wants, earlier)
                for piece, (partner, first, _) in zip(sent, wants):
                    maps[partner][starts_in.index(first)] = swap(piece, partner)
                earlier = (*earlier, sent[0])
        return earlier

    first_sent = send_in((0,), True, ())
    entries = film_weight.shape[0]
    bundle = pl.pallas_call(
        bundle_kernel,
        in_specs=[pl.BlockSpec(memory_space=pltpu.VMEM)] * 8 + anywhere(1),
        out_shape=jax.ShapeDtypeStruct((7 * rows + 16, 3 * C), BF16),
        compiler_params=kernel_params(0),
        name="bundle",
        cost_estimate=lasting(1.0),
    )(
        jnp.transpose(filter_two, (2, 3, 0, 1)),
        jnp.transpose(filter_three, (2, 3, 0, 1)),
        jnp.transpose(film_weight, (1, 2, 0)),
        film_bias,
        *[vector[None] for vector in (gain_two, shift_two, gain_three, shift_three)],
        first_sent[0],
    )
    bundles = {0: bundle}
    bit = partners // 2
    while bit:
        bundles.update({partner | bit: swap(piece, bit) for partner, piece in bundles.items()})
        bit //= 2

    sent_in = {
        part: send_in((part,), False, (maps[far[0]][0],))
        for part in range(1, len(sizes_in))
    }

    task = position // group
    slot = (position % group) * images_each + jnp.arange(images_each, dtype=jnp.int32)
    limit = lax.dynamic_index_in_dim(counts, task, 0, keepdims=False)
    live = (slot < limit).astype(F32)
    ahead_two, behind_two, ahead_three, behind_three, film, vectors = pl.pallas_call(
        functools.partial(unbundle_kernel, partners),
        in_specs=[smem(), smem(), *[pl.BlockSpec(memory_space=pltpu.VMEM)] * (1 + partners)],
        out_shape=[jax.ShapeDtypeStruct((3 * C, 3 * C), BF16)] * 4
        + [jax.ShapeDtypeStruct((2, C, entries), F32), jax.ShapeDtypeStruct((8, C), F32)],
        compiler_params=kernel_params(0),
        name="unbundle",
        cost_estimate=lasting(2.0),
    )(me, jnp.reshape(task, (1,)).astype(jnp.int32), context, *[bundles[partner] for partner in range(partners)])

    told = lax.dynamic_index_in_dim(context, position % context.shape[0], 0)
    told = jnp.pad(told, ((0, 7), (0, C - entries)))

    conv_two = whole_maps = state = None
    for part, (first, count) in enumerate(zip(starts_in, sizes_in)):
        given = [maps[partner][0 if partner < near else part] for partner in range(partners)]
        specs = [
            each(rows, CELLS_TWO, first=first // pair if partner < near else 0, count=pair)
            for partner in range(partners)
        ]
        aliases = {}
        final = part == len(sizes_in) - 1
        if part:
            aliases = {5 + partners: 0, 6 + partners: 1}
            given = given + [state, conv_two, whole_maps]
            specs = specs + [whole(C, C), *anywhere(2)]
        waits = [] if final else [sent_in[part + 1][-1]]
        given = given + waits
        specs = specs + anywhere(len(waits))
        conv_two, whole_maps, state = pl.pallas_call(
            functools.partial(first_conv_kernel, partners, first, final),
            grid=(count // pair,),
            in_specs=[smem(), smem(), whole(8, C), whole(3 * C, 3 * C), *specs],
            out_specs=[
                each(C, LANES_TWO, first=first // pair, count=pair),
                each(C, LANES_TWO, first=first // pair, count=pair),
                whole(devices, SENT, C) if final else whole(C, C),
            ],
            out_shape=[
                jax.ShapeDtypeStruct((images_each, C, LANES_TWO), F32),
                jax.ShapeDtypeStruct((images_each, C, LANES_TWO), BF16),
                jax.ShapeDtypeStruct((devices, SENT, C) if final else (C, C), F32),
            ],
            scratch_shapes=[
                pltpu.VMEM((pair, 3 * C, LANES_TWO), BF16),
                pltpu.VMEM((C, C), F32),
            ],
            input_output_aliases=aliases,
            compiler_params=kernel_params(),
            name="first_conv",
            cost_estimate=lasting(2.3 * count),
        )(me, live, told, ahead_two, *given)
    heard_two = share(state)
    turned = jnp.transpose(cotangent, (1, 0, 2))
    targets = [
        swap(lax.dynamic_slice_in_dim(turned, (position ^ partner) * images_each, images_each, 0), partner)
        for partner in range(partners)
    ]

    pool = pool_matrix(MAP, LANES_TWO, LANES_THREE)
    pool_out = pool_matrix(HALF, LANES_THREE, LANES_OUT)
    *block_pieces, hidden, conv_three, norm_two, levels, sums_three = pl.pallas_call(
        functools.partial(middle_kernel, partners),
        grid=(images_each // pair,),
        in_specs=[
            smem(),
            smem(),
            whole(devices, SENT, C),
            whole(8, C),
            whole(1152, 256),
            whole(896, 256),
            whole(3 * C, 3 * C),
            each(C, LANES_TWO, count=pair),
        ],
        out_specs=[each(rows, CELLS_THREE, count=pair)] * partners
        + [each(C, LANES_THREE, count=pair), each(C, LANES_THREE, count=pair), whole(8, C), whole(8, C), whole(devices, SENT, C)],
        out_shape=[jax.ShapeDtypeStruct((images_each, rows, CELLS_THREE), BF16)] * partners
        + [
            jax.ShapeDtypeStruct((images_each, C, LANES_THREE), BF16),
            jax.ShapeDtypeStruct((images_each, C, LANES_THREE), F32),
            jax.ShapeDtypeStruct((8, C), F32),
            jax.ShapeDtypeStruct((8, C), F32),
            jax.ShapeDtypeStruct((devices, SENT, C), F32),
        ],
        scratch_shapes=[
            pltpu.VMEM((C, C), F32),
            pltpu.VMEM((C, C), F32),
            pltpu.VMEM((pair, 3 * C, LANES_THREE), BF16),
        ],
        compiler_params=kernel_params(),
        name="middle",
            cost_estimate=lasting(2.0 * images_each),
    )(
        me,
        live,
        heard_two,
        vectors,
        jnp.asarray(pool[:1152, :256], BF16),
        jnp.asarray(pool[896:, 256:], BF16),
        ahead_three,
        conv_two,
    )
    heard_three = share(sums_three)

    *out_pieces, grad_three, norm_three, levels, sums_top = pl.pallas_call(
        functools.partial(top_kernel, partners),
        grid=(images_each // some,),
        in_specs=[
            smem(),
            smem(),
            whole(devices, SENT, C),
            whole(1, SENT, C),
            whole(8, C),
            whole(8, C),
            whole(LANES_THREE, LANES_OUT),
            whole(LANES_OUT, LANES_THREE),
            each(C, LANES_THREE, count=some),
            *[each(rows, CELLS_OUT, count=some)] * partners,
        ],
        out_specs=[each(rows, CELLS_OUT, count=some)] * partners
        + [each(C, LANES_THREE, count=some), whole(8, C), whole(8, C), whole(devices, SENT, C)],
        out_shape=[jax.ShapeDtypeStruct((images_each, rows, CELLS_OUT), BF16)] * partners
        + [
            jax.ShapeDtypeStruct((images_each, C, LANES_THREE), F32),
            jax.ShapeDtypeStruct((8, C), F32),
            jax.ShapeDtypeStruct((8, C), F32),
            jax.ShapeDtypeStruct((devices, SENT, C), F32),
        ],
        scratch_shapes=[
            pltpu.VMEM((C, C), F32),
            pltpu.VMEM((some, C, LANES_OUT), BF16),
            pltpu.VMEM((some, C, LANES_OUT), BF16),
            pltpu.VMEM((C, C), F32),
        ],
        compiler_params=kernel_params(),
        name="top",
            cost_estimate=lasting(0.8 * images_each),
    )(
        me,
        live,
        heard_three,
        sums_three,
        levels,
        vectors,
        jnp.asarray(pool_out, BF16),
        jnp.asarray(pool_out.T, BF16),
        conv_three,
        *targets,
    )
    heard_top = share(sums_top)
    block_two = [[swap(block_pieces[k], k)] for k in range(partners)]
    out_pieces = [[swap(out_pieces[k], k)] for k in range(partners)]

    filter_shape = jax.ShapeDtypeStruct((partners, 2, 3, rows, 3 * C), BF16)

    def filter_spec(block):
        return pl.BlockSpec((partners, None, 3, rows, 3 * C), lambda n: (0, block, 0, 0, 0))

    grad_two, away_two, error_three, sums_two = pl.pallas_call(
        back_kernel,
        grid=(images_each // pair,),
        in_specs=[
            smem(),
            whole(devices, SENT, C),
            whole(8, C),
            whole(8, C),
            whole(8, C),
            whole(8, C),
            whole(3 * C, 3 * C),
            whole(256, 896),
            whole(384, 896),
            each(C, LANES_THREE, count=pair),
            each(C, LANES_THREE, count=pair),
            each(C, LANES_TWO, count=pair),
        ],
        out_specs=[
            each(C, LANES_TWO, count=pair),
            each(C, LANES_TWO, count=pair),
            each(C, LANES_THREE, count=pair),
            whole(devices, SENT, C),
        ],
        out_shape=[
            jax.ShapeDtypeStruct((images_each, C, LANES_TWO), BF16),
            jax.ShapeDtypeStruct((images_each, C, LANES_TWO), BF16),
            jax.ShapeDtypeStruct((images_each, C, LANES_THREE), BF16),
            jax.ShapeDtypeStruct((devices, SENT, C), F32),
        ],
        scratch_shapes=[
            pltpu.VMEM((C, C), F32),
            pltpu.VMEM((C, C), F32),
            pltpu.VMEM((C, C), F32),
            pltpu.VMEM((pair, 3 * C, LANES_THREE), BF16),
        ],
        compiler_params=kernel_params(),
        name="back",
            cost_estimate=lasting(2.0 * images_each),
    )(
        live,
        heard_top,
        norm_three,
        norm_two,
        levels,
        vectors,
        behind_three,
        jnp.asarray(pool[:896, :256].T, BF16),
        jnp.asarray(pool[896:, 128:].T, BF16),
        grad_three,
        conv_three,
        conv_two,
    )
    heard_back = share(sums_two)

    filter_sums = pl.pallas_call(
        filter_three_kernel,
        grid=(images_each // some,),
        in_specs=[*[each(C, LANES_THREE, count=some)] * 2, *anywhere(1)],
        out_specs=filter_spec(1),
        out_shape=filter_shape,
        scratch_shapes=[
            pltpu.VMEM((3 * C, 3 * C), F32),
            pltpu.VMEM((some, 3 * C, LANES_THREE), BF16),
            pltpu.VMEM((some, 3 * C, LANES_THREE), BF16),
        ],
        compiler_params=kernel_params(),
        name="filter_three",
        cost_estimate=lasting(5.0),
    )(error_three, hidden, sums_two)

    returned = [[] for partner in range(partners)]
    waits = [filter_sums, *(pieces[0] for pieces in (*block_two, *out_pieces))]
    common = [heard_back, norm_two, vectors]
    common_specs = [whole(devices, SENT, C), whole(8, C), whole(8, C)]
    kept = []
    first = 0
    for sizes in calls_out:
        count = sum(sizes)
        steps = [some // one for some in sizes]
        out_specs = [each(rows, CELLS_TWO, first=first // one, count=one)] * near
        out_shape = [jax.ShapeDtypeStruct((images_each, rows, CELLS_TWO), BF16)] * near
        for place, length in enumerate(steps):
            start = sum(steps[:place])
            out_specs += [
                pl.BlockSpec(
                    (one, rows, CELLS_TWO),
                    lambda n, start=start, length=length: (jnp.clip(n - start, 0, length - 1), 0, 0),
                )
            ] * len(far)
            out_shape += [jax.ShapeDtypeStruct((length * one, rows, CELLS_TWO), BF16)] * len(far)
        inputs = [me, live, *common, behind_two, grad_two, away_two]
        pieces = pl.pallas_call(
            functools.partial(last_conv_kernel, partners, near, first, steps),
            grid=(count // one,),
            in_specs=[
                smem(),
                smem(),
                *common_specs,
                whole(3 * C, 3 * C),
                *[each(C, LANES_TWO, first=first // one, count=one)] * 2,
                *anywhere(len(waits) + len(kept)),
            ],
            out_specs=out_specs,
            out_shape=out_shape,
            scratch_shapes=[
                pltpu.VMEM((C, C), F32),
                pltpu.VMEM((one, C, LANES_TWO), BF16),
                pltpu.VMEM((one, 3 * C, LANES_TWO), BF16),
            ],
            input_output_aliases={len(inputs) + len(waits) + k: k for k in range(len(kept))},
            compiler_params=kernel_params(),
            name="last_conv",
            cost_estimate=lasting(1.5 * count),
        )(*inputs, *waits, *kept)
        kept, waits, first = pieces[:near], [], first + count
        for place in range(len(sizes)):
            for partner in reversed(far):
                returned[partner].append(swap(pieces[near + place * len(far) + partner - near], partner))
        if first < images_each:
            product = pl.pallas_call(
                last_filter_kernel,
                grid=(images_each // pair,),
                in_specs=[
                    smem(),
                    *common_specs,
                    *[each(C, LANES_TWO, count=pair)] * 3,
                    *anywhere(2),
                ],
                out_specs=filter_spec(0),
                out_shape=filter_shape,
                scratch_shapes=[
                    pltpu.VMEM((3 * C, 3 * C), F32),
                    pltpu.VMEM((C, C), F32),
                    pltpu.VMEM((pair, 3 * C, LANES_TWO), BF16),
                    pltpu.VMEM((pair, 3 * C, LANES_TWO), BF16),
                ],
                input_output_aliases={7: 0},
                compiler_params=kernel_params(),
                name="last_filter",
                cost_estimate=lasting(1.2 * images_each),
            )(live, *common, grad_two, away_two, whole_maps, filter_sums, kept[0])
            waits = [product, *(piece for partner in far[:-1] for piece in returned[partner]), returned[near][0]]
    for partner in range(near):
        returned[partner].append(swap(kept[partner], partner))

    arrivals = [returned[partner][place] for place in range(len(returned[near])) for partner in reversed(far)]
    count_first = len(far) * len(calls_out[0])
    blocks = ()
    for place in range(partners // group):
        blocks = unpack([block_two, out_pieces], me, images_each, BF16, place, blocks, [kept[0]])
    block_two, block_three = blocks

    strip = 6 * rows // columns
    heard = lax.all_to_all(product.reshape(devices, strip, 3 * C), ("tensor", "dp"), 0, 0)
    strips = pl.pallas_call(
        strips_kernel,
        in_specs=[pl.BlockSpec(memory_space=pltpu.VMEM), *anywhere(1)],
        out_shape=jax.ShapeDtypeStruct((columns, strip, 3 * C), F32),
        compiler_params=kernel_params(0),
        name="strips",
        cost_estimate=lasting(1.5),
    )(heard, kept[0])
    strips = lax.all_to_all(strips, "dp", 0, 0)
    grad_filters = jnp.transpose(strips.reshape(2, 3, rows, 3, C), (0, 2, 4, 1, 3))

    grad_images = ()
    for place in range(partners // group):
        waits = (strips,) if grad_images else (returned[near][1],)
        grad_images = unpack([returned], me, images_each, F32, place, grad_images, waits)
    (grad_images,) = grad_images

    contexts = context.shape[0]
    grad_film_w, grad_film_b, grad_context, *norm_sums, levels = pl.pallas_call(
        functools.partial(finish_kernel, partners, group),
        in_specs=[smem(), smem(), *[pl.BlockSpec(memory_space=pltpu.VMEM)] * 7, *anywhere(1)],
        out_shape=[
            jax.ShapeDtypeStruct((2, rows, entries), F32),
            jax.ShapeDtypeStruct((2, rows), F32),
            jax.ShapeDtypeStruct((contexts, entries), F32),
            *[jax.ShapeDtypeStruct((rows,), F32)] * 4,
            jax.ShapeDtypeStruct((9,), F32),
        ],
        scratch_shapes=[pltpu.VMEM((C, C), F32)],
        compiler_params=kernel_params(0),
        name="finish",
        cost_estimate=lasting(2.0),
    )(
        jnp.reshape(lax.axis_index("dp"), (1,)).astype(jnp.int32),
        me,
        heard_two,
        heard_top,
        heard_back,
        norm_two,
        norm_three,
        vectors,
        film,
        kept[0],
    )
    return (
        block_two,
        block_three,
        grad_images,
        grad_filters[0],
        norm_sums[0],
        norm_sums[1],
        grad_filters[1],
        norm_sums[2],
        norm_sums[3],
        jnp.transpose(grad_film_w, (2, 0, 1)),
        grad_film_b,
        grad_context,
        levels,
    )


def solution(mesh):
    step = functools.partial(local, partners=mesh.shape["tensor"], columns=mesh.shape["dp"])
    placed = (
        P("tensor", "dp", None),
        P("dp"),
        P("dp", None),
        P("tensor", None, None, None),
        P("tensor"),
        P("tensor"),
        P("tensor", None, None, None),
        P("tensor"),
        P("tensor"),
        P(None, None, "tensor"),
        P(None, "tensor"),
        P("tensor", "dp", None),
    )
    return jax.shard_map(
        step,
        mesh=mesh,
        in_specs=placed,
        out_specs=(
            P("tensor", "dp", None),
            P("tensor", "dp", None),
            P("tensor", "dp", None),
            P("tensor", None, None, None),
            P("tensor"),
            P("tensor"),
            P("tensor", None, None, None),
            P("tensor"),
            P("tensor"),
            P(None, None, "tensor"),
            P(None, "tensor"),
            P("dp", None),
            P(),
        ),
        check_vma=False,
    )
```

```python
import functools

import jax
import jax.numpy as jnp
import numpy as np
from jax import lax
from jax.experimental import pallas as pl
from jax.experimental.pallas import tpu as pltpu
from jax.sharding import PartitionSpec as P

C = 128
MAP = 42
CAP = 16
HALF = 21
QUART = 10
SENT = 4
VMEM_BYTES = 63 << 20
WIDE = 256

CELLS_TWO = MAP * MAP
CELLS_THREE = HALF * HALF
CELLS_OUT = QUART * QUART
LANES_TWO = 1792
LANES_THREE = 512
LANES_OUT = 128
EPSILON = 1e-05
PRECISE = lax.Precision.HIGHEST
F32 = jnp.float32
BF16 = jnp.bfloat16
ROOT = 0.7978845608028654
CUBIC = 0.044715


def lane_ids(width):
    return lax.broadcasted_iota(jnp.int32, (1, width), 1)


def as_columns(rows):
    return jnp.concatenate([rows] * (C // 8), axis=0).T


def column_tile(columns):
    ids = lax.broadcasted_iota(jnp.int32, (C, C), 1)
    tile = jnp.zeros((C, C), F32)
    for place, column in enumerate(columns):
        tile = jnp.where(ids == place, column, tile)
    return tile


def row_tile(rows, count=8):
    ids = lax.broadcasted_iota(jnp.int32, (count, C), 0)
    tile = jnp.zeros((count, C), F32)
    for place, row in enumerate(rows):
        tile = jnp.where(ids == place, row, tile)
    return tile


def row(tile_ref, place):
    return tile_ref[place : place + 1, :]


def column(tile_ref, place):
    return tile_ref[:, place : place + 1]


def merge_moments(state, weight, mean, spread, cells):
    count, middle, total = state
    added = weight * cells
    both = count + added
    away = mean - middle
    share = added / jnp.maximum(both, 1.0)
    return both, middle + away * share, total + weight * spread + away * away * count * share


def slice_norm(heard_ref):
    means, spreads, counts = heard_ref[:, 0, :], heard_ref[:, 1, :], heard_ref[:, 2, :]
    extent = jnp.sum(counts, axis=0, keepdims=True)
    middle = jnp.sum(counts * means, axis=0, keepdims=True) / extent
    away = means - middle
    variance = jnp.sum(spreads + counts * away * away, axis=0, keepdims=True) / extent
    return middle, lax.rsqrt(variance + EPSILON), variance, extent


def level_row(columns):
    return jnp.sum(column_tile(columns), axis=0, keepdims=True)


def spread_rows(tile, out_ref):
    out_ref[...] = jnp.broadcast_to(tile[None], out_ref.shape)


def trim(values, first, last):
    tiles = cut(values, 128)
    ids = lane_ids(128)
    if first > 0:
        tiles[0] = jnp.where(ids >= first, tiles[0], jnp.zeros_like(tiles[0]))
    if last < values.shape[1]:
        tiles[-1] = jnp.where(ids < last - (values.shape[1] - 128), tiles[-1], jnp.zeros_like(tiles[-1]))
    return jnp.concatenate(tiles, axis=1)


def cut(values, wide):
    return [values[:, first : first + wide] for first in range(0, values.shape[1], wide)]


def shift_lanes(blocks, by):
    moved = [pltpu.roll(block, by % block.shape[1], 1) for block in blocks]
    nothing = jnp.zeros_like(moved[0][:, :128])
    ids = lane_ids(128)
    shifted = []
    for place, block in enumerate(moved):
        if by > 0:
            near = moved[place - 1][:, :128] if place else nothing
            edge = jnp.where(ids < by, near, block[:, :128])
            shifted.append(jnp.concatenate([edge, block[:, 128:]], axis=1) if block.shape[1] > 128 else edge)
        else:
            near = moved[place + 1][:, -128:] if place + 1 < len(moved) else nothing
            edge = jnp.where(ids >= 128 + by, near, block[:, -128:])
            shifted.append(jnp.concatenate([block[:, :-128], edge], axis=1) if block.shape[1] > 128 else edge)
    return shifted


def shift_column(blocks, by, side):
    shifted = []
    first = 0
    for block in shift_lanes(blocks, by):
        column = (lane_ids(block.shape[1]) + first) % side
        shifted.append(jnp.where(column == (0 if by > 0 else side - 1), jnp.zeros_like(block), block))
        first += block.shape[1]
    return shifted


def write(out_ref, blocks):
    first = 0
    for block in blocks:
        out_ref[:, first : first + block.shape[1]] = block
        first += block.shape[1]


def fill(stack_ref, tap, blocks):
    first = 0
    for block in blocks:
        stack_ref[tap * C : (tap + 1) * C, first : first + block.shape[1]] = block
        first += block.shape[1]


def stack_sideways(low, side, stack_ref):
    fill(stack_ref, 0, shift_column(low, 1, side))
    fill(stack_ref, 1, low)
    fill(stack_ref, 2, shift_column(low, -1, side))


def stack_upright(low, side, stack_ref):
    fill(stack_ref, 0, shift_lanes(low, -side))
    fill(stack_ref, 1, low)
    fill(stack_ref, 2, shift_lanes(low, side))


def conv_blocks(weights_ref, stack_ref):
    width = stack_ref.shape[1]
    parts = [
        jnp.dot(weights_ref[...], stack_ref[:, first : first + WIDE], preferred_element_type=F32)
        for first in range(0, width, WIDE)
    ]
    return [[part[tap * C : (tap + 1) * C] for part in parts] for tap in range(3)]


def conv_ahead(weights_ref, stack_ref, side):
    above, here, below = conv_blocks(weights_ref, stack_ref)
    total = [a + b + c for a, b, c in zip(shift_lanes(above, side), here, shift_lanes(below, -side))]
    total[-1] = trim(total[-1], 0, side * side - (stack_ref.shape[1] - total[-1].shape[1]))
    return total


def conv_behind(weights_ref, stack_ref, side):
    left, here, right = conv_blocks(weights_ref, stack_ref)
    return [a + b + c for a, b, c in zip(shift_column(left, -1, side), here, shift_column(right, 1, side))]


def across_cells(left_ref, right_ref):
    return lax.dot_general(left_ref[...], right_ref[...], (((1,), (1,)), ((), ())), preferred_element_type=F32)


def lane_sum(values):
    return jnp.sum(values, axis=1, keepdims=True)


def moments(blocks, cells):
    pivot = lane_sum(blocks[0]) * (1.0 / blocks[0].shape[1])
    total, squares = 0.0, 0.0
    for place, block in enumerate(blocks):
        away = block - pivot
        if place == len(blocks) - 1:
            away = trim(away, 0, cells - sum(b.shape[1] for b in blocks[:-1]))
        total = total + sum(cut(away, 128))
        squares = squares + sum(cut(away * away, 128))
    away = lane_sum(total) * (1.0 / cells)
    return pivot + away, lane_sum(squares) - cells * away * away


def gelu_gate(values):
    return 0.5 + 0.5 * jnp.tanh(values * (ROOT + (ROOT * CUBIC) * (values * values)))


def gelu_slope(values, gate):
    return gate * (1.0 + (1.0 - gate) * (values * (2.0 * ROOT + (6.0 * ROOT * CUBIC) * (values * values))))


def halves(values):
    high = values.astype(BF16)
    return jnp.concatenate([high, (values - high.astype(F32)).astype(BF16)], axis=0)


def dot_halves(split, weights_ref):
    both = jnp.dot(split, weights_ref[...], preferred_element_type=F32)
    return [both[first : first + C] + both[first + C : first + 2 * C] for first in range(0, both.shape[0], 2 * C)]


def own_rows(me, partner, count):
    return pl.ds(pl.multiple_of((me ^ partner) * count, count), count)


def kernel_params(axes=1):
    return pltpu.CompilerParams(vmem_limit_bytes=VMEM_BYTES, dimension_semantics=("arbitrary",) * axes)


def pack_kernel(images_each, group, wants, me_ref, maps_ref, *refs):
    piece_refs = refs[-len(wants) :]
    turned = jnp.swapaxes(maps_ref[...], 0, 1)
    for lead in range(group):

        @pl.when(me_ref[0] % group == lead)
        def _():
            for piece_ref, (partner, first, count) in zip(piece_refs, wants):
                start = (lead ^ (partner % group)) * images_each + first
                piece_ref[...] = turned[start : start + count]


def unpack_kernel(counts, me_ref, *refs):
    out_refs = refs[-len(counts) :]
    group = len(counts[0])
    for lead in range(group):

        @pl.when(me_ref[0] % group == lead)
        def _():
            start = 0
            for out_ref, parts in zip(out_refs, counts):
                ordered = []
                for slot in range(group):
                    place = start + sum(len(some) for some in parts[: slot ^ lead])
                    ordered += [refs[place + part][...] for part in range(len(parts[slot ^ lead]))]
                joined = jnp.concatenate(ordered, axis=0) if len(ordered) > 1 else ordered[0]
                out_ref[...] = jnp.swapaxes(joined, 0, 1).astype(out_ref.dtype)
                start += sum(len(some) for some in parts)


def bundle_kernel(filter_two_ref, filter_three_ref, film_ref, bias_ref, *refs):
    vector_refs, out_ref = refs[:4], refs[-1]
    rows = filter_two_ref.shape[2]
    out_ref[...] = jnp.zeros_like(out_ref)
    for place, filter_ref in enumerate((filter_two_ref, filter_three_ref)):
        for down in range(3):
            first = (3 * place + down) * rows
            for across in range(3):
                out_ref[first : first + rows, across * C : (across + 1) * C] = filter_ref[down, across]
    for kind in range(2):
        out_ref[6 * rows : 7 * rows, kind * C : kind * C + film_ref.shape[2]] = film_ref[kind]
    for place, vector_ref in enumerate(vector_refs):
        out_ref[7 * rows + place : 7 * rows + place + 1, 0:rows] = vector_ref[...]
    for kind in range(2):
        out_ref[7 * rows + 4 + kind : 7 * rows + 5 + kind, 0:rows] = bias_ref[kind : kind + 1]


def unbundle_kernel(partners, me_ref, task_ref, context_ref, *refs):
    piece_refs = refs[:partners]
    ahead_two_ref, behind_two_ref, ahead_three_ref, behind_three_ref, film_ref, vectors_ref = refs[partners:]
    rows = C // partners
    entries = film_ref.shape[2]
    lanes = jnp.zeros((8, C), F32)
    ids = lane_ids(C)
    for partner, piece_ref in enumerate(piece_refs):
        owner = me_ref[0] ^ partner
        for place, ahead_ref in enumerate((ahead_two_ref, ahead_three_ref)):
            for down in range(3):
                first = (3 * place + down) * rows
                ahead_ref[pl.ds(pl.multiple_of(down * C + owner * rows, rows), rows), :] = piece_ref[first : first + rows]
        for kind in range(2):
            film_ref[kind, own_rows(me_ref[0], partner, rows), :] = piece_ref[
                6 * rows : 7 * rows, kind * C : kind * C + entries
            ].astype(F32)
        own = jnp.where(ids < rows, piece_ref[7 * rows : 7 * rows + 16, 0:C].astype(F32)[:8], 0.0)
        lanes = lanes + pltpu.roll(own, owner * rows, 1)
    behind_two_ref[...] = ahead_two_ref[...].T
    behind_three_ref[...] = ahead_three_ref[...].T
    context = context_ref[pl.ds(task_ref[0], 1), :]
    told = [lane_sum(film_ref[kind] * context) for kind in range(2)]
    told = column_tile(told).T[:8]
    scale = 1.0 + told[0:1] + lanes[4:5]
    shift = told[1:2] + lanes[5:6]
    vectors_ref[...] = row_tile([lanes[0:1], lanes[1:2], lanes[2:3], lanes[3:4], scale, shift])


def assemble(maps, cells, me, piece_refs, index):
    rows = C // len(piece_refs)
    for partner, piece_ref in enumerate(piece_refs):
        maps[own_rows(me, partner, rows), 0:cells] = piece_ref[index]


def disperse(piece_refs, index, me, output, cells):
    rows = C // len(piece_refs)
    for partner, piece_ref in enumerate(piece_refs):
        piece_ref[index] = output[own_rows(me, partner, rows), 0:cells]


def first_conv_kernel(partners, first, final, me_ref, live_ref, told_ref, weights_ref, *refs):
    piece_refs = refs[:partners]
    conv_ref, maps_ref, state_ref, stack, state = refs[-5:]
    step = pl.program_id(0)
    count = conv_ref.shape[0]

    @pl.when(step == 0)
    def _():
        state[...] = refs[partners][...] if first else jnp.zeros_like(state)

    merged = [column(state, k) for k in range(3)]
    for image in range(count):
        maps_ref[image, :, CELLS_TWO // 128 * 128 :] = jnp.zeros((C, LANES_TWO - CELLS_TWO // 128 * 128), BF16)
        assemble(maps_ref.at[image], CELLS_TWO, me_ref[0], piece_refs, image)
        stack_sideways(cut(maps_ref[image], WIDE), MAP, stack.at[image])
        conv = conv_ahead(weights_ref, stack.at[image], MAP)
        write(conv_ref.at[image], conv)
        mean, spread = moments(conv, CELLS_TWO)
        live = live_ref[first + step * count + image]
        merged = merge_moments(merged, live, mean, spread, CELLS_TWO)
    state[...] = column_tile(merged)

    @pl.when(step == pl.num_programs(0) - 1)
    def _():
        if final:
            turned = state[...].T
            spread_rows(row_tile([turned[1:2], turned[2:3], turned[0:1], row(told_ref, 0)], SENT), state_ref)
        else:
            state_ref[...] = state[...]


def middle_kernel(
    partners, me_ref, live_ref, heard_ref, vectors_ref, pool_a_ref, pool_b_ref, weights_ref, conv_ref, *refs
):
    hidden_ref, conv_three_ref, norm_ref, levels_ref, sums_ref, columns, state, stack = refs[-8:]
    piece_refs = refs[-8 - partners : -8]
    step = pl.program_id(0)
    count = conv_ref.shape[0]

    @pl.when(step == 0)
    def _():
        middle, factor, variance, extent = slice_norm(heard_ref)
        norm_ref[...] = row_tile([middle, factor, variance, extent])
        columns[...] = as_columns(row_tile([middle, row(vectors_ref, 0) * factor, row(vectors_ref, 1)]))
        state[...] = jnp.zeros_like(state)

    merged = [column(state, k) for k in range(3)]
    active_squares, hidden_squares = column(state, 3), column(state, 4)
    lives = [live_ref[step * count + image] for image in range(count)]

    def activate(image):
        pre = (conv_ref[image] - column(columns, 0)) * column(columns, 1) + column(columns, 2)
        active = pre * gelu_gate(pre)
        counted = trim(active, 0, CELLS_TWO)
        return halves(active), lives[image] * lane_sum(counted * counted)

    def pool(split):
        (left,) = dot_halves(split[:, :1152], pool_a_ref)
        (right,) = dot_halves(split[:, 896:], pool_b_ref)
        return jnp.concatenate([left, right], axis=1)

    split, squares = activate(0)
    for image in range(count):
        hidden = lives[image] * pool(split)
        active_squares = active_squares + squares
        if image + 1 < count:
            split, squares = activate(image + 1)
        hidden_squares = hidden_squares + lane_sum(hidden * hidden)
        hidden_low = hidden.astype(BF16)
        hidden_ref[image] = hidden_low
        disperse(piece_refs, image, me_ref[0], hidden_ref.at[image], CELLS_THREE)
        stack_sideways(cut(hidden_low, WIDE), HALF, stack.at[image])
        conv = conv_ahead(weights_ref, stack.at[image], HALF)
        write(conv_three_ref.at[image], conv)
        mean, spread = moments(conv, CELLS_THREE)
        merged = merge_moments(merged, lives[image], mean, spread, CELLS_THREE)
    state[...] = column_tile([*merged, active_squares, hidden_squares])

    @pl.when(step == pl.num_programs(0) - 1)
    def _():
        turned = state[...].T
        spread_rows(row_tile([turned[k : k + 1] for k in (1, 2, 0)], SENT), sums_ref)
        levels_ref[...] = row_tile([level_row([column(state, 3), column(state, 4)])])


def top_kernel(
    partners, me_ref, live_ref, heard_ref, own_ref, before_ref, vectors_ref, pool_ref, spread_ref, conv_ref, *refs
):
    target_refs = refs[:partners]
    piece_refs = refs[partners : 2 * partners]
    grad_ref, norm_ref, levels_ref, sums_ref, columns, target, output, totals = refs[2 * partners :]
    step = pl.program_id(0)
    count = conv_ref.shape[0]

    @pl.when(step == 0)
    def _():
        middle, factor, variance, extent = slice_norm(heard_ref)
        norm_ref[...] = row_tile([middle, factor, variance, extent])
        columns[...] = as_columns(row_tile([middle, factor] + [row(vectors_ref, k) for k in (2, 3, 4, 5)]))
        target[...] = jnp.zeros_like(target)
        totals[...] = jnp.zeros_like(totals)

    scale = column(columns, 4)
    slope = scale * column(columns, 2)
    offset = scale * column(columns, 3) + column(columns, 5)
    sums = [jnp.zeros((C, 1), F32)] * 4
    for image in range(count):
        live = live_ref[step * count + image]
        assemble(target.at[image], CELLS_OUT, me_ref[0], target_refs, image)
        normed = (conv_ref[image] - column(columns, 0)) * column(columns, 1)
        filmed = slope * normed + offset
        gate = gelu_gate(filmed)
        active = filmed * gate
        counted = trim(active, 0, CELLS_THREE)
        (pooled,) = dot_halves(halves(active), pool_ref)
        pooled = live * pooled
        output[image] = pooled.astype(BF16)
        disperse(piece_refs, image, me_ref[0], output.at[image], CELLS_OUT)
        spread = jnp.dot(target[image], spread_ref[...], preferred_element_type=F32)
        grad_filmed = live * spread * gelu_slope(filmed, gate)
        grad_ref[image] = scale * grad_filmed
        parts = (
            lane_sum(grad_filmed),
            lane_sum(grad_filmed * normed),
            live * lane_sum(counted * counted),
            lane_sum(pooled * pooled),
        )
        sums = [total + part for total, part in zip(sums, parts)]
    totals[...] += column_tile(sums)

    @pl.when(step == pl.num_programs(0) - 1)
    def _():
        turned = totals[...].T
        shift_sum, scale_sum = turned[0:1], turned[1:2]
        film_scale = row(vectors_ref, 4)
        slope = film_scale * row(vectors_ref, 2) * row(norm_ref, 1)
        offset = film_scale * row(vectors_ref, 3) + row(vectors_ref, 5)
        extent = own_ref[0, 2:3, :]
        away = own_ref[0, 0:1, :] - row(norm_ref, 0)
        filmed_squares = (
            slope * slope * (own_ref[0, 1:2, :] + extent * away * away)
            + 2.0 * slope * offset * extent * away
            + extent * offset * offset
        )
        spread_rows(
            row_tile([shift_sum, scale_sum, film_scale * shift_sum, film_scale * scale_sum], SENT), sums_ref
        )
        nothing = jnp.zeros((C, 1), F32)
        others = level_row([nothing, nothing, nothing, column(totals, 2), column(totals, 3)])
        lanes = lane_ids(C)
        filmed_total = lane_sum(filmed_squares)
        levels_ref[...] = before_ref[...] + row_tile([others + jnp.where(lanes == 2, filmed_total, 0.0)])


def norm_back(live, columns, grad, away, cells):
    scaled = [live * column(columns, k) for k in (1, 2, 3)]
    error = grad.astype(F32) * scaled[0] - scaled[1] - away.astype(F32) * scaled[2]
    return trim(error, 0, cells).astype(BF16)


def norm_back_columns(norm_ref, gain, bias_sum, gain_sum):
    factor, extent = row(norm_ref, 1), row(norm_ref, 3)
    front = gain * factor
    return as_columns(
        row_tile([row(norm_ref, 0), front, front * bias_sum / extent, front * factor * gain_sum / extent])
    )


def back_kernel(
    live_ref,
    heard_ref,
    norm_three_ref,
    norm_two_ref,
    levels_ref,
    vectors_ref,
    weights_ref,
    unpool_a_ref,
    unpool_b_ref,
    grad_ref,
    conv_three_ref,
    conv_two_ref,
    *refs,
):
    out_ref, away_ref, error_ref, sums_ref, columns_three, columns_two, totals, upright = refs[-8:]
    step = pl.program_id(0)
    count = conv_two_ref.shape[0]

    @pl.when(step == 0)
    def _():
        sums = jnp.sum(heard_ref[...], axis=0)
        columns_three[...] = norm_back_columns(norm_three_ref, row(vectors_ref, 2), sums[2:3], sums[3:4])
        columns_two[...] = as_columns(
            row_tile([row(norm_two_ref, 0), row(vectors_ref, 0) * row(norm_two_ref, 1), row(vectors_ref, 1)])
        )
        totals[...] = jnp.zeros_like(totals)

    grad_tile = product_tile = jnp.zeros((C, C), F32)
    for image in range(count):
        away = conv_three_ref[image] - column(columns_three, 0)
        error = norm_back(live_ref[step * count + image], columns_three, grad_ref[image], away, CELLS_THREE)
        error_ref[image] = error
        stack_upright(cut(error, WIDE), HALF, upright.at[image])
    split = jnp.concatenate(
        [
            halves(jnp.concatenate(conv_behind(weights_ref, upright.at[image], HALF), axis=1))
            for image in range(count)
        ],
        axis=0,
    )
    for image in range(count):
        both = split[2 * C * image : 2 * C * (image + 1)]
        for first, (half, unpool_ref) in enumerate(((both[:, :256], unpool_a_ref), (both[:, 128:], unpool_b_ref))):
            for start, stop in ((0, 384), (384, 640), (640, 896)):
                (spread,) = dot_halves(half, unpool_ref.at[:, start:stop])
                cells = slice(first * 896 + start, first * 896 + stop)
                away = conv_two_ref[image, :, cells] - column(columns_two, 0)
                away_ref[image, :, cells] = away.astype(BF16)
                pre = away * column(columns_two, 1) + column(columns_two, 2)
                grad_pre = spread * gelu_slope(pre, gelu_gate(pre))
                out_ref[image, :, cells] = grad_pre.astype(BF16)
                grad_tile = grad_tile + sum(cut(grad_pre, 128))
                product_tile = product_tile + sum(cut(grad_pre * away, 128))
    grad_sum = column(totals, 0) + lane_sum(grad_tile)
    product_sum = column(totals, 1) + lane_sum(product_tile)
    totals[...] = column_tile([grad_sum, product_sum])

    @pl.when(step == pl.num_programs(0) - 1)
    def _():
        turned = totals[...].T
        normed_sum = turned[1:2] * row(norm_two_ref, 1)
        spread_rows(row_tile([turned[0:1], normed_sum, levels_ref[0:1, :]], SENT), sums_ref)


def split_filter(product, filter_ref):
    partners, _, rows, _ = filter_ref.shape
    for tap in range(3):
        for owner in range(partners):
            filter_ref[owner, tap] = product[tap * C + owner * rows : tap * C + (owner + 1) * rows].astype(BF16)


def filter_three_kernel(error_ref, hidden_ref, *refs):
    filter_ref, product, stack, upright = refs[-4:]
    step = pl.program_id(0)
    count = error_ref.shape[0]

    @pl.when(step == 0)
    def _():
        product[...] = jnp.zeros_like(product)

    for image in range(count):
        stack_upright(cut(error_ref[image], WIDE), HALF, upright.at[image])
        stack_sideways(cut(hidden_ref[image], WIDE), HALF, stack.at[image])
        product[...] += across_cells(upright.at[image], stack.at[image])

    @pl.when(step == pl.num_programs(0) - 1)
    def _():
        split_filter(product, filter_ref)


def last_columns(heard_ref, norm_ref, vectors_ref):
    sums = jnp.sum(heard_ref[...], axis=0)
    return norm_back_columns(norm_ref, row(vectors_ref, 0), sums[0:1], sums[1:2])


def last_conv_kernel(
    partners,
    near,
    first,
    steps,
    me_ref,
    live_ref,
    heard_ref,
    norm_ref,
    vectors_ref,
    weights_ref,
    grad_ref,
    away_ref,
    *refs,
):
    far = partners - near
    piece_refs, (columns, output, upright) = refs[-3 - near - far * len(steps) : -3], refs[-3:]
    step = pl.program_id(0)
    count = grad_ref.shape[0]

    @pl.when(step == 0)
    def _():
        columns[...] = last_columns(heard_ref, norm_ref, vectors_ref)

    for image in range(count):
        live = live_ref[first + step * count + image]
        error = norm_back(live, columns, grad_ref[image], away_ref[image], CELLS_TWO)
        stack_upright(cut(error, WIDE), MAP, upright.at[image])
        write(output.at[image], [block.astype(BF16) for block in conv_behind(weights_ref, upright.at[image], MAP)])
    rows = C // partners
    start = 0
    for place, length in enumerate(steps):

        @pl.when((step >= start) & (step < start + length))
        def _():
            for image in range(count):
                for partner in range(partners):
                    piece_ref = piece_refs[partner if partner < near else near + place * far + partner - near]
                    piece_ref[image] = output[image, own_rows(me_ref[0], partner, rows), 0:CELLS_TWO]

        start += length


def last_filter_kernel(live_ref, heard_ref, norm_ref, vectors_ref, grad_ref, away_ref, maps_ref, *refs):
    filter_ref, product, columns, stack, upright = refs[-5:]
    step = pl.program_id(0)
    count = grad_ref.shape[0]

    @pl.when(step == 0)
    def _():
        columns[...] = last_columns(heard_ref, norm_ref, vectors_ref)
        product[...] = jnp.zeros_like(product)

    for image in range(count):
        error = norm_back(live_ref[step * count + image], columns, grad_ref[image], away_ref[image], CELLS_TWO)
        stack_upright(cut(error, WIDE), MAP, upright.at[image])
        stack_sideways(cut(maps_ref[image], WIDE), MAP, stack.at[image])
        product[...] += across_cells(upright.at[image], stack.at[image])

    @pl.when(step == pl.num_programs(0) - 1)
    def _():
        split_filter(product, filter_ref)


def strips_kernel(heard_ref, *refs):
    out_ref = refs[-1]
    out_ref[...] = jnp.broadcast_to(jnp.sum(heard_ref[...].astype(F32), axis=0)[None], out_ref.shape)


def one_hot(rows, columns, wanted):
    row_ids = lax.broadcasted_iota(jnp.int32, (rows, columns), 0)
    column_ids = lax.broadcasted_iota(jnp.int32, (rows, columns), 1)
    return jnp.where(wanted(row_ids, column_ids), 1.0, 0.0)


def exact_dot(left, right, contract=((1,), (0,))):
    return lax.dot_general(left, right, (contract, ((), ())), precision=PRECISE, preferred_element_type=F32)


def finish_kernel(
    partners,
    group,
    here_ref,
    me_ref,
    heard_two_ref,
    heard_top_ref,
    heard_back_ref,
    norm_two_ref,
    norm_three_ref,
    vectors_ref,
    film_ref,
    *refs,
):
    film_w_ref, film_b_ref, context_ref, *sum_refs, levels_ref, product = refs[-9:]
    devices = heard_two_ref.shape[0]
    tasks = devices // group
    contexts = context_ref.shape[0]
    rows = C // partners
    entries = film_ref.shape[2]
    turn = (C - me_ref[0] * rows) % C

    def own_lanes(values):
        return pltpu.roll(values, turn, 1)[:, :rows]

    by_task = one_hot(tasks, devices, lambda t, d: d // group == t)
    of_task = one_hot(
        tasks, devices, lambda t, d: (d // partners == t // contexts) & (d % partners == t % contexts)
    )
    mine = one_hot(contexts, devices, lambda t, d: d // group == here_ref[0] * contexts + t)
    shift, normed = heard_top_ref[:, 0, :], heard_top_ref[:, 1, :]
    scale = row(vectors_ref, 2) * normed + row(vectors_ref, 3) * shift
    told = exact_dot(of_task, heard_two_ref[:, 3, :])
    total = jnp.zeros((contexts, entries), F32)
    for kind, grads in enumerate((scale, shift)):
        grads_by_task = exact_dot(by_task, grads)
        product[...] = exact_dot(grads_by_task, told, ((0,), (0,)))
        film_w_ref[kind] = product[pl.ds(pl.multiple_of(me_ref[0] * rows, rows), rows), :entries]
        film_b_ref[kind : kind + 1] = own_lanes(jnp.sum(grads_by_task, axis=0, keepdims=True))
        total = total + exact_dot(exact_dot(mine, grads), film_ref[kind])
    context_ref[...] = total

    back = jnp.sum(heard_back_ref[...], axis=0)
    top = jnp.sum(heard_top_ref[...], axis=0)
    for sum_ref, sums in zip(sum_refs, (back[1:2], back[0:1], top[3:4], top[2:3])):
        sum_ref[...] = own_lanes(sums)[0]

    live = norm_two_ref[3:4, 0:1] * (1.0 / CELLS_TWO)
    lanes = lane_ids(C)

    def mean_square(norm_ref, gain, shift):
        factor, variance = row(norm_ref, 1), row(norm_ref, 2)
        return jnp.sum(gain * gain * variance * factor * factor + shift * shift, axis=1, keepdims=True) * (1.0 / C)

    def mean_conv(norm_ref):
        middle = row(norm_ref, 0)
        return jnp.sum(row(norm_ref, 2) + middle * middle, axis=1, keepdims=True) * (1.0 / C)

    known = (
        mean_conv(norm_two_ref),
        mean_square(norm_two_ref, row(vectors_ref, 0), row(vectors_ref, 1)),
        back[2:3, 0:1] / (live * (C * CELLS_TWO)),
        back[2:3, 1:2] / (live * (C * CELLS_THREE)),
        mean_conv(norm_three_ref),
        mean_square(norm_three_ref, row(vectors_ref, 2), row(vectors_ref, 3)),
        back[2:3, 2:3] / (live * (C * CELLS_THREE)),
        back[2:3, 3:4] / (live * (C * CELLS_THREE)),
        back[2:3, 4:5] / (live * (C * CELLS_OUT)),
    )
    level = jnp.zeros((1, C), F32)
    for place, value in enumerate(known):
        level = jnp.where(lanes == place, value, level)
    levels_ref[...] = jnp.sqrt(level)[0, : levels_ref.shape[0]]


def pool_matrix(side, width, out_width):
    half = side // 2
    matrix = np.zeros((width, out_width), np.float32)
    for row in range(2 * half):
        for column in range(2 * half):
            matrix[row * side + column, (row // 2) * half + column // 2] = 0.25
    return matrix


def lasting(microseconds):
    return pl.CostEstimate(
        flops=int(microseconds * 1.1e9), bytes_accessed=int(microseconds * 3.5e6), transcendentals=0
    )


def smem():
    return pl.BlockSpec(memory_space=pltpu.SMEM)


def anywhere(count):
    return [pl.BlockSpec(memory_space=pl.ANY)] * count


def whole(*shape):
    return pl.BlockSpec(shape, lambda n: (0,) * len(shape))


def each(*shape, first=0, count=1):
    return pl.BlockSpec((count, *shape), lambda n: (first + n,) + (0,) * len(shape))


def pack(maps, me, images_each, wants, earlier=()):
    rows, slots, cells = maps.shape
    group = CAP // images_each
    halves = 2
    block = wants[0][0] // group
    return pl.pallas_call(
        functools.partial(pack_kernel, images_each, group, wants),
        grid_spec=pltpu.PrefetchScalarGridSpec(
            num_scalar_prefetch=1,
            grid=(halves,),
            in_specs=[
                pl.BlockSpec((rows // halves, CAP, cells), lambda n, me_ref: (n, (me_ref[0] // group) ^ block, 0)),
                *anywhere(len(earlier)),
            ],
            out_specs=[
                pl.BlockSpec((count, rows // halves, cells), lambda n, me_ref: (0, n, 0)) for _, _, count in wants
            ],
        ),
        out_shape=[jax.ShapeDtypeStruct((count, rows, cells), maps.dtype) for _, _, count in wants],
        compiler_params=kernel_params(),
        name="pack",
        cost_estimate=lasting(2.5),
    )(me, maps, *earlier)


def unpack(arrays, me, images_each, dtype, place, outs=(), earlier=()):
    partners = len(arrays[0])
    group = CAP // images_each
    halves = 2
    given, specs, counts, shapes, out_specs = [], [], [], [], []
    for pieces in arrays:
        here = pieces[place * group : (place + 1) * group]
        counts.append(tuple(tuple(piece.shape[0] for piece in parts) for parts in here))
        rows, cells = here[0][0].shape[1:]
        for piece in (piece for parts in here for piece in parts):
            given.append(piece)
            specs.append(pl.BlockSpec((piece.shape[0], rows // halves, cells), lambda n, me_ref: (0, n, 0)))
        shapes.append(jax.ShapeDtypeStruct((rows, partners * images_each, cells), dtype))
        out_specs.append(
            pl.BlockSpec((rows // halves, CAP, cells), lambda n, me_ref: (n, (me_ref[0] // group) ^ place, 0))
        )
    aliases = {1 + len(given) + k: k for k in range(len(outs))}
    given += [*outs, *earlier]
    specs += anywhere(len(given) - len(specs))
    return pl.pallas_call(
        functools.partial(unpack_kernel, counts),
        grid_spec=pltpu.PrefetchScalarGridSpec(
            num_scalar_prefetch=1, grid=(halves,), in_specs=specs, out_specs=out_specs
        ),
        out_shape=shapes,
        input_output_aliases=aliases,
        compiler_params=kernel_params(),
        name="unpack",
        cost_estimate=lasting(2.0),
    )(me, *given)


def local(
    images,
    counts,
    context,
    filter_two,
    gain_two,
    shift_two,
    filter_three,
    gain_three,
    shift_three,
    film_weight,
    film_bias,
    cotangent,
    *,
    partners,
    columns,
):
    devices = partners * columns
    rows, slots = images.shape[:2]
    images_each = slots // partners
    group = CAP // images_each
    one = min(images_each, 2)
    pair, some = min(images_each, 2), min(images_each, 4)
    position = lax.axis_index("tensor")
    me = jnp.reshape(position, (1,)).astype(jnp.int32)

    def swap(value, partner):
        if partner == 0:
            return value
        return lax.ppermute(value, "tensor", [(i, i ^ partner) for i in range(partners)])

    def share(copies):
        return lax.all_to_all(copies, ("dp", "tensor"), 0, 0)

    near = 2
    half, quarter = images_each // 2, images_each // 4
    sizes_in = (half, quarter, quarter) if quarter >= pair else (half, half)
    half = images_each // 2
    calls_out = (*[(pair,)] * (half // pair), (half,))
    starts_in = [sum(sizes_in[:part]) for part in range(len(sizes_in))]
    counts_of = [(images_each,) if partner < near else sizes_in for partner in range(partners)]
    far = [partner for partner in reversed(range(partners)) if partner >= near]
    maps = [[None] * len(counts_of[partner]) for partner in range(partners)]

    def send_in(some_parts, whole_near, earlier):
        for block in reversed(range(partners // group)):
            wants = [
                (partner, starts_in[part], sizes_in[part])
                for part in some_parts
                for partner in far
                if partner // group == block
            ]
            if block == 0 and whole_near:
                wants += [(partner, 0, images_each) for partner in range(near)]
            if wants:
                sent = pack(images, me, images_each, wants, earlier)
                for piece, (partner, first, _) in zip(sent, wants):
                    maps[partner][starts_in.index(first)] = swap(piece, partner)
                earlier = (*earlier, sent[0])
        return earlier

    first_sent = send_in((0,), True, ())
    entries = film_weight.shape[0]
    bundle = pl.pallas_call(
        bundle_kernel,
        in_specs=[pl.BlockSpec(memory_space=pltpu.VMEM)] * 8 + anywhere(1),
        out_shape=jax.ShapeDtypeStruct((7 * rows + 16, 3 * C), BF16),
        compiler_params=kernel_params(0),
        name="bundle",
        cost_estimate=lasting(1.0),
    )(
        jnp.transpose(filter_two, (2, 3, 0, 1)),
        jnp.transpose(filter_three, (2, 3, 0, 1)),
        jnp.transpose(film_weight, (1, 2, 0)),
        film_bias,
        *[vector[None] for vector in (gain_two, shift_two, gain_three, shift_three)],
        first_sent[0],
    )
    bundles = {0: bundle}
    bit = partners // 2
    while bit:
        bundles.update({partner | bit: swap(piece, bit) for partner, piece in bundles.items()})
        bit //= 2

    sent_in = {
        part: send_in((part,), False, (maps[far[0]][0],))
        for part in range(1, len(sizes_in))
    }

    task = position // group
    slot = (position % group) * images_each + jnp.arange(images_each, dtype=jnp.int32)
    limit = lax.dynamic_index_in_dim(counts, task, 0, keepdims=False)
    live = (slot < limit).astype(F32)
    ahead_two, behind_two, ahead_three, behind_three, film, vectors = pl.pallas_call(
        functools.partial(unbundle_kernel, partners),
        in_specs=[smem(), smem(), *[pl.BlockSpec(memory_space=pltpu.VMEM)] * (1 + partners)],
        out_shape=[jax.ShapeDtypeStruct((3 * C, 3 * C), BF16)] * 4
        + [jax.ShapeDtypeStruct((2, C, entries), F32), jax.ShapeDtypeStruct((8, C), F32)],
        compiler_params=kernel_params(0),
        name="unbundle",
        cost_estimate=lasting(2.0),
    )(me, jnp.reshape(task, (1,)).astype(jnp.int32), context, *[bundles[partner] for partner in range(partners)])

    told = lax.dynamic_index_in_dim(context, position % context.shape[0], 0)
    told = jnp.pad(told, ((0, 7), (0, C - entries)))

    conv_two = whole_maps = state = None
    for part, (first, count) in enumerate(zip(starts_in, sizes_in)):
        given = [maps[partner][0 if partner < near else part] for partner in range(partners)]
        specs = [
            each(rows, CELLS_TWO, first=first // pair if partner < near else 0, count=pair)
            for partner in range(partners)
        ]
        aliases = {}
        final = part == len(sizes_in) - 1
        if part:
            aliases = {5 + partners: 0, 6 + partners: 1}
            given = given + [state, conv_two, whole_maps]
            specs = specs + [whole(C, C), *anywhere(2)]
        waits = [] if final else [sent_in[part + 1][-1]]
        given = given + waits
        specs = specs + anywhere(len(waits))
        conv_two, whole_maps, state = pl.pallas_call(
            functools.partial(first_conv_kernel, partners, first, final),
            grid=(count // pair,),
            in_specs=[smem(), smem(), whole(8, C), whole(3 * C, 3 * C), *specs],
            out_specs=[
                each(C, LANES_TWO, first=first // pair, count=pair),
                each(C, LANES_TWO, first=first // pair, count=pair),
                whole(devices, SENT, C) if final else whole(C, C),
            ],
            out_shape=[
                jax.ShapeDtypeStruct((images_each, C, LANES_TWO), F32),
                jax.ShapeDtypeStruct((images_each, C, LANES_TWO), BF16),
                jax.ShapeDtypeStruct((devices, SENT, C) if final else (C, C), F32),
            ],
            scratch_shapes=[
                pltpu.VMEM((pair, 3 * C, LANES_TWO), BF16),
                pltpu.VMEM((C, C), F32),
            ],
            input_output_aliases=aliases,
            compiler_params=kernel_params(),
            name="first_conv",
            cost_estimate=lasting(2.3 * count),
        )(me, live, told, ahead_two, *given)
    heard_two = share(state)
    turned = jnp.transpose(cotangent, (1, 0, 2))
    targets = [
        swap(lax.dynamic_slice_in_dim(turned, (position ^ partner) * images_each, images_each, 0), partner)
        for partner in range(partners)
    ]

    pool = pool_matrix(MAP, LANES_TWO, LANES_THREE)
    pool_out = pool_matrix(HALF, LANES_THREE, LANES_OUT)
    *block_pieces, hidden, conv_three, norm_two, levels, sums_three = pl.pallas_call(
        functools.partial(middle_kernel, partners),
        grid=(images_each // pair,),
        in_specs=[
            smem(),
            smem(),
            whole(devices, SENT, C),
            whole(8, C),
            whole(1152, 256),
            whole(896, 256),
            whole(3 * C, 3 * C),
            each(C, LANES_TWO, count=pair),
        ],
        out_specs=[each(rows, CELLS_THREE, count=pair)] * partners
        + [each(C, LANES_THREE, count=pair), each(C, LANES_THREE, count=pair), whole(8, C), whole(8, C), whole(devices, SENT, C)],
        out_shape=[jax.ShapeDtypeStruct((images_each, rows, CELLS_THREE), BF16)] * partners
        + [
            jax.ShapeDtypeStruct((images_each, C, LANES_THREE), BF16),
            jax.ShapeDtypeStruct((images_each, C, LANES_THREE), F32),
            jax.ShapeDtypeStruct((8, C), F32),
            jax.ShapeDtypeStruct((8, C), F32),
            jax.ShapeDtypeStruct((devices, SENT, C), F32),
        ],
        scratch_shapes=[
            pltpu.VMEM((C, C), F32),
            pltpu.VMEM((C, C), F32),
            pltpu.VMEM((pair, 3 * C, LANES_THREE), BF16),
        ],
        compiler_params=kernel_params(),
        name="middle",
            cost_estimate=lasting(2.0 * images_each),
    )(
        me,
        live,
        heard_two,
        vectors,
        jnp.asarray(pool[:1152, :256], BF16),
        jnp.asarray(pool[896:, 256:], BF16),
        ahead_three,
        conv_two,
    )
    heard_three = share(sums_three)

    *out_pieces, grad_three, norm_three, levels, sums_top = pl.pallas_call(
        functools.partial(top_kernel, partners),
        grid=(images_each // some,),
        in_specs=[
            smem(),
            smem(),
            whole(devices, SENT, C),
            whole(1, SENT, C),
            whole(8, C),
            whole(8, C),
            whole(LANES_THREE, LANES_OUT),
            whole(LANES_OUT, LANES_THREE),
            each(C, LANES_THREE, count=some),
            *[each(rows, CELLS_OUT, count=some)] * partners,
        ],
        out_specs=[each(rows, CELLS_OUT, count=some)] * partners
        + [each(C, LANES_THREE, count=some), whole(8, C), whole(8, C), whole(devices, SENT, C)],
        out_shape=[jax.ShapeDtypeStruct((images_each, rows, CELLS_OUT), BF16)] * partners
        + [
            jax.ShapeDtypeStruct((images_each, C, LANES_THREE), F32),
            jax.ShapeDtypeStruct((8, C), F32),
            jax.ShapeDtypeStruct((8, C), F32),
            jax.ShapeDtypeStruct((devices, SENT, C), F32),
        ],
        scratch_shapes=[
            pltpu.VMEM((C, C), F32),
            pltpu.VMEM((some, C, LANES_OUT), BF16),
            pltpu.VMEM((some, C, LANES_OUT), BF16),
            pltpu.VMEM((C, C), F32),
        ],
        compiler_params=kernel_params(),
        name="top",
            cost_estimate=lasting(0.8 * images_each),
    )(
        me,
        live,
        heard_three,
        sums_three,
        levels,
        vectors,
        jnp.asarray(pool_out, BF16),
        jnp.asarray(pool_out.T, BF16),
        conv_three,
        *targets,
    )
    heard_top = share(sums_top)
    block_two = [[swap(block_pieces[k], k)] for k in range(partners)]
    out_pieces = [[swap(out_pieces[k], k)] for k in range(partners)]

    filter_shape = jax.ShapeDtypeStruct((partners, 2, 3, rows, 3 * C), BF16)

    def filter_spec(block):
        return pl.BlockSpec((partners, None, 3, rows, 3 * C), lambda n: (0, block, 0, 0, 0))

    grad_two, away_two, error_three, sums_two = pl.pallas_call(
        back_kernel,
        grid=(images_each // pair,),
        in_specs=[
            smem(),
            whole(devices, SENT, C),
            whole(8, C),
            whole(8, C),
            whole(8, C),
            whole(8, C),
            whole(3 * C, 3 * C),
            whole(256, 896),
            whole(384, 896),
            each(C, LANES_THREE, count=pair),
            each(C, LANES_THREE, count=pair),
            each(C, LANES_TWO, count=pair),
        ],
        out_specs=[
            each(C, LANES_TWO, count=pair),
            each(C, LANES_TWO, count=pair),
            each(C, LANES_THREE, count=pair),
            whole(devices, SENT, C),
        ],
        out_shape=[
            jax.ShapeDtypeStruct((images_each, C, LANES_TWO), BF16),
            jax.ShapeDtypeStruct((images_each, C, LANES_TWO), BF16),
            jax.ShapeDtypeStruct((images_each, C, LANES_THREE), BF16),
            jax.ShapeDtypeStruct((devices, SENT, C), F32),
        ],
        scratch_shapes=[
            pltpu.VMEM((C, C), F32),
            pltpu.VMEM((C, C), F32),
            pltpu.VMEM((C, C), F32),
            pltpu.VMEM((pair, 3 * C, LANES_THREE), BF16),
        ],
        compiler_params=kernel_params(),
        name="back",
            cost_estimate=lasting(2.0 * images_each),
    )(
        live,
        heard_top,
        norm_three,
        norm_two,
        levels,
        vectors,
        behind_three,
        jnp.asarray(pool[:896, :256].T, BF16),
        jnp.asarray(pool[896:, 128:].T, BF16),
        grad_three,
        conv_three,
        conv_two,
    )
    heard_back = share(sums_two)

    filter_sums = pl.pallas_call(
        filter_three_kernel,
        grid=(images_each // some,),
        in_specs=[*[each(C, LANES_THREE, count=some)] * 2, *anywhere(1)],
        out_specs=filter_spec(1),
        out_shape=filter_shape,
        scratch_shapes=[
            pltpu.VMEM((3 * C, 3 * C), F32),
            pltpu.VMEM((some, 3 * C, LANES_THREE), BF16),
            pltpu.VMEM((some, 3 * C, LANES_THREE), BF16),
        ],
        compiler_params=kernel_params(),
        name="filter_three",
        cost_estimate=lasting(5.0),
    )(error_three, hidden, sums_two)

    returned = [[] for partner in range(partners)]
    waits = [filter_sums, *(pieces[0] for pieces in (*block_two, *out_pieces))]
    common = [heard_back, norm_two, vectors]
    common_specs = [whole(devices, SENT, C), whole(8, C), whole(8, C)]
    kept = []
    first = 0
    for sizes in calls_out:
        count = sum(sizes)
        steps = [some // one for some in sizes]
        out_specs = [each(rows, CELLS_TWO, first=first // one, count=one)] * near
        out_shape = [jax.ShapeDtypeStruct((images_each, rows, CELLS_TWO), BF16)] * near
        for place, length in enumerate(steps):
            start = sum(steps[:place])
            out_specs += [
                pl.BlockSpec(
                    (one, rows, CELLS_TWO),
                    lambda n, start=start, length=length: (jnp.clip(n - start, 0, length - 1), 0, 0),
                )
            ] * len(far)
            out_shape += [jax.ShapeDtypeStruct((length * one, rows, CELLS_TWO), BF16)] * len(far)
        inputs = [me, live, *common, behind_two, grad_two, away_two]
        pieces = pl.pallas_call(
            functools.partial(last_conv_kernel, partners, near, first, steps),
            grid=(count // one,),
            in_specs=[
                smem(),
                smem(),
                *common_specs,
                whole(3 * C, 3 * C),
                *[each(C, LANES_TWO, first=first // one, count=one)] * 2,
                *anywhere(len(waits) + len(kept)),
            ],
            out_specs=out_specs,
            out_shape=out_shape,
            scratch_shapes=[
                pltpu.VMEM((C, C), F32),
                pltpu.VMEM((one, C, LANES_TWO), BF16),
                pltpu.VMEM((one, 3 * C, LANES_TWO), BF16),
            ],
            input_output_aliases={len(inputs) + len(waits) + k: k for k in range(len(kept))},
            compiler_params=kernel_params(),
            name="last_conv",
            cost_estimate=lasting(1.5 * count),
        )(*inputs, *waits, *kept)
        kept, waits, first = pieces[:near], [], first + count
        for place in range(len(sizes)):
            for partner in reversed(far):
                returned[partner].append(swap(pieces[near + place * len(far) + partner - near], partner))
        if first == half:
            product = pl.pallas_call(
                last_filter_kernel,
                grid=(images_each // pair,),
                in_specs=[
                    smem(),
                    *common_specs,
                    *[each(C, LANES_TWO, count=pair)] * 3,
                    *anywhere(2),
                ],
                out_specs=filter_spec(0),
                out_shape=filter_shape,
                scratch_shapes=[
                    pltpu.VMEM((3 * C, 3 * C), F32),
                    pltpu.VMEM((C, C), F32),
                    pltpu.VMEM((pair, 3 * C, LANES_TWO), BF16),
                    pltpu.VMEM((pair, 3 * C, LANES_TWO), BF16),
                ],
                input_output_aliases={7: 0},
                compiler_params=kernel_params(),
                name="last_filter",
                cost_estimate=lasting(1.2 * images_each),
            )(live, *common, grad_two, away_two, whole_maps, filter_sums, kept[0])
            waits = [product, *(piece for partner in far for piece in returned[partner])]
    for partner in range(near):
        returned[partner].append(swap(kept[partner], partner))

    blocks = ()
    for place in range(partners // group):
        blocks = unpack([block_two, out_pieces], me, images_each, BF16, place, blocks, [kept[0]])
    block_two, block_three = blocks

    contexts = context.shape[0]
    grad_film_w, grad_film_b, grad_context, *norm_sums, levels = pl.pallas_call(
        functools.partial(finish_kernel, partners, group),
        in_specs=[smem(), smem(), *[pl.BlockSpec(memory_space=pltpu.VMEM)] * 7, *anywhere(1)],
        out_shape=[
            jax.ShapeDtypeStruct((2, rows, entries), F32),
            jax.ShapeDtypeStruct((2, rows), F32),
            jax.ShapeDtypeStruct((contexts, entries), F32),
            *[jax.ShapeDtypeStruct((rows,), F32)] * 4,
            jax.ShapeDtypeStruct((9,), F32),
        ],
        scratch_shapes=[pltpu.VMEM((C, C), F32)],
        compiler_params=kernel_params(0),
        name="finish",
        cost_estimate=lasting(2.0),
    )(
        jnp.reshape(lax.axis_index("dp"), (1,)).astype(jnp.int32),
        me,
        heard_two,
        heard_top,
        heard_back,
        norm_two,
        norm_three,
        vectors,
        film,
        kept[0],
    )

    strip = 6 * rows // columns
    heard = lax.all_to_all(product.reshape(devices, strip, 3 * C), ("tensor", "dp"), 0, 0)
    strips = pl.pallas_call(
        strips_kernel,
        in_specs=[pl.BlockSpec(memory_space=pltpu.VMEM), *anywhere(2)],
        out_shape=jax.ShapeDtypeStruct((columns, strip, 3 * C), F32),
        compiler_params=kernel_params(0),
        name="strips",
        cost_estimate=lasting(1.5),
    )(heard, block_two, norm_sums[0])
    strips = lax.all_to_all(strips, "dp", 0, 0)
    grad_filters = jnp.transpose(strips.reshape(2, 3, rows, 3, C), (0, 2, 4, 1, 3))

    grad_images = ()
    for place in range(partners // group):
        waits = () if grad_images else (kept[0],)
        grad_images = unpack([returned], me, images_each, F32, place, grad_images, waits)
    (grad_images,) = grad_images

    return (
        block_two,
        block_three,
        grad_images,
        grad_filters[0],
        norm_sums[0],
        norm_sums[1],
        grad_filters[1],
        norm_sums[2],
        norm_sums[3],
        jnp.transpose(grad_film_w, (2, 0, 1)),
        grad_film_b,
        grad_context,
        levels,
    )


def solution(mesh):
    step = functools.partial(local, partners=mesh.shape["tensor"], columns=mesh.shape["dp"])
    placed = (
        P("tensor", "dp", None),
        P("dp"),
        P("dp", None),
        P("tensor", None, None, None),
        P("tensor"),
        P("tensor"),
        P("tensor", None, None, None),
        P("tensor"),
        P("tensor"),
        P(None, None, "tensor"),
        P(None, "tensor"),
        P("tensor", "dp", None),
    )
    return jax.shard_map(
        step,
        mesh=mesh,
        in_specs=placed,
        out_specs=(
            P("tensor", "dp", None),
            P("tensor", "dp", None),
            P("tensor", "dp", None),
            P("tensor", None, None, None),
            P("tensor"),
            P("tensor"),
            P("tensor", None, None, None),
            P("tensor"),
            P("tensor"),
            P(None, None, "tensor"),
            P(None, "tensor"),
            P("dp", None),
            P(),
        ),
        check_vma=False,
    )
```

```python
import functools

import jax
import jax.numpy as jnp
import numpy as np
from jax import lax
from jax.experimental import pallas as pl
from jax.experimental.pallas import tpu as pltpu
from jax.sharding import PartitionSpec as P

C = 128
MAP = 42
CAP = 16
HALF = 21
QUART = 10
SENT = 4
VMEM_BYTES = 63 << 20
WIDE = 256

CELLS_TWO = MAP * MAP
CELLS_THREE = HALF * HALF
CELLS_OUT = QUART * QUART
LANES_TWO = 1792
LANES_THREE = 512
LANES_OUT = 128
EPSILON = 1e-05
PRECISE = lax.Precision.HIGHEST
F32 = jnp.float32
BF16 = jnp.bfloat16
ROOT = 0.7978845608028654
CUBIC = 0.044715


def lane_ids(width):
    return lax.broadcasted_iota(jnp.int32, (1, width), 1)


def as_columns(rows):
    return jnp.concatenate([rows] * (C // 8), axis=0).T


def column_tile(columns):
    ids = lax.broadcasted_iota(jnp.int32, (C, C), 1)
    tile = jnp.zeros((C, C), F32)
    for place, column in enumerate(columns):
        tile = jnp.where(ids == place, column, tile)
    return tile


def row_tile(rows, count=8):
    ids = lax.broadcasted_iota(jnp.int32, (count, C), 0)
    tile = jnp.zeros((count, C), F32)
    for place, row in enumerate(rows):
        tile = jnp.where(ids == place, row, tile)
    return tile


def row(tile_ref, place):
    return tile_ref[place : place + 1, :]


def column(tile_ref, place):
    return tile_ref[:, place : place + 1]


def merge_moments(state, weight, mean, spread, cells):
    count, middle, total = state
    added = weight * cells
    both = count + added
    away = mean - middle
    share = added / jnp.maximum(both, 1.0)
    return both, middle + away * share, total + weight * spread + away * away * count * share


def slice_norm(heard_ref):
    means, spreads, counts = heard_ref[:, 0, :], heard_ref[:, 1, :], heard_ref[:, 2, :]
    extent = jnp.sum(counts, axis=0, keepdims=True)
    middle = jnp.sum(counts * means, axis=0, keepdims=True) / extent
    away = means - middle
    variance = jnp.sum(spreads + counts * away * away, axis=0, keepdims=True) / extent
    return middle, lax.rsqrt(variance + EPSILON), variance, extent


def level_row(columns):
    return jnp.sum(column_tile(columns), axis=0, keepdims=True)


def spread_rows(tile, out_ref):
    out_ref[...] = jnp.broadcast_to(tile[None], out_ref.shape)


def trim(values, first, last):
    tiles = cut(values, 128)
    ids = lane_ids(128)
    if first > 0:
        tiles[0] = jnp.where(ids >= first, tiles[0], jnp.zeros_like(tiles[0]))
    if last < values.shape[1]:
        tiles[-1] = jnp.where(ids < last - (values.shape[1] - 128), tiles[-1], jnp.zeros_like(tiles[-1]))
    return jnp.concatenate(tiles, axis=1)


def cut(values, wide):
    return [values[:, first : first + wide] for first in range(0, values.shape[1], wide)]


def shift_lanes(blocks, by):
    moved = [pltpu.roll(block, by % block.shape[1], 1) for block in blocks]
    nothing = jnp.zeros_like(moved[0][:, :128])
    ids = lane_ids(128)
    shifted = []
    for place, block in enumerate(moved):
        if by > 0:
            near = moved[place - 1][:, :128] if place else nothing
            edge = jnp.where(ids < by, near, block[:, :128])
            shifted.append(jnp.concatenate([edge, block[:, 128:]], axis=1) if block.shape[1] > 128 else edge)
        else:
            near = moved[place + 1][:, -128:] if place + 1 < len(moved) else nothing
            edge = jnp.where(ids >= 128 + by, near, block[:, -128:])
            shifted.append(jnp.concatenate([block[:, :-128], edge], axis=1) if block.shape[1] > 128 else edge)
    return shifted


def shift_column(blocks, by, side):
    shifted = []
    first = 0
    for block in shift_lanes(blocks, by):
        column = (lane_ids(block.shape[1]) + first) % side
        shifted.append(jnp.where(column == (0 if by > 0 else side - 1), jnp.zeros_like(block), block))
        first += block.shape[1]
    return shifted


def write(out_ref, blocks):
    first = 0
    for block in blocks:
        out_ref[:, first : first + block.shape[1]] = block
        first += block.shape[1]


def fill(stack_ref, tap, blocks):
    first = 0
    for block in blocks:
        stack_ref[tap * C : (tap + 1) * C, first : first + block.shape[1]] = block
        first += block.shape[1]


def stack_sideways(low, side, stack_ref):
    fill(stack_ref, 0, shift_column(low, 1, side))
    fill(stack_ref, 1, low)
    fill(stack_ref, 2, shift_column(low, -1, side))


def stack_upright(low, side, stack_ref):
    fill(stack_ref, 0, shift_lanes(low, -side))
    fill(stack_ref, 1, low)
    fill(stack_ref, 2, shift_lanes(low, side))


def conv_blocks(weights_ref, stack_ref):
    width = stack_ref.shape[1]
    parts = [
        jnp.dot(weights_ref[...], stack_ref[:, first : first + WIDE], preferred_element_type=F32)
        for first in range(0, width, WIDE)
    ]
    return [[part[tap * C : (tap + 1) * C] for part in parts] for tap in range(3)]


def conv_ahead(weights_ref, stack_ref, side):
    above, here, below = conv_blocks(weights_ref, stack_ref)
    total = [a + b + c for a, b, c in zip(shift_lanes(above, side), here, shift_lanes(below, -side))]
    total[-1] = trim(total[-1], 0, side * side - (stack_ref.shape[1] - total[-1].shape[1]))
    return total


def conv_behind(weights_ref, stack_ref, side):
    left, here, right = conv_blocks(weights_ref, stack_ref)
    return [a + b + c for a, b, c in zip(shift_column(left, -1, side), here, shift_column(right, 1, side))]


def across_cells(left_ref, right_ref):
    return lax.dot_general(left_ref[...], right_ref[...], (((1,), (1,)), ((), ())), preferred_element_type=F32)


def lane_sum(values):
    return jnp.sum(values, axis=1, keepdims=True)


def moments(blocks, cells):
    pivot = lane_sum(blocks[0]) * (1.0 / blocks[0].shape[1])
    total, squares = 0.0, 0.0
    for place, block in enumerate(blocks):
        away = block - pivot
        if place == len(blocks) - 1:
            away = trim(away, 0, cells - sum(b.shape[1] for b in blocks[:-1]))
        total = total + sum(cut(away, 128))
        squares = squares + sum(cut(away * away, 128))
    away = lane_sum(total) * (1.0 / cells)
    return pivot + away, lane_sum(squares) - cells * away * away


def gelu_gate(values):
    return 0.5 + 0.5 * jnp.tanh(values * (ROOT + (ROOT * CUBIC) * (values * values)))


def gelu_slope(values, gate):
    return gate * (1.0 + (1.0 - gate) * (values * (2.0 * ROOT + (6.0 * ROOT * CUBIC) * (values * values))))


def halves(values):
    high = values.astype(BF16)
    return jnp.concatenate([high, (values - high.astype(F32)).astype(BF16)], axis=0)


def dot_halves(split, weights_ref):
    both = jnp.dot(split, weights_ref[...], preferred_element_type=F32)
    return [both[first : first + C] + both[first + C : first + 2 * C] for first in range(0, both.shape[0], 2 * C)]


def own_rows(me, partner, count):
    return pl.ds(pl.multiple_of((me ^ partner) * count, count), count)


def kernel_params(axes=1):
    return pltpu.CompilerParams(vmem_limit_bytes=VMEM_BYTES, dimension_semantics=("arbitrary",) * axes)


def pack_kernel(images_each, group, wants, me_ref, maps_ref, *refs):
    piece_refs = refs[-len(wants) :]
    turned = jnp.swapaxes(maps_ref[...], 0, 1)
    for lead in range(group):

        @pl.when(me_ref[0] % group == lead)
        def _():
            for piece_ref, (partner, first, count) in zip(piece_refs, wants):
                start = (lead ^ (partner % group)) * images_each + first
                piece_ref[...] = turned[start : start + count]


def unpack_kernel(counts, me_ref, *refs):
    out_refs = refs[-len(counts) :]
    group = len(counts[0])
    for lead in range(group):

        @pl.when(me_ref[0] % group == lead)
        def _():
            start = 0
            for out_ref, parts in zip(out_refs, counts):
                ordered = []
                for slot in range(group):
                    place = start + sum(len(some) for some in parts[: slot ^ lead])
                    ordered += [refs[place + part][...] for part in range(len(parts[slot ^ lead]))]
                joined = jnp.concatenate(ordered, axis=0) if len(ordered) > 1 else ordered[0]
                out_ref[...] = jnp.swapaxes(joined, 0, 1).astype(out_ref.dtype)
                start += sum(len(some) for some in parts)


def bundle_kernel(filter_two_ref, filter_three_ref, film_ref, bias_ref, *refs):
    vector_refs, out_ref = refs[:4], refs[-1]
    rows = filter_two_ref.shape[2]
    out_ref[...] = jnp.zeros_like(out_ref)
    for place, filter_ref in enumerate((filter_two_ref, filter_three_ref)):
        for down in range(3):
            first = (3 * place + down) * rows
            for across in range(3):
                out_ref[first : first + rows, across * C : (across + 1) * C] = filter_ref[down, across]
    for kind in range(2):
        out_ref[6 * rows : 7 * rows, kind * C : kind * C + film_ref.shape[2]] = film_ref[kind]
    for place, vector_ref in enumerate(vector_refs):
        out_ref[7 * rows + place : 7 * rows + place + 1, 0:rows] = vector_ref[...]
    for kind in range(2):
        out_ref[7 * rows + 4 + kind : 7 * rows + 5 + kind, 0:rows] = bias_ref[kind : kind + 1]


def unbundle_kernel(partners, me_ref, task_ref, context_ref, *refs):
    piece_refs = refs[:partners]
    ahead_two_ref, behind_two_ref, ahead_three_ref, behind_three_ref, film_ref, vectors_ref = refs[partners:]
    rows = C // partners
    entries = film_ref.shape[2]
    lanes = jnp.zeros((8, C), F32)
    ids = lane_ids(C)
    for partner, piece_ref in enumerate(piece_refs):
        owner = me_ref[0] ^ partner
        for place, ahead_ref in enumerate((ahead_two_ref, ahead_three_ref)):
            for down in range(3):
                first = (3 * place + down) * rows
                ahead_ref[pl.ds(pl.multiple_of(down * C + owner * rows, rows), rows), :] = piece_ref[first : first + rows]
        for kind in range(2):
            film_ref[kind, own_rows(me_ref[0], partner, rows), :] = piece_ref[
                6 * rows : 7 * rows, kind * C : kind * C + entries
            ].astype(F32)
        own = jnp.where(ids < rows, piece_ref[7 * rows : 7 * rows + 16, 0:C].astype(F32)[:8], 0.0)
        lanes = lanes + pltpu.roll(own, owner * rows, 1)
    behind_two_ref[...] = ahead_two_ref[...].T
    behind_three_ref[...] = ahead_three_ref[...].T
    context = context_ref[pl.ds(task_ref[0], 1), :]
    told = [lane_sum(film_ref[kind] * context) for kind in range(2)]
    told = column_tile(told).T[:8]
    scale = 1.0 + told[0:1] + lanes[4:5]
    shift = told[1:2] + lanes[5:6]
    vectors_ref[...] = row_tile([lanes[0:1], lanes[1:2], lanes[2:3], lanes[3:4], scale, shift])


def assemble(maps, cells, me, piece_refs, index):
    rows = C // len(piece_refs)
    for partner, piece_ref in enumerate(piece_refs):
        maps[own_rows(me, partner, rows), 0:cells] = piece_ref[index]


def disperse(piece_refs, index, me, output, cells):
    rows = C // len(piece_refs)
    for partner, piece_ref in enumerate(piece_refs):
        piece_ref[index] = output[own_rows(me, partner, rows), 0:cells]


def first_conv_kernel(partners, first, final, me_ref, live_ref, told_ref, weights_ref, *refs):
    piece_refs = refs[:partners]
    conv_ref, maps_ref, state_ref, stack, state = refs[-5:]
    step = pl.program_id(0)
    count = conv_ref.shape[0]

    @pl.when(step == 0)
    def _():
        state[...] = refs[partners][...] if first else jnp.zeros_like(state)

    merged = [column(state, k) for k in range(3)]
    for image in range(count):
        maps_ref[image, :, CELLS_TWO // 128 * 128 :] = jnp.zeros((C, LANES_TWO - CELLS_TWO // 128 * 128), BF16)
        assemble(maps_ref.at[image], CELLS_TWO, me_ref[0], piece_refs, image)
        stack_sideways(cut(maps_ref[image], WIDE), MAP, stack.at[image])
        conv = conv_ahead(weights_ref, stack.at[image], MAP)
        write(conv_ref.at[image], conv)
        mean, spread = moments(conv, CELLS_TWO)
        live = live_ref[first + step * count + image]
        merged = merge_moments(merged, live, mean, spread, CELLS_TWO)
    state[...] = column_tile(merged)

    @pl.when(step == pl.num_programs(0) - 1)
    def _():
        if final:
            turned = state[...].T
            spread_rows(row_tile([turned[1:2], turned[2:3], turned[0:1], row(told_ref, 0)], SENT), state_ref)
        else:
            state_ref[...] = state[...]


def middle_kernel(
    partners, me_ref, live_ref, heard_ref, vectors_ref, pool_a_ref, pool_b_ref, weights_ref, conv_ref, *refs
):
    hidden_ref, conv_three_ref, norm_ref, levels_ref, sums_ref, columns, state, stack = refs[-8:]
    piece_refs = refs[-8 - partners : -8]
    step = pl.program_id(0)
    count = conv_ref.shape[0]

    @pl.when(step == 0)
    def _():
        middle, factor, variance, extent = slice_norm(heard_ref)
        norm_ref[...] = row_tile([middle, factor, variance, extent])
        columns[...] = as_columns(row_tile([middle, row(vectors_ref, 0) * factor, row(vectors_ref, 1)]))
        state[...] = jnp.zeros_like(state)

    merged = [column(state, k) for k in range(3)]
    active_squares, hidden_squares = column(state, 3), column(state, 4)
    lives = [live_ref[step * count + image] for image in range(count)]

    def activate(image):
        pre = (conv_ref[image] - column(columns, 0)) * column(columns, 1) + column(columns, 2)
        active = pre * gelu_gate(pre)
        counted = trim(active, 0, CELLS_TWO)
        return halves(active), lives[image] * lane_sum(counted * counted)

    def pool(split):
        (left,) = dot_halves(split[:, :1152], pool_a_ref)
        (right,) = dot_halves(split[:, 896:], pool_b_ref)
        return jnp.concatenate([left, right], axis=1)

    split, squares = activate(0)
    for image in range(count):
        hidden = lives[image] * pool(split)
        active_squares = active_squares + squares
        if image + 1 < count:
            split, squares = activate(image + 1)
        hidden_squares = hidden_squares + lane_sum(hidden * hidden)
        hidden_low = hidden.astype(BF16)
        hidden_ref[image] = hidden_low
        disperse(piece_refs, image, me_ref[0], hidden_ref.at[image], CELLS_THREE)
        stack_sideways(cut(hidden_low, WIDE), HALF, stack.at[image])
        conv = conv_ahead(weights_ref, stack.at[image], HALF)
        write(conv_three_ref.at[image], conv)
        mean, spread = moments(conv, CELLS_THREE)
        merged = merge_moments(merged, lives[image], mean, spread, CELLS_THREE)
    state[...] = column_tile([*merged, active_squares, hidden_squares])

    @pl.when(step == pl.num_programs(0) - 1)
    def _():
        turned = state[...].T
        spread_rows(row_tile([turned[k : k + 1] for k in (1, 2, 0)], SENT), sums_ref)
        levels_ref[...] = row_tile([level_row([column(state, 3), column(state, 4)])])


def top_kernel(
    partners, me_ref, live_ref, heard_ref, own_ref, before_ref, vectors_ref, pool_ref, spread_ref, conv_ref, *refs
):
    target_refs = refs[:partners]
    piece_refs = refs[partners : 2 * partners]
    grad_ref, norm_ref, levels_ref, sums_ref, columns, target, output, totals = refs[2 * partners :]
    step = pl.program_id(0)
    count = conv_ref.shape[0]

    @pl.when(step == 0)
    def _():
        middle, factor, variance, extent = slice_norm(heard_ref)
        norm_ref[...] = row_tile([middle, factor, variance, extent])
        columns[...] = as_columns(row_tile([middle, factor] + [row(vectors_ref, k) for k in (2, 3, 4, 5)]))
        target[...] = jnp.zeros_like(target)
        totals[...] = jnp.zeros_like(totals)

    scale = column(columns, 4)
    slope = scale * column(columns, 2)
    offset = scale * column(columns, 3) + column(columns, 5)
    sums = [jnp.zeros((C, 1), F32)] * 4
    for image in range(count):
        live = live_ref[step * count + image]
        assemble(target.at[image], CELLS_OUT, me_ref[0], target_refs, image)
        normed = (conv_ref[image] - column(columns, 0)) * column(columns, 1)
        filmed = slope * normed + offset
        gate = gelu_gate(filmed)
        active = filmed * gate
        counted = trim(active, 0, CELLS_THREE)
        (pooled,) = dot_halves(halves(active), pool_ref)
        pooled = live * pooled
        output[image] = pooled.astype(BF16)
        disperse(piece_refs, image, me_ref[0], output.at[image], CELLS_OUT)
        spread = jnp.dot(target[image], spread_ref[...], preferred_element_type=F32)
        grad_filmed = live * spread * gelu_slope(filmed, gate)
        grad_ref[image] = scale * grad_filmed
        parts = (
            lane_sum(grad_filmed),
            lane_sum(grad_filmed * normed),
            live * lane_sum(counted * counted),
            lane_sum(pooled * pooled),
        )
        sums = [total + part for total, part in zip(sums, parts)]
    totals[...] += column_tile(sums)

    @pl.when(step == pl.num_programs(0) - 1)
    def _():
        turned = totals[...].T
        shift_sum, scale_sum = turned[0:1], turned[1:2]
        film_scale = row(vectors_ref, 4)
        slope = film_scale * row(vectors_ref, 2) * row(norm_ref, 1)
        offset = film_scale * row(vectors_ref, 3) + row(vectors_ref, 5)
        extent = own_ref[0, 2:3, :]
        away = own_ref[0, 0:1, :] - row(norm_ref, 0)
        filmed_squares = (
            slope * slope * (own_ref[0, 1:2, :] + extent * away * away)
            + 2.0 * slope * offset * extent * away
            + extent * offset * offset
        )
        spread_rows(
            row_tile([shift_sum, scale_sum, film_scale * shift_sum, film_scale * scale_sum], SENT), sums_ref
        )
        nothing = jnp.zeros((C, 1), F32)
        others = level_row([nothing, nothing, nothing, column(totals, 2), column(totals, 3)])
        lanes = lane_ids(C)
        filmed_total = lane_sum(filmed_squares)
        levels_ref[...] = before_ref[...] + row_tile([others + jnp.where(lanes == 2, filmed_total, 0.0)])


def norm_back(live, columns, grad, away, cells):
    scaled = [live * column(columns, k) for k in (1, 2, 3)]
    error = grad.astype(F32) * scaled[0] - scaled[1] - away.astype(F32) * scaled[2]
    return trim(error, 0, cells).astype(BF16)


def norm_back_columns(norm_ref, gain, bias_sum, gain_sum):
    factor, extent = row(norm_ref, 1), row(norm_ref, 3)
    front = gain * factor
    return as_columns(
        row_tile([row(norm_ref, 0), front, front * bias_sum / extent, front * factor * gain_sum / extent])
    )


def back_kernel(
    live_ref,
    heard_ref,
    norm_three_ref,
    norm_two_ref,
    levels_ref,
    vectors_ref,
    weights_ref,
    unpool_a_ref,
    unpool_b_ref,
    grad_ref,
    conv_three_ref,
    conv_two_ref,
    *refs,
):
    out_ref, error_ref, sums_ref, columns_three, columns_two, totals, upright = refs[-7:]
    step = pl.program_id(0)
    count = conv_two_ref.shape[0]

    @pl.when(step == 0)
    def _():
        sums = jnp.sum(heard_ref[...], axis=0)
        columns_three[...] = norm_back_columns(norm_three_ref, row(vectors_ref, 2), sums[2:3], sums[3:4])
        columns_two[...] = as_columns(
            row_tile([row(norm_two_ref, 0), row(vectors_ref, 0) * row(norm_two_ref, 1), row(vectors_ref, 1)])
        )
        totals[...] = jnp.zeros_like(totals)

    grad_tile = product_tile = jnp.zeros((C, C), F32)
    for image in range(count):
        away = conv_three_ref[image] - column(columns_three, 0)
        error = norm_back(live_ref[step * count + image], columns_three, grad_ref[image], away, CELLS_THREE)
        error_ref[image] = error
        stack_upright(cut(error, WIDE), HALF, upright.at[image])
    split = jnp.concatenate(
        [
            halves(jnp.concatenate(conv_behind(weights_ref, upright.at[image], HALF), axis=1))
            for image in range(count)
        ],
        axis=0,
    )
    for image in range(count):
        both = split[2 * C * image : 2 * C * (image + 1)]
        for first, (half, unpool_ref) in enumerate(((both[:, :256], unpool_a_ref), (both[:, 128:], unpool_b_ref))):
            for start, stop in ((0, 384), (384, 640), (640, 896)):
                (spread,) = dot_halves(half, unpool_ref.at[:, start:stop])
                cells = slice(first * 896 + start, first * 896 + stop)
                away = conv_two_ref[image, :, cells] - column(columns_two, 0)
                pre = away * column(columns_two, 1) + column(columns_two, 2)
                grad_pre = spread * gelu_slope(pre, gelu_gate(pre))
                out_ref[image, :, cells] = grad_pre
                grad_tile = grad_tile + sum(cut(grad_pre, 128))
                product_tile = product_tile + sum(cut(grad_pre * away, 128))
    grad_sum = column(totals, 0) + lane_sum(grad_tile)
    product_sum = column(totals, 1) + lane_sum(product_tile)
    totals[...] = column_tile([grad_sum, product_sum])

    @pl.when(step == pl.num_programs(0) - 1)
    def _():
        turned = totals[...].T
        normed_sum = turned[1:2] * row(norm_two_ref, 1)
        spread_rows(row_tile([turned[0:1], normed_sum, levels_ref[0:1, :]], SENT), sums_ref)


def split_filter(product, filter_ref):
    partners, _, rows, _ = filter_ref.shape
    for tap in range(3):
        for owner in range(partners):
            filter_ref[owner, tap] = product[tap * C + owner * rows : tap * C + (owner + 1) * rows]


def filter_three_kernel(error_ref, hidden_ref, *refs):
    filter_ref, product, stack, upright = refs[-4:]
    step = pl.program_id(0)
    count = error_ref.shape[0]

    @pl.when(step == 0)
    def _():
        product[...] = jnp.zeros_like(product)

    for image in range(count):
        stack_upright(cut(error_ref[image], WIDE), HALF, upright.at[image])
        stack_sideways(cut(hidden_ref[image], WIDE), HALF, stack.at[image])
        product[...] += across_cells(upright.at[image], stack.at[image])

    @pl.when(step == pl.num_programs(0) - 1)
    def _():
        split_filter(product, filter_ref)


def last_columns(heard_ref, norm_ref, vectors_ref):
    sums = jnp.sum(heard_ref[...], axis=0)
    return norm_back_columns(norm_ref, row(vectors_ref, 0), sums[0:1], sums[1:2])


def last_conv_kernel(
    partners,
    near,
    first,
    steps,
    me_ref,
    live_ref,
    heard_ref,
    norm_ref,
    vectors_ref,
    weights_ref,
    grad_ref,
    conv_ref,
    *refs,
):
    far = partners - near
    piece_refs, (columns, output, upright) = refs[-3 - near - far * len(steps) : -3], refs[-3:]
    step = pl.program_id(0)
    count = grad_ref.shape[0]

    @pl.when(step == 0)
    def _():
        columns[...] = last_columns(heard_ref, norm_ref, vectors_ref)

    for image in range(count):
        live = live_ref[first + step * count + image]
        away = conv_ref[image] - column(columns, 0)
        error = norm_back(live, columns, grad_ref[image], away, CELLS_TWO)
        stack_upright(cut(error, WIDE), MAP, upright.at[image])
        write(output.at[image], [block.astype(BF16) for block in conv_behind(weights_ref, upright.at[image], MAP)])
    rows = C // partners
    start = 0
    for place, length in enumerate(steps):

        @pl.when((step >= start) & (step < start + length))
        def _():
            for image in range(count):
                for partner in range(partners):
                    piece_ref = piece_refs[partner if partner < near else near + place * far + partner - near]
                    piece_ref[image] = output[image, own_rows(me_ref[0], partner, rows), 0:CELLS_TWO]

        start += length


def last_filter_kernel(live_ref, heard_ref, norm_ref, vectors_ref, grad_ref, conv_ref, maps_ref, *refs):
    filter_ref, product, columns, stack, upright = refs[-5:]
    step = pl.program_id(0)
    count = grad_ref.shape[0]

    @pl.when(step == 0)
    def _():
        columns[...] = last_columns(heard_ref, norm_ref, vectors_ref)
        product[...] = jnp.zeros_like(product)

    for image in range(count):
        away = conv_ref[image] - column(columns, 0)
        error = norm_back(live_ref[step * count + image], columns, grad_ref[image], away, CELLS_TWO)
        stack_upright(cut(error, WIDE), MAP, upright.at[image])
        stack_sideways(cut(maps_ref[image], WIDE), MAP, stack.at[image])
        product[...] += across_cells(upright.at[image], stack.at[image])

    @pl.when(step == pl.num_programs(0) - 1)
    def _():
        split_filter(product, filter_ref)


def strips_kernel(heard_ref, *refs):
    out_ref = refs[-1]
    out_ref[...] = jnp.broadcast_to(jnp.sum(heard_ref[...].astype(F32), axis=0)[None], out_ref.shape)


def one_hot(rows, columns, wanted):
    row_ids = lax.broadcasted_iota(jnp.int32, (rows, columns), 0)
    column_ids = lax.broadcasted_iota(jnp.int32, (rows, columns), 1)
    return jnp.where(wanted(row_ids, column_ids), 1.0, 0.0)


def exact_dot(left, right, contract=((1,), (0,))):
    return lax.dot_general(left, right, (contract, ((), ())), precision=PRECISE, preferred_element_type=F32)


def finish_kernel(
    partners,
    group,
    here_ref,
    me_ref,
    heard_two_ref,
    heard_top_ref,
    heard_back_ref,
    norm_two_ref,
    norm_three_ref,
    vectors_ref,
    film_ref,
    *refs,
):
    film_w_ref, film_b_ref, context_ref, *sum_refs, levels_ref, product = refs[-9:]
    devices = heard_two_ref.shape[0]
    tasks = devices // group
    contexts = context_ref.shape[0]
    rows = C // partners
    entries = film_ref.shape[2]
    turn = (C - me_ref[0] * rows) % C

    def own_lanes(values):
        return pltpu.roll(values, turn, 1)[:, :rows]

    by_task = one_hot(tasks, devices, lambda t, d: d // group == t)
    of_task = one_hot(
        tasks, devices, lambda t, d: (d // partners == t // contexts) & (d % partners == t % contexts)
    )
    mine = one_hot(contexts, devices, lambda t, d: d // group == here_ref[0] * contexts + t)
    shift, normed = heard_top_ref[:, 0, :], heard_top_ref[:, 1, :]
    scale = row(vectors_ref, 2) * normed + row(vectors_ref, 3) * shift
    told = exact_dot(of_task, heard_two_ref[:, 3, :])
    total = jnp.zeros((contexts, entries), F32)
    for kind, grads in enumerate((scale, shift)):
        grads_by_task = exact_dot(by_task, grads)
        product[...] = exact_dot(grads_by_task, told, ((0,), (0,)))
        film_w_ref[kind] = product[pl.ds(pl.multiple_of(me_ref[0] * rows, rows), rows), :entries]
        film_b_ref[kind : kind + 1] = own_lanes(jnp.sum(grads_by_task, axis=0, keepdims=True))
        total = total + exact_dot(exact_dot(mine, grads), film_ref[kind])
    context_ref[...] = total

    back = jnp.sum(heard_back_ref[...], axis=0)
    top = jnp.sum(heard_top_ref[...], axis=0)
    for sum_ref, sums in zip(sum_refs, (back[1:2], back[0:1], top[3:4], top[2:3])):
        sum_ref[...] = own_lanes(sums)[0]

    live = norm_two_ref[3:4, 0:1] * (1.0 / CELLS_TWO)
    lanes = lane_ids(C)

    def mean_square(norm_ref, gain, shift):
        factor, variance = row(norm_ref, 1), row(norm_ref, 2)
        return jnp.sum(gain * gain * variance * factor * factor + shift * shift, axis=1, keepdims=True) * (1.0 / C)

    def mean_conv(norm_ref):
        middle = row(norm_ref, 0)
        return jnp.sum(row(norm_ref, 2) + middle * middle, axis=1, keepdims=True) * (1.0 / C)

    known = (
        mean_conv(norm_two_ref),
        mean_square(norm_two_ref, row(vectors_ref, 0), row(vectors_ref, 1)),
        back[2:3, 0:1] / (live * (C * CELLS_TWO)),
        back[2:3, 1:2] / (live * (C * CELLS_THREE)),
        mean_conv(norm_three_ref),
        mean_square(norm_three_ref, row(vectors_ref, 2), row(vectors_ref, 3)),
        back[2:3, 2:3] / (live * (C * CELLS_THREE)),
        back[2:3, 3:4] / (live * (C * CELLS_THREE)),
        back[2:3, 4:5] / (live * (C * CELLS_OUT)),
    )
    level = jnp.zeros((1, C), F32)
    for place, value in enumerate(known):
        level = jnp.where(lanes == place, value, level)
    levels_ref[...] = jnp.sqrt(level)[0, : levels_ref.shape[0]]


def pool_matrix(side, width, out_width):
    half = side // 2
    matrix = np.zeros((width, out_width), np.float32)
    for row in range(2 * half):
        for column in range(2 * half):
            matrix[row * side + column, (row // 2) * half + column // 2] = 0.25
    return matrix


def lasting(microseconds):
    return pl.CostEstimate(
        flops=int(microseconds * 1.1e9), bytes_accessed=int(microseconds * 3.5e6), transcendentals=0
    )


def smem():
    return pl.BlockSpec(memory_space=pltpu.SMEM)


def anywhere(count):
    return [pl.BlockSpec(memory_space=pl.ANY)] * count


def whole(*shape):
    return pl.BlockSpec(shape, lambda n: (0,) * len(shape))


def each(*shape, first=0, count=1):
    return pl.BlockSpec((count, *shape), lambda n: (first + n,) + (0,) * len(shape))


def pack(maps, me, images_each, wants, earlier=()):
    rows, slots, cells = maps.shape
    group = CAP // images_each
    halves = 2
    block = wants[0][0] // group
    return pl.pallas_call(
        functools.partial(pack_kernel, images_each, group, wants),
        grid_spec=pltpu.PrefetchScalarGridSpec(
            num_scalar_prefetch=1,
            grid=(halves,),
            in_specs=[
                pl.BlockSpec((rows // halves, CAP, cells), lambda n, me_ref: (n, (me_ref[0] // group) ^ block, 0)),
                *anywhere(len(earlier)),
            ],
            out_specs=[
                pl.BlockSpec((count, rows // halves, cells), lambda n, me_ref: (0, n, 0)) for _, _, count in wants
            ],
        ),
        out_shape=[jax.ShapeDtypeStruct((count, rows, cells), maps.dtype) for _, _, count in wants],
        compiler_params=kernel_params(),
        name="pack",
        cost_estimate=lasting(2.5),
    )(me, maps, *earlier)


def unpack(arrays, me, images_each, dtype, place, outs=(), earlier=()):
    partners = len(arrays[0])
    group = CAP // images_each
    halves = 2
    given, specs, counts, shapes, out_specs = [], [], [], [], []
    for pieces in arrays:
        here = pieces[place * group : (place + 1) * group]
        counts.append(tuple(tuple(piece.shape[0] for piece in parts) for parts in here))
        rows, cells = here[0][0].shape[1:]
        for piece in (piece for parts in here for piece in parts):
            given.append(piece)
            specs.append(pl.BlockSpec((piece.shape[0], rows // halves, cells), lambda n, me_ref: (0, n, 0)))
        shapes.append(jax.ShapeDtypeStruct((rows, partners * images_each, cells), dtype))
        out_specs.append(
            pl.BlockSpec((rows // halves, CAP, cells), lambda n, me_ref: (n, (me_ref[0] // group) ^ place, 0))
        )
    aliases = {1 + len(given) + k: k for k in range(len(outs))}
    given += [*outs, *earlier]
    specs += anywhere(len(given) - len(specs))
    return pl.pallas_call(
        functools.partial(unpack_kernel, counts),
        grid_spec=pltpu.PrefetchScalarGridSpec(
            num_scalar_prefetch=1, grid=(halves,), in_specs=specs, out_specs=out_specs
        ),
        out_shape=shapes,
        input_output_aliases=aliases,
        compiler_params=kernel_params(),
        name="unpack",
        cost_estimate=lasting(2.0),
    )(me, *given)


def local(
    images,
    counts,
    context,
    filter_two,
    gain_two,
    shift_two,
    filter_three,
    gain_three,
    shift_three,
    film_weight,
    film_bias,
    cotangent,
    *,
    partners,
    columns,
):
    devices = partners * columns
    rows, slots = images.shape[:2]
    images_each = slots // partners
    group = CAP // images_each
    one = min(images_each, 2)
    pair, some = min(images_each, 2), min(images_each, 4)
    position = lax.axis_index("tensor")
    me = jnp.reshape(position, (1,)).astype(jnp.int32)

    def swap(value, partner):
        if partner == 0:
            return value
        return lax.ppermute(value, "tensor", [(i, i ^ partner) for i in range(partners)])

    def share(copies):
        return lax.all_to_all(copies, ("dp", "tensor"), 0, 0)

    near = 2
    half, quarter = images_each // 2, images_each // 4
    sizes_in = (half, quarter, quarter) if quarter >= pair else (half, half)
    half = images_each // 2
    calls_out = (*[(pair,)] * (half // pair), (half,))
    starts_in = [sum(sizes_in[:part]) for part in range(len(sizes_in))]
    counts_of = [(images_each,) if partner < near else sizes_in for partner in range(partners)]
    far = [partner for partner in reversed(range(partners)) if partner >= near]
    maps = [[None] * len(counts_of[partner]) for partner in range(partners)]

    def send_in(some_parts, whole_near, earlier):
        for block in reversed(range(partners // group)):
            wants = [
                (partner, starts_in[part], sizes_in[part])
                for part in some_parts
                for partner in far
                if partner // group == block
            ]
            if block == 0 and whole_near:
                wants += [(partner, 0, images_each) for partner in range(near)]
            if wants:
                sent = pack(images, me, images_each, wants, earlier)
                for piece, (partner, first, _) in zip(sent, wants):
                    maps[partner][starts_in.index(first)] = swap(piece, partner)
                earlier = (*earlier, sent[0])
        return earlier

    first_sent = send_in((0,), True, ())
    entries = film_weight.shape[0]
    bundle = pl.pallas_call(
        bundle_kernel,
        in_specs=[pl.BlockSpec(memory_space=pltpu.VMEM)] * 8 + anywhere(1),
        out_shape=jax.ShapeDtypeStruct((7 * rows + 16, 3 * C), BF16),
        compiler_params=kernel_params(0),
        name="bundle",
        cost_estimate=lasting(1.0),
    )(
        jnp.transpose(filter_two, (2, 3, 0, 1)),
        jnp.transpose(filter_three, (2, 3, 0, 1)),
        jnp.transpose(film_weight, (1, 2, 0)),
        film_bias,
        *[vector[None] for vector in (gain_two, shift_two, gain_three, shift_three)],
        first_sent[0],
    )
    bundles = {0: bundle}
    bit = partners // 2
    while bit:
        bundles.update({partner | bit: swap(piece, bit) for partner, piece in bundles.items()})
        bit //= 2

    sent_in = {
        part: send_in((part,), False, (maps[far[0]][0],))
        for part in range(1, len(sizes_in))
    }

    task = position // group
    slot = (position % group) * images_each + jnp.arange(images_each, dtype=jnp.int32)
    limit = lax.dynamic_index_in_dim(counts, task, 0, keepdims=False)
    live = (slot < limit).astype(F32)
    ahead_two, behind_two, ahead_three, behind_three, film, vectors = pl.pallas_call(
        functools.partial(unbundle_kernel, partners),
        in_specs=[smem(), smem(), *[pl.BlockSpec(memory_space=pltpu.VMEM)] * (1 + partners)],
        out_shape=[jax.ShapeDtypeStruct((3 * C, 3 * C), BF16)] * 4
        + [jax.ShapeDtypeStruct((2, C, entries), F32), jax.ShapeDtypeStruct((8, C), F32)],
        compiler_params=kernel_params(0),
        name="unbundle",
        cost_estimate=lasting(2.0),
    )(me, jnp.reshape(task, (1,)).astype(jnp.int32), context, *[bundles[partner] for partner in range(partners)])

    told = lax.dynamic_index_in_dim(context, position % context.shape[0], 0)
    told = jnp.pad(told, ((0, 7), (0, C - entries)))

    conv_two = whole_maps = state = None
    for part, (first, count) in enumerate(zip(starts_in, sizes_in)):
        given = [maps[partner][0 if partner < near else part] for partner in range(partners)]
        specs = [
            each(rows, CELLS_TWO, first=first // pair if partner < near else 0, count=pair)
            for partner in range(partners)
        ]
        aliases = {}
        final = part == len(sizes_in) - 1
        if part:
            aliases = {5 + partners: 0, 6 + partners: 1}
            given = given + [state, conv_two, whole_maps]
            specs = specs + [whole(C, C), *anywhere(2)]
        waits = [] if final else [sent_in[part + 1][-1]]
        given = given + waits
        specs = specs + anywhere(len(waits))
        conv_two, whole_maps, state = pl.pallas_call(
            functools.partial(first_conv_kernel, partners, first, final),
            grid=(count // pair,),
            in_specs=[smem(), smem(), whole(8, C), whole(3 * C, 3 * C), *specs],
            out_specs=[
                each(C, LANES_TWO, first=first // pair, count=pair),
                each(C, LANES_TWO, first=first // pair, count=pair),
                whole(devices, SENT, C) if final else whole(C, C),
            ],
            out_shape=[
                jax.ShapeDtypeStruct((images_each, C, LANES_TWO), F32),
                jax.ShapeDtypeStruct((images_each, C, LANES_TWO), BF16),
                jax.ShapeDtypeStruct((devices, SENT, C) if final else (C, C), F32),
            ],
            scratch_shapes=[
                pltpu.VMEM((pair, 3 * C, LANES_TWO), BF16),
                pltpu.VMEM((C, C), F32),
            ],
            input_output_aliases=aliases,
            compiler_params=kernel_params(),
            name="first_conv",
            cost_estimate=lasting(2.3 * count),
        )(me, live, told, ahead_two, *given)
    heard_two = share(state)
    turned = jnp.transpose(cotangent, (1, 0, 2))
    targets = [
        swap(lax.dynamic_slice_in_dim(turned, (position ^ partner) * images_each, images_each, 0), partner)
        for partner in range(partners)
    ]

    pool = pool_matrix(MAP, LANES_TWO, LANES_THREE)
    pool_out = pool_matrix(HALF, LANES_THREE, LANES_OUT)
    *block_pieces, hidden, conv_three, norm_two, levels, sums_three = pl.pallas_call(
        functools.partial(middle_kernel, partners),
        grid=(images_each // pair,),
        in_specs=[
            smem(),
            smem(),
            whole(devices, SENT, C),
            whole(8, C),
            whole(1152, 256),
            whole(896, 256),
            whole(3 * C, 3 * C),
            each(C, LANES_TWO, count=pair),
        ],
        out_specs=[each(rows, CELLS_THREE, count=pair)] * partners
        + [each(C, LANES_THREE, count=pair), each(C, LANES_THREE, count=pair), whole(8, C), whole(8, C), whole(devices, SENT, C)],
        out_shape=[jax.ShapeDtypeStruct((images_each, rows, CELLS_THREE), BF16)] * partners
        + [
            jax.ShapeDtypeStruct((images_each, C, LANES_THREE), BF16),
            jax.ShapeDtypeStruct((images_each, C, LANES_THREE), F32),
            jax.ShapeDtypeStruct((8, C), F32),
            jax.ShapeDtypeStruct((8, C), F32),
            jax.ShapeDtypeStruct((devices, SENT, C), F32),
        ],
        scratch_shapes=[
            pltpu.VMEM((C, C), F32),
            pltpu.VMEM((C, C), F32),
            pltpu.VMEM((pair, 3 * C, LANES_THREE), BF16),
        ],
        compiler_params=kernel_params(),
        name="middle",
            cost_estimate=lasting(2.0 * images_each),
    )(
        me,
        live,
        heard_two,
        vectors,
        jnp.asarray(pool[:1152, :256], BF16),
        jnp.asarray(pool[896:, 256:], BF16),
        ahead_three,
        conv_two,
    )
    heard_three = share(sums_three)

    *out_pieces, grad_three, norm_three, levels, sums_top = pl.pallas_call(
        functools.partial(top_kernel, partners),
        grid=(images_each // some,),
        in_specs=[
            smem(),
            smem(),
            whole(devices, SENT, C),
            whole(1, SENT, C),
            whole(8, C),
            whole(8, C),
            whole(LANES_THREE, LANES_OUT),
            whole(LANES_OUT, LANES_THREE),
            each(C, LANES_THREE, count=some),
            *[each(rows, CELLS_OUT, count=some)] * partners,
        ],
        out_specs=[each(rows, CELLS_OUT, count=some)] * partners
        + [each(C, LANES_THREE, count=some), whole(8, C), whole(8, C), whole(devices, SENT, C)],
        out_shape=[jax.ShapeDtypeStruct((images_each, rows, CELLS_OUT), BF16)] * partners
        + [
            jax.ShapeDtypeStruct((images_each, C, LANES_THREE), F32),
            jax.ShapeDtypeStruct((8, C), F32),
            jax.ShapeDtypeStruct((8, C), F32),
            jax.ShapeDtypeStruct((devices, SENT, C), F32),
        ],
        scratch_shapes=[
            pltpu.VMEM((C, C), F32),
            pltpu.VMEM((some, C, LANES_OUT), BF16),
            pltpu.VMEM((some, C, LANES_OUT), BF16),
            pltpu.VMEM((C, C), F32),
        ],
        compiler_params=kernel_params(),
        name="top",
            cost_estimate=lasting(0.8 * images_each),
    )(
        me,
        live,
        heard_three,
        sums_three,
        levels,
        vectors,
        jnp.asarray(pool_out, BF16),
        jnp.asarray(pool_out.T, BF16),
        conv_three,
        *targets,
    )
    heard_top = share(sums_top)
    block_two = [[swap(block_pieces[k], k)] for k in range(partners)]
    out_pieces = [[swap(out_pieces[k], k)] for k in range(partners)]

    filter_shape = jax.ShapeDtypeStruct((partners, 2, 3, rows, 3 * C), F32)

    def filter_spec(block):
        return pl.BlockSpec((partners, None, 3, rows, 3 * C), lambda n: (0, block, 0, 0, 0))

    grad_two, error_three, sums_two = pl.pallas_call(
        back_kernel,
        grid=(images_each // pair,),
        in_specs=[
            smem(),
            whole(devices, SENT, C),
            whole(8, C),
            whole(8, C),
            whole(8, C),
            whole(8, C),
            whole(3 * C, 3 * C),
            whole(256, 896),
            whole(384, 896),
            each(C, LANES_THREE, count=pair),
            each(C, LANES_THREE, count=pair),
            each(C, LANES_TWO, count=pair),
        ],
        out_specs=[
            each(C, LANES_TWO, count=pair),
            each(C, LANES_THREE, count=pair),
            whole(devices, SENT, C),
        ],
        out_shape=[
            jax.ShapeDtypeStruct((images_each, C, LANES_TWO), F32),
            jax.ShapeDtypeStruct((images_each, C, LANES_THREE), BF16),
            jax.ShapeDtypeStruct((devices, SENT, C), F32),
        ],
        scratch_shapes=[
            pltpu.VMEM((C, C), F32),
            pltpu.VMEM((C, C), F32),
            pltpu.VMEM((C, C), F32),
            pltpu.VMEM((pair, 3 * C, LANES_THREE), BF16),
        ],
        compiler_params=kernel_params(),
        name="back",
            cost_estimate=lasting(2.0 * images_each),
    )(
        live,
        heard_top,
        norm_three,
        norm_two,
        levels,
        vectors,
        behind_three,
        jnp.asarray(pool[:896, :256].T, BF16),
        jnp.asarray(pool[896:, 128:].T, BF16),
        grad_three,
        conv_three,
        conv_two,
    )
    heard_back = share(sums_two)

    filter_sums = pl.pallas_call(
        filter_three_kernel,
        grid=(images_each // some,),
        in_specs=[*[each(C, LANES_THREE, count=some)] * 2, *anywhere(1)],
        out_specs=filter_spec(1),
        out_shape=filter_shape,
        scratch_shapes=[
            pltpu.VMEM((3 * C, 3 * C), F32),
            pltpu.VMEM((some, 3 * C, LANES_THREE), BF16),
            pltpu.VMEM((some, 3 * C, LANES_THREE), BF16),
        ],
        compiler_params=kernel_params(),
        name="filter_three",
        cost_estimate=lasting(5.0),
    )(error_three, hidden, sums_two)

    returned = [[] for partner in range(partners)]
    waits = [filter_sums, *(pieces[0] for pieces in (*block_two, *out_pieces))]
    common = [heard_back, norm_two, vectors]
    common_specs = [whole(devices, SENT, C), whole(8, C), whole(8, C)]
    kept = []
    first = 0
    for sizes in calls_out:
        count = sum(sizes)
        steps = [some // one for some in sizes]
        out_specs = [each(rows, CELLS_TWO, first=first // one, count=one)] * near
        out_shape = [jax.ShapeDtypeStruct((images_each, rows, CELLS_TWO), BF16)] * near
        for place, length in enumerate(steps):
            start = sum(steps[:place])
            out_specs += [
                pl.BlockSpec(
                    (one, rows, CELLS_TWO),
                    lambda n, start=start, length=length: (jnp.clip(n - start, 0, length - 1), 0, 0),
                )
            ] * len(far)
            out_shape += [jax.ShapeDtypeStruct((length * one, rows, CELLS_TWO), BF16)] * len(far)
        inputs = [me, live, *common, behind_two, grad_two, conv_two]
        pieces = pl.pallas_call(
            functools.partial(last_conv_kernel, partners, near, first, steps),
            grid=(count // one,),
            in_specs=[
                smem(),
                smem(),
                *common_specs,
                whole(3 * C, 3 * C),
                *[each(C, LANES_TWO, first=first // one, count=one)] * 2,
                *anywhere(len(waits) + len(kept)),
            ],
            out_specs=out_specs,
            out_shape=out_shape,
            scratch_shapes=[
                pltpu.VMEM((C, C), F32),
                pltpu.VMEM((one, C, LANES_TWO), BF16),
                pltpu.VMEM((one, 3 * C, LANES_TWO), BF16),
            ],
            input_output_aliases={len(inputs) + len(waits) + k: k for k in range(len(kept))},
            compiler_params=kernel_params(),
            name="last_conv",
            cost_estimate=lasting(1.5 * count),
        )(*inputs, *waits, *kept)
        kept, waits, first = pieces[:near], [], first + count
        for place in range(len(sizes)):
            for partner in reversed(far):
                returned[partner].append(swap(pieces[near + place * len(far) + partner - near], partner))
        if first == half:
            product = pl.pallas_call(
                last_filter_kernel,
                grid=(images_each // pair,),
                in_specs=[
                    smem(),
                    *common_specs,
                    *[each(C, LANES_TWO, count=pair)] * 3,
                    *anywhere(2),
                ],
                out_specs=filter_spec(0),
                out_shape=filter_shape,
                scratch_shapes=[
                    pltpu.VMEM((3 * C, 3 * C), F32),
                    pltpu.VMEM((C, C), F32),
                    pltpu.VMEM((pair, 3 * C, LANES_TWO), BF16),
                    pltpu.VMEM((pair, 3 * C, LANES_TWO), BF16),
                ],
                input_output_aliases={7: 0},
                compiler_params=kernel_params(),
                name="last_filter",
                cost_estimate=lasting(1.2 * images_each),
            )(live, *common, grad_two, conv_two, whole_maps, filter_sums, kept[0])
            waits = [product, *(piece for partner in far for piece in returned[partner])]
    for partner in range(near):
        returned[partner].append(swap(kept[partner], partner))

    blocks = ()
    for place in range(partners // group):
        blocks = unpack([block_two, out_pieces], me, images_each, BF16, place, blocks, [kept[0]])
    block_two, block_three = blocks

    contexts = context.shape[0]
    grad_film_w, grad_film_b, grad_context, *norm_sums, levels = pl.pallas_call(
        functools.partial(finish_kernel, partners, group),
        in_specs=[smem(), smem(), *[pl.BlockSpec(memory_space=pltpu.VMEM)] * 7, *anywhere(1)],
        out_shape=[
            jax.ShapeDtypeStruct((2, rows, entries), F32),
            jax.ShapeDtypeStruct((2, rows), F32),
            jax.ShapeDtypeStruct((contexts, entries), F32),
            *[jax.ShapeDtypeStruct((rows,), F32)] * 4,
            jax.ShapeDtypeStruct((9,), F32),
        ],
        scratch_shapes=[pltpu.VMEM((C, C), F32)],
        compiler_params=kernel_params(0),
        name="finish",
        cost_estimate=lasting(2.0),
    )(
        jnp.reshape(lax.axis_index("dp"), (1,)).astype(jnp.int32),
        me,
        heard_two,
        heard_top,
        heard_back,
        norm_two,
        norm_three,
        vectors,
        film,
        kept[0],
    )

    strip = 6 * rows // columns
    heard = lax.all_to_all(product.reshape(devices, strip, 3 * C), ("tensor", "dp"), 0, 0)
    strips = pl.pallas_call(
        strips_kernel,
        in_specs=[pl.BlockSpec(memory_space=pltpu.VMEM), *anywhere(2)],
        out_shape=jax.ShapeDtypeStruct((columns, strip, 3 * C), F32),
        compiler_params=kernel_params(0),
        name="strips",
        cost_estimate=lasting(1.5),
    )(heard, block_two, norm_sums[0])
    strips = lax.all_to_all(strips, "dp", 0, 0)
    grad_filters = jnp.transpose(strips.reshape(2, 3, rows, 3, C), (0, 2, 4, 1, 3))

    grad_images = ()
    for place in range(partners // group):
        waits = () if grad_images else (kept[0],)
        grad_images = unpack([returned], me, images_each, F32, place, grad_images, waits)
    (grad_images,) = grad_images

    return (
        block_two,
        block_three,
        grad_images,
        grad_filters[0],
        norm_sums[0],
        norm_sums[1],
        grad_filters[1],
        norm_sums[2],
        norm_sums[3],
        jnp.transpose(grad_film_w, (2, 0, 1)),
        grad_film_b,
        grad_context,
        levels,
    )


def solution(mesh):
    step = functools.partial(local, partners=mesh.shape["tensor"], columns=mesh.shape["dp"])
    placed = (
        P("tensor", "dp", None),
        P("dp"),
        P("dp", None),
        P("tensor", None, None, None),
        P("tensor"),
        P("tensor"),
        P("tensor", None, None, None),
        P("tensor"),
        P("tensor"),
        P(None, None, "tensor"),
        P(None, "tensor"),
        P("tensor", "dp", None),
    )
    return jax.shard_map(
        step,
        mesh=mesh,
        in_specs=placed,
        out_specs=(
            P("tensor", "dp", None),
            P("tensor", "dp", None),
            P("tensor", "dp", None),
            P("tensor", None, None, None),
            P("tensor"),
            P("tensor"),
            P("tensor", None, None, None),
            P("tensor"),
            P("tensor"),
            P(None, None, "tensor"),
            P(None, "tensor"),
            P("dp", None),
            P(),
        ),
        check_vma=False,
    )
```

```python
import functools

import jax
import jax.numpy as jnp
import numpy as np
from jax import lax
from jax.experimental import pallas as pl
from jax.experimental.pallas import tpu as pltpu
from jax.sharding import PartitionSpec as P

C = 128
MAP = 42
CAP = 16
HALF = 21
QUART = 10
SENT = 4
VMEM_BYTES = 63 << 20
WIDE = 256

CELLS_TWO = MAP * MAP
CELLS_THREE = HALF * HALF
CELLS_OUT = QUART * QUART
LANES_TWO = 1792
LANES_THREE = 512
LANES_OUT = 128
EPSILON = 1e-05
PRECISE = lax.Precision.HIGHEST
F32 = jnp.float32
BF16 = jnp.bfloat16
ROOT = 0.7978845608028654
CUBIC = 0.044715


def lane_ids(width):
    return lax.broadcasted_iota(jnp.int32, (1, width), 1)


def as_columns(rows):
    return jnp.concatenate([rows] * (C // 8), axis=0).T


def column_tile(columns):
    ids = lax.broadcasted_iota(jnp.int32, (C, C), 1)
    tile = jnp.zeros((C, C), F32)
    for place, column in enumerate(columns):
        tile = jnp.where(ids == place, column, tile)
    return tile


def row_tile(rows, count=8):
    ids = lax.broadcasted_iota(jnp.int32, (count, C), 0)
    tile = jnp.zeros((count, C), F32)
    for place, row in enumerate(rows):
        tile = jnp.where(ids == place, row, tile)
    return tile


def row(tile_ref, place):
    return tile_ref[place : place + 1, :]


def column(tile_ref, place):
    return tile_ref[:, place : place + 1]


def merge_moments(state, weight, mean, spread, cells):
    count, middle, total = state
    added = weight * cells
    both = count + added
    away = mean - middle
    share = added / jnp.maximum(both, 1.0)
    return both, middle + away * share, total + weight * spread + away * away * count * share


def slice_norm(heard_ref):
    means, spreads, counts = heard_ref[:, 0, :], heard_ref[:, 1, :], heard_ref[:, 2, :]
    extent = jnp.sum(counts, axis=0, keepdims=True)
    middle = jnp.sum(counts * means, axis=0, keepdims=True) / extent
    away = means - middle
    variance = jnp.sum(spreads + counts * away * away, axis=0, keepdims=True) / extent
    return middle, lax.rsqrt(variance + EPSILON), variance, extent


def level_row(columns):
    return jnp.sum(column_tile(columns), axis=0, keepdims=True)


def spread_rows(tile, out_ref):
    out_ref[...] = jnp.broadcast_to(tile[None], out_ref.shape)


def trim(values, first, last):
    tiles = cut(values, 128)
    ids = lane_ids(128)
    if first > 0:
        tiles[0] = jnp.where(ids >= first, tiles[0], jnp.zeros_like(tiles[0]))
    if last < values.shape[1]:
        tiles[-1] = jnp.where(ids < last - (values.shape[1] - 128), tiles[-1], jnp.zeros_like(tiles[-1]))
    return jnp.concatenate(tiles, axis=1)


def cut(values, wide):
    return [values[:, first : first + wide] for first in range(0, values.shape[1], wide)]


def shift_lanes(blocks, by):
    moved = [pltpu.roll(block, by % block.shape[1], 1) for block in blocks]
    nothing = jnp.zeros_like(moved[0][:, :128])
    ids = lane_ids(128)
    shifted = []
    for place, block in enumerate(moved):
        if by > 0:
            near = moved[place - 1][:, :128] if place else nothing
            edge = jnp.where(ids < by, near, block[:, :128])
            shifted.append(jnp.concatenate([edge, block[:, 128:]], axis=1) if block.shape[1] > 128 else edge)
        else:
            near = moved[place + 1][:, -128:] if place + 1 < len(moved) else nothing
            edge = jnp.where(ids >= 128 + by, near, block[:, -128:])
            shifted.append(jnp.concatenate([block[:, :-128], edge], axis=1) if block.shape[1] > 128 else edge)
    return shifted


def shift_column(blocks, by, side):
    shifted = []
    first = 0
    for block in shift_lanes(blocks, by):
        column = (lane_ids(block.shape[1]) + first) % side
        shifted.append(jnp.where(column == (0 if by > 0 else side - 1), jnp.zeros_like(block), block))
        first += block.shape[1]
    return shifted


def write(out_ref, blocks):
    first = 0
    for block in blocks:
        out_ref[:, first : first + block.shape[1]] = block
        first += block.shape[1]


def fill(stack_ref, tap, blocks):
    first = 0
    for block in blocks:
        stack_ref[tap * C : (tap + 1) * C, first : first + block.shape[1]] = block
        first += block.shape[1]


def stack_sideways(low, side, stack_ref):
    fill(stack_ref, 0, shift_column(low, 1, side))
    fill(stack_ref, 1, low)
    fill(stack_ref, 2, shift_column(low, -1, side))


def stack_upright(low, side, stack_ref):
    fill(stack_ref, 0, shift_lanes(low, -side))
    fill(stack_ref, 1, low)
    fill(stack_ref, 2, shift_lanes(low, side))


def conv_blocks(weights_ref, stack_ref):
    width = stack_ref.shape[1]
    parts = [
        jnp.dot(weights_ref[...], stack_ref[:, first : first + WIDE], preferred_element_type=F32)
        for first in range(0, width, WIDE)
    ]
    return [[part[tap * C : (tap + 1) * C] for part in parts] for tap in range(3)]


def conv_ahead(weights_ref, stack_ref, side):
    above, here, below = conv_blocks(weights_ref, stack_ref)
    total = [a + b + c for a, b, c in zip(shift_lanes(above, side), here, shift_lanes(below, -side))]
    total[-1] = trim(total[-1], 0, side * side - (stack_ref.shape[1] - total[-1].shape[1]))
    return total


def conv_behind(weights_ref, stack_ref, side):
    left, here, right = conv_blocks(weights_ref, stack_ref)
    return [a + b + c for a, b, c in zip(shift_column(left, -1, side), here, shift_column(right, 1, side))]


def across_cells(left_ref, right_ref):
    return lax.dot_general(left_ref[...], right_ref[...], (((1,), (1,)), ((), ())), preferred_element_type=F32)


def lane_sum(values):
    return jnp.sum(values, axis=1, keepdims=True)


def moments(blocks, cells):
    pivot = lane_sum(blocks[0]) * (1.0 / blocks[0].shape[1])
    total, squares = 0.0, 0.0
    for place, block in enumerate(blocks):
        away = block - pivot
        if place == len(blocks) - 1:
            away = trim(away, 0, cells - sum(b.shape[1] for b in blocks[:-1]))
        total = total + sum(cut(away, 128))
        squares = squares + sum(cut(away * away, 128))
    away = lane_sum(total) * (1.0 / cells)
    return pivot + away, lane_sum(squares) - cells * away * away


def gelu_gate(values):
    return 0.5 + 0.5 * jnp.tanh(values * (ROOT + (ROOT * CUBIC) * (values * values)))


def gelu_slope(values, gate):
    return gate * (1.0 + (1.0 - gate) * (values * (2.0 * ROOT + (6.0 * ROOT * CUBIC) * (values * values))))


def halves(values):
    high = values.astype(BF16)
    return jnp.concatenate([high, (values - high.astype(F32)).astype(BF16)], axis=0)


def dot_halves(split, weights_ref):
    both = jnp.dot(split, weights_ref[...], preferred_element_type=F32)
    return [both[first : first + C] + both[first + C : first + 2 * C] for first in range(0, both.shape[0], 2 * C)]


def own_rows(me, partner, count):
    return pl.ds(pl.multiple_of((me ^ partner) * count, count), count)


def kernel_params(axes=1):
    return pltpu.CompilerParams(vmem_limit_bytes=VMEM_BYTES, dimension_semantics=("arbitrary",) * axes)


def pack_kernel(images_each, group, wants, me_ref, maps_ref, *refs):
    piece_refs = refs[-len(wants) :]
    turned = jnp.swapaxes(maps_ref[...], 0, 1)
    for lead in range(group):

        @pl.when(me_ref[0] % group == lead)
        def _():
            for piece_ref, (partner, first, count) in zip(piece_refs, wants):
                start = (lead ^ (partner % group)) * images_each + first
                piece_ref[...] = turned[start : start + count]


def unpack_kernel(counts, me_ref, *refs):
    out_refs = refs[-len(counts) :]
    group = len(counts[0])
    for lead in range(group):

        @pl.when(me_ref[0] % group == lead)
        def _():
            start = 0
            for out_ref, parts in zip(out_refs, counts):
                ordered = []
                for slot in range(group):
                    place = start + sum(len(some) for some in parts[: slot ^ lead])
                    ordered += [refs[place + part][...] for part in range(len(parts[slot ^ lead]))]
                joined = jnp.concatenate(ordered, axis=0) if len(ordered) > 1 else ordered[0]
                out_ref[...] = jnp.swapaxes(joined, 0, 1).astype(out_ref.dtype)
                start += sum(len(some) for some in parts)


def bundle_kernel(filter_two_ref, filter_three_ref, film_ref, bias_ref, *refs):
    vector_refs, out_ref = refs[:4], refs[-1]
    rows = filter_two_ref.shape[2]
    out_ref[...] = jnp.zeros_like(out_ref)
    for place, filter_ref in enumerate((filter_two_ref, filter_three_ref)):
        for down in range(3):
            first = (3 * place + down) * rows
            for across in range(3):
                out_ref[first : first + rows, across * C : (across + 1) * C] = filter_ref[down, across]
    for kind in range(2):
        out_ref[6 * rows : 7 * rows, kind * C : kind * C + film_ref.shape[2]] = film_ref[kind]
    for place, vector_ref in enumerate(vector_refs):
        out_ref[7 * rows + place : 7 * rows + place + 1, 0:rows] = vector_ref[...]
    for kind in range(2):
        out_ref[7 * rows + 4 + kind : 7 * rows + 5 + kind, 0:rows] = bias_ref[kind : kind + 1]


def unbundle_kernel(partners, me_ref, task_ref, context_ref, *refs):
    piece_refs = refs[:partners]
    ahead_two_ref, behind_two_ref, ahead_three_ref, behind_three_ref, film_ref, vectors_ref = refs[partners:]
    rows = C // partners
    entries = film_ref.shape[2]
    lanes = jnp.zeros((8, C), F32)
    ids = lane_ids(C)
    for partner, piece_ref in enumerate(piece_refs):
        owner = me_ref[0] ^ partner
        for place, ahead_ref in enumerate((ahead_two_ref, ahead_three_ref)):
            for down in range(3):
                first = (3 * place + down) * rows
                ahead_ref[pl.ds(pl.multiple_of(down * C + owner * rows, rows), rows), :] = piece_ref[first : first + rows]
        for kind in range(2):
            film_ref[kind, own_rows(me_ref[0], partner, rows), :] = piece_ref[
                6 * rows : 7 * rows, kind * C : kind * C + entries
            ].astype(F32)
        own = jnp.where(ids < rows, piece_ref[7 * rows : 7 * rows + 16, 0:C].astype(F32)[:8], 0.0)
        lanes = lanes + pltpu.roll(own, owner * rows, 1)
    behind_two_ref[...] = ahead_two_ref[...].T
    behind_three_ref[...] = ahead_three_ref[...].T
    context = context_ref[pl.ds(task_ref[0], 1), :]
    told = [lane_sum(film_ref[kind] * context) for kind in range(2)]
    told = column_tile(told).T[:8]
    scale = 1.0 + told[0:1] + lanes[4:5]
    shift = told[1:2] + lanes[5:6]
    vectors_ref[...] = row_tile([lanes[0:1], lanes[1:2], lanes[2:3], lanes[3:4], scale, shift])


def assemble(maps, cells, me, piece_refs, index):
    rows = C // len(piece_refs)
    for partner, piece_ref in enumerate(piece_refs):
        maps[own_rows(me, partner, rows), 0:cells] = piece_ref[index]


def disperse(piece_refs, index, me, output, cells):
    rows = C // len(piece_refs)
    for partner, piece_ref in enumerate(piece_refs):
        piece_ref[index] = output[own_rows(me, partner, rows), 0:cells]


def first_conv_kernel(partners, first, final, me_ref, live_ref, told_ref, weights_ref, *refs):
    piece_refs = refs[:partners]
    conv_ref, maps_ref, state_ref, stack, state = refs[-5:]
    step = pl.program_id(0)
    count = conv_ref.shape[0]

    @pl.when(step == 0)
    def _():
        state[...] = refs[partners][...] if first else jnp.zeros_like(state)

    merged = [column(state, k) for k in range(3)]
    for image in range(count):
        maps_ref[image, :, CELLS_TWO // 128 * 128 :] = jnp.zeros((C, LANES_TWO - CELLS_TWO // 128 * 128), BF16)
        assemble(maps_ref.at[image], CELLS_TWO, me_ref[0], piece_refs, image)
        stack_sideways(cut(maps_ref[image], WIDE), MAP, stack.at[image])
        conv = conv_ahead(weights_ref, stack.at[image], MAP)
        write(conv_ref.at[image], conv)
        mean, spread = moments(conv, CELLS_TWO)
        live = live_ref[first + step * count + image]
        merged = merge_moments(merged, live, mean, spread, CELLS_TWO)
    state[...] = column_tile(merged)

    @pl.when(step == pl.num_programs(0) - 1)
    def _():
        if final:
            turned = state[...].T
            spread_rows(row_tile([turned[1:2], turned[2:3], turned[0:1], row(told_ref, 0)], SENT), state_ref)
        else:
            state_ref[...] = state[...]


def middle_kernel(
    partners, me_ref, live_ref, heard_ref, vectors_ref, pool_a_ref, pool_b_ref, weights_ref, conv_ref, *refs
):
    hidden_ref, conv_three_ref, norm_ref, levels_ref, sums_ref, columns, state, stack = refs[-8:]
    piece_refs = refs[-8 - partners : -8]
    step = pl.program_id(0)
    count = conv_ref.shape[0]

    @pl.when(step == 0)
    def _():
        middle, factor, variance, extent = slice_norm(heard_ref)
        norm_ref[...] = row_tile([middle, factor, variance, extent])
        columns[...] = as_columns(row_tile([middle, row(vectors_ref, 0) * factor, row(vectors_ref, 1)]))
        state[...] = jnp.zeros_like(state)

    merged = [column(state, k) for k in range(3)]
    active_squares, hidden_squares = column(state, 3), column(state, 4)
    lives = [live_ref[step * count + image] for image in range(count)]

    def activate(image):
        pre = (conv_ref[image] - column(columns, 0)) * column(columns, 1) + column(columns, 2)
        active = pre * gelu_gate(pre)
        counted = trim(active, 0, CELLS_TWO)
        return halves(active), lives[image] * lane_sum(counted * counted)

    def pool(split):
        (left,) = dot_halves(split[:, :1152], pool_a_ref)
        (right,) = dot_halves(split[:, 896:], pool_b_ref)
        return jnp.concatenate([left, right], axis=1)

    split, squares = activate(0)
    for image in range(count):
        hidden = lives[image] * pool(split)
        active_squares = active_squares + squares
        if image + 1 < count:
            split, squares = activate(image + 1)
        hidden_squares = hidden_squares + lane_sum(hidden * hidden)
        hidden_low = hidden.astype(BF16)
        hidden_ref[image] = hidden_low
        disperse(piece_refs, image, me_ref[0], hidden_ref.at[image], CELLS_THREE)
        stack_sideways(cut(hidden_low, WIDE), HALF, stack.at[image])
        conv = conv_ahead(weights_ref, stack.at[image], HALF)
        write(conv_three_ref.at[image], conv)
        mean, spread = moments(conv, CELLS_THREE)
        merged = merge_moments(merged, lives[image], mean, spread, CELLS_THREE)
    state[...] = column_tile([*merged, active_squares, hidden_squares])

    @pl.when(step == pl.num_programs(0) - 1)
    def _():
        turned = state[...].T
        spread_rows(row_tile([turned[k : k + 1] for k in (1, 2, 0)], SENT), sums_ref)
        levels_ref[...] = row_tile([level_row([column(state, 3), column(state, 4)])])


def top_kernel(
    partners, me_ref, live_ref, heard_ref, own_ref, before_ref, vectors_ref, pool_ref, spread_ref, conv_ref, *refs
):
    target_refs = refs[:partners]
    piece_refs = refs[partners : 2 * partners]
    grad_ref, norm_ref, levels_ref, sums_ref, columns, target, output, totals = refs[2 * partners :]
    step = pl.program_id(0)
    count = conv_ref.shape[0]

    @pl.when(step == 0)
    def _():
        middle, factor, variance, extent = slice_norm(heard_ref)
        norm_ref[...] = row_tile([middle, factor, variance, extent])
        columns[...] = as_columns(row_tile([middle, factor] + [row(vectors_ref, k) for k in (2, 3, 4, 5)]))
        target[...] = jnp.zeros_like(target)
        totals[...] = jnp.zeros_like(totals)

    scale = column(columns, 4)
    slope = scale * column(columns, 2)
    offset = scale * column(columns, 3) + column(columns, 5)
    sums = [jnp.zeros((C, 1), F32)] * 4
    for image in range(count):
        live = live_ref[step * count + image]
        assemble(target.at[image], CELLS_OUT, me_ref[0], target_refs, image)
        normed = (conv_ref[image] - column(columns, 0)) * column(columns, 1)
        filmed = slope * normed + offset
        gate = gelu_gate(filmed)
        active = filmed * gate
        counted = trim(active, 0, CELLS_THREE)
        (pooled,) = dot_halves(halves(active), pool_ref)
        pooled = live * pooled
        output[image] = pooled.astype(BF16)
        disperse(piece_refs, image, me_ref[0], output.at[image], CELLS_OUT)
        spread = jnp.dot(target[image], spread_ref[...], preferred_element_type=F32)
        grad_filmed = live * spread * gelu_slope(filmed, gate)
        grad_ref[image] = scale * grad_filmed
        parts = (
            lane_sum(grad_filmed),
            lane_sum(grad_filmed * normed),
            live * lane_sum(counted * counted),
            lane_sum(pooled * pooled),
        )
        sums = [total + part for total, part in zip(sums, parts)]
    totals[...] += column_tile(sums)

    @pl.when(step == pl.num_programs(0) - 1)
    def _():
        turned = totals[...].T
        shift_sum, scale_sum = turned[0:1], turned[1:2]
        film_scale = row(vectors_ref, 4)
        slope = film_scale * row(vectors_ref, 2) * row(norm_ref, 1)
        offset = film_scale * row(vectors_ref, 3) + row(vectors_ref, 5)
        extent = own_ref[0, 2:3, :]
        away = own_ref[0, 0:1, :] - row(norm_ref, 0)
        filmed_squares = (
            slope * slope * (own_ref[0, 1:2, :] + extent * away * away)
            + 2.0 * slope * offset * extent * away
            + extent * offset * offset
        )
        spread_rows(
            row_tile([shift_sum, scale_sum, film_scale * shift_sum, film_scale * scale_sum], SENT), sums_ref
        )
        nothing = jnp.zeros((C, 1), F32)
        others = level_row([nothing, nothing, nothing, column(totals, 2), column(totals, 3)])
        lanes = lane_ids(C)
        filmed_total = lane_sum(filmed_squares)
        levels_ref[...] = before_ref[...] + row_tile([others + jnp.where(lanes == 2, filmed_total, 0.0)])


def norm_back(live, columns, grad, away, cells):
    scaled = [live * column(columns, k) for k in (1, 2, 3)]
    error = grad.astype(F32) * scaled[0] - scaled[1] - away.astype(F32) * scaled[2]
    return trim(error, 0, cells).astype(BF16)


def norm_back_columns(norm_ref, gain, bias_sum, gain_sum):
    factor, extent = row(norm_ref, 1), row(norm_ref, 3)
    front = gain * factor
    return as_columns(
        row_tile([row(norm_ref, 0), front, front * bias_sum / extent, front * factor * gain_sum / extent])
    )


def back_kernel(
    live_ref,
    heard_ref,
    norm_three_ref,
    norm_two_ref,
    levels_ref,
    vectors_ref,
    weights_ref,
    unpool_a_ref,
    unpool_b_ref,
    grad_ref,
    conv_three_ref,
    conv_two_ref,
    *refs,
):
    out_ref, error_ref, sums_ref, columns_three, columns_two, totals, upright = refs[-7:]
    step = pl.program_id(0)
    count = conv_two_ref.shape[0]

    @pl.when(step == 0)
    def _():
        sums = jnp.sum(heard_ref[...], axis=0)
        columns_three[...] = norm_back_columns(norm_three_ref, row(vectors_ref, 2), sums[2:3], sums[3:4])
        columns_two[...] = as_columns(
            row_tile([row(norm_two_ref, 0), row(vectors_ref, 0) * row(norm_two_ref, 1), row(vectors_ref, 1)])
        )
        totals[...] = jnp.zeros_like(totals)

    grad_tile = product_tile = jnp.zeros((C, C), F32)
    for image in range(count):
        away = conv_three_ref[image] - column(columns_three, 0)
        error = norm_back(live_ref[step * count + image], columns_three, grad_ref[image], away, CELLS_THREE)
        error_ref[image] = error
        stack_upright(cut(error, WIDE), HALF, upright.at[image])
    split = jnp.concatenate(
        [
            halves(jnp.concatenate(conv_behind(weights_ref, upright.at[image], HALF), axis=1))
            for image in range(count)
        ],
        axis=0,
    )
    for image in range(count):
        both = split[2 * C * image : 2 * C * (image + 1)]
        for first, (half, unpool_ref) in enumerate(((both[:, :256], unpool_a_ref), (both[:, 128:], unpool_b_ref))):
            for start, stop in ((0, 384), (384, 640), (640, 896)):
                (spread,) = dot_halves(half, unpool_ref.at[:, start:stop])
                cells = slice(first * 896 + start, first * 896 + stop)
                away = conv_two_ref[image, :, cells] - column(columns_two, 0)
                pre = away * column(columns_two, 1) + column(columns_two, 2)
                grad_pre = spread * gelu_slope(pre, gelu_gate(pre))
                out_ref[image, :, cells] = grad_pre
                grad_tile = grad_tile + sum(cut(grad_pre, 128))
                product_tile = product_tile + sum(cut(grad_pre * away, 128))
    grad_sum = column(totals, 0) + lane_sum(grad_tile)
    product_sum = column(totals, 1) + lane_sum(product_tile)
    totals[...] = column_tile([grad_sum, product_sum])

    @pl.when(step == pl.num_programs(0) - 1)
    def _():
        turned = totals[...].T
        normed_sum = turned[1:2] * row(norm_two_ref, 1)
        spread_rows(row_tile([turned[0:1], normed_sum, levels_ref[0:1, :]], SENT), sums_ref)


def split_filter(product, filter_ref):
    partners, _, rows, _ = filter_ref.shape
    for tap in range(3):
        for owner in range(partners):
            filter_ref[owner, tap] = product[tap * C + owner * rows : tap * C + (owner + 1) * rows]


def filter_three_kernel(error_ref, hidden_ref, *refs):
    filter_ref, product, stack, upright = refs[-4:]
    step = pl.program_id(0)
    count = error_ref.shape[0]

    @pl.when(step == 0)
    def _():
        product[...] = jnp.zeros_like(product)

    for image in range(count):
        stack_upright(cut(error_ref[image], WIDE), HALF, upright.at[image])
        stack_sideways(cut(hidden_ref[image], WIDE), HALF, stack.at[image])
        product[...] += across_cells(upright.at[image], stack.at[image])

    @pl.when(step == pl.num_programs(0) - 1)
    def _():
        split_filter(product, filter_ref)


def last_columns(heard_ref, norm_ref, vectors_ref):
    sums = jnp.sum(heard_ref[...], axis=0)
    return norm_back_columns(norm_ref, row(vectors_ref, 0), sums[0:1], sums[1:2])


def last_conv_kernel(
    partners,
    near,
    first,
    steps,
    me_ref,
    live_ref,
    heard_ref,
    norm_ref,
    vectors_ref,
    weights_ref,
    grad_ref,
    conv_ref,
    *refs,
):
    far = partners - near
    piece_refs, (columns, output, upright) = refs[-3 - near - far * len(steps) : -3], refs[-3:]
    step = pl.program_id(0)
    count = grad_ref.shape[0]

    @pl.when(step == 0)
    def _():
        columns[...] = last_columns(heard_ref, norm_ref, vectors_ref)

    for image in range(count):
        live = live_ref[first + step * count + image]
        away = conv_ref[image] - column(columns, 0)
        error = norm_back(live, columns, grad_ref[image], away, CELLS_TWO)
        stack_upright(cut(error, WIDE), MAP, upright.at[image])
        write(output.at[image], [block.astype(BF16) for block in conv_behind(weights_ref, upright.at[image], MAP)])
    rows = C // partners
    start = 0
    for place, length in enumerate(steps):

        @pl.when((step >= start) & (step < start + length))
        def _():
            for image in range(count):
                for partner in range(partners):
                    piece_ref = piece_refs[partner if partner < near else near + place * far + partner - near]
                    piece_ref[image] = output[image, own_rows(me_ref[0], partner, rows), 0:CELLS_TWO]

        start += length


def last_filter_kernel(live_ref, heard_ref, norm_ref, vectors_ref, grad_ref, conv_ref, maps_ref, *refs):
    product, columns, stack, upright = refs[-4:]
    step = pl.program_id(0)
    count = grad_ref.shape[0]

    @pl.when(step == 0)
    def _():
        columns[...] = last_columns(heard_ref, norm_ref, vectors_ref)
        product[...] = jnp.zeros_like(product)

    for image in range(count):
        away = conv_ref[image] - column(columns, 0)
        error = norm_back(live_ref[step * count + image], columns, grad_ref[image], away, CELLS_TWO)
        stack_upright(cut(error, WIDE), MAP, upright.at[image])
        stack_sideways(cut(maps_ref[image], WIDE), MAP, stack.at[image])
        product[...] += across_cells(upright.at[image], stack.at[image])


def split_kernel(product_ref, *refs):
    split_filter(product_ref, refs[-1])


def strips_kernel(heard_ref, *refs):
    out_ref = refs[-1]
    out_ref[...] = jnp.broadcast_to(jnp.sum(heard_ref[...].astype(F32), axis=0)[None], out_ref.shape)


def one_hot(rows, columns, wanted):
    row_ids = lax.broadcasted_iota(jnp.int32, (rows, columns), 0)
    column_ids = lax.broadcasted_iota(jnp.int32, (rows, columns), 1)
    return jnp.where(wanted(row_ids, column_ids), 1.0, 0.0)


def exact_dot(left, right, contract=((1,), (0,))):
    return lax.dot_general(left, right, (contract, ((), ())), precision=PRECISE, preferred_element_type=F32)


def finish_kernel(
    partners,
    group,
    here_ref,
    me_ref,
    heard_two_ref,
    heard_top_ref,
    heard_back_ref,
    norm_two_ref,
    norm_three_ref,
    vectors_ref,
    film_ref,
    *refs,
):
    film_w_ref, film_b_ref, context_ref, *sum_refs, levels_ref, product = refs[-9:]
    devices = heard_two_ref.shape[0]
    tasks = devices // group
    contexts = context_ref.shape[0]
    rows = C // partners
    entries = film_ref.shape[2]
    turn = (C - me_ref[0] * rows) % C

    def own_lanes(values):
        return pltpu.roll(values, turn, 1)[:, :rows]

    by_task = one_hot(tasks, devices, lambda t, d: d // group == t)
    of_task = one_hot(
        tasks, devices, lambda t, d: (d // partners == t // contexts) & (d % partners == t % contexts)
    )
    mine = one_hot(contexts, devices, lambda t, d: d // group == here_ref[0] * contexts + t)
    shift, normed = heard_top_ref[:, 0, :], heard_top_ref[:, 1, :]
    scale = row(vectors_ref, 2) * normed + row(vectors_ref, 3) * shift
    told = exact_dot(of_task, heard_two_ref[:, 3, :])
    total = jnp.zeros((contexts, entries), F32)
    for kind, grads in enumerate((scale, shift)):
        grads_by_task = exact_dot(by_task, grads)
        product[...] = exact_dot(grads_by_task, told, ((0,), (0,)))
        film_w_ref[kind] = product[pl.ds(pl.multiple_of(me_ref[0] * rows, rows), rows), :entries]
        film_b_ref[kind : kind + 1] = own_lanes(jnp.sum(grads_by_task, axis=0, keepdims=True))
        total = total + exact_dot(exact_dot(mine, grads), film_ref[kind])
    context_ref[...] = total

    back = jnp.sum(heard_back_ref[...], axis=0)
    top = jnp.sum(heard_top_ref[...], axis=0)
    for sum_ref, sums in zip(sum_refs, (back[1:2], back[0:1], top[3:4], top[2:3])):
        sum_ref[...] = own_lanes(sums)[0]

    live = norm_two_ref[3:4, 0:1] * (1.0 / CELLS_TWO)
    lanes = lane_ids(C)

    def mean_square(norm_ref, gain, shift):
        factor, variance = row(norm_ref, 1), row(norm_ref, 2)
        return jnp.sum(gain * gain * variance * factor * factor + shift * shift, axis=1, keepdims=True) * (1.0 / C)

    def mean_conv(norm_ref):
        middle = row(norm_ref, 0)
        return jnp.sum(row(norm_ref, 2) + middle * middle, axis=1, keepdims=True) * (1.0 / C)

    known = (
        mean_conv(norm_two_ref),
        mean_square(norm_two_ref, row(vectors_ref, 0), row(vectors_ref, 1)),
        back[2:3, 0:1] / (live * (C * CELLS_TWO)),
        back[2:3, 1:2] / (live * (C * CELLS_THREE)),
        mean_conv(norm_three_ref),
        mean_square(norm_three_ref, row(vectors_ref, 2), row(vectors_ref, 3)),
        back[2:3, 2:3] / (live * (C * CELLS_THREE)),
        back[2:3, 3:4] / (live * (C * CELLS_THREE)),
        back[2:3, 4:5] / (live * (C * CELLS_OUT)),
    )
    level = jnp.zeros((1, C), F32)
    for place, value in enumerate(known):
        level = jnp.where(lanes == place, value, level)
    levels_ref[...] = jnp.sqrt(level)[0, : levels_ref.shape[0]]


def pool_matrix(side, width, out_width):
    half = side // 2
    matrix = np.zeros((width, out_width), np.float32)
    for row in range(2 * half):
        for column in range(2 * half):
            matrix[row * side + column, (row // 2) * half + column // 2] = 0.25
    return matrix


def lasting(microseconds):
    return pl.CostEstimate(
        flops=int(microseconds * 1.1e9), bytes_accessed=int(microseconds * 3.5e6), transcendentals=0
    )


def smem():
    return pl.BlockSpec(memory_space=pltpu.SMEM)


def anywhere(count):
    return [pl.BlockSpec(memory_space=pl.ANY)] * count


def whole(*shape):
    return pl.BlockSpec(shape, lambda n: (0,) * len(shape))


def each(*shape, first=0, count=1):
    return pl.BlockSpec((count, *shape), lambda n: (first + n,) + (0,) * len(shape))


def pack(maps, me, images_each, wants, earlier=()):
    rows, slots, cells = maps.shape
    group = CAP // images_each
    halves = 2
    block = wants[0][0] // group
    return pl.pallas_call(
        functools.partial(pack_kernel, images_each, group, wants),
        grid_spec=pltpu.PrefetchScalarGridSpec(
            num_scalar_prefetch=1,
            grid=(halves,),
            in_specs=[
                pl.BlockSpec((rows // halves, CAP, cells), lambda n, me_ref: (n, (me_ref[0] // group) ^ block, 0)),
                *anywhere(len(earlier)),
            ],
            out_specs=[
                pl.BlockSpec((count, rows // halves, cells), lambda n, me_ref: (0, n, 0)) for _, _, count in wants
            ],
        ),
        out_shape=[jax.ShapeDtypeStruct((count, rows, cells), maps.dtype) for _, _, count in wants],
        compiler_params=kernel_params(),
        name="pack",
        cost_estimate=lasting(2.5),
    )(me, maps, *earlier)


def unpack(arrays, me, images_each, dtype, place, outs=(), earlier=()):
    partners = len(arrays[0])
    group = CAP // images_each
    halves = 2
    given, specs, counts, shapes, out_specs = [], [], [], [], []
    for pieces in arrays:
        here = pieces[place * group : (place + 1) * group]
        counts.append(tuple(tuple(piece.shape[0] for piece in parts) for parts in here))
        rows, cells = here[0][0].shape[1:]
        for piece in (piece for parts in here for piece in parts):
            given.append(piece)
            specs.append(pl.BlockSpec((piece.shape[0], rows // halves, cells), lambda n, me_ref: (0, n, 0)))
        shapes.append(jax.ShapeDtypeStruct((rows, partners * images_each, cells), dtype))
        out_specs.append(
            pl.BlockSpec((rows // halves, CAP, cells), lambda n, me_ref: (n, (me_ref[0] // group) ^ place, 0))
        )
    aliases = {1 + len(given) + k: k for k in range(len(outs))}
    given += [*outs, *earlier]
    specs += anywhere(len(given) - len(specs))
    return pl.pallas_call(
        functools.partial(unpack_kernel, counts),
        grid_spec=pltpu.PrefetchScalarGridSpec(
            num_scalar_prefetch=1, grid=(halves,), in_specs=specs, out_specs=out_specs
        ),
        out_shape=shapes,
        input_output_aliases=aliases,
        compiler_params=kernel_params(),
        name="unpack",
        cost_estimate=lasting(2.0),
    )(me, *given)


def local(
    images,
    counts,
    context,
    filter_two,
    gain_two,
    shift_two,
    filter_three,
    gain_three,
    shift_three,
    film_weight,
    film_bias,
    cotangent,
    *,
    partners,
    columns,
):
    devices = partners * columns
    rows, slots = images.shape[:2]
    images_each = slots // partners
    group = CAP // images_each
    one = min(images_each, 2)
    pair, some = min(images_each, 2), min(images_each, 4)
    position = lax.axis_index("tensor")
    me = jnp.reshape(position, (1,)).astype(jnp.int32)

    def swap(value, partner):
        if partner == 0:
            return value
        return lax.ppermute(value, "tensor", [(i, i ^ partner) for i in range(partners)])

    def share(copies):
        return lax.all_to_all(copies, ("dp", "tensor"), 0, 0)

    near = 2
    half, quarter = images_each // 2, images_each // 4
    sizes_in = (half, quarter, quarter) if quarter >= pair else (half, half)
    half = images_each // 2
    calls_out = (*[(pair,)] * (half // pair), (half,))
    starts_in = [sum(sizes_in[:part]) for part in range(len(sizes_in))]
    counts_of = [(images_each,) if partner < near else sizes_in for partner in range(partners)]
    far = [partner for partner in reversed(range(partners)) if partner >= near]
    maps = [[None] * len(counts_of[partner]) for partner in range(partners)]

    def send_in(some_parts, whole_near, earlier):
        for block in reversed(range(partners // group)):
            wants = [
                (partner, starts_in[part], sizes_in[part])
                for part in some_parts
                for partner in far
                if partner // group == block
            ]
            if block == 0 and whole_near:
                wants += [(partner, 0, images_each) for partner in range(near)]
            if wants:
                sent = pack(images, me, images_each, wants, earlier)
                for piece, (partner, first, _) in zip(sent, wants):
                    maps[partner][starts_in.index(first)] = swap(piece, partner)
                earlier = (*earlier, sent[0])
        return earlier

    first_sent = send_in((0,), True, ())
    entries = film_weight.shape[0]
    bundle = pl.pallas_call(
        bundle_kernel,
        in_specs=[pl.BlockSpec(memory_space=pltpu.VMEM)] * 8 + anywhere(1),
        out_shape=jax.ShapeDtypeStruct((7 * rows + 16, 3 * C), BF16),
        compiler_params=kernel_params(0),
        name="bundle",
        cost_estimate=lasting(1.0),
    )(
        jnp.transpose(filter_two, (2, 3, 0, 1)),
        jnp.transpose(filter_three, (2, 3, 0, 1)),
        jnp.transpose(film_weight, (1, 2, 0)),
        film_bias,
        *[vector[None] for vector in (gain_two, shift_two, gain_three, shift_three)],
        first_sent[0],
    )
    bundles = {0: bundle}
    bit = partners // 2
    while bit:
        bundles.update({partner | bit: swap(piece, bit) for partner, piece in bundles.items()})
        bit //= 2

    sent_in = {
        part: send_in((part,), False, (maps[far[0]][0],))
        for part in range(1, len(sizes_in))
    }

    task = position // group
    slot = (position % group) * images_each + jnp.arange(images_each, dtype=jnp.int32)
    limit = lax.dynamic_index_in_dim(counts, task, 0, keepdims=False)
    live = (slot < limit).astype(F32)
    ahead_two, behind_two, ahead_three, behind_three, film, vectors = pl.pallas_call(
        functools.partial(unbundle_kernel, partners),
        in_specs=[smem(), smem(), *[pl.BlockSpec(memory_space=pltpu.VMEM)] * (1 + partners)],
        out_shape=[jax.ShapeDtypeStruct((3 * C, 3 * C), BF16)] * 4
        + [jax.ShapeDtypeStruct((2, C, entries), F32), jax.ShapeDtypeStruct((8, C), F32)],
        compiler_params=kernel_params(0),
        name="unbundle",
        cost_estimate=lasting(2.0),
    )(me, jnp.reshape(task, (1,)).astype(jnp.int32), context, *[bundles[partner] for partner in range(partners)])

    told = lax.dynamic_index_in_dim(context, position % context.shape[0], 0)
    told = jnp.pad(told, ((0, 7), (0, C - entries)))

    conv_two = whole_maps = state = None
    for part, (first, count) in enumerate(zip(starts_in, sizes_in)):
        given = [maps[partner][0 if partner < near else part] for partner in range(partners)]
        specs = [
            each(rows, CELLS_TWO, first=first // pair if partner < near else 0, count=pair)
            for partner in range(partners)
        ]
        aliases = {}
        final = part == len(sizes_in) - 1
        if part:
            aliases = {5 + partners: 0, 6 + partners: 1}
            given = given + [state, conv_two, whole_maps]
            specs = specs + [whole(C, C), *anywhere(2)]
        waits = [] if final else [sent_in[part + 1][-1]]
        given = given + waits
        specs = specs + anywhere(len(waits))
        conv_two, whole_maps, state = pl.pallas_call(
            functools.partial(first_conv_kernel, partners, first, final),
            grid=(count // pair,),
            in_specs=[smem(), smem(), whole(8, C), whole(3 * C, 3 * C), *specs],
            out_specs=[
                each(C, LANES_TWO, first=first // pair, count=pair),
                each(C, LANES_TWO, first=first // pair, count=pair),
                whole(devices, SENT, C) if final else whole(C, C),
            ],
            out_shape=[
                jax.ShapeDtypeStruct((images_each, C, LANES_TWO), F32),
                jax.ShapeDtypeStruct((images_each, C, LANES_TWO), BF16),
                jax.ShapeDtypeStruct((devices, SENT, C) if final else (C, C), F32),
            ],
            scratch_shapes=[
                pltpu.VMEM((pair, 3 * C, LANES_TWO), BF16),
                pltpu.VMEM((C, C), F32),
            ],
            input_output_aliases=aliases,
            compiler_params=kernel_params(),
            name="first_conv",
            cost_estimate=lasting(2.3 * count),
        )(me, live, told, ahead_two, *given)
    heard_two = share(state)
    turned = jnp.transpose(cotangent, (1, 0, 2))
    targets = [
        swap(lax.dynamic_slice_in_dim(turned, (position ^ partner) * images_each, images_each, 0), partner)
        for partner in range(partners)
    ]

    pool = pool_matrix(MAP, LANES_TWO, LANES_THREE)
    pool_out = pool_matrix(HALF, LANES_THREE, LANES_OUT)
    *block_pieces, hidden, conv_three, norm_two, levels, sums_three = pl.pallas_call(
        functools.partial(middle_kernel, partners),
        grid=(images_each // pair,),
        in_specs=[
            smem(),
            smem(),
            whole(devices, SENT, C),
            whole(8, C),
            whole(1152, 256),
            whole(896, 256),
            whole(3 * C, 3 * C),
            each(C, LANES_TWO, count=pair),
        ],
        out_specs=[each(rows, CELLS_THREE, count=pair)] * partners
        + [each(C, LANES_THREE, count=pair), each(C, LANES_THREE, count=pair), whole(8, C), whole(8, C), whole(devices, SENT, C)],
        out_shape=[jax.ShapeDtypeStruct((images_each, rows, CELLS_THREE), BF16)] * partners
        + [
            jax.ShapeDtypeStruct((images_each, C, LANES_THREE), BF16),
            jax.ShapeDtypeStruct((images_each, C, LANES_THREE), F32),
            jax.ShapeDtypeStruct((8, C), F32),
            jax.ShapeDtypeStruct((8, C), F32),
            jax.ShapeDtypeStruct((devices, SENT, C), F32),
        ],
        scratch_shapes=[
            pltpu.VMEM((C, C), F32),
            pltpu.VMEM((C, C), F32),
            pltpu.VMEM((pair, 3 * C, LANES_THREE), BF16),
        ],
        compiler_params=kernel_params(),
        name="middle",
            cost_estimate=lasting(2.0 * images_each),
    )(
        me,
        live,
        heard_two,
        vectors,
        jnp.asarray(pool[:1152, :256], BF16),
        jnp.asarray(pool[896:, 256:], BF16),
        ahead_three,
        conv_two,
    )
    heard_three = share(sums_three)

    *out_pieces, grad_three, norm_three, levels, sums_top = pl.pallas_call(
        functools.partial(top_kernel, partners),
        grid=(images_each // some,),
        in_specs=[
            smem(),
            smem(),
            whole(devices, SENT, C),
            whole(1, SENT, C),
            whole(8, C),
            whole(8, C),
            whole(LANES_THREE, LANES_OUT),
            whole(LANES_OUT, LANES_THREE),
            each(C, LANES_THREE, count=some),
            *[each(rows, CELLS_OUT, count=some)] * partners,
        ],
        out_specs=[each(rows, CELLS_OUT, count=some)] * partners
        + [each(C, LANES_THREE, count=some), whole(8, C), whole(8, C), whole(devices, SENT, C)],
        out_shape=[jax.ShapeDtypeStruct((images_each, rows, CELLS_OUT), BF16)] * partners
        + [
            jax.ShapeDtypeStruct((images_each, C, LANES_THREE), F32),
            jax.ShapeDtypeStruct((8, C), F32),
            jax.ShapeDtypeStruct((8, C), F32),
            jax.ShapeDtypeStruct((devices, SENT, C), F32),
        ],
        scratch_shapes=[
            pltpu.VMEM((C, C), F32),
            pltpu.VMEM((some, C, LANES_OUT), BF16),
            pltpu.VMEM((some, C, LANES_OUT), BF16),
            pltpu.VMEM((C, C), F32),
        ],
        compiler_params=kernel_params(),
        name="top",
            cost_estimate=lasting(0.8 * images_each),
    )(
        me,
        live,
        heard_three,
        sums_three,
        levels,
        vectors,
        jnp.asarray(pool_out, BF16),
        jnp.asarray(pool_out.T, BF16),
        conv_three,
        *targets,
    )
    heard_top = share(sums_top)
    block_two = [[swap(block_pieces[k], k)] for k in range(partners)]
    out_pieces = [[swap(out_pieces[k], k)] for k in range(partners)]

    filter_shape = jax.ShapeDtypeStruct((partners, 2, 3, rows, 3 * C), F32)

    def filter_spec(block):
        return pl.BlockSpec((partners, None, 3, rows, 3 * C), lambda n: (0, block, 0, 0, 0))

    grad_two, error_three, sums_two = pl.pallas_call(
        back_kernel,
        grid=(images_each // pair,),
        in_specs=[
            smem(),
            whole(devices, SENT, C),
            whole(8, C),
            whole(8, C),
            whole(8, C),
            whole(8, C),
            whole(3 * C, 3 * C),
            whole(256, 896),
            whole(384, 896),
            each(C, LANES_THREE, count=pair),
            each(C, LANES_THREE, count=pair),
            each(C, LANES_TWO, count=pair),
        ],
        out_specs=[
            each(C, LANES_TWO, count=pair),
            each(C, LANES_THREE, count=pair),
            whole(devices, SENT, C),
        ],
        out_shape=[
            jax.ShapeDtypeStruct((images_each, C, LANES_TWO), F32),
            jax.ShapeDtypeStruct((images_each, C, LANES_THREE), BF16),
            jax.ShapeDtypeStruct((devices, SENT, C), F32),
        ],
        scratch_shapes=[
            pltpu.VMEM((C, C), F32),
            pltpu.VMEM((C, C), F32),
            pltpu.VMEM((C, C), F32),
            pltpu.VMEM((pair, 3 * C, LANES_THREE), BF16),
        ],
        compiler_params=kernel_params(),
        name="back",
            cost_estimate=lasting(2.0 * images_each),
    )(
        live,
        heard_top,
        norm_three,
        norm_two,
        levels,
        vectors,
        behind_three,
        jnp.asarray(pool[:896, :256].T, BF16),
        jnp.asarray(pool[896:, 128:].T, BF16),
        grad_three,
        conv_three,
        conv_two,
    )
    heard_back = share(sums_two)

    filter_sums = pl.pallas_call(
        filter_three_kernel,
        grid=(images_each // some,),
        in_specs=[*[each(C, LANES_THREE, count=some)] * 2, *anywhere(1)],
        out_specs=filter_spec(1),
        out_shape=filter_shape,
        scratch_shapes=[
            pltpu.VMEM((3 * C, 3 * C), F32),
            pltpu.VMEM((some, 3 * C, LANES_THREE), BF16),
            pltpu.VMEM((some, 3 * C, LANES_THREE), BF16),
        ],
        compiler_params=kernel_params(),
        name="filter_three",
        cost_estimate=lasting(5.0),
    )(error_three, hidden, sums_two)

    returned = [[] for partner in range(partners)]
    waits = [filter_sums, *(pieces[0] for pieces in (*block_two, *out_pieces))]
    common = [heard_back, norm_two, vectors]
    common_specs = [whole(devices, SENT, C), whole(8, C), whole(8, C)]
    kept = []
    first = 0
    for sizes in calls_out:
        count = sum(sizes)
        steps = [some // one for some in sizes]
        out_specs = [each(rows, CELLS_TWO, first=first // one, count=one)] * near
        out_shape = [jax.ShapeDtypeStruct((images_each, rows, CELLS_TWO), BF16)] * near
        for place, length in enumerate(steps):
            start = sum(steps[:place])
            out_specs += [
                pl.BlockSpec(
                    (one, rows, CELLS_TWO),
                    lambda n, start=start, length=length: (jnp.clip(n - start, 0, length - 1), 0, 0),
                )
            ] * len(far)
            out_shape += [jax.ShapeDtypeStruct((length * one, rows, CELLS_TWO), BF16)] * len(far)
        inputs = [me, live, *common, behind_two, grad_two, conv_two]
        pieces = pl.pallas_call(
            functools.partial(last_conv_kernel, partners, near, first, steps),
            grid=(count // one,),
            in_specs=[
                smem(),
                smem(),
                *common_specs,
                whole(3 * C, 3 * C),
                *[each(C, LANES_TWO, first=first // one, count=one)] * 2,
                *anywhere(len(waits) + len(kept)),
            ],
            out_specs=out_specs,
            out_shape=out_shape,
            scratch_shapes=[
                pltpu.VMEM((C, C), F32),
                pltpu.VMEM((one, C, LANES_TWO), BF16),
                pltpu.VMEM((one, 3 * C, LANES_TWO), BF16),
            ],
            input_output_aliases={len(inputs) + len(waits) + k: k for k in range(len(kept))},
            compiler_params=kernel_params(),
            name="last_conv",
            cost_estimate=lasting(1.5 * count),
        )(*inputs, *waits, *kept)
        kept, waits, first = pieces[:near], [], first + count
        for place in range(len(sizes)):
            for partner in reversed(far):
                returned[partner].append(swap(pieces[near + place * len(far) + partner - near], partner))
        if first == half:
            product = pl.pallas_call(
                last_filter_kernel,
                grid=(images_each // pair,),
                in_specs=[
                    smem(),
                    *common_specs,
                    *[each(C, LANES_TWO, count=pair)] * 3,
                    *anywhere(1),
                ],
                out_specs=whole(3 * C, 3 * C),
                out_shape=jax.ShapeDtypeStruct((3 * C, 3 * C), F32),
                scratch_shapes=[
                    pltpu.VMEM((C, C), F32),
                    pltpu.VMEM((pair, 3 * C, LANES_TWO), BF16),
                    pltpu.VMEM((pair, 3 * C, LANES_TWO), BF16),
                ],
                compiler_params=kernel_params(),
                name="last_filter",
                cost_estimate=lasting(1.2 * images_each),
            )(live, *common, grad_two, conv_two, whole_maps, kept[0])
            waits = [piece for partner in far for piece in returned[partner]]
            product = pl.pallas_call(
                split_kernel,
                grid=(1,),
                in_specs=[whole(3 * C, 3 * C), *anywhere(1 + len(waits))],
                out_specs=filter_spec(0),
                out_shape=filter_shape,
                input_output_aliases={1: 0},
                compiler_params=kernel_params(),
                name="split",
                cost_estimate=lasting(1.5),
            )(product, filter_sums, *waits)
            waits = [product, *waits]
    for partner in range(near):
        returned[partner].append(swap(kept[partner], partner))

    blocks = ()
    for place in range(partners // group):
        blocks = unpack([block_two, out_pieces], me, images_each, BF16, place, blocks, [kept[0]])
    block_two, block_three = blocks

    contexts = context.shape[0]
    grad_film_w, grad_film_b, grad_context, *norm_sums, levels = pl.pallas_call(
        functools.partial(finish_kernel, partners, group),
        in_specs=[smem(), smem(), *[pl.BlockSpec(memory_space=pltpu.VMEM)] * 7, *anywhere(1)],
        out_shape=[
            jax.ShapeDtypeStruct((2, rows, entries), F32),
            jax.ShapeDtypeStruct((2, rows), F32),
            jax.ShapeDtypeStruct((contexts, entries), F32),
            *[jax.ShapeDtypeStruct((rows,), F32)] * 4,
            jax.ShapeDtypeStruct((9,), F32),
        ],
        scratch_shapes=[pltpu.VMEM((C, C), F32)],
        compiler_params=kernel_params(0),
        name="finish",
        cost_estimate=lasting(2.0),
    )(
        jnp.reshape(lax.axis_index("dp"), (1,)).astype(jnp.int32),
        me,
        heard_two,
        heard_top,
        heard_back,
        norm_two,
        norm_three,
        vectors,
        film,
        kept[0],
    )

    strip = 6 * rows // columns
    heard = lax.all_to_all(product.reshape(devices, strip, 3 * C), ("tensor", "dp"), 0, 0)
    strips = pl.pallas_call(
        strips_kernel,
        in_specs=[pl.BlockSpec(memory_space=pltpu.VMEM), *anywhere(2)],
        out_shape=jax.ShapeDtypeStruct((columns, strip, 3 * C), F32),
        compiler_params=kernel_params(0),
        name="strips",
        cost_estimate=lasting(1.5),
    )(heard, block_two, norm_sums[0])
    strips = lax.all_to_all(strips, "dp", 0, 0)
    grad_filters = jnp.transpose(strips.reshape(2, 3, rows, 3, C), (0, 2, 4, 1, 3))

    grad_images = ()
    for place in range(partners // group):
        waits = () if grad_images else (kept[0],)
        grad_images = unpack([returned], me, images_each, F32, place, grad_images, waits)
    (grad_images,) = grad_images

    return (
        block_two,
        block_three,
        grad_images,
        grad_filters[0],
        norm_sums[0],
        norm_sums[1],
        grad_filters[1],
        norm_sums[2],
        norm_sums[3],
        jnp.transpose(grad_film_w, (2, 0, 1)),
        grad_film_b,
        grad_context,
        levels,
    )


def solution(mesh):
    step = functools.partial(local, partners=mesh.shape["tensor"], columns=mesh.shape["dp"])
    placed = (
        P("tensor", "dp", None),
        P("dp"),
        P("dp", None),
        P("tensor", None, None, None),
        P("tensor"),
        P("tensor"),
        P("tensor", None, None, None),
        P("tensor"),
        P("tensor"),
        P(None, None, "tensor"),
        P(None, "tensor"),
        P("tensor", "dp", None),
    )
    return jax.shard_map(
        step,
        mesh=mesh,
        in_specs=placed,
        out_specs=(
            P("tensor", "dp", None),
            P("tensor", "dp", None),
            P("tensor", "dp", None),
            P("tensor", None, None, None),
            P("tensor"),
            P("tensor"),
            P("tensor", None, None, None),
            P("tensor"),
            P("tensor"),
            P(None, None, "tensor"),
            P(None, "tensor"),
            P("dp", None),
            P(),
        ),
        check_vma=False,
    )
```

```python
import functools

import jax
import jax.numpy as jnp
import numpy as np
from jax import lax
from jax.experimental import pallas as pl
from jax.experimental.pallas import tpu as pltpu
from jax.sharding import PartitionSpec as P

C = 128
MAP = 42
CAP = 16
HALF = 21
QUART = 10
SENT = 4
VMEM_BYTES = 63 << 20
WIDE = 256

CELLS_TWO = MAP * MAP
CELLS_THREE = HALF * HALF
CELLS_OUT = QUART * QUART
LANES_TWO = 1792
LANES_THREE = 512
LANES_OUT = 128
EPSILON = 1e-05
PRECISE = lax.Precision.HIGHEST
F32 = jnp.float32
BF16 = jnp.bfloat16
ROOT = 0.7978845608028654
CUBIC = 0.044715


def lane_ids(width):
    return lax.broadcasted_iota(jnp.int32, (1, width), 1)


def as_columns(rows):
    return jnp.concatenate([rows] * (C // 8), axis=0).T


def column_tile(columns):
    ids = lax.broadcasted_iota(jnp.int32, (C, C), 1)
    tile = jnp.zeros((C, C), F32)
    for place, column in enumerate(columns):
        tile = jnp.where(ids == place, column, tile)
    return tile


def row_tile(rows, count=8):
    ids = lax.broadcasted_iota(jnp.int32, (count, C), 0)
    tile = jnp.zeros((count, C), F32)
    for place, row in enumerate(rows):
        tile = jnp.where(ids == place, row, tile)
    return tile


def row(tile_ref, place):
    return tile_ref[place : place + 1, :]


def column(tile_ref, place):
    return tile_ref[:, place : place + 1]


def merge_moments(state, weight, mean, spread, cells):
    count, middle, total = state
    added = weight * cells
    both = count + added
    away = mean - middle
    share = added / jnp.maximum(both, 1.0)
    return both, middle + away * share, total + weight * spread + away * away * count * share


def slice_norm(heard_ref):
    means, spreads, counts = heard_ref[:, 0, :], heard_ref[:, 1, :], heard_ref[:, 2, :]
    extent = jnp.sum(counts, axis=0, keepdims=True)
    middle = jnp.sum(counts * means, axis=0, keepdims=True) / extent
    away = means - middle
    variance = jnp.sum(spreads + counts * away * away, axis=0, keepdims=True) / extent
    return middle, lax.rsqrt(variance + EPSILON), variance, extent


def level_row(columns):
    return jnp.sum(column_tile(columns), axis=0, keepdims=True)


def spread_rows(tile, out_ref):
    out_ref[...] = jnp.broadcast_to(tile[None], out_ref.shape)


def trim(values, first, last):
    tiles = cut(values, 128)
    ids = lane_ids(128)
    if first > 0:
        tiles[0] = jnp.where(ids >= first, tiles[0], jnp.zeros_like(tiles[0]))
    if last < values.shape[1]:
        tiles[-1] = jnp.where(ids < last - (values.shape[1] - 128), tiles[-1], jnp.zeros_like(tiles[-1]))
    return jnp.concatenate(tiles, axis=1)


def cut(values, wide):
    return [values[:, first : first + wide] for first in range(0, values.shape[1], wide)]


def shift_lanes(blocks, by):
    moved = [pltpu.roll(block, by % block.shape[1], 1) for block in blocks]
    nothing = jnp.zeros_like(moved[0][:, :128])
    ids = lane_ids(128)
    shifted = []
    for place, block in enumerate(moved):
        if by > 0:
            near = moved[place - 1][:, :128] if place else nothing
            edge = jnp.where(ids < by, near, block[:, :128])
            shifted.append(jnp.concatenate([edge, block[:, 128:]], axis=1) if block.shape[1] > 128 else edge)
        else:
            near = moved[place + 1][:, -128:] if place + 1 < len(moved) else nothing
            edge = jnp.where(ids >= 128 + by, near, block[:, -128:])
            shifted.append(jnp.concatenate([block[:, :-128], edge], axis=1) if block.shape[1] > 128 else edge)
    return shifted


def shift_column(blocks, by, side):
    shifted = []
    first = 0
    for block in shift_lanes(blocks, by):
        column = (lane_ids(block.shape[1]) + first) % side
        shifted.append(jnp.where(column == (0 if by > 0 else side - 1), jnp.zeros_like(block), block))
        first += block.shape[1]
    return shifted


def write(out_ref, blocks):
    first = 0
    for block in blocks:
        out_ref[:, first : first + block.shape[1]] = block
        first += block.shape[1]


def fill(stack_ref, tap, blocks):
    first = 0
    for block in blocks:
        stack_ref[tap * C : (tap + 1) * C, first : first + block.shape[1]] = block
        first += block.shape[1]


def stack_sideways(low, side, stack_ref):
    fill(stack_ref, 0, shift_column(low, 1, side))
    fill(stack_ref, 1, low)
    fill(stack_ref, 2, shift_column(low, -1, side))


def stack_upright(low, side, stack_ref):
    fill(stack_ref, 0, shift_lanes(low, -side))
    fill(stack_ref, 1, low)
    fill(stack_ref, 2, shift_lanes(low, side))


def conv_blocks(weights_ref, stack_ref):
    width = stack_ref.shape[1]
    parts = [
        jnp.dot(weights_ref[...], stack_ref[:, first : first + WIDE], preferred_element_type=F32)
        for first in range(0, width, WIDE)
    ]
    return [[part[tap * C : (tap + 1) * C] for part in parts] for tap in range(3)]


def conv_ahead(weights_ref, stack_ref, side):
    above, here, below = conv_blocks(weights_ref, stack_ref)
    total = [a + b + c for a, b, c in zip(shift_lanes(above, side), here, shift_lanes(below, -side))]
    total[-1] = trim(total[-1], 0, side * side - (stack_ref.shape[1] - total[-1].shape[1]))
    return total


def conv_behind(weights_ref, stack_ref, side):
    left, here, right = conv_blocks(weights_ref, stack_ref)
    return [a + b + c for a, b, c in zip(shift_column(left, -1, side), here, shift_column(right, 1, side))]


def across_cells(left_ref, right_ref):
    return lax.dot_general(left_ref[...], right_ref[...], (((1,), (1,)), ((), ())), preferred_element_type=F32)


def lane_sum(values):
    return jnp.sum(values, axis=1, keepdims=True)


def moments(blocks, cells):
    pivot = lane_sum(blocks[0]) * (1.0 / blocks[0].shape[1])
    total, squares = 0.0, 0.0
    for place, block in enumerate(blocks):
        away = block - pivot
        if place == len(blocks) - 1:
            away = trim(away, 0, cells - sum(b.shape[1] for b in blocks[:-1]))
        total = total + sum(cut(away, 128))
        squares = squares + sum(cut(away * away, 128))
    away = lane_sum(total) * (1.0 / cells)
    return pivot + away, lane_sum(squares) - cells * away * away


def gelu_gate(values):
    return 0.5 + 0.5 * jnp.tanh(values * (ROOT + (ROOT * CUBIC) * (values * values)))


def gelu_slope(values, gate):
    return gate * (1.0 + (1.0 - gate) * (values * (2.0 * ROOT + (6.0 * ROOT * CUBIC) * (values * values))))


def halves(values):
    high = values.astype(BF16)
    return jnp.concatenate([high, (values - high.astype(F32)).astype(BF16)], axis=0)


def dot_halves(split, weights_ref):
    both = jnp.dot(split, weights_ref[...], preferred_element_type=F32)
    return [both[first : first + C] + both[first + C : first + 2 * C] for first in range(0, both.shape[0], 2 * C)]


def own_rows(me, partner, count):
    return pl.ds(pl.multiple_of((me ^ partner) * count, count), count)


def kernel_params(axes=1):
    return pltpu.CompilerParams(vmem_limit_bytes=VMEM_BYTES, dimension_semantics=("arbitrary",) * axes)


def pack_kernel(images_each, group, wants, me_ref, maps_ref, *refs):
    piece_refs = refs[-len(wants) :]
    turned = jnp.swapaxes(maps_ref[...], 0, 1)
    for lead in range(group):

        @pl.when(me_ref[0] % group == lead)
        def _():
            for piece_ref, (partner, first, count) in zip(piece_refs, wants):
                start = (lead ^ (partner % group)) * images_each + first
                piece_ref[...] = turned[start : start + count]


def unpack_kernel(counts, me_ref, *refs):
    out_refs = refs[-len(counts) :]
    group = len(counts[0])
    for lead in range(group):

        @pl.when(me_ref[0] % group == lead)
        def _():
            start = 0
            for out_ref, parts in zip(out_refs, counts):
                ordered = []
                for slot in range(group):
                    place = start + sum(len(some) for some in parts[: slot ^ lead])
                    ordered += [refs[place + part][...] for part in range(len(parts[slot ^ lead]))]
                joined = jnp.concatenate(ordered, axis=0) if len(ordered) > 1 else ordered[0]
                out_ref[...] = jnp.swapaxes(joined, 0, 1).astype(out_ref.dtype)
                start += sum(len(some) for some in parts)


def bundle_kernel(filter_two_ref, filter_three_ref, film_ref, bias_ref, *refs):
    vector_refs, out_ref = refs[:4], refs[-1]
    rows = filter_two_ref.shape[2]
    out_ref[...] = jnp.zeros_like(out_ref)
    for place, filter_ref in enumerate((filter_two_ref, filter_three_ref)):
        for down in range(3):
            first = (3 * place + down) * rows
            for across in range(3):
                out_ref[first : first + rows, across * C : (across + 1) * C] = filter_ref[down, across]
    for kind in range(2):
        out_ref[6 * rows : 7 * rows, kind * C : kind * C + film_ref.shape[2]] = film_ref[kind]
    for place, vector_ref in enumerate(vector_refs):
        out_ref[7 * rows + place : 7 * rows + place + 1, 0:rows] = vector_ref[...]
    for kind in range(2):
        out_ref[7 * rows + 4 + kind : 7 * rows + 5 + kind, 0:rows] = bias_ref[kind : kind + 1]


def unbundle_kernel(partners, me_ref, task_ref, context_ref, *refs):
    piece_refs = refs[:partners]
    ahead_two_ref, behind_two_ref, ahead_three_ref, behind_three_ref, film_ref, vectors_ref = refs[partners:]
    rows = C // partners
    entries = film_ref.shape[2]
    lanes = jnp.zeros((8, C), F32)
    ids = lane_ids(C)
    for partner, piece_ref in enumerate(piece_refs):
        owner = me_ref[0] ^ partner
        for place, ahead_ref in enumerate((ahead_two_ref, ahead_three_ref)):
            for down in range(3):
                first = (3 * place + down) * rows
                ahead_ref[pl.ds(pl.multiple_of(down * C + owner * rows, rows), rows), :] = piece_ref[first : first + rows]
        for kind in range(2):
            film_ref[kind, own_rows(me_ref[0], partner, rows), :] = piece_ref[
                6 * rows : 7 * rows, kind * C : kind * C + entries
            ].astype(F32)
        own = jnp.where(ids < rows, piece_ref[7 * rows : 7 * rows + 16, 0:C].astype(F32)[:8], 0.0)
        lanes = lanes + pltpu.roll(own, owner * rows, 1)
    behind_two_ref[...] = ahead_two_ref[...].T
    behind_three_ref[...] = ahead_three_ref[...].T
    context = context_ref[pl.ds(task_ref[0], 1), :]
    told = [lane_sum(film_ref[kind] * context) for kind in range(2)]
    told = column_tile(told).T[:8]
    scale = 1.0 + told[0:1] + lanes[4:5]
    shift = told[1:2] + lanes[5:6]
    vectors_ref[...] = row_tile([lanes[0:1], lanes[1:2], lanes[2:3], lanes[3:4], scale, shift])


def assemble(maps, cells, me, piece_refs, index):
    rows = C // len(piece_refs)
    for partner, piece_ref in enumerate(piece_refs):
        maps[own_rows(me, partner, rows), 0:cells] = piece_ref[index]


def disperse(piece_refs, index, me, output, cells):
    rows = C // len(piece_refs)
    for partner, piece_ref in enumerate(piece_refs):
        piece_ref[index] = output[own_rows(me, partner, rows), 0:cells]


def first_conv_kernel(partners, first, final, me_ref, live_ref, told_ref, weights_ref, *refs):
    piece_refs = refs[:partners]
    conv_ref, maps_ref, state_ref, stack, state = refs[-5:]
    step = pl.program_id(0)
    count = conv_ref.shape[0]

    @pl.when(step == 0)
    def _():
        state[...] = refs[partners][...] if first else jnp.zeros_like(state)

    merged = [column(state, k) for k in range(3)]
    for image in range(count):
        maps_ref[image, :, CELLS_TWO // 128 * 128 :] = jnp.zeros((C, LANES_TWO - CELLS_TWO // 128 * 128), BF16)
        assemble(maps_ref.at[image], CELLS_TWO, me_ref[0], piece_refs, image)
        stack_sideways(cut(maps_ref[image], WIDE), MAP, stack.at[image])
        conv = conv_ahead(weights_ref, stack.at[image], MAP)
        write(conv_ref.at[image], conv)
        mean, spread = moments(conv, CELLS_TWO)
        live = live_ref[first + step * count + image]
        merged = merge_moments(merged, live, mean, spread, CELLS_TWO)
    state[...] = column_tile(merged)

    @pl.when(step == pl.num_programs(0) - 1)
    def _():
        if final:
            turned = state[...].T
            spread_rows(row_tile([turned[1:2], turned[2:3], turned[0:1], row(told_ref, 0)], SENT), state_ref)
        else:
            state_ref[...] = state[...]


def middle_kernel(
    partners, me_ref, live_ref, heard_ref, vectors_ref, pool_a_ref, pool_b_ref, weights_ref, conv_ref, *refs
):
    hidden_ref, conv_three_ref, norm_ref, levels_ref, sums_ref, columns, state, stack = refs[-8:]
    piece_refs = refs[-8 - partners : -8]
    step = pl.program_id(0)
    count = conv_ref.shape[0]

    @pl.when(step == 0)
    def _():
        middle, factor, variance, extent = slice_norm(heard_ref)
        norm_ref[...] = row_tile([middle, factor, variance, extent])
        columns[...] = as_columns(row_tile([middle, row(vectors_ref, 0) * factor, row(vectors_ref, 1)]))
        state[...] = jnp.zeros_like(state)

    merged = [column(state, k) for k in range(3)]
    active_squares, hidden_squares = column(state, 3), column(state, 4)
    lives = [live_ref[step * count + image] for image in range(count)]

    def activate(image):
        pre = (conv_ref[image] - column(columns, 0)) * column(columns, 1) + column(columns, 2)
        active = pre * gelu_gate(pre)
        counted = trim(active, 0, CELLS_TWO)
        return halves(active), lives[image] * lane_sum(counted * counted)

    def pool(split):
        (left,) = dot_halves(split[:, :1152], pool_a_ref)
        (right,) = dot_halves(split[:, 896:], pool_b_ref)
        return jnp.concatenate([left, right], axis=1)

    split, squares = activate(0)
    for image in range(count):
        hidden = lives[image] * pool(split)
        active_squares = active_squares + squares
        if image + 1 < count:
            split, squares = activate(image + 1)
        hidden_squares = hidden_squares + lane_sum(hidden * hidden)
        hidden_low = hidden.astype(BF16)
        hidden_ref[image] = hidden_low
        disperse(piece_refs, image, me_ref[0], hidden_ref.at[image], CELLS_THREE)
        stack_sideways(cut(hidden_low, WIDE), HALF, stack.at[image])
        conv = conv_ahead(weights_ref, stack.at[image], HALF)
        write(conv_three_ref.at[image], conv)
        mean, spread = moments(conv, CELLS_THREE)
        merged = merge_moments(merged, lives[image], mean, spread, CELLS_THREE)
    state[...] = column_tile([*merged, active_squares, hidden_squares])

    @pl.when(step == pl.num_programs(0) - 1)
    def _():
        turned = state[...].T
        spread_rows(row_tile([turned[k : k + 1] for k in (1, 2, 0)], SENT), sums_ref)
        levels_ref[...] = row_tile([level_row([column(state, 3), column(state, 4)])])


def top_kernel(
    partners, me_ref, live_ref, heard_ref, own_ref, before_ref, vectors_ref, pool_ref, spread_ref, conv_ref, *refs
):
    target_refs = refs[:partners]
    piece_refs = refs[partners : 2 * partners]
    grad_ref, norm_ref, levels_ref, sums_ref, columns, target, output, totals = refs[2 * partners :]
    step = pl.program_id(0)
    count = conv_ref.shape[0]

    @pl.when(step == 0)
    def _():
        middle, factor, variance, extent = slice_norm(heard_ref)
        norm_ref[...] = row_tile([middle, factor, variance, extent])
        columns[...] = as_columns(row_tile([middle, factor] + [row(vectors_ref, k) for k in (2, 3, 4, 5)]))
        target[...] = jnp.zeros_like(target)
        totals[...] = jnp.zeros_like(totals)

    scale = column(columns, 4)
    slope = scale * column(columns, 2)
    offset = scale * column(columns, 3) + column(columns, 5)
    sums = [jnp.zeros((C, 1), F32)] * 4
    for image in range(count):
        live = live_ref[step * count + image]
        assemble(target.at[image], CELLS_OUT, me_ref[0], target_refs, image)
        normed = (conv_ref[image] - column(columns, 0)) * column(columns, 1)
        filmed = slope * normed + offset
        gate = gelu_gate(filmed)
        active = filmed * gate
        counted = trim(active, 0, CELLS_THREE)
        (pooled,) = dot_halves(halves(active), pool_ref)
        pooled = live * pooled
        output[image] = pooled.astype(BF16)
        disperse(piece_refs, image, me_ref[0], output.at[image], CELLS_OUT)
        spread = jnp.dot(target[image], spread_ref[...], preferred_element_type=F32)
        grad_filmed = live * spread * gelu_slope(filmed, gate)
        grad_ref[image] = scale * grad_filmed
        parts = (
            lane_sum(grad_filmed),
            lane_sum(grad_filmed * normed),
            live * lane_sum(counted * counted),
            lane_sum(pooled * pooled),
        )
        sums = [total + part for total, part in zip(sums, parts)]
    totals[...] += column_tile(sums)

    @pl.when(step == pl.num_programs(0) - 1)
    def _():
        turned = totals[...].T
        shift_sum, scale_sum = turned[0:1], turned[1:2]
        film_scale = row(vectors_ref, 4)
        slope = film_scale * row(vectors_ref, 2) * row(norm_ref, 1)
        offset = film_scale * row(vectors_ref, 3) + row(vectors_ref, 5)
        extent = own_ref[0, 2:3, :]
        away = own_ref[0, 0:1, :] - row(norm_ref, 0)
        filmed_squares = (
            slope * slope * (own_ref[0, 1:2, :] + extent * away * away)
            + 2.0 * slope * offset * extent * away
            + extent * offset * offset
        )
        spread_rows(
            row_tile([shift_sum, scale_sum, film_scale * shift_sum, film_scale * scale_sum], SENT), sums_ref
        )
        nothing = jnp.zeros((C, 1), F32)
        others = level_row([nothing, nothing, nothing, column(totals, 2), column(totals, 3)])
        lanes = lane_ids(C)
        filmed_total = lane_sum(filmed_squares)
        levels_ref[...] = before_ref[...] + row_tile([others + jnp.where(lanes == 2, filmed_total, 0.0)])


def norm_back(live, columns, grad, away, cells):
    scaled = [live * column(columns, k) for k in (1, 2, 3)]
    error = grad.astype(F32) * scaled[0] - scaled[1] - away.astype(F32) * scaled[2]
    return trim(error, 0, cells).astype(BF16)


def norm_back_columns(norm_ref, gain, bias_sum, gain_sum):
    factor, extent = row(norm_ref, 1), row(norm_ref, 3)
    front = gain * factor
    return as_columns(
        row_tile([row(norm_ref, 0), front, front * bias_sum / extent, front * factor * gain_sum / extent])
    )


def back_kernel(
    live_ref,
    heard_ref,
    norm_three_ref,
    norm_two_ref,
    levels_ref,
    vectors_ref,
    weights_ref,
    unpool_a_ref,
    unpool_b_ref,
    grad_ref,
    conv_three_ref,
    conv_two_ref,
    *refs,
):
    out_ref, error_ref, sums_ref, columns_three, columns_two, totals, upright = refs[-7:]
    step = pl.program_id(0)
    count = conv_two_ref.shape[0]

    @pl.when(step == 0)
    def _():
        sums = jnp.sum(heard_ref[...], axis=0)
        columns_three[...] = norm_back_columns(norm_three_ref, row(vectors_ref, 2), sums[2:3], sums[3:4])
        columns_two[...] = as_columns(
            row_tile([row(norm_two_ref, 0), row(vectors_ref, 0) * row(norm_two_ref, 1), row(vectors_ref, 1)])
        )
        totals[...] = jnp.zeros_like(totals)

    grad_tile = product_tile = jnp.zeros((C, C), F32)
    for image in range(count):
        away = conv_three_ref[image] - column(columns_three, 0)
        error = norm_back(live_ref[step * count + image], columns_three, grad_ref[image], away, CELLS_THREE)
        error_ref[image] = error
        stack_upright(cut(error, WIDE), HALF, upright.at[image])
    split = jnp.concatenate(
        [
            halves(jnp.concatenate(conv_behind(weights_ref, upright.at[image], HALF), axis=1))
            for image in range(count)
        ],
        axis=0,
    )
    for image in range(count):
        both = split[2 * C * image : 2 * C * (image + 1)]
        for first, (half, unpool_ref) in enumerate(((both[:, :256], unpool_a_ref), (both[:, 128:], unpool_b_ref))):
            for start, stop in ((0, 384), (384, 640), (640, 896)):
                (spread,) = dot_halves(half, unpool_ref.at[:, start:stop])
                cells = slice(first * 896 + start, first * 896 + stop)
                away = conv_two_ref[image, :, cells] - column(columns_two, 0)
                pre = away * column(columns_two, 1) + column(columns_two, 2)
                grad_pre = spread * gelu_slope(pre, gelu_gate(pre))
                out_ref[image, :, cells] = grad_pre
                grad_tile = grad_tile + sum(cut(grad_pre, 128))
                product_tile = product_tile + sum(cut(grad_pre * away, 128))
    grad_sum = column(totals, 0) + lane_sum(grad_tile)
    product_sum = column(totals, 1) + lane_sum(product_tile)
    totals[...] = column_tile([grad_sum, product_sum])

    @pl.when(step == pl.num_programs(0) - 1)
    def _():
        turned = totals[...].T
        normed_sum = turned[1:2] * row(norm_two_ref, 1)
        spread_rows(row_tile([turned[0:1], normed_sum, levels_ref[0:1, :]], SENT), sums_ref)


def split_filter(product, filter_ref):
    partners, _, rows, _ = filter_ref.shape
    for tap in range(3):
        for owner in range(partners):
            filter_ref[owner, tap] = product[tap * C + owner * rows : tap * C + (owner + 1) * rows]


def filter_three_kernel(error_ref, hidden_ref, *refs):
    filter_ref, product, stack, upright = refs[-4:]
    step = pl.program_id(0)
    count = error_ref.shape[0]

    @pl.when(step == 0)
    def _():
        product[...] = jnp.zeros_like(product)

    for image in range(count):
        stack_upright(cut(error_ref[image], WIDE), HALF, upright.at[image])
        stack_sideways(cut(hidden_ref[image], WIDE), HALF, stack.at[image])
        product[...] += across_cells(upright.at[image], stack.at[image])

    @pl.when(step == pl.num_programs(0) - 1)
    def _():
        split_filter(product, filter_ref)


def last_columns(heard_ref, norm_ref, vectors_ref):
    sums = jnp.sum(heard_ref[...], axis=0)
    return norm_back_columns(norm_ref, row(vectors_ref, 0), sums[0:1], sums[1:2])


def last_conv_kernel(
    partners,
    near,
    first,
    steps,
    me_ref,
    live_ref,
    heard_ref,
    norm_ref,
    vectors_ref,
    weights_ref,
    grad_ref,
    conv_ref,
    *refs,
):
    far = partners - near
    piece_refs, (columns, output, upright) = refs[-3 - near - far * len(steps) : -3], refs[-3:]
    step = pl.program_id(0)
    count = grad_ref.shape[0]

    @pl.when(step == 0)
    def _():
        columns[...] = last_columns(heard_ref, norm_ref, vectors_ref)

    for image in range(count):
        live = live_ref[first + step * count + image]
        away = conv_ref[image] - column(columns, 0)
        error = norm_back(live, columns, grad_ref[image], away, CELLS_TWO)
        stack_upright(cut(error, WIDE), MAP, upright.at[image])
        write(output.at[image], [block.astype(BF16) for block in conv_behind(weights_ref, upright.at[image], MAP)])
    rows = C // partners
    start = 0
    for place, length in enumerate(steps):

        @pl.when((step >= start) & (step < start + length))
        def _():
            for image in range(count):
                for partner in range(partners):
                    piece_ref = piece_refs[partner if partner < near else near + place * far + partner - near]
                    piece_ref[image] = output[image, own_rows(me_ref[0], partner, rows), 0:CELLS_TWO]

        start += length


def last_filter_kernel(live_ref, heard_ref, norm_ref, vectors_ref, grad_ref, conv_ref, maps_ref, *refs):
    product, columns, stack, upright = refs[-4:]
    step = pl.program_id(0)
    count = grad_ref.shape[0]

    @pl.when(step == 0)
    def _():
        columns[...] = last_columns(heard_ref, norm_ref, vectors_ref)
        product[...] = jnp.zeros_like(product)

    for image in range(count):
        away = conv_ref[image] - column(columns, 0)
        error = norm_back(live_ref[step * count + image], columns, grad_ref[image], away, CELLS_TWO)
        stack_upright(cut(error, WIDE), MAP, upright.at[image])
        stack_sideways(cut(maps_ref[image], WIDE), MAP, stack.at[image])
        product[...] += across_cells(upright.at[image], stack.at[image])


def split_kernel(product_ref, *refs):
    split_filter(product_ref, refs[-1])


def strips_kernel(heard_ref, *refs):
    out_ref = refs[-1]
    out_ref[...] = jnp.broadcast_to(jnp.sum(heard_ref[...].astype(F32), axis=0)[None], out_ref.shape)


def one_hot(rows, columns, wanted):
    row_ids = lax.broadcasted_iota(jnp.int32, (rows, columns), 0)
    column_ids = lax.broadcasted_iota(jnp.int32, (rows, columns), 1)
    return jnp.where(wanted(row_ids, column_ids), 1.0, 0.0)


def exact_dot(left, right, contract=((1,), (0,))):
    return lax.dot_general(left, right, (contract, ((), ())), precision=PRECISE, preferred_element_type=F32)


def finish_kernel(
    partners,
    group,
    here_ref,
    me_ref,
    heard_two_ref,
    heard_top_ref,
    heard_back_ref,
    norm_two_ref,
    norm_three_ref,
    vectors_ref,
    film_ref,
    *refs,
):
    film_w_ref, film_b_ref, context_ref, *sum_refs, levels_ref, product = refs[-9:]
    devices = heard_two_ref.shape[0]
    tasks = devices // group
    contexts = context_ref.shape[0]
    rows = C // partners
    entries = film_ref.shape[2]
    turn = (C - me_ref[0] * rows) % C

    def own_lanes(values):
        return pltpu.roll(values, turn, 1)[:, :rows]

    by_task = one_hot(tasks, devices, lambda t, d: d // group == t)
    of_task = one_hot(
        tasks, devices, lambda t, d: (d // partners == t // contexts) & (d % partners == t % contexts)
    )
    mine = one_hot(contexts, devices, lambda t, d: d // group == here_ref[0] * contexts + t)
    shift, normed = heard_top_ref[:, 0, :], heard_top_ref[:, 1, :]
    scale = row(vectors_ref, 2) * normed + row(vectors_ref, 3) * shift
    told = exact_dot(of_task, heard_two_ref[:, 3, :])
    total = jnp.zeros((contexts, entries), F32)
    for kind, grads in enumerate((scale, shift)):
        grads_by_task = exact_dot(by_task, grads)
        product[...] = exact_dot(grads_by_task, told, ((0,), (0,)))
        film_w_ref[kind] = product[pl.ds(pl.multiple_of(me_ref[0] * rows, rows), rows), :entries]
        film_b_ref[kind : kind + 1] = own_lanes(jnp.sum(grads_by_task, axis=0, keepdims=True))
        total = total + exact_dot(exact_dot(mine, grads), film_ref[kind])
    context_ref[...] = total

    back = jnp.sum(heard_back_ref[...], axis=0)
    top = jnp.sum(heard_top_ref[...], axis=0)
    for sum_ref, sums in zip(sum_refs, (back[1:2], back[0:1], top[3:4], top[2:3])):
        sum_ref[...] = own_lanes(sums)[0]

    live = norm_two_ref[3:4, 0:1] * (1.0 / CELLS_TWO)
    lanes = lane_ids(C)

    def mean_square(norm_ref, gain, shift):
        factor, variance = row(norm_ref, 1), row(norm_ref, 2)
        return jnp.sum(gain * gain * variance * factor * factor + shift * shift, axis=1, keepdims=True) * (1.0 / C)

    def mean_conv(norm_ref):
        middle = row(norm_ref, 0)
        return jnp.sum(row(norm_ref, 2) + middle * middle, axis=1, keepdims=True) * (1.0 / C)

    known = (
        mean_conv(norm_two_ref),
        mean_square(norm_two_ref, row(vectors_ref, 0), row(vectors_ref, 1)),
        back[2:3, 0:1] / (live * (C * CELLS_TWO)),
        back[2:3, 1:2] / (live * (C * CELLS_THREE)),
        mean_conv(norm_three_ref),
        mean_square(norm_three_ref, row(vectors_ref, 2), row(vectors_ref, 3)),
        back[2:3, 2:3] / (live * (C * CELLS_THREE)),
        back[2:3, 3:4] / (live * (C * CELLS_THREE)),
        back[2:3, 4:5] / (live * (C * CELLS_OUT)),
    )
    level = jnp.zeros((1, C), F32)
    for place, value in enumerate(known):
        level = jnp.where(lanes == place, value, level)
    levels_ref[...] = jnp.sqrt(level)[0, : levels_ref.shape[0]]


def pool_matrix(side, width, out_width):
    half = side // 2
    matrix = np.zeros((width, out_width), np.float32)
    for row in range(2 * half):
        for column in range(2 * half):
            matrix[row * side + column, (row // 2) * half + column // 2] = 0.25
    return matrix


def lasting(microseconds):
    return pl.CostEstimate(
        flops=int(microseconds * 1.1e9), bytes_accessed=int(microseconds * 3.5e6), transcendentals=0
    )


def smem():
    return pl.BlockSpec(memory_space=pltpu.SMEM)


def anywhere(count):
    return [pl.BlockSpec(memory_space=pl.ANY)] * count


def whole(*shape):
    return pl.BlockSpec(shape, lambda n: (0,) * len(shape))


def each(*shape, first=0, count=1):
    return pl.BlockSpec((count, *shape), lambda n: (first + n,) + (0,) * len(shape))


def pack(maps, me, images_each, wants, earlier=()):
    rows, slots, cells = maps.shape
    group = CAP // images_each
    halves = 2
    block = wants[0][0] // group
    return pl.pallas_call(
        functools.partial(pack_kernel, images_each, group, wants),
        grid_spec=pltpu.PrefetchScalarGridSpec(
            num_scalar_prefetch=1,
            grid=(halves,),
            in_specs=[
                pl.BlockSpec((rows // halves, CAP, cells), lambda n, me_ref: (n, (me_ref[0] // group) ^ block, 0)),
                *anywhere(len(earlier)),
            ],
            out_specs=[
                pl.BlockSpec((count, rows // halves, cells), lambda n, me_ref: (0, n, 0)) for _, _, count in wants
            ],
        ),
        out_shape=[jax.ShapeDtypeStruct((count, rows, cells), maps.dtype) for _, _, count in wants],
        compiler_params=kernel_params(),
        name="pack",
        cost_estimate=lasting(2.5),
    )(me, maps, *earlier)


def unpack(arrays, me, images_each, dtype, place, outs=(), earlier=()):
    partners = len(arrays[0])
    group = CAP // images_each
    halves = 2
    given, specs, counts, shapes, out_specs = [], [], [], [], []
    for pieces in arrays:
        here = pieces[place * group : (place + 1) * group]
        counts.append(tuple(tuple(piece.shape[0] for piece in parts) for parts in here))
        rows, cells = here[0][0].shape[1:]
        for piece in (piece for parts in here for piece in parts):
            given.append(piece)
            specs.append(pl.BlockSpec((piece.shape[0], rows // halves, cells), lambda n, me_ref: (0, n, 0)))
        shapes.append(jax.ShapeDtypeStruct((rows, partners * images_each, cells), dtype))
        out_specs.append(
            pl.BlockSpec((rows // halves, CAP, cells), lambda n, me_ref: (n, (me_ref[0] // group) ^ place, 0))
        )
    aliases = {1 + len(given) + k: k for k in range(len(outs))}
    given += [*outs, *earlier]
    specs += anywhere(len(given) - len(specs))
    return pl.pallas_call(
        functools.partial(unpack_kernel, counts),
        grid_spec=pltpu.PrefetchScalarGridSpec(
            num_scalar_prefetch=1, grid=(halves,), in_specs=specs, out_specs=out_specs
        ),
        out_shape=shapes,
        input_output_aliases=aliases,
        compiler_params=kernel_params(),
        name="unpack",
        cost_estimate=lasting(2.0),
    )(me, *given)


def local(
    images,
    counts,
    context,
    filter_two,
    gain_two,
    shift_two,
    filter_three,
    gain_three,
    shift_three,
    film_weight,
    film_bias,
    cotangent,
    *,
    partners,
    columns,
):
    devices = partners * columns
    rows, slots = images.shape[:2]
    images_each = slots // partners
    group = CAP // images_each
    one = min(images_each, 2)
    pair, some = min(images_each, 2), min(images_each, 4)
    position = lax.axis_index("tensor")
    me = jnp.reshape(position, (1,)).astype(jnp.int32)

    def swap(value, partner):
        if partner == 0:
            return value
        return lax.ppermute(value, "tensor", [(i, i ^ partner) for i in range(partners)])

    def share(copies):
        return lax.all_to_all(copies, ("dp", "tensor"), 0, 0)

    near = 2
    half, quarter = images_each // 2, images_each // 4
    sizes_in = (half, quarter, quarter) if quarter >= pair else (half, half)
    half = images_each // 2
    calls_out = (*[(pair,)] * (half // pair), (half,))
    starts_in = [sum(sizes_in[:part]) for part in range(len(sizes_in))]
    counts_of = [(images_each,) if partner < near else sizes_in for partner in range(partners)]
    far = [partner for partner in reversed(range(partners)) if partner >= near]
    maps = [[None] * len(counts_of[partner]) for partner in range(partners)]

    def send_in(some_parts, whole_near, earlier):
        for block in reversed(range(partners // group)):
            wants = [
                (partner, starts_in[part], sizes_in[part])
                for part in some_parts
                for partner in far
                if partner // group == block
            ]
            if block == 0 and whole_near:
                wants += [(partner, 0, images_each) for partner in range(near)]
            if wants:
                sent = pack(images, me, images_each, wants, earlier)
                for piece, (partner, first, _) in zip(sent, wants):
                    maps[partner][starts_in.index(first)] = swap(piece, partner)
                earlier = (*earlier, sent[0])
        return earlier

    first_sent = send_in((0,), True, ())
    entries = film_weight.shape[0]
    bundle = pl.pallas_call(
        bundle_kernel,
        in_specs=[pl.BlockSpec(memory_space=pltpu.VMEM)] * 8 + anywhere(1),
        out_shape=jax.ShapeDtypeStruct((7 * rows + 16, 3 * C), BF16),
        compiler_params=kernel_params(0),
        name="bundle",
        cost_estimate=lasting(1.0),
    )(
        jnp.transpose(filter_two, (2, 3, 0, 1)),
        jnp.transpose(filter_three, (2, 3, 0, 1)),
        jnp.transpose(film_weight, (1, 2, 0)),
        film_bias,
        *[vector[None] for vector in (gain_two, shift_two, gain_three, shift_three)],
        first_sent[0],
    )
    bundles = {0: bundle}
    bit = partners // 2
    while bit:
        bundles.update({partner | bit: swap(piece, bit) for partner, piece in bundles.items()})
        bit //= 2

    sent_in = {
        part: send_in((part,), False, (maps[far[0]][0],))
        for part in range(1, len(sizes_in))
    }

    task = position // group
    slot = (position % group) * images_each + jnp.arange(images_each, dtype=jnp.int32)
    limit = lax.dynamic_index_in_dim(counts, task, 0, keepdims=False)
    live = (slot < limit).astype(F32)
    ahead_two, behind_two, ahead_three, behind_three, film, vectors = pl.pallas_call(
        functools.partial(unbundle_kernel, partners),
        in_specs=[smem(), smem(), *[pl.BlockSpec(memory_space=pltpu.VMEM)] * (1 + partners)],
        out_shape=[jax.ShapeDtypeStruct((3 * C, 3 * C), BF16)] * 4
        + [jax.ShapeDtypeStruct((2, C, entries), F32), jax.ShapeDtypeStruct((8, C), F32)],
        compiler_params=kernel_params(0),
        name="unbundle",
        cost_estimate=lasting(2.0),
    )(me, jnp.reshape(task, (1,)).astype(jnp.int32), context, *[bundles[partner] for partner in range(partners)])

    told = lax.dynamic_index_in_dim(context, position % context.shape[0], 0)
    told = jnp.pad(told, ((0, 7), (0, C - entries)))

    conv_two = whole_maps = state = None
    for part, (first, count) in enumerate(zip(starts_in, sizes_in)):
        given = [maps[partner][0 if partner < near else part] for partner in range(partners)]
        specs = [
            each(rows, CELLS_TWO, first=first // pair if partner < near else 0, count=pair)
            for partner in range(partners)
        ]
        aliases = {}
        final = part == len(sizes_in) - 1
        if part:
            aliases = {5 + partners: 0, 6 + partners: 1}
            given = given + [state, conv_two, whole_maps]
            specs = specs + [whole(C, C), *anywhere(2)]
        waits = [] if final else [sent_in[part + 1][-1]]
        given = given + waits
        specs = specs + anywhere(len(waits))
        conv_two, whole_maps, state = pl.pallas_call(
            functools.partial(first_conv_kernel, partners, first, final),
            grid=(count // pair,),
            in_specs=[smem(), smem(), whole(8, C), whole(3 * C, 3 * C), *specs],
            out_specs=[
                each(C, LANES_TWO, first=first // pair, count=pair),
                each(C, LANES_TWO, first=first // pair, count=pair),
                whole(devices, SENT, C) if final else whole(C, C),
            ],
            out_shape=[
                jax.ShapeDtypeStruct((images_each, C, LANES_TWO), F32),
                jax.ShapeDtypeStruct((images_each, C, LANES_TWO), BF16),
                jax.ShapeDtypeStruct((devices, SENT, C) if final else (C, C), F32),
            ],
            scratch_shapes=[
                pltpu.VMEM((pair, 3 * C, LANES_TWO), BF16),
                pltpu.VMEM((C, C), F32),
            ],
            input_output_aliases=aliases,
            compiler_params=kernel_params(),
            name="first_conv",
            cost_estimate=lasting(2.3 * count),
        )(me, live, told, ahead_two, *given)
    heard_two = share(state)
    turned = jnp.transpose(cotangent, (1, 0, 2))
    targets = [
        swap(lax.dynamic_slice_in_dim(turned, (position ^ partner) * images_each, images_each, 0), partner)
        for partner in range(partners)
    ]

    pool = pool_matrix(MAP, LANES_TWO, LANES_THREE)
    pool_out = pool_matrix(HALF, LANES_THREE, LANES_OUT)
    *block_pieces, hidden, conv_three, norm_two, levels, sums_three = pl.pallas_call(
        functools.partial(middle_kernel, partners),
        grid=(images_each // pair,),
        in_specs=[
            smem(),
            smem(),
            whole(devices, SENT, C),
            whole(8, C),
            whole(1152, 256),
            whole(896, 256),
            whole(3 * C, 3 * C),
            each(C, LANES_TWO, count=pair),
        ],
        out_specs=[each(rows, CELLS_THREE, count=pair)] * partners
        + [each(C, LANES_THREE, count=pair), each(C, LANES_THREE, count=pair), whole(8, C), whole(8, C), whole(devices, SENT, C)],
        out_shape=[jax.ShapeDtypeStruct((images_each, rows, CELLS_THREE), BF16)] * partners
        + [
            jax.ShapeDtypeStruct((images_each, C, LANES_THREE), BF16),
            jax.ShapeDtypeStruct((images_each, C, LANES_THREE), F32),
            jax.ShapeDtypeStruct((8, C), F32),
            jax.ShapeDtypeStruct((8, C), F32),
            jax.ShapeDtypeStruct((devices, SENT, C), F32),
        ],
        scratch_shapes=[
            pltpu.VMEM((C, C), F32),
            pltpu.VMEM((C, C), F32),
            pltpu.VMEM((pair, 3 * C, LANES_THREE), BF16),
        ],
        compiler_params=kernel_params(),
        name="middle",
            cost_estimate=lasting(2.0 * images_each),
    )(
        me,
        live,
        heard_two,
        vectors,
        jnp.asarray(pool[:1152, :256], BF16),
        jnp.asarray(pool[896:, 256:], BF16),
        ahead_three,
        conv_two,
    )
    heard_three = share(sums_three)

    *out_pieces, grad_three, norm_three, levels, sums_top = pl.pallas_call(
        functools.partial(top_kernel, partners),
        grid=(images_each // some,),
        in_specs=[
            smem(),
            smem(),
            whole(devices, SENT, C),
            whole(1, SENT, C),
            whole(8, C),
            whole(8, C),
            whole(LANES_THREE, LANES_OUT),
            whole(LANES_OUT, LANES_THREE),
            each(C, LANES_THREE, count=some),
            *[each(rows, CELLS_OUT, count=some)] * partners,
        ],
        out_specs=[each(rows, CELLS_OUT, count=some)] * partners
        + [each(C, LANES_THREE, count=some), whole(8, C), whole(8, C), whole(devices, SENT, C)],
        out_shape=[jax.ShapeDtypeStruct((images_each, rows, CELLS_OUT), BF16)] * partners
        + [
            jax.ShapeDtypeStruct((images_each, C, LANES_THREE), F32),
            jax.ShapeDtypeStruct((8, C), F32),
            jax.ShapeDtypeStruct((8, C), F32),
            jax.ShapeDtypeStruct((devices, SENT, C), F32),
        ],
        scratch_shapes=[
            pltpu.VMEM((C, C), F32),
            pltpu.VMEM((some, C, LANES_OUT), BF16),
            pltpu.VMEM((some, C, LANES_OUT), BF16),
            pltpu.VMEM((C, C), F32),
        ],
        compiler_params=kernel_params(),
        name="top",
            cost_estimate=lasting(0.8 * images_each),
    )(
        me,
        live,
        heard_three,
        sums_three,
        levels,
        vectors,
        jnp.asarray(pool_out, BF16),
        jnp.asarray(pool_out.T, BF16),
        conv_three,
        *targets,
    )
    heard_top = share(sums_top)
    block_two = [[swap(block_pieces[k], k)] for k in range(partners)]
    out_pieces = [[swap(out_pieces[k], k)] for k in range(partners)]

    filter_shape = jax.ShapeDtypeStruct((partners, 2, 3, rows, 3 * C), F32)

    def filter_spec(block):
        return pl.BlockSpec((partners, None, 3, rows, 3 * C), lambda n: (0, block, 0, 0, 0))

    grad_two, error_three, sums_two = pl.pallas_call(
        back_kernel,
        grid=(images_each // pair,),
        in_specs=[
            smem(),
            whole(devices, SENT, C),
            whole(8, C),
            whole(8, C),
            whole(8, C),
            whole(8, C),
            whole(3 * C, 3 * C),
            whole(256, 896),
            whole(384, 896),
            each(C, LANES_THREE, count=pair),
            each(C, LANES_THREE, count=pair),
            each(C, LANES_TWO, count=pair),
        ],
        out_specs=[
            each(C, LANES_TWO, count=pair),
            each(C, LANES_THREE, count=pair),
            whole(devices, SENT, C),
        ],
        out_shape=[
            jax.ShapeDtypeStruct((images_each, C, LANES_TWO), F32),
            jax.ShapeDtypeStruct((images_each, C, LANES_THREE), BF16),
            jax.ShapeDtypeStruct((devices, SENT, C), F32),
        ],
        scratch_shapes=[
            pltpu.VMEM((C, C), F32),
            pltpu.VMEM((C, C), F32),
            pltpu.VMEM((C, C), F32),
            pltpu.VMEM((pair, 3 * C, LANES_THREE), BF16),
        ],
        compiler_params=kernel_params(),
        name="back",
            cost_estimate=lasting(2.0 * images_each),
    )(
        live,
        heard_top,
        norm_three,
        norm_two,
        levels,
        vectors,
        behind_three,
        jnp.asarray(pool[:896, :256].T, BF16),
        jnp.asarray(pool[896:, 128:].T, BF16),
        grad_three,
        conv_three,
        conv_two,
    )
    heard_back = share(sums_two)

    filter_sums = pl.pallas_call(
        filter_three_kernel,
        grid=(images_each // some,),
        in_specs=[*[each(C, LANES_THREE, count=some)] * 2, *anywhere(1)],
        out_specs=filter_spec(1),
        out_shape=filter_shape,
        scratch_shapes=[
            pltpu.VMEM((3 * C, 3 * C), F32),
            pltpu.VMEM((some, 3 * C, LANES_THREE), BF16),
            pltpu.VMEM((some, 3 * C, LANES_THREE), BF16),
        ],
        compiler_params=kernel_params(),
        name="filter_three",
        cost_estimate=lasting(5.0),
    )(error_three, hidden, sums_two)

    returned = [[] for partner in range(partners)]
    waits = [filter_sums, *(pieces[0] for pieces in (*block_two, *out_pieces))]
    common = [heard_back, norm_two, vectors]
    common_specs = [whole(devices, SENT, C), whole(8, C), whole(8, C)]
    kept = []
    first = 0
    for sizes in calls_out:
        count = sum(sizes)
        steps = [some // one for some in sizes]
        out_specs = [each(rows, CELLS_TWO, first=first // one, count=one)] * near
        out_shape = [jax.ShapeDtypeStruct((images_each, rows, CELLS_TWO), BF16)] * near
        for place, length in enumerate(steps):
            start = sum(steps[:place])
            out_specs += [
                pl.BlockSpec(
                    (one, rows, CELLS_TWO),
                    lambda n, start=start, length=length: (jnp.clip(n - start, 0, length - 1), 0, 0),
                )
            ] * len(far)
            out_shape += [jax.ShapeDtypeStruct((length * one, rows, CELLS_TWO), BF16)] * len(far)
        inputs = [me, live, *common, behind_two, grad_two, conv_two]
        pieces = pl.pallas_call(
            functools.partial(last_conv_kernel, partners, near, first, steps),
            grid=(count // one,),
            in_specs=[
                smem(),
                smem(),
                *common_specs,
                whole(3 * C, 3 * C),
                *[each(C, LANES_TWO, first=first // one, count=one)] * 2,
                *anywhere(len(waits) + len(kept)),
            ],
            out_specs=out_specs,
            out_shape=out_shape,
            scratch_shapes=[
                pltpu.VMEM((C, C), F32),
                pltpu.VMEM((one, C, LANES_TWO), BF16),
                pltpu.VMEM((one, 3 * C, LANES_TWO), BF16),
            ],
            input_output_aliases={len(inputs) + len(waits) + k: k for k in range(len(kept))},
            compiler_params=kernel_params(),
            name="last_conv",
            cost_estimate=lasting(1.5 * count),
        )(*inputs, *waits, *kept)
        kept, waits, first = pieces[:near], [], first + count
        for place in range(len(sizes)):
            for partner in reversed(far):
                returned[partner].append(swap(pieces[near + place * len(far) + partner - near], partner))
        if first == half:
            product = pl.pallas_call(
                last_filter_kernel,
                grid=(images_each // pair,),
                in_specs=[
                    smem(),
                    *common_specs,
                    *[each(C, LANES_TWO, count=pair)] * 3,
                    *anywhere(1),
                ],
                out_specs=whole(3 * C, 3 * C),
                out_shape=jax.ShapeDtypeStruct((3 * C, 3 * C), F32),
                scratch_shapes=[
                    pltpu.VMEM((C, C), F32),
                    pltpu.VMEM((pair, 3 * C, LANES_TWO), BF16),
                    pltpu.VMEM((pair, 3 * C, LANES_TWO), BF16),
                ],
                compiler_params=kernel_params(),
                name="last_filter",
                cost_estimate=lasting(1.2 * images_each),
            )(live, *common, grad_two, conv_two, whole_maps, kept[0])
            waits = [piece for partner in far for piece in returned[partner]]
            product = pl.pallas_call(
                split_kernel,
                grid=(1,),
                in_specs=[whole(3 * C, 3 * C), *anywhere(len(waits))],
                out_specs=filter_spec(0),
                out_shape=filter_shape,
                input_output_aliases={1: 0},
                compiler_params=kernel_params(),
                name="split",
                cost_estimate=lasting(1.5),
            )(product, filter_sums, *waits[:-1])
            waits = [product, *waits]
    for partner in range(near):
        returned[partner].append(swap(kept[partner], partner))

    blocks = ()
    for place in range(partners // group):
        blocks = unpack([block_two, out_pieces], me, images_each, BF16, place, blocks, [kept[0]])
    block_two, block_three = blocks

    contexts = context.shape[0]
    grad_film_w, grad_film_b, grad_context, *norm_sums, levels = pl.pallas_call(
        functools.partial(finish_kernel, partners, group),
        in_specs=[smem(), smem(), *[pl.BlockSpec(memory_space=pltpu.VMEM)] * 7, *anywhere(1)],
        out_shape=[
            jax.ShapeDtypeStruct((2, rows, entries), F32),
            jax.ShapeDtypeStruct((2, rows), F32),
            jax.ShapeDtypeStruct((contexts, entries), F32),
            *[jax.ShapeDtypeStruct((rows,), F32)] * 4,
            jax.ShapeDtypeStruct((9,), F32),
        ],
        scratch_shapes=[pltpu.VMEM((C, C), F32)],
        compiler_params=kernel_params(0),
        name="finish",
        cost_estimate=lasting(2.0),
    )(
        jnp.reshape(lax.axis_index("dp"), (1,)).astype(jnp.int32),
        me,
        heard_two,
        heard_top,
        heard_back,
        norm_two,
        norm_three,
        vectors,
        film,
        kept[0],
    )

    strip = 6 * rows // columns
    heard = lax.all_to_all(product.reshape(devices, strip, 3 * C), ("tensor", "dp"), 0, 0)
    strips = pl.pallas_call(
        strips_kernel,
        in_specs=[pl.BlockSpec(memory_space=pltpu.VMEM), *anywhere(2)],
        out_shape=jax.ShapeDtypeStruct((columns, strip, 3 * C), F32),
        compiler_params=kernel_params(0),
        name="strips",
        cost_estimate=lasting(1.5),
    )(heard, block_two, norm_sums[0])
    strips = lax.all_to_all(strips, "dp", 0, 0)
    grad_filters = jnp.transpose(strips.reshape(2, 3, rows, 3, C), (0, 2, 4, 1, 3))

    grad_images = ()
    for place in range(partners // group):
        waits = () if grad_images else (kept[0],)
        grad_images = unpack([returned], me, images_each, F32, place, grad_images, waits)
    (grad_images,) = grad_images

    return (
        block_two,
        block_three,
        grad_images,
        grad_filters[0],
        norm_sums[0],
        norm_sums[1],
        grad_filters[1],
        norm_sums[2],
        norm_sums[3],
        jnp.transpose(grad_film_w, (2, 0, 1)),
        grad_film_b,
        grad_context,
        levels,
    )


def solution(mesh):
    step = functools.partial(local, partners=mesh.shape["tensor"], columns=mesh.shape["dp"])
    placed = (
        P("tensor", "dp", None),
        P("dp"),
        P("dp", None),
        P("tensor", None, None, None),
        P("tensor"),
        P("tensor"),
        P("tensor", None, None, None),
        P("tensor"),
        P("tensor"),
        P(None, None, "tensor"),
        P(None, "tensor"),
        P("tensor", "dp", None),
    )
    return jax.shard_map(
        step,
        mesh=mesh,
        in_specs=placed,
        out_specs=(
            P("tensor", "dp", None),
            P("tensor", "dp", None),
            P("tensor", "dp", None),
            P("tensor", None, None, None),
            P("tensor"),
            P("tensor"),
            P("tensor", None, None, None),
            P("tensor"),
            P("tensor"),
            P(None, None, "tensor"),
            P(None, "tensor"),
            P("dp", None),
            P(),
        ),
        check_vma=False,
    )
```
